32 devices in a mesh: dp: 16 (over z, y, core), mp: 2 (over x).
Axes of the slice: x: 2, y: 2, z: 4, core: 2. Of those that a mesh axis runs over, the one named last changes fastest.
Arguments:
- inputs: bfloat16 [16384, 768], P(('dp', 'mp')), may hold values from -6 to 6
- cotangent: bfloat16 [16384, 768], P(('dp', 'mp')), may hold values from -6 to 6
- w_query: bfloat16 [768, 768], replicated, may hold values from -0.21875 to 0.21875
- b_query: bfloat16 [768], replicated, may hold values from -3 to 3
- w_key: bfloat16 [768, 768], replicated, may hold values from -0.21875 to 0.21875
- b_key: bfloat16 [768], replicated, may hold values from -3 to 3
- w_value: bfloat16 [768, 768], replicated, may hold values from -0.21875 to 0.21875
- b_value: bfloat16 [768], replicated, may hold values from -3 to 3
- w_output: bfloat16 [768, 768], replicated, may hold values from -1.25 to 1.25
- b_output: bfloat16 [768], replicated, may hold values from -3 to 3
- norm1_gain: bfloat16 [768], replicated, may hold values from 0.5 to 1.5
- norm1_shift: bfloat16 [768], replicated, may hold values from -3 to 3
- w_inner: bfloat16 [768, 3072], P(None, 'mp'), may hold values from -0.21875 to 0.21875
- b_inner: bfloat16 [3072], P('mp'), may hold values from -3 to 3
- w_outer: bfloat16 [3072, 768], P('mp'), may hold values from -0.109375 to 0.109375
- b_outer: bfloat16 [768], replicated, may hold values from -3 to 3
- norm2_gain: bfloat16 [768], replicated, may hold values from 0.5 to 1.5
- norm2_shift: bfloat16 [768], replicated, may hold values from -3 to 3
- rel_table: bfloat16 [512, 768], replicated, may hold values from -6 to 6
- rel_gain: bfloat16 [768], replicated, may hold values from 0.5 to 1.5
- rel_shift: bfloat16 [768], replicated, may hold values from -3 to 3
- block_group: int32 [32], P(('dp', 'mp')), may hold values from 0 to 2, as said below
- seq_lengths: int32 [32, 4], P(('dp', 'mp')), may hold values from 0 to 512, as said below
Outputs:
- layer_out: float32 [16384, 768], P(('dp', 'mp'))
- input_grad: float32 [16384, 768], P(('dp', 'mp'))
- grad_w_query: float32 [768, 768], replicated
- grad_b_query: float32 [768], replicated
- grad_w_key: float32 [768, 768], replicated
- grad_b_key: float32 [768], replicated
- grad_w_value: float32 [768, 768], replicated
- grad_b_value: float32 [768], replicated
- grad_w_output: float32 [768, 768], replicated
- grad_b_output: float32 [768], replicated
- grad_norm1_gain: float32 [768], replicated
- grad_norm1_shift: float32 [768], replicated
- grad_w_inner: float32 [768, 3072], P(None, 'mp')
- grad_b_inner: float32 [3072], P('mp')
- grad_w_outer: float32 [3072, 768], P('mp')
- grad_b_outer: float32 [768], replicated
- grad_norm2_gain: float32 [768], replicated
- grad_norm2_shift: float32 [768], replicated
- grad_rel_table: float32 [512, 768], replicated
- grad_rel_gain: float32 [768], replicated
- grad_rel_shift: float32 [768], replicated
The draws below stay inside these ranges and needn't reach their ends.
Inputs may be any that keep to these rules, and one draw needn't show every extreme that they name: `block_group`: A block of group 0 holds one sequence of up to 512 tokens, of group 1 two of up to 256, of group 2 four of up to 128. `seq_lengths`: entry s is the live length of the block's sequence s; entries past the group's sequences are 0; every sequence has at least a quarter of its places, and the first sequence of every block fills its places.
All inputs are finite; a program needn't handle non-finite values.
Results may differ from the reference program's by a relative error of at most 0.024.
Values may be sent and summed in bfloat16 or wider, within the bound.
No kernel may reach another device: no remote copies, remote signals or barrier semaphores. Data moves between devices by JAX's collectives and lax.ppermute only.
A program may use at most 256 MiB of HBM per device.

```python
import math
import jax
import jax.numpy as jnp
import numpy as np
from jax import lax

D = 768
HEADS = 12
HEAD_DIM = 64
FF = 3072
BUCKETS = 256
BLOCKS_DEV = 1
BLOCK = 512
BLOCKS = 32
TOKENS = 16384
N_DP = 16
N_MP = 2


def block_kinds(key):
    spots = jax.random.randint(jax.random.fold_in(key, 17), (BLOCKS,), 0, 22)
    kinds = jnp.where(spots < 15, 0, jnp.where(spots < 20, 1, 2))
    full_spot = jax.random.randint(jax.random.fold_in(key, 19), (), 0, BLOCKS)
    other_spot = (full_spot + 1 + jax.random.randint(jax.random.fold_in(key, 23), (), 0, BLOCKS - 1)) % BLOCKS
    places = jnp.arange(BLOCKS)
    kinds = jnp.where(places == full_spot, 0, kinds)
    kinds = jnp.where(places == other_spot, 2, kinds)
    return kinds.astype(jnp.int32)


def draw_block_group(key, part):
    kinds = block_kinds(key)
    return kinds


def draw_seq_lengths(key, part):
    kinds = block_kinds(key)
    key = jax.random.fold_in(key, 5)
    capacity = jnp.right_shift(jnp.int32(BLOCK), kinds)
    drawn = jax.random.randint(key, (BLOCKS, 4), 0, 1 << 20)
    least = capacity // 4
    width_range = capacity - least + 1
    lengths = least[:, None] + drawn % width_range[:, None]
    slot_ids = jnp.arange(4, dtype=jnp.int32)
    seq_count = jnp.left_shift(jnp.int32(1), kinds)
    lengths = jnp.where(slot_ids[None, :] < seq_count[:, None], lengths, 0)
    lengths = jnp.where(slot_ids[None, :] == 0, capacity[:, None], lengths)
    return lengths.astype(jnp.int32)


def shard_levels(key, extent, cuts, low, high):
    def one(position, blocks):
        heights = jax.random.uniform(jax.random.fold_in(jax.random.fold_in(key, 6), position), (blocks,), jnp.float32, low / len(cuts), high / len(cuts))
        return jnp.repeat(jnp.exp(heights), extent[position] // blocks).reshape((-1,) + (1,) * (len(extent) - position - 1))

    factor_of = one(*cuts[0])
    for cut in cuts[1:]:
        factor_of = factor_of * one(*cut)
    return factor_of


def centred(rng, shape, scale, bound, cuts=(), kind=jnp.bfloat16):
    array = jax.random.normal(rng, shape, jnp.float32) * scale
    if len(cuts) > 0:
        array = shard_levels(rng, shape, cuts, -0.22, 0.18) * array
    return jnp.clip(array, min=-bound, max=bound).astype(kind)


def setup_inputs(seed: int = 0) -> dict:
    seeds = jax.random.split(jax.random.key(seed), 24)
    inputs = centred(seeds[0], (TOKENS, D), 1.0, 6.0, ((0, 32),))
    cotangent = centred(seeds[1], (TOKENS, D), 1.0, 6.0, ((0, 32),))
    w_query = centred(seeds[2], (D, D), D ** -0.5, 0.21875)
    b_query = centred(seeds[3], (D,), 0.5, 3.0)
    w_key = centred(seeds[4], (D, D), D ** -0.5, 0.21875)
    b_key = centred(seeds[5], (D,), 0.5, 3.0)
    w_value = centred(seeds[6], (D, D), D ** -0.5, 0.21875)
    b_value = centred(seeds[7], (D,), 0.5, 3.0)
    w_output = centred(seeds[8], (D, D), (D // 32) ** -0.5, 1.25)
    b_output = centred(seeds[9], (D,), 0.5, 3.0)
    norm1_gain = jnp.clip(1.0 + 0.1 * jax.random.normal(seeds[10], (D,), jnp.float32), 0.5, 1.5).astype(jnp.bfloat16)
    norm1_shift = centred(seeds[11], (D,), 0.5, 3.0)
    w_inner = centred(seeds[12], (D, FF), D ** -0.5, 0.21875, ((1, 2),))
    b_inner = centred(seeds[13], (FF,), 0.5, 3.0, ((0, 2),))
    w_outer = centred(seeds[14], (FF, D), FF ** -0.5, 0.109375, ((0, 2),))
    b_outer = centred(seeds[15], (D,), 0.5, 3.0)
    norm2_gain = jnp.clip(1.0 + 0.1 * jax.random.normal(seeds[16], (D,), jnp.float32), 0.5, 1.5).astype(jnp.bfloat16)
    norm2_shift = centred(seeds[17], (D,), 0.5, 3.0)
    rel_table = centred(seeds[18], (BLOCK, D), 1.0, 6.0)
    rel_gain = jnp.clip(1.0 + 0.1 * jax.random.normal(seeds[19], (D,), jnp.float32), 0.5, 1.5).astype(jnp.bfloat16)
    rel_shift = centred(seeds[20], (D,), 0.5, 3.0)
    block_group = draw_block_group(jax.random.fold_in(seeds[23], 71), 0)
    seq_lengths = draw_seq_lengths(jax.random.fold_in(seeds[23], 71), 0)
    return dict(inputs=inputs, cotangent=cotangent, w_query=w_query, b_query=b_query, w_key=w_key, b_key=b_key, w_value=w_value, b_value=b_value, w_output=w_output, b_output=b_output, norm1_gain=norm1_gain, norm1_shift=norm1_shift, w_inner=w_inner, b_inner=b_inner, w_outer=w_outer, b_outer=b_outer, norm2_gain=norm2_gain, norm2_shift=norm2_shift, rel_table=rel_table, rel_gain=rel_gain, rel_shift=rel_shift, block_group=block_group, seq_lengths=seq_lengths)


EPS = 1e-06
MAXIMAL_PRECISION = lax.Precision.HIGHEST

@jax.custom_vjp
def low(v):
    return lax.optimization_barrier(v.astype(jnp.bfloat16)).astype(jnp.float32)

@jax.custom_vjp
def low_back(v):
    return v

def low_keep(v):
    return (low(v), None)

def low_pass(kept, grad):
    return (grad,)

def back_keep(v):
    return (v, None)

def back_low(kept, grad):
    return (low(grad),)
low.defvjp(low_keep, low_pass)
low_back.defvjp(back_keep, back_low)

def both_ways(array_in):
    return low(low_back(array_in))

def bucket_index(half_rows):
    table_rows = 2 * half_rows
    middle = half_rows // 2
    relative = np.arange(table_rows)[:, None] - np.arange(table_rows)[None, :]
    signed = np.sign(relative)
    absolute = np.where((relative < middle) & (relative > -middle), middle - 1, np.abs(relative))
    log_place = np.ceil(np.log(absolute / middle) / np.log((table_rows - 1) / middle) * (middle - 1)) + middle
    placed = np.where(absolute <= middle, relative, log_place * signed)
    return (placed + half_rows).astype(np.int32)

def layer_norm(array_in, gains, offsets):
    average = lax.optimization_barrier(jnp.mean(array_in, axis=-1, keepdims=True))
    center = array_in - average
    variance = lax.optimization_barrier(jnp.mean(center * center, axis=-1, keepdims=True))
    return center * lax.rsqrt(variance + EPS) * gains + offsets

def valid_pairs(group_kind, lengths, block_rows):
    capacity = jnp.right_shift(jnp.int32(block_rows), group_kind.astype(jnp.int32))
    places = jnp.arange(block_rows, dtype=jnp.int32)
    owner_slot = places // capacity
    offset = places - owner_slot * capacity
    slot_ids = jnp.arange(4, dtype=jnp.int32)
    limits = lax.optimization_barrier(jnp.sum(jnp.where(owner_slot[:, None] == slot_ids[None, :], lengths[None, :].astype(jnp.int32), 0), axis=1))
    return (owner_slot[:, None] == owner_slot[None, :]) & (offset < limits)[None, :]

def score_parts(content, query_position_rows, key_position_rows, forward_table, backward_table, score_scale):
    head_count = content.shape[0]
    query_side = jnp.take_along_axis(query_position_rows, jnp.broadcast_to(forward_table, (head_count,) + forward_table.shape), axis=2)
    key_side = jnp.take_along_axis(key_position_rows, jnp.broadcast_to(backward_table, (head_count,) + backward_table.shape), axis=2)
    return (content + query_side + jnp.swapaxes(key_side, 1, 2)) * score_scale

def product(left, right):
    return jnp.dot(left, right, precision=MAXIMAL_PRECISION, preferred_element_type=jnp.float32)

def block_layer(params, rows_in, groups, lengths):
    w_query, b_query, w_key, b_key, w_value, b_value, w_output, b_output, norm1_gain, norm1_shift, w_inner, b_inner, w_outer, b_outer, norm2_gain, norm2_shift, rel_table, rel_gain, rel_shift = params
    forward_table = jnp.asarray(bucket_index(BUCKETS))
    backward_table = forward_table.T
    score_scale = 1.0 / math.sqrt(3 * HEAD_DIM)
    rel_low = low(layer_norm(rel_table, rel_gain, rel_shift))
    position_key_rows = both_ways(product(rel_low, w_key) + b_key).reshape(BLOCK, HEADS, HEAD_DIM)
    position_query_rows = both_ways(product(rel_low, w_query) + b_query).reshape(BLOCK, HEADS, HEAD_DIM)
    query_rows = both_ways(product(rows_in, w_query) + b_query).reshape(BLOCKS_DEV, BLOCK, HEADS, HEAD_DIM)
    key_rows = both_ways(product(rows_in, w_key) + b_key).reshape(BLOCKS_DEV, BLOCK, HEADS, HEAD_DIM)
    value_rows = both_ways(product(rows_in, w_value) + b_value).reshape(BLOCKS_DEV, BLOCK, HEADS, HEAD_DIM)

    def attend(pieces):
        query_tile_block, key_tile_block, v_block, group_kind, block_lengths = pieces
        content = low_back(jnp.einsum('ihd,jhd->hij', query_tile_block, key_tile_block, precision=MAXIMAL_PRECISION))
        query_position_rows = low_back(jnp.einsum('aon,von->oav', query_tile_block, position_key_rows, precision=MAXIMAL_PRECISION))
        key_position_rows = low_back(jnp.einsum('vwa,nwa->wvn', key_tile_block, position_query_rows, precision=MAXIMAL_PRECISION))
        valid_mask = valid_pairs(group_kind, block_lengths, BLOCK)
        scores = jnp.where(valid_mask[None], score_parts(content, query_position_rows, key_position_rows, forward_table, backward_table, score_scale), -1e+30)
        row_top = lax.optimization_barrier(jnp.max(scores, axis=2, keepdims=True))
        exp_scores = jnp.exp(scores - row_top)
        att_probs = exp_scores / lax.optimization_barrier(jnp.sum(exp_scores, axis=2, keepdims=True))
        attended = jnp.einsum('hij,jhd->ihd', low(att_probs), v_block, precision=MAXIMAL_PRECISION)
        return attended.reshape(BLOCK, D)
    mixed = lax.map(jax.checkpoint(attend), (query_rows, key_rows, value_rows, groups, lengths))
    mixed = both_ways(mixed.reshape(BLOCKS_DEV * BLOCK, D))
    residual = low_back(product(mixed, w_output) + b_output) + rows_in
    hidden = layer_norm(residual, norm1_gain, norm1_shift)
    inner_pre = low_back(product(low(hidden), w_inner) + b_inner)
    active = low(jax.nn.gelu(inner_pre, approximate=False))
    branch = low_back(product(active, w_outer) + b_outer)
    return layer_norm(hidden + branch, norm2_gain, norm2_shift)

def reference(inputs, cotangent, w_query, b_query, w_key, b_key, w_value, b_value, w_output, b_output, norm1_gain, norm1_shift, w_inner, b_inner, w_outer, b_outer, norm2_gain, norm2_shift, rel_table, rel_gain, rel_shift, block_group, seq_lengths):
    weights = (w_query, b_query, w_key, b_key, w_value, b_value, w_output, b_output, norm1_gain, norm1_shift, w_inner, b_inner, w_outer, b_outer, norm2_gain, norm2_shift, rel_table, rel_gain, rel_shift)
    params = tuple((weight.astype(jnp.float32) for weight in weights))
    device_count = N_DP * N_MP
    rows_dev = BLOCKS_DEV * BLOCK
    input_rows = inputs.astype(jnp.float32).reshape(device_count, rows_dev, D)
    cot_rows = cotangent.astype(jnp.float32).reshape(device_count, rows_dev, D)
    groups = block_group.astype(jnp.int32).reshape(device_count, BLOCKS_DEV)
    lengths = seq_lengths.astype(jnp.int32).reshape(device_count, BLOCKS_DEV, 4)

    def scan_step(totals, pieces):
        rows_x, rows_cot, group_part, length_part = pieces
        layer_rows, pullback = jax.vjp(lambda params_in, rows_in: block_layer(params_in, rows_in, group_part, length_part), params, rows_x)
        param_grads, row_grads = pullback(rows_cot)
        totals = jax.tree.map(lambda total_in, grad_in: total_in + grad_in, totals, param_grads)
        return (totals, (layer_rows, row_grads))
    zeros_init = jax.tree.map(jnp.zeros_like, params)
    totals, (layer_rows, row_grads) = lax.scan(scan_step, zeros_init, (input_rows, cot_rows, groups, lengths))
    return (layer_rows.reshape(TOKENS, D), row_grads.reshape(TOKENS, D), totals[0], totals[1], totals[2], totals[3], totals[4], totals[5], totals[6], totals[7], totals[8], totals[9], totals[10], totals[11], totals[12], totals[13], totals[14], totals[15], totals[16], totals[17], totals[18])
```

```python
import functools
import math

import jax
import jax.numpy as jnp
import numpy as np
from jax import lax
from jax.experimental import pallas as pl
from jax.experimental.pallas import tpu as pltpu
from jax.sharding import PartitionSpec as P

HEADS = 12
EPS = 1e-06
LOG2E = 1.4426950408889634
TILE = 128
CHUNK = 384
BOTH = ("dp", "mp")
f32 = jnp.float32
bf16 = jnp.bfloat16


def bucket_line(half_rows):
    table_rows = 2 * half_rows
    middle = half_rows // 2
    relative = table_rows - 1 - np.arange(2 * table_rows - 1)
    signed = np.sign(relative)
    absolute = np.where((relative < middle) & (relative > -middle), middle - 1, np.abs(relative))
    log_place = (
        np.ceil(np.log(absolute / middle) / np.log((table_rows - 1) / middle) * (middle - 1))
        + middle
    )
    placed = np.where(absolute <= middle, relative, log_place * signed)
    return (placed + half_rows).astype(np.int32)


def valid_pairs(group_kind, lengths, block_rows):
    capacity = jnp.right_shift(jnp.int32(block_rows), group_kind)
    places = jnp.arange(block_rows, dtype=jnp.int32)
    owner_slot = places // capacity
    offset = places - owner_slot * capacity
    slot_ids = jnp.arange(4, dtype=jnp.int32)
    limits = jnp.sum(
        jnp.where(owner_slot[:, None] == slot_ids[None, :], lengths[None, :], 0), axis=1
    )
    return (owner_slot[:, None] == owner_slot[None, :]) & (offset < limits)[None, :]


def dot(a, b):
    return jnp.dot(a, b, preferred_element_type=f32)


def dot_nt(a, b):
    return lax.dot_general(a, b, (((1,), (1,)), ((), ())), preferred_element_type=f32)


def dot_tn(a, b):
    return lax.dot_general(a, b, (((0,), (0,)), ((), ())), preferred_element_type=f32)


def wide(v):
    return v.astype(f32)


def ln_parts(v):
    average = jnp.mean(v, axis=-1, keepdims=True)
    center = v - average
    root = lax.rsqrt(jnp.mean(center * center, axis=-1, keepdims=True) + EPS)
    return center * root, root


def ln_back(dy, normed, root, gain):
    return (
        ln_back_rows(dy, normed, root, gain),
        jnp.sum(dy * normed, axis=0, keepdims=True),
        jnp.sum(dy, axis=0, keepdims=True),
    )


def ln_back_rows(dy, normed, root, gain):
    dn = dy * gain
    first = jnp.mean(dn, axis=-1, keepdims=True)
    second = jnp.mean(dn * normed, axis=-1, keepdims=True)
    return root * (dn - first - normed * second)


def gelu_parts(v):
    bell = jnp.exp(-0.5 * v * v)
    t = 1.0 / (1.0 + (0.3275911 * math.sqrt(0.5)) * jnp.abs(v))
    poly = t * (
        0.254829592
        + t * (-0.284496736 + t * (1.421413741 + t * (-1.453152027 + t * 1.061405429)))
    )
    tail = 0.5 * poly * bell
    below = jnp.where(v >= 0, 1.0 - tail, tail)
    return v * below, below + v * bell * (1.0 / math.sqrt(2.0 * math.pi))


def skewed(x, keep):
    turned = [
        pltpu.roll(x[:, TILE * b : TILE * (b + 1)], 1, 1, stride=1, stride_axis=0)
        for b in range(5)
    ]
    return [jnp.where(keep, turned[b], turned[b + 1]) for b in range(4)]


def unskewed(tiles, keep):
    zero = jnp.zeros((TILE, TILE), f32)
    turned = [zero] + [pltpu.roll(t, 0, 1, stride=1, stride_axis=0) for t in tiles] + [zero]
    return [jnp.where(keep, turned[b + 1], turned[b]) for b in range(5)]


def attend_kernel(
    q_ref, k_ref, v_ref, key_line_ref, query_line_ref, bias_ref, out_ref, exp_ref, inv_ref, side_ref
):
    lane = lax.broadcasted_iota(jnp.int32, (1, TILE), 1)
    keep = lax.broadcasted_iota(jnp.int32, (TILE, TILE), 1) <= lax.broadcasted_iota(
        jnp.int32, (TILE, TILE), 0
    )
    mine = [lane < 64, lane >= 64]
    scale = LOG2E / math.sqrt(192)
    for h in range(2):
        for t in range(4):
            km = jnp.where(mine[h], k_ref[TILE * t : TILE * (t + 1), :], 0)
            start = 384 - TILE * t
            sk = skewed(dot_nt(km, query_line_ref[start : start + 640, :]), keep)
            for b in range(4):
                side_ref[h, TILE * b : TILE * (b + 1), TILE * t : TILE * (t + 1)] = sk[b].T
        for t in range(4):
            rows = slice(TILE * t, TILE * (t + 1))
            qm = jnp.where(mine[h], q_ref[rows, :], 0)
            start = 384 - TILE * t
            near = skewed(dot_nt(qm, key_line_ref[start : start + 640, :]), keep)
            content = dot_nt(qm, k_ref[...])
            parts = []
            for b in range(4):
                cols = slice(TILE * b, TILE * (b + 1))
                total = content[:, cols] + near[b] + side_ref[h, rows, cols]
                parts.append(total * scale + bias_ref[rows, cols])
            top = jnp.max(
                jnp.maximum(jnp.maximum(parts[0], parts[1]), jnp.maximum(parts[2], parts[3])),
                axis=1,
                keepdims=True,
            )
            low = [jnp.exp2(p - top).astype(bf16) for p in parts]
            total = jnp.sum(
                (wide(low[0]) + wide(low[1])) + (wide(low[2]) + wide(low[3])),
                axis=1,
                keepdims=True,
            )
            exps = jnp.concatenate(low, axis=1)
            exp_ref[h, rows, :] = exps
            inverse = 1.0 / total
            out = (dot(exps, v_ref[...]) * inverse).astype(bf16)
            inverse = jnp.broadcast_to(inverse, (TILE, TILE))
            if h == 0:
                inv_ref[0, rows, :] = inverse
                out_ref[rows, :] = out
            else:
                inv_ref[0, rows, :] = jnp.where(mine[0], inv_ref[0, rows, :], inverse)
                out_ref[rows, :] = jnp.where(mine[0], out_ref[rows, :], out)


def attend(q, k, v, key_line, query_line, bias):
    rows, width = q.shape
    pairs = width // TILE
    col = pl.BlockSpec((rows, TILE), lambda g: (0, g))
    line = pl.BlockSpec((2 * rows, TILE), lambda g: (0, g))
    return pl.pallas_call(
        attend_kernel,
        grid=(pairs,),
        in_specs=[col, col, col, line, line, pl.BlockSpec((rows, rows), lambda g: (0, 0))],
        out_specs=[
            col,
            pl.BlockSpec((2, rows, rows), lambda g: (g, 0, 0)),
            pl.BlockSpec((1, rows, TILE), lambda g: (g, 0, 0)),
        ],
        out_shape=[
            jax.ShapeDtypeStruct((rows, width), bf16),
            jax.ShapeDtypeStruct((2 * pairs, rows, rows), bf16),
            jax.ShapeDtypeStruct((pairs, rows, TILE), f32),
        ],
        scratch_shapes=[pltpu.VMEM((2, rows, rows), f32)],
        compiler_params=pltpu.CompilerParams(vmem_limit_bytes=32 * 1024 * 1024),
        cost_estimate=pl.CostEstimate(
            flops=18_000_000_000, bytes_accessed=16_000_000, transcendentals=3_200_000
        ),
        name="attend",
    )(q, k, v, key_line, query_line, bias)


def attend_back_kernel(
    q_ref,
    k_ref,
    v_ref,
    do_ref,
    exp_ref,
    inv_ref,
    key_line_ref,
    query_line_ref,
    places_ref,
    dq_ref,
    dk_ref,
    dv_ref,
    ds_ref,
    dst_ref,
    query_band,
    key_band,
):
    @pl.when(pl.program_id(0) == 0)
    def _():
        query_band[...] = jnp.zeros_like(query_band)
        key_band[...] = jnp.zeros_like(key_band)

    scale = 1.0 / math.sqrt(192)
    lane = lax.broadcasted_iota(jnp.int32, (1, TILE), 1)
    sub = lax.broadcasted_iota(jnp.int32, (TILE, 1), 0)
    keep = lax.broadcasted_iota(jnp.int32, (TILE, TILE), 1) >= lax.broadcasted_iota(
        jnp.int32, (TILE, TILE), 0
    )
    mine = [lane < 64, lane >= 64]
    mine_t = [sub < 64, sub >= 64]
    flip = (
        lax.broadcasted_iota(jnp.int32, (256, 256), 0)
        + lax.broadcasted_iota(jnp.int32, (256, 256), 1)
        == 255
    )
    flip = flip.astype(f32).astype(bf16)

    def reverse(x):
        return jnp.concatenate([dot(flip, x[256:]), dot(flip, x[:256])], axis=0).astype(bf16)

    q = q_ref[...]
    k = reverse(k_ref[...])
    v = reverse(v_ref[...])
    q_t = q.T
    k_t = k.T
    do = (wide(do_ref[...]) * inv_ref[0]).astype(bf16)
    do_t = do.T
    dv_t = None
    dqs, dks, key_lines, query_lines = [], [], [], []
    for h in range(2):
        dom = jnp.where(mine[h], do, 0)
        for t in range(4):
            rows = slice(TILE * t, TILE * (t + 1))
            dp = dot_nt(dom[rows], v)
            e = jnp.concatenate(
                [dot(exp_ref[h, rows, 256:], flip), dot(exp_ref[h, rows, :256], flip)], axis=1
            )
            ep = e * dp
            mean = jnp.sum(ep, axis=1, keepdims=True) * inv_ref[0, rows, 64 * h : 64 * h + 1]
            ds = ep - e * mean
            ds_ref[h, rows, :] = ds.astype(bf16)
            out = unskewed([ds[:, TILE * b : TILE * (b + 1)] for b in range(4)], keep)
            for b in range(5):
                query_band[h, rows, TILE * (t + b) : TILE * (t + b + 1)] = out[b].astype(bf16)
        for t in range(4):
            rows = slice(TILE * t, TILE * (t + 1))
            turned = [ds_ref[h, TILE * b : TILE * (b + 1), rows].T for b in range(4)]
            for b in range(4):
                dst_ref[h, rows, TILE * b : TILE * (b + 1)] = turned[b]
            out = unskewed([wide(x) for x in turned], keep)
            for b in range(5):
                key_band[h, rows, TILE * (t + b) : TILE * (t + b + 1)] = out[b].astype(bf16)
        part = dot(jnp.where(mine_t[h], do_t, 0), exp_ref[h])
        dv_t = part if dv_t is None else dv_t + part
        dq, dk, key_line, query_line = [], [], [], []
        for i in range(2):
            rows = slice(256 * i, 256 * (i + 1))
            band = slice(256 * i, 256 * i + 768)
            dq.append(dot(ds_ref[h, rows, :], k) + dot(query_band[h, rows, band], key_line_ref[band, :]))
            dk.append(dot(dst_ref[h, rows, :], q) + dot(key_band[h, rows, band], query_line_ref[band, :]))
            key_line.append(dot(jnp.where(mine_t[h], q_t[:, rows], 0), query_band[h, rows, band]))
            query_line.append(dot(jnp.where(mine_t[h], k_t[:, rows], 0), key_band[h, rows, band]))
        dqs.append(jnp.concatenate(dq, axis=0))
        dks.append(jnp.concatenate(dk, axis=0))
        key_lines.append(key_line)
        query_lines.append(query_line)
    size = q.shape[0]
    dq_ref[:size, :] = (jnp.where(mine[0], dqs[0], dqs[1]) * scale).astype(bf16)
    dk_ref[:size, :] = reverse((jnp.where(mine[0], dks[0], dks[1]) * scale).astype(bf16))
    dv_ref[...] = dv_t.T.astype(bf16)
    for lines, ref in ((key_lines, dk_ref), (query_lines, dq_ref)):
        first = lines[0][0] + lines[1][0]
        second = lines[0][1] + lines[1][1]
        whole = jnp.concatenate(
            [first[:, :256], first[:, 256:] + second[:, :512], second[:, 512:]], axis=1
        )
        ref[size:, :] = dot((whole * scale).astype(bf16), places_ref[...]).T.astype(bf16)


def attend_back(q, k, v, do, exps, inverse, key_line, query_line, places, first, count):
    rows = q.shape[0]
    col = pl.BlockSpec((rows, TILE), lambda g: (0, first + g))
    line = pl.BlockSpec((2 * rows, TILE), lambda g: (0, first + g))
    both = pl.BlockSpec((2 * rows, TILE), lambda g: (0, g))
    return pl.pallas_call(
        attend_back_kernel,
        grid=(count,),
        in_specs=[
            col,
            col,
            col,
            col,
            pl.BlockSpec((2, rows, rows), lambda g: (first + g, 0, 0)),
            pl.BlockSpec((1, rows, TILE), lambda g: (first + g, 0, 0)),
            line,
            line,
            pl.BlockSpec((2 * rows, rows), lambda g: (0, 0)),
        ],
        out_specs=[both, both, pl.BlockSpec((rows, TILE), lambda g: (0, g))],
        out_shape=[
            jax.ShapeDtypeStruct((2 * rows, count * TILE), bf16),
            jax.ShapeDtypeStruct((2 * rows, count * TILE), bf16),
            jax.ShapeDtypeStruct((rows, count * TILE), bf16),
        ],
        scratch_shapes=[
            pltpu.VMEM((2, rows, rows), bf16),
            pltpu.VMEM((2, rows, rows), bf16),
            pltpu.VMEM((2, rows, 2 * rows), bf16),
            pltpu.VMEM((2, rows, 2 * rows), bf16),
        ],
        compiler_params=pltpu.CompilerParams(vmem_limit_bytes=40 * 1024 * 1024),
        cost_estimate=pl.CostEstimate(
            flops=count * 4_000_000_000, bytes_accessed=count * 3_000_000, transcendentals=0
        ),
        name="attend_back",
    )(q, k, v, do, exps, inverse, key_line, query_line, places)


def ffn_step(h_ref, w_in, b_in, w_out, slope_ref, active_ref, total_ref):
    for r in range(0, h_ref.shape[0], 256):
        rows = slice(r, r + 256)
        active, slope = gelu_parts(dot(h_ref[rows, :], w_in) + wide(b_in))
        active = active.astype(bf16)
        slope_ref[0, rows, :] = slope.astype(bf16)
        if active_ref is not None:
            active_ref[rows, :] = active
        total_ref[rows, :] += dot(active, w_out)


def ffn_own_kernel(h_ref, win_ref, bin_ref, wout_ref, part_ref, active_ref, slope_ref):
    @pl.when(pl.program_id(0) == 0)
    def _():
        part_ref[...] = jnp.zeros_like(part_ref)

    ffn_step(h_ref, win_ref[0], bin_ref[0, 0], wout_ref[0], slope_ref, active_ref, part_ref)


def ffn_own(h, w_in, b_in, w_out):
    rows, width = h.shape
    units = w_in.shape[-1]
    return pl.pallas_call(
        ffn_own_kernel,
        grid=(units // CHUNK,),
        in_specs=[
            pl.BlockSpec((rows, width), lambda c: (0, 0)),
            pl.BlockSpec((1, width, CHUNK), lambda c: (0, 0, c)),
            pl.BlockSpec((1, 1, CHUNK), lambda c: (0, 0, c)),
            pl.BlockSpec((1, CHUNK, width), lambda c: (0, c, 0)),
        ],
        out_specs=[
            pl.BlockSpec((rows, width), lambda c: (0, 0)),
            pl.BlockSpec((rows, CHUNK), lambda c: (0, c)),
            pl.BlockSpec((1, rows, CHUNK), lambda c: (0, 0, c)),
        ],
        out_shape=[
            jax.ShapeDtypeStruct((rows, width), f32),
            jax.ShapeDtypeStruct((rows, units), bf16),
            jax.ShapeDtypeStruct((1, rows, units), bf16),
        ],
        compiler_params=pltpu.CompilerParams(vmem_limit_bytes=32 * 1024 * 1024),
        cost_estimate=pl.CostEstimate(
            flops=4 * rows * width * units, bytes_accessed=10_000_000, transcendentals=2 * rows * units
        ),
        name="ffn_own",
    )(h, w_in, b_in, w_out)


def ffn_rest_kernel(
    h_ref,
    win_ref,
    bin_ref,
    wout_ref,
    part_ref,
    normed_ref,
    cot_ref,
    vec_ref,
    slope_ref,
    out_ref,
    dpre_ref,
    dbranch_ref,
    sums_ref,
    total_ref,
):
    s, c = pl.program_id(0), pl.program_id(1)

    @pl.when((s == 0) & (c == 0))
    def _():
        total_ref[...] = part_ref[...]

    ffn_step(h_ref, win_ref[0], bin_ref[0, 0], wout_ref[0], slope_ref, None, total_ref)

    @pl.when((s == pl.num_programs(0) - 1) & (c == pl.num_programs(1) - 1))
    def _():
        gain1, shift1, b_outer, gain2, shift2 = [vec_ref[i : i + 1, :] for i in range(5)]
        sums = [jnp.zeros(gain1.shape, f32) for _ in range(3)]
        for r in range(0, h_ref.shape[0], TILE):
            rows = slice(r, r + TILE)
            normed, root = ln_parts(
                normed_ref[rows, :] * gain1 + shift1 + total_ref[rows, :] + b_outer
            )
            out_ref[rows, :] = normed * gain2 + shift2
            dy = wide(cot_ref[rows, :])
            d = ln_back_rows(dy, normed, root, gain2)
            dpre_ref[rows, :] = d
            low = d.astype(bf16)
            dbranch_ref[rows, :] = low
            sums[0] += jnp.sum(dy * normed, axis=0, keepdims=True)
            sums[1] += jnp.sum(dy, axis=0, keepdims=True)
            sums[2] += jnp.sum(wide(low), axis=0, keepdims=True)
        pad = jnp.zeros((5, gain1.shape[1]), f32)
        sums_ref[...] = jnp.concatenate(sums + [pad], axis=0)


def ffn_rest(h, w_in, b_in, w_out, part, normed, cot, vec):
    rows, width = h.shape
    n, _, units = w_in.shape
    full = pl.BlockSpec((rows, width), lambda s, c: (0, 0))
    eight = pl.BlockSpec((8, width), lambda s, c: (0, 0))
    return pl.pallas_call(
        ffn_rest_kernel,
        grid=(n, units // CHUNK),
        in_specs=[
            full,
            pl.BlockSpec((1, width, CHUNK), lambda s, c: (s, 0, c)),
            pl.BlockSpec((1, 1, CHUNK), lambda s, c: (s, 0, c)),
            pl.BlockSpec((1, CHUNK, width), lambda s, c: (s, c, 0)),
            full,
            full,
            full,
            eight,
        ],
        out_specs=[
            pl.BlockSpec((1, rows, CHUNK), lambda s, c: (s, 0, c)),
            full,
            full,
            full,
            eight,
        ],
        out_shape=[
            jax.ShapeDtypeStruct((n, rows, units), bf16),
            jax.ShapeDtypeStruct((rows, width), f32),
            jax.ShapeDtypeStruct((rows, width), f32),
            jax.ShapeDtypeStruct((rows, width), bf16),
            jax.ShapeDtypeStruct((8, width), f32),
        ],
        scratch_shapes=[pltpu.VMEM((rows, width), f32)],
        compiler_params=pltpu.CompilerParams(vmem_limit_bytes=40 * 1024 * 1024),
        cost_estimate=pl.CostEstimate(
            flops=4 * n * rows * width * units,
            bytes_accessed=16_000_000,
            transcendentals=2 * n * rows * units,
        ),
        name="ffn_rest",
    )(h, w_in, b_in, w_out, part, normed, cot, vec)


def ffn_back_kernel(
    db_ref,
    win_ref,
    wout_ref,
    slope_ref,
    win_far_ref,
    wout_far_ref,
    slope_far_ref,
    dpre_ref,
    normed_ref,
    root_ref,
    w_output_ref,
    vec_ref,
    dinner_ref,
    dres_ref,
    dattn_ref,
    dmixed_ref,
    sums_ref,
    total_ref,
    *,
    own,
):
    c = pl.program_id(0)

    @pl.when(c == 0)
    def _():
        total_ref[...] = dpre_ref[...]

    def step(win, wout, slope, out):
        for r in range(0, db_ref.shape[0], 256):
            rows = slice(r, r + 256)
            d = (dot_nt(db_ref[rows, :], wout[0]) * wide(slope[0, rows, :])).astype(bf16)
            if out is not None:
                out[rows, :] = d
            total_ref[rows, :] += dot_nt(d, win[0])

    @pl.when(c < own)
    def _():
        step(win_ref, wout_ref, slope_ref, dinner_ref)

    @pl.when(c >= own)
    def _():
        step(win_far_ref, wout_far_ref, slope_far_ref, None)

    @pl.when(c == pl.num_programs(0) - 1)
    def _():
        gain = vec_ref[0:1, :]
        sums = [jnp.zeros(gain.shape, f32) for _ in range(3)]
        for r in range(0, db_ref.shape[0], TILE):
            rows = slice(r, r + TILE)
            dy = total_ref[rows, :]
            normed = normed_ref[rows, :]
            d = ln_back_rows(dy, normed, root_ref[rows, 0:1], gain)
            dres_ref[rows, :] = d
            low = d.astype(bf16)
            dattn_ref[rows, :] = low
            dmixed_ref[rows, :] = dot_nt(low, w_output_ref[...]).astype(bf16)
            sums[0] += jnp.sum(dy * normed, axis=0, keepdims=True)
            sums[1] += jnp.sum(dy, axis=0, keepdims=True)
            sums[2] += jnp.sum(wide(low), axis=0, keepdims=True)
        pad = jnp.zeros((5, gain.shape[1]), f32)
        sums_ref[...] = jnp.concatenate(sums + [pad], axis=0)


def ffn_back(db, w_in, w_out, slope, far_in, far_out, far_slope, dpre, normed, root, w_output, vec):
    rows, width = db.shape
    units = w_in.shape[-1]
    n = far_in.shape[0]
    own = units // CHUNK
    full = pl.BlockSpec((rows, width), lambda c: (0, 0))
    eight = pl.BlockSpec((8, width), lambda c: (0, 0))

    def near(c):
        return jnp.minimum(c, own - 1)

    def share(c):
        return jnp.maximum(c - own, 0) // own

    def far(c):
        return jnp.maximum(c - own, 0) % own

    return pl.pallas_call(
        functools.partial(ffn_back_kernel, own=own),
        grid=((n + 1) * own,),
        in_specs=[
            full,
            pl.BlockSpec((1, width, CHUNK), lambda c: (0, 0, near(c))),
            pl.BlockSpec((1, CHUNK, width), lambda c: (0, near(c), 0)),
            pl.BlockSpec((1, rows, CHUNK), lambda c: (0, 0, near(c))),
            pl.BlockSpec((1, width, CHUNK), lambda c: (share(c), 0, far(c))),
            pl.BlockSpec((1, CHUNK, width), lambda c: (share(c), far(c), 0)),
            pl.BlockSpec((1, rows, CHUNK), lambda c: (share(c), 0, far(c))),
            full,
            full,
            pl.BlockSpec((rows, TILE), lambda c: (0, 0)),
            pl.BlockSpec((width, width), lambda c: (0, 0)),
            eight,
        ],
        out_specs=[pl.BlockSpec((rows, CHUNK), lambda c: (0, near(c))), full, full, full, eight],
        out_shape=[
            jax.ShapeDtypeStruct((rows, units), bf16),
            jax.ShapeDtypeStruct((rows, width), f32),
            jax.ShapeDtypeStruct((rows, width), bf16),
            jax.ShapeDtypeStruct((rows, width), bf16),
            jax.ShapeDtypeStruct((8, width), f32),
        ],
        scratch_shapes=[pltpu.VMEM((rows, width), f32)],
        compiler_params=pltpu.CompilerParams(vmem_limit_bytes=40 * 1024 * 1024),
        cost_estimate=pl.CostEstimate(
            flops=4 * (n + 1) * rows * width * units, bytes_accessed=20_000_000, transcendentals=0
        ),
        name="ffn_back",
    )(db, w_in, w_out, slope, far_in, far_out, far_slope, dpre, normed, root, w_output, vec)


def ffn_grads_kernel(
    h_ref,
    db_ref,
    active_ref,
    dinner_ref,
    far_h_ref,
    far_db_ref,
    win_ref,
    bin_ref,
    wout_ref,
    out_ref,
    h_t,
    far_t,
    *,
    chunks,
):
    c = pl.program_id(0)
    tail = 4 * CHUNK * chunks

    @pl.when(c == 0)
    def _():
        h_t[...] = h_ref[...].T
        far_t[...] = far_h_ref[...].T
        out_ref[tail:, :] = jnp.zeros_like(out_ref[tail:, :])

    w_in, w_out = win_ref[0], wout_ref[0]
    active, dinner = [], []
    for r in range(0, far_h_ref.shape[0], 256):
        rows = slice(r, r + 256)
        a, slope = gelu_parts(dot(far_h_ref[rows, :], w_in) + wide(bin_ref[0, 0]))
        active.append(a.astype(bf16))
        dinner.append((dot_nt(far_db_ref[rows, :], w_out) * slope).astype(bf16))
    active = jnp.concatenate(active, axis=0)
    dinner = jnp.concatenate(dinner, axis=0)
    base = pl.multiple_of(c * 4 * CHUNK, 4 * CHUNK)
    out_ref[pl.ds(base, 2 * CHUNK), :] = (
        dot(h_t[...], dinner_ref[...]) + dot(far_t[...], dinner)
    ).astype(bf16)
    grad = (dot(active_ref[...].T, db_ref[...]) + dot(active.T, far_db_ref[...])).astype(bf16)
    out_ref[pl.ds(base + 2 * CHUNK, CHUNK), :] = grad[:, :CHUNK]
    out_ref[pl.ds(base + 3 * CHUNK, CHUNK), :] = grad[:, CHUNK:]
    bias = jnp.sum(wide(dinner_ref[...]), axis=0, keepdims=True)
    bias = bias + jnp.sum(wide(dinner), axis=0, keepdims=True)
    place = lax.broadcasted_iota(jnp.int32, (16, 1), 0) == c
    out_ref[tail : tail + 16, :] = jnp.where(place, bias.astype(bf16), out_ref[tail : tail + 16, :])


def ffn_grads(h, db, active, dinner, far_h, far_db, w_in, b_in, w_out, extra):
    rows, width = h.shape
    units = w_in.shape[-1]
    chunks = units // CHUNK
    far = far_h.shape[0]

    def fixed(r, w):
        return pl.BlockSpec((r, w), lambda c: (0, 0))

    total = chunks * 4 * CHUNK + extra
    return pl.pallas_call(
        functools.partial(ffn_grads_kernel, chunks=chunks),
        grid=(chunks,),
        in_specs=[
            fixed(rows, width),
            fixed(rows, width),
            pl.BlockSpec((rows, CHUNK), lambda c: (0, c)),
            pl.BlockSpec((rows, CHUNK), lambda c: (0, c)),
            fixed(far, width),
            fixed(far, width),
            pl.BlockSpec((1, width, CHUNK), lambda c: (0, 0, c)),
            pl.BlockSpec((1, 1, CHUNK), lambda c: (0, 0, c)),
            pl.BlockSpec((1, CHUNK, width), lambda c: (0, c, 0)),
        ],
        out_specs=fixed(total, CHUNK),
        out_shape=jax.ShapeDtypeStruct((total, CHUNK), bf16),
        scratch_shapes=[pltpu.VMEM((width, rows), bf16), pltpu.VMEM((width, far), bf16)],
        compiler_params=pltpu.CompilerParams(vmem_limit_bytes=48 * 1024 * 1024),
        cost_estimate=pl.CostEstimate(
            flops=4 * (rows + 2 * far) * width * units,
            bytes_accessed=16_000_000,
            transcendentals=2 * far * units,
        ),
        name="ffn_grads",
    )(h, db, active, dinner, far_h, far_db, w_in, b_in, w_out)


class Moves:
    def __init__(self, n_dp, n_mp):
        self.n_dp, self.n_mp = n_dp, n_mp
        self.dp = lax.axis_index("dp")
        self.mp = lax.axis_index("mp")
        self.core = self.dp % 2
        self.dp_bits = [("dp", 1 << b) for b in range(1, n_dp.bit_length() - 1)]
        self.mp_bits = [("mp", 1 << b) for b in range(n_mp.bit_length() - 1)]

    def swap(self, x, pair):
        perm = []
        for d in range(self.n_dp):
            for m in range(self.n_mp):
                axis, bit = pair[d % 2]
                dest = (d ^ bit, m) if axis == "dp" else (d, m ^ bit)
                perm.append((d * self.n_mp + m, dest[0] * self.n_mp + dest[1]))
        return lax.ppermute(x, BOTH, perm)

    def side(self, pair):
        values = [((self.dp if axis == "dp" else self.mp) // bit) % 2 for axis, bit in pair]
        return jnp.where(self.core == 0, values[0], values[1])

    def scatter(self, x, pair):
        half = x.shape[0] // 2
        side = self.side(pair)
        sent = lax.dynamic_slice_in_dim(x, (1 - side) * half, half, 0)
        kept = lax.dynamic_slice_in_dim(x, side * half, half, 0)
        return (wide(kept) + wide(self.swap(sent, pair))).astype(bf16)

    def gather(self, x, pair):
        other = self.swap(x, pair)
        side = self.side(pair)
        first = jnp.where(side == 0, x, other)
        second = jnp.where(side == 0, other, x)
        return jnp.concatenate([first, second], axis=0)

    def steps(self, first, second):
        core = ("dp", 1)
        pairs = [(core, core)] + list(zip(first, second, strict=True))
        down = [functools.partial(self.scatter, pair=pair) for pair in pairs]
        up = [functools.partial(self.gather, pair=pair) for pair in reversed(pairs)]
        return down + up


def tie(*arrays):
    return lax.optimization_barrier(arrays)


def per_device(
    inputs,
    cotangent,
    w_query,
    b_query,
    w_key,
    b_key,
    w_value,
    b_value,
    w_output,
    b_output,
    norm1_gain,
    norm1_shift,
    w_inner,
    b_inner,
    w_outer,
    b_outer,
    norm2_gain,
    norm2_shift,
    rel_table,
    rel_gain,
    rel_shift,
    block_group,
    seq_lengths,
    *,
    n_dp,
    n_mp,
):
    rows, width = inputs.shape
    units = w_inner.shape[1]
    moves = Moves(n_dp, n_mp)
    core = ("dp", 1)

    def all_shares(x):
        half = x.shape[0] // 2
        x = lax.dynamic_slice_in_dim(x, moves.core * half, half, 0)[None]
        shares = [x]
        for bit in moves.mp_bits:
            shares = [jnp.concatenate(shares, axis=0)]
            shares.append(moves.swap(shares[0], (bit, bit)))
        got = jnp.concatenate(shares, axis=0)[1:]
        other = moves.swap(got, (core, core))
        first = jnp.where(moves.core == 0, got, other)
        second = jnp.where(moves.core == 0, other, got)
        return jnp.concatenate([first, second], axis=1)

    bias_rows = -(-units // width)
    bias_block = jnp.pad(b_inner, (0, 32 * width - units)).reshape(32, width)
    far_in = all_shares(w_inner)
    far_out = all_shares(jnp.concatenate([w_outer, bias_block], axis=0))
    far_bias = far_out[:, units : units + bias_rows].reshape(n_mp - 1, 1, -1)[:, :, :units]

    line = bucket_line(rows // 2)
    place_ids = np.arange(rows)[None, :]
    forward = jnp.asarray(np.append(line, -1)[:, None] == place_ids).astype(bf16)
    backward = jnp.asarray(np.append(line[::-1], -1)[:, None] == place_ids).astype(bf16)
    rel_normed, rel_root = ln_parts(wide(rel_table))
    rel = (rel_normed * wide(rel_gain) + wide(rel_shift)).astype(bf16)

    def project(left, weight, bias):
        return (dot(left, weight) + wide(bias)).astype(bf16)

    query = project(inputs, w_query, b_query)
    key = project(inputs, w_key, b_key)
    value = project(inputs, w_value, b_value)
    pos_query = project(rel, w_query, b_query)
    pos_key = project(rel, w_key, b_key)
    key_line = dot(forward, pos_key).astype(bf16)
    key_line_back = dot(backward, pos_key).astype(bf16)
    query_line = dot(backward, pos_query).astype(bf16)
    bias = jnp.where(valid_pairs(block_group[0], seq_lengths[0], rows), 0.0, -1e30).astype(f32)

    mixed, exps, inverse = attend(query, key, value, key_line, query_line, bias)

    residual = dot(mixed, w_output) + wide(b_output) + wide(inputs)
    normed1, root1 = ln_parts(residual)
    hidden_low = (normed1 * wide(norm1_gain) + wide(norm1_shift)).astype(bf16)
    root1 = jnp.broadcast_to(root1, (rows, TILE))

    def far(x):
        whole = x
        for bit in moves.mp_bits:
            whole = jnp.concatenate([whole, moves.swap(whole, (bit, bit))], axis=0)
        return whole[rows:]

    far_hidden = far(hidden_low)
    own_in, own_out, own_bias = w_inner[None], w_outer[None], b_inner[None, None]
    part, active, slope = ffn_own(hidden_low, own_in, own_bias, own_out)
    zero = jnp.zeros((width,), bf16)
    vec = jnp.stack(
        [norm1_gain, norm1_shift, b_outer, norm2_gain, norm2_shift, zero, zero, zero]
    ).astype(f32)
    far_slope, layer_out, d_pre2, d_branch, sums2 = ffn_rest(
        hidden_low, far_in, far_bias, far_out, part, normed1, cotangent, vec
    )
    far_branch = far(d_branch)
    d_inner, d_residual, d_attn, d_mixed, sums1 = ffn_back(
        d_branch,
        own_in,
        own_out,
        slope,
        far_in,
        far_out,
        far_slope,
        d_pre2,
        normed1,
        root1,
        w_output,
        vec,
    )
    grad_w_output = dot_tn(mixed, d_attn).astype(bf16)
    ffn = ffn_grads(
        hidden_low,
        d_branch,
        active,
        d_inner,
        far_hidden,
        far_branch,
        own_in,
        own_bias,
        own_out,
        8 * n_dp,
    )

    dp_bits, mp_bits = moves.dp_bits, moves.mp_bits
    turned_bits = dp_bits[1:2] + dp_bits[:1] + dp_bits[2:]
    ffn_steps = moves.steps(dp_bits, turned_bits)
    first = mp_bits + dp_bits
    second = dp_bits[1:2] + mp_bits + dp_bits[:1] + dp_bits[2:]

    both = jnp.concatenate([inputs, rel], axis=0)
    cut = 2 * TILE
    groups = width // cut
    pieces, blocks = [], []
    early = None
    for g in range(groups):
        ffn, d_mixed = tie(ffn, d_mixed)
        if g == groups - 1:
            early = jnp.concatenate(
                [grad_w_output[:, cut * i : cut * (i + 1)] for i in range(groups)] + blocks, axis=0
            )
            blocks = []
            early, d_mixed = tie(early, d_mixed)
        ffn = ffn_steps.pop(0)(ffn)
        d_query, d_key, d_value = attend_back(
            query, key, value, d_mixed, exps, inverse, key_line_back, query_line, backward, 2 * g, 2
        )
        pieces.append((d_query, d_key, d_value))
        blocks.append(dot_tn(both, d_query).astype(bf16))
        blocks.append(dot_tn(both, d_key).astype(bf16))
        blocks.append(dot_tn(inputs, d_value).astype(bf16))
    early_steps = moves.steps(first, second)
    for step in early_steps:
        early = step(early)
    for step in ffn_steps:
        ffn = step(ffn)

    d_query, d_key, d_value = [jnp.concatenate(p, axis=1) for p in zip(*pieces, strict=True)]

    def column_sums(x):
        return jnp.sum(wide(x), axis=0, keepdims=True)

    back = dot_nt(d_query, w_query) + dot_nt(d_key, w_key)
    input_grad = d_residual + back[:rows] + dot_nt(d_value, w_value)
    grad_rel_table, grad_rel_gain, grad_rel_shift = ln_back(
        back[rows:], rel_normed, rel_root, wide(rel_gain)
    )
    vectors = jnp.concatenate(
        [
            sums1,
            sums2,
            column_sums(d_query),
            column_sums(d_key),
            column_sums(d_value),
            grad_rel_gain,
            grad_rel_shift,
            jnp.zeros((11, width), f32),
        ],
        axis=0,
    ).astype(bf16)
    grad_rel_table = grad_rel_table.astype(bf16)
    late = jnp.concatenate(
        blocks
        + [grad_rel_table[:, cut * i : cut * (i + 1)] for i in range(groups)]
        + [vectors[:, cut * i : cut * (i + 1)] for i in range(groups)]
        + [jnp.zeros((256 - 32 * groups, cut), bf16)],
        axis=0,
    )
    for step in moves.steps(first, second):
        late = step(late)

    early, late, ffn = wide(early), wide(late), wide(ffn)

    def rows_of(x, index, size=width):
        return x[index : index + size]

    def columns(parts):
        return jnp.concatenate(parts, axis=1)

    after = 3 * width
    table = columns([rows_of(late, after + rows * i, rows) for i in range(groups)])
    after = after + groups * rows
    vectors = columns([rows_of(late, after + 32 * i, 32) for i in range(groups)])
    grads = []
    for i in range(3):
        parts = [rows_of(early, (groups + 3 * g + i) * width) for g in range(groups - 1)]
        grads.append(columns(parts + [rows_of(late, i * width)]))
    chunks = units // CHUNK
    ffn_in = columns([rows_of(ffn, 4 * CHUNK * c) for c in range(chunks)])
    ffn_out = jnp.concatenate(
        [
            columns([rows_of(ffn, 4 * CHUNK * c + (2 + i) * CHUNK, CHUNK) for i in range(2)])
            for c in range(chunks)
        ],
        axis=0,
    )
    ffn_bias = rows_of(ffn, 4 * CHUNK * chunks, chunks).reshape(units)
    return (
        layer_out,
        input_grad,
        grads[0],
        vectors[16],
        grads[1],
        vectors[17],
        grads[2],
        vectors[18],
        columns([rows_of(early, i * width) for i in range(groups)]),
        vectors[2],
        vectors[0],
        vectors[1],
        ffn_in,
        ffn_bias,
        ffn_out,
        vectors[10],
        vectors[8],
        vectors[9],
        table,
        vectors[19],
        vectors[20],
    )


def solution(mesh):
    n_dp, n_mp = mesh.shape["dp"], mesh.shape["mp"]

    def body(*args):
        return per_device(*args, n_dp=n_dp, n_mp=n_mp)

    split = P(("dp", "mp"), None)
    weights = [P()] * 10 + [P(None, "mp"), P("mp"), P("mp", None)] + [P()] * 6
    return jax.shard_map(
        body,
        mesh=mesh,
        in_specs=(split, split, *weights, P(("dp", "mp")), split),
        out_specs=(
            split,
            split,
            *([P()] * 10),
            P(None, "mp"),
            P("mp"),
            P("mp", None),
            *([P()] * 6),
        ),
        check_vma=False,
    )
```

```python
import functools
import math

import jax
import jax.numpy as jnp
import numpy as np
from jax import lax
from jax.experimental import pallas as pl
from jax.experimental.pallas import tpu as pltpu
from jax.sharding import PartitionSpec as P

HEADS = 12
EPS = 1e-06
LOG2E = 1.4426950408889634
TILE = 128
CHUNK = 384
BOTH = ("dp", "mp")
f32 = jnp.float32
bf16 = jnp.bfloat16


def bucket_line(half_rows):
    table_rows = 2 * half_rows
    middle = half_rows // 2
    relative = table_rows - 1 - np.arange(2 * table_rows - 1)
    signed = np.sign(relative)
    absolute = np.where((relative < middle) & (relative > -middle), middle - 1, np.abs(relative))
    log_place = (
        np.ceil(np.log(absolute / middle) / np.log((table_rows - 1) / middle) * (middle - 1))
        + middle
    )
    placed = np.where(absolute <= middle, relative, log_place * signed)
    return (placed + half_rows).astype(np.int32)


def dot(a, b):
    return jnp.dot(a, b, preferred_element_type=f32)


def dot_nt(a, b):
    return lax.dot_general(a, b, (((1,), (1,)), ((), ())), preferred_element_type=f32)


def dot_tn(a, b):
    return lax.dot_general(a, b, (((0,), (0,)), ((), ())), preferred_element_type=f32)


def wide(v):
    return v.astype(f32)


def ln_parts(v):
    average = jnp.mean(v, axis=-1, keepdims=True)
    center = v - average
    root = lax.rsqrt(jnp.mean(center * center, axis=-1, keepdims=True) + EPS)
    return center * root, root


def ln_back_rows(dy, normed, root, gain):
    dn = dy * gain
    first = jnp.mean(dn, axis=-1, keepdims=True)
    second = jnp.mean(dn * normed, axis=-1, keepdims=True)
    return root * (dn - first - normed * second)


def gelu_parts(v):
    bell = jnp.exp(-0.5 * v * v)
    t = 1.0 / (1.0 + (0.3275911 * math.sqrt(0.5)) * jnp.abs(v))
    poly = t * (
        0.254829592
        + t * (-0.284496736 + t * (1.421413741 + t * (-1.453152027 + t * 1.061405429)))
    )
    tail = 0.5 * poly * bell
    below = jnp.where(v >= 0, 1.0 - tail, tail)
    return v * below, below + v * bell * (1.0 / math.sqrt(2.0 * math.pi))


def pre_kernel(
    x_ref,
    table_ref,
    gain_ref,
    shift_ref,
    wq_ref,
    bq_ref,
    wk_ref,
    bk_ref,
    wv_ref,
    bv_ref,
    forward_ref,
    backward_ref,
    q_ref,
    k_ref,
    v_ref,
    key_line_ref,
    key_back_ref,
    query_line_ref,
    both_t_ref,
    both_ref,
):
    rows = x_ref.shape[0]

    @pl.when(pl.program_id(0) == 0)
    def _():
        both_ref[:rows, :] = x_ref[...]
        normed, _ = ln_parts(wide(table_ref[...]))
        rel = normed * wide(gain_ref[...])[None, :] + wide(shift_ref[...])[None, :]
        both_ref[rows:, :] = rel.astype(bf16)
        both_t_ref[...] = both_ref[...].T

    def project(w_ref, b_ref, part):
        return (dot(both_ref[part, :], w_ref[...]) + wide(b_ref[...])[None, :]).astype(bf16)

    here, there = slice(0, rows), slice(rows, 2 * rows)
    q_ref[...] = project(wq_ref, bq_ref, here)
    k_ref[...] = project(wk_ref, bk_ref, here)
    v_ref[...] = project(wv_ref, bv_ref, here)
    pos_query = project(wq_ref, bq_ref, there)
    pos_key = project(wk_ref, bk_ref, there)
    key_line_ref[...] = dot(forward_ref[...], pos_key).astype(bf16)
    key_back_ref[...] = dot(backward_ref[...], pos_key).astype(bf16)
    query_line_ref[...] = dot(backward_ref[...], pos_query).astype(bf16)


def pre(x, table, gain, shift, w_q, b_q, w_k, b_k, w_v, b_v, forward, backward):
    rows, width = x.shape
    cut = 2 * TILE

    def fixed(r, w):
        return pl.BlockSpec((r, w), lambda c: (0, 0))

    whole = pl.BlockSpec((width,), lambda c: (0,))
    weight = pl.BlockSpec((width, cut), lambda c: (0, c))
    vector = pl.BlockSpec((cut,), lambda c: (c,))
    one = pl.BlockSpec((rows, cut), lambda c: (0, c))
    two = pl.BlockSpec((2 * rows, cut), lambda c: (0, c))
    return pl.pallas_call(
        pre_kernel,
        grid=(width // cut,),
        in_specs=[fixed(rows, width), fixed(rows, width), whole, whole]
        + [weight, vector] * 3
        + [fixed(2 * rows, rows)] * 2,
        out_specs=[one] * 3 + [two] * 3 + [fixed(width, 2 * rows)],
        out_shape=[jax.ShapeDtypeStruct((rows, width), bf16)] * 3
        + [jax.ShapeDtypeStruct((2 * rows, width), bf16)] * 3
        + [jax.ShapeDtypeStruct((width, 2 * rows), bf16)],
        scratch_shapes=[pltpu.VMEM((2 * rows, width), bf16)],
        compiler_params=pltpu.CompilerParams(vmem_limit_bytes=32 * 1024 * 1024),
        cost_estimate=pl.CostEstimate(
            flops=5_500_000_000, bytes_accessed=14_000_000, transcendentals=0
        ),
        name="pre",
    )(x, table, gain, shift, w_q, b_q, w_k, b_k, w_v, b_v, forward, backward)


def skewed(x, keep):
    turned = [
        pltpu.roll(x[:, TILE * b : TILE * (b + 1)], 1, 1, stride=1, stride_axis=0)
        for b in range(5)
    ]
    return [jnp.where(keep, turned[b], turned[b + 1]) for b in range(4)]


def unskewed(tiles, keep):
    zero = jnp.zeros((TILE, TILE), f32)
    turned = [zero] + [pltpu.roll(t, 0, 1, stride=1, stride_axis=0) for t in tiles] + [zero]
    return [jnp.where(keep, turned[b + 1], turned[b]) for b in range(5)]


def attend_kernel(
    group_ref,
    lengths_ref,
    q_ref,
    k_ref,
    v_ref,
    key_line_ref,
    query_line_ref,
    out_ref,
    exp_ref,
    inv_ref,
    side_ref,
    bias_ref,
):
    @pl.when(pl.program_id(0) == 0)
    def _():
        size = bias_ref.shape[0]
        shift = size.bit_length() - 1 - group_ref[0]
        row = lax.broadcasted_iota(jnp.int32, (size, 1), 0)
        col = lax.broadcasted_iota(jnp.int32, (1, size), 1)
        owner = jnp.right_shift(col, shift)
        limit = jnp.zeros((1, size), jnp.int32)
        for slot in range(4):
            limit = jnp.where(owner == slot, lengths_ref[0, slot], limit)
        owner = jnp.where(col - jnp.left_shift(owner, shift) < limit, owner, -1)
        valid = jnp.right_shift(row, shift) == owner
        bias_ref[...] = jnp.where(valid, 0.0, -1e30).astype(f32)

    lane = lax.broadcasted_iota(jnp.int32, (1, TILE), 1)
    keep = lax.broadcasted_iota(jnp.int32, (TILE, TILE), 1) <= lax.broadcasted_iota(
        jnp.int32, (TILE, TILE), 0
    )
    mine = [lane < 64, lane >= 64]
    scale = LOG2E / math.sqrt(192)
    for h in range(2):
        for t in range(4):
            km = jnp.where(mine[h], k_ref[TILE * t : TILE * (t + 1), :], 0)
            start = 384 - TILE * t
            sk = skewed(dot_nt(km, query_line_ref[start : start + 640, :]), keep)
            for b in range(4):
                side_ref[h, TILE * b : TILE * (b + 1), TILE * t : TILE * (t + 1)] = sk[b].T
        for t in range(4):
            rows = slice(TILE * t, TILE * (t + 1))
            qm = jnp.where(mine[h], q_ref[rows, :], 0)
            start = 384 - TILE * t
            near = skewed(dot_nt(qm, key_line_ref[start : start + 640, :]), keep)
            content = dot_nt(qm, k_ref[...])
            parts = []
            for b in range(4):
                cols = slice(TILE * b, TILE * (b + 1))
                total = content[:, cols] + near[b] + side_ref[h, rows, cols]
                parts.append(total * scale + bias_ref[rows, cols])
            top = jnp.max(
                jnp.maximum(jnp.maximum(parts[0], parts[1]), jnp.maximum(parts[2], parts[3])),
                axis=1,
                keepdims=True,
            )
            low = [jnp.exp2(p - top).astype(bf16) for p in parts]
            total = jnp.sum(
                (wide(low[0]) + wide(low[1])) + (wide(low[2]) + wide(low[3])),
                axis=1,
                keepdims=True,
            )
            exps = jnp.concatenate(low, axis=1)
            exp_ref[h, rows, :] = exps
            inverse = 1.0 / total
            out = (dot(exps, v_ref[...]) * inverse).astype(bf16)
            inverse = jnp.broadcast_to(inverse, (TILE, TILE))
            if h == 0:
                inv_ref[0, rows, :] = inverse
                out_ref[rows, :] = out
            else:
                inv_ref[0, rows, :] = jnp.where(mine[0], inv_ref[0, rows, :], inverse)
                out_ref[rows, :] = jnp.where(mine[0], out_ref[rows, :], out)


def attend(group, lengths, q, k, v, key_line, query_line):
    rows, width = q.shape
    pairs = width // TILE
    col = pl.BlockSpec((rows, TILE), lambda g: (0, g))
    line = pl.BlockSpec((2 * rows, TILE), lambda g: (0, g))
    scalars = pl.BlockSpec(memory_space=pltpu.SMEM)
    return pl.pallas_call(
        attend_kernel,
        grid=(pairs,),
        in_specs=[scalars, scalars, col, col, col, line, line],
        out_specs=[
            col,
            pl.BlockSpec((2, rows, rows), lambda g: (g, 0, 0)),
            pl.BlockSpec((1, rows, TILE), lambda g: (g, 0, 0)),
        ],
        out_shape=[
            jax.ShapeDtypeStruct((rows, width), bf16),
            jax.ShapeDtypeStruct((2 * pairs, rows, rows), bf16),
            jax.ShapeDtypeStruct((pairs, rows, TILE), f32),
        ],
        scratch_shapes=[pltpu.VMEM((2, rows, rows), f32), pltpu.VMEM((rows, rows), f32)],
        compiler_params=pltpu.CompilerParams(vmem_limit_bytes=32 * 1024 * 1024),
        cost_estimate=pl.CostEstimate(
            flops=18_000_000_000, bytes_accessed=16_000_000, transcendentals=3_200_000
        ),
        name="attend",
    )(group, lengths, q, k, v, key_line, query_line)


def attend_back_kernel(
    q_ref,
    k_ref,
    v_ref,
    do_ref,
    exp_ref,
    inv_ref,
    key_line_ref,
    query_line_ref,
    places_ref,
    both_t_ref,
    dq_ref,
    dk_ref,
    dv_ref,
    grad_ref,
    ds_ref,
    dst_ref,
    query_band,
    key_band,
):
    @pl.when(pl.program_id(0) == 0)
    def _():
        query_band[...] = jnp.zeros_like(query_band)
        key_band[...] = jnp.zeros_like(key_band)

    scale = 1.0 / math.sqrt(192)
    lane = lax.broadcasted_iota(jnp.int32, (1, TILE), 1)
    sub = lax.broadcasted_iota(jnp.int32, (TILE, 1), 0)
    keep = lax.broadcasted_iota(jnp.int32, (TILE, TILE), 1) >= lax.broadcasted_iota(
        jnp.int32, (TILE, TILE), 0
    )
    mine = [lane < 64, lane >= 64]
    mine_t = [sub < 64, sub >= 64]
    flip = (
        lax.broadcasted_iota(jnp.int32, (256, 256), 0)
        + lax.broadcasted_iota(jnp.int32, (256, 256), 1)
        == 255
    )
    flip = flip.astype(f32).astype(bf16)

    def reverse(x):
        return jnp.concatenate([dot(flip, x[256:]), dot(flip, x[:256])], axis=0).astype(bf16)

    q = q_ref[...]
    k = reverse(k_ref[...])
    v = reverse(v_ref[...])
    q_t = q.T
    k_t = k.T
    do = (wide(do_ref[...]) * inv_ref[0]).astype(bf16)
    do_t = do.T
    dv_t = None
    dqs, dks, key_lines, query_lines = [], [], [], []
    for h in range(2):
        dom = jnp.where(mine[h], do, 0)
        for t in range(4):
            rows = slice(TILE * t, TILE * (t + 1))
            dp = dot_nt(dom[rows], v)
            e = jnp.concatenate(
                [dot(exp_ref[h, rows, 256:], flip), dot(exp_ref[h, rows, :256], flip)], axis=1
            )
            ep = e * dp
            mean = jnp.sum(ep, axis=1, keepdims=True) * inv_ref[0, rows, 64 * h : 64 * h + 1]
            ds = ep - e * mean
            ds_ref[h, rows, :] = ds.astype(bf16)
            out = unskewed([ds[:, TILE * b : TILE * (b + 1)] for b in range(4)], keep)
            for b in range(5):
                query_band[h, rows, TILE * (t + b) : TILE * (t + b + 1)] = out[b].astype(bf16)
        for t in range(4):
            rows = slice(TILE * t, TILE * (t + 1))
            turned = [ds_ref[h, TILE * b : TILE * (b + 1), rows].T for b in range(4)]
            for b in range(4):
                dst_ref[h, rows, TILE * b : TILE * (b + 1)] = turned[b]
            out = unskewed([wide(x) for x in turned], keep)
            for b in range(5):
                key_band[h, rows, TILE * (t + b) : TILE * (t + b + 1)] = out[b].astype(bf16)
        part = dot(jnp.where(mine_t[h], do_t, 0), exp_ref[h])
        dv_t = part if dv_t is None else dv_t + part
        dq, dk, key_line, query_line = [], [], [], []
        for i in range(2):
            rows = slice(256 * i, 256 * (i + 1))
            band = slice(256 * i, 256 * i + 768)
            dq.append(dot(ds_ref[h, rows, :], k) + dot(query_band[h, rows, band], key_line_ref[band, :]))
            dk.append(dot(dst_ref[h, rows, :], q) + dot(key_band[h, rows, band], query_line_ref[band, :]))
            key_line.append(dot(jnp.where(mine_t[h], q_t[:, rows], 0), query_band[h, rows, band]))
            query_line.append(dot(jnp.where(mine_t[h], k_t[:, rows], 0), key_band[h, rows, band]))
        dqs.append(jnp.concatenate(dq, axis=0))
        dks.append(jnp.concatenate(dk, axis=0))
        key_lines.append(key_line)
        query_lines.append(query_line)
    size = q.shape[0]
    dq_ref[:size, :] = (jnp.where(mine[0], dqs[0], dqs[1]) * scale).astype(bf16)
    dk_ref[:size, :] = reverse((jnp.where(mine[0], dks[0], dks[1]) * scale).astype(bf16))
    dv_ref[...] = dv_t.T.astype(bf16)
    for lines, ref in ((key_lines, dk_ref), (query_lines, dq_ref)):
        first = lines[0][0] + lines[1][0]
        second = lines[0][1] + lines[1][1]
        whole = jnp.concatenate(
            [first[:, :256], first[:, 256:] + second[:, :512], second[:, 512:]], axis=1
        )
        ref[size:, :] = dot((whole * scale).astype(bf16), places_ref[...]).T.astype(bf16)
    width = both_t_ref.shape[0]
    grad_ref[0, :width, :] = dot(both_t_ref[...], dq_ref[...]).astype(bf16)
    grad_ref[0, width : 2 * width, :] = dot(both_t_ref[...], dk_ref[...]).astype(bf16)
    grad_ref[0, 2 * width :, :] = dot(both_t_ref[:, :size], dv_ref[...]).astype(bf16)


def attend_back(
    q, k, v, do, exps, inverse, key_line, query_line, places, both_t, first, count
):
    rows, width = q.shape
    col = pl.BlockSpec((rows, TILE), lambda g: (0, first + g))
    line = pl.BlockSpec((2 * rows, TILE), lambda g: (0, first + g))
    both = pl.BlockSpec((2 * rows, TILE), lambda g: (0, g))
    return pl.pallas_call(
        attend_back_kernel,
        grid=(count,),
        in_specs=[
            col,
            col,
            col,
            col,
            pl.BlockSpec((2, rows, rows), lambda g: (first + g, 0, 0)),
            pl.BlockSpec((1, rows, TILE), lambda g: (first + g, 0, 0)),
            line,
            line,
            pl.BlockSpec((2 * rows, rows), lambda g: (0, 0)),
            pl.BlockSpec((width, 2 * rows), lambda g: (0, 0)),
        ],
        out_specs=[
            both,
            both,
            pl.BlockSpec((rows, TILE), lambda g: (0, g)),
            pl.BlockSpec((1, 3 * width, TILE), lambda g: (g // 2, 0, g % 2)),
        ],
        out_shape=[
            jax.ShapeDtypeStruct((2 * rows, count * TILE), bf16),
            jax.ShapeDtypeStruct((2 * rows, count * TILE), bf16),
            jax.ShapeDtypeStruct((rows, count * TILE), bf16),
            jax.ShapeDtypeStruct((count // 2, 3 * width, 2 * TILE), bf16),
        ],
        scratch_shapes=[
            pltpu.VMEM((2, rows, rows), bf16),
            pltpu.VMEM((2, rows, rows), bf16),
            pltpu.VMEM((2, rows, 2 * rows), bf16),
            pltpu.VMEM((2, rows, 2 * rows), bf16),
        ],
        compiler_params=pltpu.CompilerParams(vmem_limit_bytes=40 * 1024 * 1024),
        cost_estimate=pl.CostEstimate(
            flops=count * 4_000_000_000, bytes_accessed=count * 3_000_000, transcendentals=0
        ),
        name="attend_back",
    )(q, k, v, do, exps, inverse, key_line, query_line, places, both_t)


def ffn_step(h_ref, w_in, b_in, w_out, slope_ref, active_ref, total_ref):
    for r in range(0, h_ref.shape[0], 256):
        rows = slice(r, r + 256)
        active, slope = gelu_parts(dot(h_ref[rows, :], w_in) + b_in)
        active = active.astype(bf16)
        slope_ref[0, rows, :] = slope.astype(bf16)
        if active_ref is not None:
            active_ref[rows, :] = active
        total_ref[rows, :] += dot(active, w_out)


def ffn_own_kernel(
    mixed_ref,
    wo_ref,
    bo_ref,
    x_ref,
    gain_ref,
    shift_ref,
    win_ref,
    bin_ref,
    wout_ref,
    h_ref,
    normed_ref,
    root_ref,
    part_ref,
    active_ref,
    slope_ref,
    bias_ref,
):
    c = pl.program_id(0)

    @pl.when(c == 0)
    def _():
        bias_ref[...] = wide(bin_ref[...])[None, :]
        bias, gain, shift = [wide(r[...])[None, :] for r in (bo_ref, gain_ref, shift_ref)]
        for r in range(0, x_ref.shape[0], TILE):
            rows = slice(r, r + TILE)
            residual = dot(mixed_ref[rows, :], wo_ref[...]) + bias + wide(x_ref[rows, :])
            normed, root = ln_parts(residual)
            normed_ref[rows, :] = normed
            root_ref[rows, :] = jnp.broadcast_to(root, (TILE, TILE))
            h_ref[rows, :] = (normed * gain + shift).astype(bf16)
        part_ref[...] = jnp.zeros_like(part_ref)

    b_in = bias_ref[:, pl.ds(pl.multiple_of(c * CHUNK, TILE), CHUNK)]
    ffn_step(h_ref, win_ref[...], b_in, wout_ref[...], slope_ref, active_ref, part_ref)


def ffn_own(mixed, w_output, b_output, x, gain, shift, w_in, b_in, w_out):
    rows, width = x.shape
    units = w_in.shape[-1]
    full = pl.BlockSpec((rows, width), lambda c: (0, 0))
    vector = pl.BlockSpec((width,), lambda c: (0,))
    return pl.pallas_call(
        ffn_own_kernel,
        grid=(units // CHUNK,),
        in_specs=[
            full,
            pl.BlockSpec((width, width), lambda c: (0, 0)),
            vector,
            full,
            vector,
            vector,
            pl.BlockSpec((width, CHUNK), lambda c: (0, c)),
            pl.BlockSpec((units,), lambda c: (0,)),
            pl.BlockSpec((CHUNK, width), lambda c: (c, 0)),
        ],
        out_specs=[
            full,
            full,
            pl.BlockSpec((rows, TILE), lambda c: (0, 0)),
            full,
            pl.BlockSpec((rows, CHUNK), lambda c: (0, c)),
            pl.BlockSpec((1, rows, CHUNK), lambda c: (0, 0, c)),
        ],
        out_shape=[
            jax.ShapeDtypeStruct((rows, width), bf16),
            jax.ShapeDtypeStruct((rows, width), f32),
            jax.ShapeDtypeStruct((rows, TILE), f32),
            jax.ShapeDtypeStruct((rows, width), f32),
            jax.ShapeDtypeStruct((rows, units), bf16),
            jax.ShapeDtypeStruct((1, rows, units), bf16),
        ],
        scratch_shapes=[pltpu.VMEM((1, units), f32)],
        compiler_params=pltpu.CompilerParams(vmem_limit_bytes=32 * 1024 * 1024),
        cost_estimate=pl.CostEstimate(
            flops=4 * rows * width * units, bytes_accessed=14_000_000, transcendentals=2 * rows * units
        ),
        name="ffn_own",
    )(mixed, w_output, b_output, x, gain, shift, w_in, b_in, w_out)


def ffn_rest_kernel(
    h_ref,
    win_ref,
    bin_ref,
    wout_ref,
    win2_ref,
    bin2_ref,
    wout2_ref,
    part_ref,
    normed_ref,
    cot_ref,
    gain1_ref,
    shift1_ref,
    b_outer_ref,
    gain2_ref,
    shift2_ref,
    slope_ref,
    out_ref,
    dpre_ref,
    dbranch_ref,
    sums_ref,
    total_ref,
    *,
    steps,
    chunk,
    chunks,
):
    c = pl.program_id(0)

    @pl.when(c == 0)
    def _():
        total_ref[...] = part_ref[...]

    def step(win, b_in, wout):
        start = 0 if chunks == 1 else pl.multiple_of(c % chunks * chunk, TILE)
        bias = wide(b_in[0, 0:1, pl.ds(start, chunk)])
        ffn_step(h_ref, win[0], bias, wout[0], slope_ref, None, total_ref)

    @pl.when(c < steps)
    def _():
        step(win_ref, bin_ref, wout_ref)

    @pl.when(c >= steps)
    def _():
        step(win2_ref, bin2_ref, wout2_ref)

    @pl.when(c == 2 * steps - 1)
    def _():
        gain1, shift1, b_outer, gain2, shift2 = [
            wide(r[...])[None, :] for r in (gain1_ref, shift1_ref, b_outer_ref, gain2_ref, shift2_ref)
        ]
        sums = [jnp.zeros(gain1.shape, f32) for _ in range(3)]
        for r in range(0, h_ref.shape[0], TILE):
            rows = slice(r, r + TILE)
            normed, root = ln_parts(
                normed_ref[rows, :] * gain1 + shift1 + total_ref[rows, :] + b_outer
            )
            out_ref[rows, :] = normed * gain2 + shift2
            dy = wide(cot_ref[rows, :])
            d = ln_back_rows(dy, normed, root, gain2)
            dpre_ref[rows, :] = d
            low = d.astype(bf16)
            dbranch_ref[rows, :] = low
            sums[0] += jnp.sum(dy * normed, axis=0, keepdims=True)
            sums[1] += jnp.sum(dy, axis=0, keepdims=True)
            sums[2] += jnp.sum(wide(low), axis=0, keepdims=True)
        pad = jnp.zeros((5, gain1.shape[1]), f32)
        sums_ref[...] = jnp.concatenate(sums + [pad], axis=0)


def far_specs(n, width, units, chunk, base, steps):
    chunks = units // chunk

    def place(c):
        c = jnp.clip(c - base, 0, steps - 1)
        return c // chunks, c % chunks

    return (
        pl.BlockSpec((1, width, chunk), lambda c: (place(c)[0], 0, place(c)[1])),
        pl.BlockSpec((1, 16, width), lambda c: (place(c)[0], units // 16, 0)),
        pl.BlockSpec((1, chunk, width), lambda c: (place(c)[0], place(c)[1], 0)),
    )


def ffn_rest(h, got, other, part, normed, cot, vectors):
    rows, width = h.shape
    n, _, units = got[0].shape
    chunk = min(CHUNK, units)
    chunks = units // chunk
    steps = n * chunks
    full = pl.BlockSpec((rows, width), lambda c: (0, 0))
    vector = pl.BlockSpec((width,), lambda c: (0,))
    eight = pl.BlockSpec((8, width), lambda c: (0, 0))
    return pl.pallas_call(
        functools.partial(ffn_rest_kernel, steps=steps, chunk=chunk, chunks=chunks),
        grid=(2 * steps,),
        in_specs=[
            full,
            *far_specs(n, width, units, chunk, 0, steps),
            *far_specs(n, width, units, chunk, steps, steps),
            full,
            full,
            full,
            *([vector] * 5),
        ],
        out_specs=[
            pl.BlockSpec((1, rows, chunk), lambda c: (c // chunks, 0, c % chunks)),
            full,
            full,
            full,
            eight,
        ],
        out_shape=[
            jax.ShapeDtypeStruct((2 * n, rows, units), bf16),
            jax.ShapeDtypeStruct((rows, width), f32),
            jax.ShapeDtypeStruct((rows, width), f32),
            jax.ShapeDtypeStruct((rows, width), bf16),
            jax.ShapeDtypeStruct((8, width), f32),
        ],
        scratch_shapes=[pltpu.VMEM((rows, width), f32)],
        compiler_params=pltpu.CompilerParams(vmem_limit_bytes=40 * 1024 * 1024),
        cost_estimate=pl.CostEstimate(
            flops=8 * n * rows * width * units,
            bytes_accessed=16_000_000,
            transcendentals=4 * n * rows * units,
        ),
        name="ffn_rest",
    )(h, got[0], got[1], got[1], other[0], other[1], other[1], part, normed, cot, *vectors)


def ffn_back_kernel(
    db_ref,
    win_ref,
    wout_ref,
    slope_ref,
    win1_ref,
    wout1_ref,
    win2_ref,
    wout2_ref,
    far_slope_ref,
    dpre_ref,
    normed_ref,
    root_ref,
    w_output_ref,
    mixed_ref,
    gain_ref,
    dinner_ref,
    dres_ref,
    dmixed_ref,
    grad_ref,
    sums_ref,
    total_ref,
    dattn_ref,
    *,
    own,
    steps,
):
    c = pl.program_id(0)

    @pl.when(c == 0)
    def _():
        total_ref[...] = dpre_ref[...]

    def step(win, wout, slope, out):
        for r in range(0, db_ref.shape[0], 256):
            rows = slice(r, r + 256)
            d = (dot_nt(db_ref[rows, :], wout) * wide(slope[0, rows, :])).astype(bf16)
            if out is not None:
                out[rows, :] = d
            total_ref[rows, :] += dot_nt(d, win)

    @pl.when(c < own)
    def _():
        step(win_ref[...], wout_ref[...], slope_ref, dinner_ref)

    @pl.when((c >= own) & (c < own + steps))
    def _():
        step(win1_ref[0], wout1_ref[0], far_slope_ref, None)

    @pl.when(c >= own + steps)
    def _():
        step(win2_ref[0], wout2_ref[0], far_slope_ref, None)

    @pl.when(c == pl.num_programs(0) - 1)
    def _():
        gain = wide(gain_ref[...])[None, :]
        sums = [jnp.zeros(gain.shape, f32) for _ in range(3)]
        for r in range(0, db_ref.shape[0], TILE):
            rows = slice(r, r + TILE)
            dy = total_ref[rows, :]
            normed = normed_ref[rows, :]
            d = ln_back_rows(dy, normed, root_ref[rows, 0:1], gain)
            dres_ref[rows, :] = d
            low = d.astype(bf16)
            dattn_ref[rows, :] = low
            dmixed_ref[rows, :] = dot_nt(low, w_output_ref[...]).astype(bf16)
            sums[0] += jnp.sum(dy * normed, axis=0, keepdims=True)
            sums[1] += jnp.sum(dy, axis=0, keepdims=True)
            sums[2] += jnp.sum(wide(low), axis=0, keepdims=True)
        pad = jnp.zeros((5, gain.shape[1]), f32)
        sums_ref[...] = jnp.concatenate(sums + [pad], axis=0)
        width = gain.shape[1]
        grad = dot(mixed_ref[...].T, dattn_ref[...]).astype(bf16)
        for i in range(width // 256):
            grad_ref[width * i : width * (i + 1), :] = grad[:, 256 * i : 256 * (i + 1)]


def ffn_back(
    db, w_in, w_out, slope, got, other, far_slope, dpre, normed, root, w_output, mixed, gain
):
    rows, width = db.shape
    own_units = w_in.shape[-1]
    n, _, units = got[0].shape
    own = own_units // CHUNK
    chunk = min(CHUNK, units)
    chunks = units // chunk
    steps = n * chunks
    full = pl.BlockSpec((rows, width), lambda c: (0, 0))
    eight = pl.BlockSpec((8, width), lambda c: (0, 0))

    def near(c):
        return jnp.minimum(c, own - 1)

    def far(c):
        return jnp.maximum(c - own, 0)

    first = far_specs(n, width, units, chunk, own, steps)
    second = far_specs(n, width, units, chunk, own + steps, steps)
    return pl.pallas_call(
        functools.partial(ffn_back_kernel, own=own, steps=steps),
        grid=(own + 2 * steps,),
        in_specs=[
            full,
            pl.BlockSpec((width, CHUNK), lambda c: (0, near(c))),
            pl.BlockSpec((CHUNK, width), lambda c: (near(c), 0)),
            pl.BlockSpec((1, rows, CHUNK), lambda c: (0, 0, near(c))),
            first[0],
            first[2],
            second[0],
            second[2],
            pl.BlockSpec((1, rows, chunk), lambda c: (far(c) // chunks, 0, far(c) % chunks)),
            full,
            full,
            pl.BlockSpec((rows, TILE), lambda c: (0, 0)),
            pl.BlockSpec((width, width), lambda c: (0, 0)),
            full,
            pl.BlockSpec((width,), lambda c: (0,)),
        ],
        out_specs=[
            pl.BlockSpec((rows, CHUNK), lambda c: (0, near(c))),
            full,
            full,
            pl.BlockSpec((width * width // 256, 256), lambda c: (0, 0)),
            eight,
        ],
        out_shape=[
            jax.ShapeDtypeStruct((rows, own_units), bf16),
            jax.ShapeDtypeStruct((rows, width), f32),
            jax.ShapeDtypeStruct((rows, width), bf16),
            jax.ShapeDtypeStruct((width * width // 256, 256), bf16),
            jax.ShapeDtypeStruct((8, width), f32),
        ],
        scratch_shapes=[pltpu.VMEM((rows, width), f32), pltpu.VMEM((rows, width), bf16)],
        compiler_params=pltpu.CompilerParams(vmem_limit_bytes=44 * 1024 * 1024),
        cost_estimate=pl.CostEstimate(
            flops=16 * rows * width * width, bytes_accessed=22_000_000, transcendentals=0
        ),
        name="ffn_back",
    )(
        db,
        w_in,
        w_out,
        slope,
        got[0],
        got[1],
        other[0],
        other[1],
        far_slope,
        dpre,
        normed,
        root,
        w_output,
        mixed,
        gain,
    )


def ffn_grads_kernel(
    h_ref,
    db_ref,
    active_ref,
    dinner_ref,
    far_h_ref,
    far_db_ref,
    win_ref,
    bin_ref,
    wout_ref,
    out_ref,
    h_t,
    far_t,
    bias_ref,
    *,
    chunks,
):
    c = pl.program_id(0)
    tail = 4 * CHUNK * chunks

    @pl.when(c == 0)
    def _():
        bias_ref[...] = wide(bin_ref[...])[None, :]
        h_t[...] = h_ref[...].T
        far_t[...] = far_h_ref[...].T
        out_ref[tail:, :] = jnp.zeros_like(out_ref[tail:, :])

    w_in, w_out = win_ref[...], wout_ref[...]
    b_in = bias_ref[:, pl.ds(pl.multiple_of(c * CHUNK, TILE), CHUNK)]
    active, dinner = [], []
    for r in range(0, far_h_ref.shape[0], 256):
        rows = slice(r, r + 256)
        a, slope = gelu_parts(dot(far_h_ref[rows, :], w_in) + b_in)
        active.append(a.astype(bf16))
        dinner.append((dot_nt(far_db_ref[rows, :], w_out) * slope).astype(bf16))
    active = jnp.concatenate(active, axis=0)
    dinner = jnp.concatenate(dinner, axis=0)
    base = pl.multiple_of(c * 4 * CHUNK, 4 * CHUNK)
    out_ref[pl.ds(base, 2 * CHUNK), :] = (
        dot(h_t[...], dinner_ref[...]) + dot(far_t[...], dinner)
    ).astype(bf16)
    grad = (dot(active_ref[...].T, db_ref[...]) + dot(active.T, far_db_ref[...])).astype(bf16)
    out_ref[pl.ds(base + 2 * CHUNK, CHUNK), :] = grad[:, :CHUNK]
    out_ref[pl.ds(base + 3 * CHUNK, CHUNK), :] = grad[:, CHUNK:]
    bias = jnp.sum(wide(dinner_ref[...]), axis=0, keepdims=True)
    bias = bias + jnp.sum(wide(dinner), axis=0, keepdims=True)
    place = lax.broadcasted_iota(jnp.int32, (16, 1), 0) == c
    out_ref[tail : tail + 16, :] = jnp.where(place, bias.astype(bf16), out_ref[tail : tail + 16, :])


def ffn_grads(h, db, active, dinner, far_h, far_db, w_in, b_in, w_out, extra):
    rows, width = h.shape
    units = w_in.shape[-1]
    chunks = units // CHUNK
    far = far_h.shape[0]

    def fixed(r, w):
        return pl.BlockSpec((r, w), lambda c: (0, 0))

    total = chunks * 4 * CHUNK + extra
    return pl.pallas_call(
        functools.partial(ffn_grads_kernel, chunks=chunks),
        grid=(chunks,),
        in_specs=[
            fixed(rows, width),
            fixed(rows, width),
            pl.BlockSpec((rows, CHUNK), lambda c: (0, c)),
            pl.BlockSpec((rows, CHUNK), lambda c: (0, c)),
            fixed(far, width),
            fixed(far, width),
            pl.BlockSpec((width, CHUNK), lambda c: (0, c)),
            pl.BlockSpec((units,), lambda c: (0,)),
            pl.BlockSpec((CHUNK, width), lambda c: (c, 0)),
        ],
        out_specs=fixed(total, CHUNK),
        out_shape=jax.ShapeDtypeStruct((total, CHUNK), bf16),
        scratch_shapes=[
            pltpu.VMEM((width, rows), bf16),
            pltpu.VMEM((width, far), bf16),
            pltpu.VMEM((1, units), f32),
        ],
        compiler_params=pltpu.CompilerParams(vmem_limit_bytes=48 * 1024 * 1024),
        cost_estimate=pl.CostEstimate(
            flops=4 * (rows + 2 * far) * width * units,
            bytes_accessed=16_000_000,
            transcendentals=2 * far * units,
        ),
        name="ffn_grads",
    )(h, db, active, dinner, far_h, far_db, w_in, b_in, w_out)


def late_kernel(
    dq_ref,
    dq2_ref,
    dk_ref,
    dk2_ref,
    dv_ref,
    dv2_ref,
    wq_ref,
    wk_ref,
    table_ref,
    gain_ref,
    sums1_ref,
    sums2_ref,
    grad_ref,
    out_ref,
):
    rows, width = table_ref.shape
    split = dq_ref.shape[1]
    there = slice(rows, 2 * rows)
    gain = wide(gain_ref[...])[None, :]

    def column_sums(a, b):
        return jnp.concatenate(
            [jnp.sum(wide(x[...]), axis=0, keepdims=True) for x in (a, b)], axis=1
        )

    out_ref[: 3 * width, :] = grad_ref[0]
    dy = dot_nt(dq_ref[there, :], wq_ref[:, :split]) + dot_nt(dq2_ref[there, :], wq_ref[:, split:])
    dy = dy + dot_nt(dk_ref[there, :], wk_ref[:, :split])
    dy = dy + dot_nt(dk2_ref[there, :], wk_ref[:, split:])
    normed, root = ln_parts(wide(table_ref[...]))
    table = ln_back_rows(dy, normed, root, gain).astype(bf16)
    vectors = jnp.concatenate(
        [
            sums1_ref[...],
            sums2_ref[...],
            column_sums(dq_ref, dq2_ref),
            column_sums(dk_ref, dk2_ref),
            column_sums(dv_ref, dv2_ref),
            jnp.sum(dy * normed, axis=0, keepdims=True),
            jnp.sum(dy, axis=0, keepdims=True),
            jnp.zeros((11, width), f32),
        ],
        axis=0,
    ).astype(bf16)
    base = 3 * width
    for i in range(width // 256):
        out_ref[base + rows * i : base + rows * (i + 1), :] = table[:, 256 * i : 256 * (i + 1)]
    base = base + rows * (width // 256)
    for i in range(width // 256):
        out_ref[base + 32 * i : base + 32 * (i + 1), :] = vectors[:, 256 * i : 256 * (i + 1)]
    base = base + 32 * (width // 256)
    out_ref[base:, :] = jnp.zeros((out_ref.shape[0] - base, 256), bf16)


def late_sums(d_query, d_key, d_value, w_query, w_key, table, gain, sums1, sums2, grad):
    rows, width = table.shape
    total = -(-(3 * width + (rows + 32) * (width // 256)) // 256) * 256
    return pl.pallas_call(
        late_kernel,
        out_shape=jax.ShapeDtypeStruct((total, 256), bf16),
        compiler_params=pltpu.CompilerParams(vmem_limit_bytes=40 * 1024 * 1024),
        cost_estimate=pl.CostEstimate(
            flops=1_300_000_000, bytes_accessed=12_000_000, transcendentals=0
        ),
        name="late_sums",
    )(*d_query, *d_key, *d_value, w_query, w_key, table, gain, sums1, sums2, grad)


class Moves:
    def __init__(self, n_dp, n_mp):
        self.n_dp, self.n_mp = n_dp, n_mp
        self.dp = lax.axis_index("dp")
        self.mp = lax.axis_index("mp")
        self.core = self.dp % 2
        self.dp_bits = [("dp", 1 << b) for b in range(1, n_dp.bit_length() - 1)]
        self.mp_bits = [("mp", 1 << b) for b in range(n_mp.bit_length() - 1)]

    def swap(self, x, pair):
        perm = []
        for d in range(self.n_dp):
            for m in range(self.n_mp):
                axis, bit = pair[d % 2]
                dest = (d ^ bit, m) if axis == "dp" else (d, m ^ bit)
                perm.append((d * self.n_mp + m, dest[0] * self.n_mp + dest[1]))
        return lax.ppermute(x, BOTH, perm)

    def side(self, pair):
        values = [((self.dp if axis == "dp" else self.mp) // bit) % 2 for axis, bit in pair]
        return jnp.where(self.core == 0, values[0], values[1])

    def scatter(self, x, pair):
        half = x.shape[0] // 2
        side = self.side(pair)
        sent = lax.dynamic_slice_in_dim(x, (1 - side) * half, half, 0)
        kept = lax.dynamic_slice_in_dim(x, side * half, half, 0)
        return (wide(kept) + wide(self.swap(sent, pair))).astype(bf16)

    def gather(self, x, pair):
        other = self.swap(x, pair)
        side = self.side(pair)
        first = jnp.where(side == 0, x, other)
        second = jnp.where(side == 0, other, x)
        return jnp.concatenate([first, second], axis=0)

    def steps(self, first, second):
        core = ("dp", 1)
        pairs = [(core, core)] + list(zip(first, second, strict=True))
        down = [functools.partial(self.scatter, pair=pair) for pair in pairs]
        up = [functools.partial(self.gather, pair=pair) for pair in reversed(pairs)]
        return down + up


def tie(*arrays):
    return lax.optimization_barrier(arrays)


def per_device(
    inputs,
    cotangent,
    w_query,
    b_query,
    w_key,
    b_key,
    w_value,
    b_value,
    w_output,
    b_output,
    norm1_gain,
    norm1_shift,
    w_inner,
    b_inner,
    w_outer,
    b_outer,
    norm2_gain,
    norm2_shift,
    rel_table,
    rel_gain,
    rel_shift,
    block_group,
    seq_lengths,
    *,
    n_dp,
    n_mp,
):
    rows, width = inputs.shape
    units = w_inner.shape[1]
    moves = Moves(n_dp, n_mp)
    core = ("dp", 1)

    def other_shares(x):
        shares = [x[None]]
        for bit in moves.mp_bits:
            shares = [jnp.concatenate(shares, axis=0)]
            shares.append(moves.swap(shares[0], (bit, bit)))
        return jnp.concatenate(shares, axis=0)[1:]

    half = units // 2
    start = moves.core * half
    half_in = lax.dynamic_slice_in_dim(w_inner, start, half, 1)
    half_out = lax.dynamic_slice_in_dim(w_outer, start, half, 0)
    half_bias = jnp.pad(lax.dynamic_slice_in_dim(b_inner, start, half, 0), (0, 16 * width - half))
    half_out = jnp.concatenate([half_out, half_bias.reshape(16, width)], axis=0)
    got = (other_shares(half_in), other_shares(half_out))
    other = tuple(moves.swap(x, (core, core)) for x in got)

    line = bucket_line(rows // 2)
    place_ids = np.arange(rows)[None, :]
    forward = jnp.asarray(np.append(line, -1)[:, None] == place_ids).astype(bf16)
    backward = jnp.asarray(np.append(line[::-1], -1)[:, None] == place_ids).astype(bf16)
    query, key, value, key_line, key_line_back, query_line, both_t = pre(
        inputs,
        rel_table,
        rel_gain,
        rel_shift,
        w_query,
        b_query,
        w_key,
        b_key,
        w_value,
        b_value,
        forward,
        backward,
    )
    mixed, exps, inverse = attend(
        block_group, seq_lengths, query, key, value, key_line, query_line
    )
    hidden_low, normed1, root1, part, active, slope = ffn_own(
        mixed, w_output, b_output, inputs, norm1_gain, norm1_shift, w_inner, b_inner, w_outer
    )

    def far(x):
        whole = x
        for bit in moves.mp_bits:
            whole = jnp.concatenate([whole, moves.swap(whole, (bit, bit))], axis=0)
        return whole[rows:]

    far_hidden = far(hidden_low)
    far_slope, layer_out, d_pre2, d_branch, sums2 = ffn_rest(
        hidden_low,
        got,
        other,
        part,
        normed1,
        cotangent,
        (norm1_gain, norm1_shift, b_outer, norm2_gain, norm2_shift),
    )
    far_branch = far(d_branch)
    d_inner, d_residual, d_mixed, grad_w_output, sums1 = ffn_back(
        d_branch,
        w_inner,
        w_outer,
        slope,
        got,
        other,
        far_slope,
        d_pre2,
        normed1,
        root1,
        w_output,
        mixed,
        norm1_gain,
    )
    ffn = ffn_grads(
        hidden_low,
        d_branch,
        active,
        d_inner,
        far_hidden,
        far_branch,
        w_inner,
        b_inner,
        w_outer,
        8 * n_dp,
    )
    ffn, d_mixed = tie(ffn, d_mixed)
    ffn = lax.psum(ffn, "dp")

    dp_bits, mp_bits = moves.dp_bits, moves.mp_bits
    first = mp_bits + dp_bits
    second = dp_bits[:1] + mp_bits + dp_bits[1:]
    cut = 2 * TILE
    groups = width // cut
    shared = (exps, inverse, key_line_back, query_line, backward, both_t)
    dq1, dk1, dv1, grad1 = attend_back(
        query, key, value, d_mixed, *shared, 0, 2 * (groups - 1)
    )
    early = jnp.concatenate([grad_w_output, grad1.reshape(-1, cut)], axis=0)
    early, d_mixed = tie(early, d_mixed)
    early_steps = moves.steps(first, second)
    early = early_steps.pop(0)(early)
    dq2, dk2, dv2, grad2 = attend_back(
        query, key, value, d_mixed, *shared, 2 * (groups - 1), 2
    )
    early, grad2 = tie(early, grad2)
    early = early_steps.pop(0)(early)
    late = late_sums(
        (dq1, dq2),
        (dk1, dk2),
        (dv1, dv2),
        w_query,
        w_key,
        rel_table,
        rel_gain,
        sums1,
        sums2,
        grad2,
    )
    for step in early_steps:
        early = step(early)
    for step in moves.steps(first, second):
        late = step(late)

    d_query, d_key, d_value = [
        jnp.concatenate([a[:rows], b[:rows]], axis=1) for a, b in ((dq1, dq2), (dk1, dk2), (dv1, dv2))
    ]
    input_grad = (
        d_residual + dot_nt(d_query, w_query) + dot_nt(d_key, w_key) + dot_nt(d_value, w_value)
    )

    early, late, ffn = wide(early), wide(late), wide(ffn)

    def rows_of(x, index, size=width):
        return x[index : index + size]

    def columns(parts):
        return jnp.concatenate(parts, axis=1)

    after = 3 * width
    table = columns([rows_of(late, after + rows * i, rows) for i in range(groups)])
    after = after + groups * rows
    vectors = columns([rows_of(late, after + 32 * i, 32) for i in range(groups)])
    grads = []
    for i in range(3):
        parts = [rows_of(early, (groups + 3 * g + i) * width) for g in range(groups - 1)]
        grads.append(columns(parts + [rows_of(late, i * width)]))
    chunks = units // CHUNK
    ffn_in = columns([rows_of(ffn, 4 * CHUNK * c) for c in range(chunks)])
    ffn_out = jnp.concatenate(
        [
            columns([rows_of(ffn, 4 * CHUNK * c + (2 + i) * CHUNK, CHUNK) for i in range(2)])
            for c in range(chunks)
        ],
        axis=0,
    )
    ffn_bias = rows_of(ffn, 4 * CHUNK * chunks, chunks).reshape(units)
    return (
        layer_out,
        input_grad,
        grads[0],
        vectors[16],
        grads[1],
        vectors[17],
        grads[2],
        vectors[18],
        columns([rows_of(early, i * width) for i in range(groups)]),
        vectors[2],
        vectors[0],
        vectors[1],
        ffn_in,
        ffn_bias,
        ffn_out,
        vectors[10],
        vectors[8],
        vectors[9],
        table,
        vectors[19],
        vectors[20],
    )


def solution(mesh):
    n_dp, n_mp = mesh.shape["dp"], mesh.shape["mp"]

    def body(*args):
        return per_device(*args, n_dp=n_dp, n_mp=n_mp)

    split = P(("dp", "mp"), None)
    weights = [P()] * 10 + [P(None, "mp"), P("mp"), P("mp", None)] + [P()] * 6
    return jax.shard_map(
        body,
        mesh=mesh,
        in_specs=(split, split, *weights, P(("dp", "mp")), split),
        out_specs=(
            split,
            split,
            *([P()] * 10),
            P(None, "mp"),
            P("mp"),
            P("mp", None),
            *([P()] * 6),
        ),
        check_vma=False,
    )
```

```python
import functools
import math

import jax
import jax.numpy as jnp
import numpy as np
from jax import lax
from jax.experimental import pallas as pl
from jax.experimental.pallas import tpu as pltpu
from jax.sharding import PartitionSpec as P

HEADS = 12
EPS = 1e-06
LOG2E = 1.4426950408889634
TILE = 128
CHUNK = 384
VMEM = 60 * 1024 * 1024
VECTOR_ROWS = (16, 17, 18, 2, 0, 1, 10, 8, 9, 19, 20)
BOTH = ("dp", "mp")
f32 = jnp.float32
bf16 = jnp.bfloat16


def bucket_line(half_rows):
    table_rows = 2 * half_rows
    middle = half_rows // 2
    relative = table_rows - 1 - np.arange(2 * table_rows - 1)
    signed = np.sign(relative)
    absolute = np.where((relative < middle) & (relative > -middle), middle - 1, np.abs(relative))
    log_place = (
        np.ceil(np.log(absolute / middle) / np.log((table_rows - 1) / middle) * (middle - 1))
        + middle
    )
    placed = np.where(absolute <= middle, relative, log_place * signed)
    return (placed + half_rows).astype(np.int32)


def dot(a, b):
    return jnp.dot(a, b, preferred_element_type=f32)


def dot_nt(a, b):
    return lax.dot_general(a, b, (((1,), (1,)), ((), ())), preferred_element_type=f32)


def dot_tn(a, b):
    return lax.dot_general(a, b, (((0,), (0,)), ((), ())), preferred_element_type=f32)


def wide(v):
    return v.astype(f32)


def ln_parts(v):
    average = jnp.mean(v, axis=-1, keepdims=True)
    center = v - average
    root = lax.rsqrt(jnp.mean(center * center, axis=-1, keepdims=True) + EPS)
    return center * root, root


def ln_back_rows(dy, normed, root, gain):
    dn = dy * gain
    first = jnp.mean(dn, axis=-1, keepdims=True)
    second = jnp.mean(dn * normed, axis=-1, keepdims=True)
    return root * (dn - first - normed * second)


def gelu_parts(v):
    bell = jnp.exp(-0.5 * v * v)
    t = 1.0 / (1.0 + (0.3275911 * math.sqrt(0.5)) * jnp.abs(v))
    poly = t * (
        0.254829592
        + t * (-0.284496736 + t * (1.421413741 + t * (-1.453152027 + t * 1.061405429)))
    )
    tail = 0.5 * poly * bell
    below = jnp.where(v >= 0, 1.0 - tail, tail)
    return v * below, below + v * bell * (1.0 / math.sqrt(2.0 * math.pi))


def pre_kernel(
    x_ref,
    table_ref,
    gain_ref,
    shift_ref,
    wq_ref,
    bq_ref,
    wk_ref,
    bk_ref,
    wv_ref,
    bv_ref,
    forward_ref,
    backward_ref,
    q_ref,
    k_ref,
    v_ref,
    key_line_ref,
    key_back_ref,
    query_line_ref,
    both_t_ref,
    both_ref,
):
    rows = x_ref.shape[0]

    @pl.when(pl.program_id(0) == 0)
    def _():
        both_ref[:rows, :] = x_ref[...]
        normed, _ = ln_parts(wide(table_ref[...]))
        rel = normed * wide(gain_ref[...])[None, :] + wide(shift_ref[...])[None, :]
        both_ref[rows:, :] = rel.astype(bf16)
        both_t_ref[...] = both_ref[...].T

    def project(w_ref, b_ref, part):
        return (dot(both_ref[part, :], w_ref[...]) + wide(b_ref[...])[None, :]).astype(bf16)

    here, there = slice(0, rows), slice(rows, 2 * rows)
    q_ref[...] = project(wq_ref, bq_ref, here)
    k_ref[...] = project(wk_ref, bk_ref, here)
    v_ref[...] = project(wv_ref, bv_ref, here)
    pos_query = project(wq_ref, bq_ref, there)
    pos_key = project(wk_ref, bk_ref, there)
    key_line_ref[...] = dot(forward_ref[...], pos_key).astype(bf16)
    key_back_ref[...] = dot(backward_ref[...], pos_key).astype(bf16)
    query_line_ref[...] = dot(backward_ref[...], pos_query).astype(bf16)


def pre(x, table, gain, shift, w_q, b_q, w_k, b_k, w_v, b_v, forward, backward):
    rows, width = x.shape
    cut = 2 * TILE

    def fixed(r, w):
        return pl.BlockSpec((r, w), lambda c: (0, 0))

    whole = pl.BlockSpec((width,), lambda c: (0,))
    weight = pl.BlockSpec((width, cut), lambda c: (0, c))
    vector = pl.BlockSpec((cut,), lambda c: (c,))
    one = pl.BlockSpec((rows, cut), lambda c: (0, c))
    two = pl.BlockSpec((2 * rows, cut), lambda c: (0, c))
    return pl.pallas_call(
        pre_kernel,
        grid=(width // cut,),
        in_specs=[fixed(rows, width), fixed(rows, width), whole, whole]
        + [weight, vector] * 3
        + [fixed(2 * rows, rows)] * 2,
        out_specs=[one] * 3 + [two] * 3 + [fixed(width, 2 * rows)],
        out_shape=[jax.ShapeDtypeStruct((rows, width), bf16)] * 3
        + [jax.ShapeDtypeStruct((2 * rows, width), bf16)] * 3
        + [jax.ShapeDtypeStruct((width, 2 * rows), bf16)],
        scratch_shapes=[pltpu.VMEM((2 * rows, width), bf16)],
        compiler_params=pltpu.CompilerParams(vmem_limit_bytes=VMEM),
        cost_estimate=pl.CostEstimate(
            flops=5_500_000_000, bytes_accessed=14_000_000, transcendentals=0
        ),
        name="pre",
    )(x, table, gain, shift, w_q, b_q, w_k, b_k, w_v, b_v, forward, backward)


def skewed(x, keep):
    turned = [
        pltpu.roll(x[:, TILE * b : TILE * (b + 1)], 1, 1, stride=1, stride_axis=0)
        for b in range(5)
    ]
    return [jnp.where(keep, turned[b], turned[b + 1]) for b in range(4)]


def unskewed(tiles, keep):
    zero = jnp.zeros((TILE, TILE), f32)
    turned = [zero] + [pltpu.roll(t, 0, 1, stride=1, stride_axis=0) for t in tiles] + [zero]
    return [jnp.where(keep, turned[b + 1], turned[b]) for b in range(5)]


def attend_kernel(
    group_ref,
    lengths_ref,
    q_ref,
    k_ref,
    v_ref,
    key_line_ref,
    query_line_ref,
    wo_ref,
    bo_ref,
    x_ref,
    gain_ref,
    shift_ref,
    out_ref,
    exp_ref,
    inv_ref,
    normed_ref,
    root_ref,
    h_ref,
    side_ref,
    bias_ref,
):
    @pl.when(pl.program_id(0) == 0)
    def _():
        normed_ref[...] = wide(x_ref[...]) + wide(bo_ref[...])[None, :]
        size = bias_ref.shape[0]
        shift = size.bit_length() - 1 - group_ref[0]
        row = lax.broadcasted_iota(jnp.int32, (size, 1), 0)
        col = lax.broadcasted_iota(jnp.int32, (1, size), 1)
        owner = jnp.right_shift(col, shift)
        limit = jnp.zeros((1, size), jnp.int32)
        for slot in range(4):
            limit = jnp.where(owner == slot, lengths_ref[0, slot], limit)
        owner = jnp.where(col - jnp.left_shift(owner, shift) < limit, owner, -1)
        valid = jnp.right_shift(row, shift) == owner
        bias_ref[...] = jnp.where(valid, 0.0, -1e30).astype(f32)

    lane = lax.broadcasted_iota(jnp.int32, (1, TILE), 1)
    keep = lax.broadcasted_iota(jnp.int32, (TILE, TILE), 1) <= lax.broadcasted_iota(
        jnp.int32, (TILE, TILE), 0
    )
    mine = [lane < 64, lane >= 64]
    scale = LOG2E / math.sqrt(192)
    for h in range(2):
        for t in range(4):
            km = jnp.where(mine[h], k_ref[TILE * t : TILE * (t + 1), :], 0)
            start = 384 - TILE * t
            sk = skewed(dot_nt(km, query_line_ref[start : start + 640, :]), keep)
            for b in range(4):
                side_ref[h, TILE * b : TILE * (b + 1), TILE * t : TILE * (t + 1)] = sk[b].T
        for t in range(4):
            rows = slice(TILE * t, TILE * (t + 1))
            qm = jnp.where(mine[h], q_ref[rows, :], 0)
            start = 384 - TILE * t
            near = skewed(dot_nt(qm, key_line_ref[start : start + 640, :]), keep)
            content = dot_nt(qm, k_ref[...])
            parts = []
            for b in range(4):
                cols = slice(TILE * b, TILE * (b + 1))
                total = content[:, cols] + near[b] + side_ref[h, rows, cols]
                parts.append(total * scale + bias_ref[rows, cols])
            top = jnp.max(
                jnp.maximum(jnp.maximum(parts[0], parts[1]), jnp.maximum(parts[2], parts[3])),
                axis=1,
                keepdims=True,
            )
            low = [jnp.exp2(p - top).astype(bf16) for p in parts]
            total = jnp.sum(
                (wide(low[0]) + wide(low[1])) + (wide(low[2]) + wide(low[3])),
                axis=1,
                keepdims=True,
            )
            exps = jnp.concatenate(low, axis=1)
            exp_ref[h, rows, :] = exps
            inverse = 1.0 / total
            out = (dot(exps, v_ref[...]) * inverse).astype(bf16)
            inverse = jnp.broadcast_to(inverse, (TILE, TILE))
            if h == 0:
                inv_ref[0, rows, :] = inverse
                out_ref[rows, :] = out
            else:
                inv_ref[0, rows, :] = jnp.where(mine[0], inv_ref[0, rows, :], inverse)
                out_ref[rows, :] = jnp.where(mine[0], out_ref[rows, :], out)
    normed_ref[...] += dot(out_ref[...], wo_ref[...])

    @pl.when(pl.program_id(0) == pl.num_programs(0) - 1)
    def _():
        gain, shift = wide(gain_ref[...])[None, :], wide(shift_ref[...])[None, :]
        for r in range(0, h_ref.shape[0], TILE):
            rows = slice(r, r + TILE)
            normed, root = ln_parts(normed_ref[rows, :])
            normed_ref[rows, :] = normed
            root_ref[rows, :] = jnp.broadcast_to(root, (TILE, TILE))
            h_ref[rows, :] = (normed * gain + shift).astype(bf16)


def attend(group, lengths, q, k, v, key_line, query_line, w_output, b_output, x, gain, shift):
    rows, width = q.shape
    pairs = width // TILE
    col = pl.BlockSpec((rows, TILE), lambda g: (0, g))
    line = pl.BlockSpec((2 * rows, TILE), lambda g: (0, g))
    scalars = pl.BlockSpec(memory_space=pltpu.SMEM)
    full = pl.BlockSpec((rows, width), lambda g: (0, 0))
    vector = pl.BlockSpec((width,), lambda g: (0,))
    return pl.pallas_call(
        attend_kernel,
        grid=(pairs,),
        in_specs=[scalars, scalars, col, col, col, line, line]
        + [pl.BlockSpec((TILE, width), lambda g: (g, 0)), vector, full, vector, vector],
        out_specs=[
            col,
            pl.BlockSpec((2, rows, rows), lambda g: (g, 0, 0)),
            pl.BlockSpec((1, rows, TILE), lambda g: (g, 0, 0)),
            full,
            pl.BlockSpec((rows, TILE), lambda g: (0, 0)),
            full,
        ],
        out_shape=[
            jax.ShapeDtypeStruct((rows, width), bf16),
            jax.ShapeDtypeStruct((2 * pairs, rows, rows), bf16),
            jax.ShapeDtypeStruct((pairs, rows, TILE), f32),
            jax.ShapeDtypeStruct((rows, width), f32),
            jax.ShapeDtypeStruct((rows, TILE), f32),
            jax.ShapeDtypeStruct((rows, width), bf16),
        ],
        scratch_shapes=[pltpu.VMEM((2, rows, rows), f32), pltpu.VMEM((rows, rows), f32)],
        compiler_params=pltpu.CompilerParams(vmem_limit_bytes=VMEM),
        cost_estimate=pl.CostEstimate(
            flops=18_000_000_000, bytes_accessed=16_000_000, transcendentals=3_200_000
        ),
        name="attend",
    )(group, lengths, q, k, v, key_line, query_line, w_output, b_output, x, gain, shift)


def attend_back_kernel(
    q_ref,
    k_ref,
    v_ref,
    do_ref,
    exp_ref,
    inv_ref,
    key_line_ref,
    query_line_ref,
    places_ref,
    both_t_ref,
    dq_ref,
    dk_ref,
    dv_ref,
    grad_ref,
    ds_ref,
    dst_ref,
    query_band,
    key_band,
):
    @pl.when(pl.program_id(0) == 0)
    def _():
        query_band[...] = jnp.zeros_like(query_band)
        key_band[...] = jnp.zeros_like(key_band)

    scale = 1.0 / math.sqrt(192)
    lane = lax.broadcasted_iota(jnp.int32, (1, TILE), 1)
    sub = lax.broadcasted_iota(jnp.int32, (TILE, 1), 0)
    keep = lax.broadcasted_iota(jnp.int32, (TILE, TILE), 1) >= lax.broadcasted_iota(
        jnp.int32, (TILE, TILE), 0
    )
    mine = [lane < 64, lane >= 64]
    mine_t = [sub < 64, sub >= 64]
    flip = (
        lax.broadcasted_iota(jnp.int32, (256, 256), 0)
        + lax.broadcasted_iota(jnp.int32, (256, 256), 1)
        == 255
    )
    flip = flip.astype(f32).astype(bf16)

    def reverse(x):
        return jnp.concatenate([dot(flip, x[256:]), dot(flip, x[:256])], axis=0).astype(bf16)

    q = q_ref[...]
    k = reverse(k_ref[...])
    v = reverse(v_ref[...])
    q_t = q.T
    k_t = k.T
    do = (wide(do_ref[...]) * inv_ref[0]).astype(bf16)
    do_t = do.T
    dv_t = None
    dqs, dks, key_lines, query_lines = [], [], [], []
    for h in range(2):
        dom = jnp.where(mine[h], do, 0)
        for t in range(4):
            rows = slice(TILE * t, TILE * (t + 1))
            dp = dot_nt(dom[rows], v)
            e = jnp.concatenate(
                [dot(exp_ref[h, rows, 256:], flip), dot(exp_ref[h, rows, :256], flip)], axis=1
            )
            ep = e * dp
            mean = jnp.sum(ep, axis=1, keepdims=True) * inv_ref[0, rows, 64 * h : 64 * h + 1]
            ds = ep - e * mean
            ds_ref[h, rows, :] = ds.astype(bf16)
            out = unskewed([ds[:, TILE * b : TILE * (b + 1)] for b in range(4)], keep)
            for b in range(5):
                query_band[h, rows, TILE * (t + b) : TILE * (t + b + 1)] = out[b].astype(bf16)
        for t in range(4):
            rows = slice(TILE * t, TILE * (t + 1))
            turned = [ds_ref[h, TILE * b : TILE * (b + 1), rows].T for b in range(4)]
            for b in range(4):
                dst_ref[h, rows, TILE * b : TILE * (b + 1)] = turned[b]
            out = unskewed([wide(x) for x in turned], keep)
            for b in range(5):
                key_band[h, rows, TILE * (t + b) : TILE * (t + b + 1)] = out[b].astype(bf16)
        part = dot(jnp.where(mine_t[h], do_t, 0), exp_ref[h])
        dv_t = part if dv_t is None else dv_t + part
        dq, dk, key_line, query_line = [], [], [], []
        for i in range(2):
            rows = slice(256 * i, 256 * (i + 1))
            band = slice(256 * i, 256 * i + 768)
            dq.append(dot(ds_ref[h, rows, :], k) + dot(query_band[h, rows, band], key_line_ref[band, :]))
            dk.append(dot(dst_ref[h, rows, :], q) + dot(key_band[h, rows, band], query_line_ref[band, :]))
            key_line.append(dot(jnp.where(mine_t[h], q_t[:, rows], 0), query_band[h, rows, band]))
            query_line.append(dot(jnp.where(mine_t[h], k_t[:, rows], 0), key_band[h, rows, band]))
        dqs.append(jnp.concatenate(dq, axis=0))
        dks.append(jnp.concatenate(dk, axis=0))
        key_lines.append(key_line)
        query_lines.append(query_line)
    size = q.shape[0]
    dq_ref[:size, :] = (jnp.where(mine[0], dqs[0], dqs[1]) * scale).astype(bf16)
    dk_ref[:size, :] = reverse((jnp.where(mine[0], dks[0], dks[1]) * scale).astype(bf16))
    dv_ref[...] = dv_t.T.astype(bf16)
    for lines, ref in ((key_lines, dk_ref), (query_lines, dq_ref)):
        first = lines[0][0] + lines[1][0]
        second = lines[0][1] + lines[1][1]
        whole = jnp.concatenate(
            [first[:, :256], first[:, 256:] + second[:, :512], second[:, 512:]], axis=1
        )
        ref[size:, :] = dot((whole * scale).astype(bf16), places_ref[...]).T.astype(bf16)
    width = both_t_ref.shape[0]
    grad_ref[0, :width, :] = dot(both_t_ref[...], dq_ref[...]).astype(bf16)
    grad_ref[0, width : 2 * width, :] = dot(both_t_ref[...], dk_ref[...]).astype(bf16)
    grad_ref[0, 2 * width :, :] = dot(both_t_ref[:, :size], dv_ref[...]).astype(bf16)


def attend_back(
    q, k, v, do, exps, inverse, key_line, query_line, places, both_t, first, count
):
    rows, width = q.shape
    col = pl.BlockSpec((rows, TILE), lambda g: (0, first + g))
    line = pl.BlockSpec((2 * rows, TILE), lambda g: (0, first + g))
    both = pl.BlockSpec((2 * rows, TILE), lambda g: (0, g))
    per = min(2, count)
    return pl.pallas_call(
        attend_back_kernel,
        grid=(count,),
        in_specs=[
            col,
            col,
            col,
            col,
            pl.BlockSpec((2, rows, rows), lambda g: (first + g, 0, 0)),
            pl.BlockSpec((1, rows, TILE), lambda g: (first + g, 0, 0)),
            line,
            line,
            pl.BlockSpec((2 * rows, rows), lambda g: (0, 0)),
            pl.BlockSpec((width, 2 * rows), lambda g: (0, 0)),
        ],
        out_specs=[
            both,
            both,
            pl.BlockSpec((rows, TILE), lambda g: (0, g)),
            pl.BlockSpec((1, 3 * width, TILE), lambda g: (g // per, 0, g % per)),
        ],
        out_shape=[
            jax.ShapeDtypeStruct((2 * rows, count * TILE), bf16),
            jax.ShapeDtypeStruct((2 * rows, count * TILE), bf16),
            jax.ShapeDtypeStruct((rows, count * TILE), bf16),
            jax.ShapeDtypeStruct((count // per, 3 * width, per * TILE), bf16),
        ],
        scratch_shapes=[
            pltpu.VMEM((2, rows, rows), bf16),
            pltpu.VMEM((2, rows, rows), bf16),
            pltpu.VMEM((2, rows, 2 * rows), bf16),
            pltpu.VMEM((2, rows, 2 * rows), bf16),
        ],
        compiler_params=pltpu.CompilerParams(vmem_limit_bytes=VMEM),
        cost_estimate=pl.CostEstimate(
            flops=count * 4_000_000_000, bytes_accessed=count * 3_000_000, transcendentals=0
        ),
        name="attend_back",
    )(q, k, v, do, exps, inverse, key_line, query_line, places, both_t)


def ffn_kernel(
    h_hbm,
    normed_hbm,
    root_ref,
    cot_hbm,
    mixed_hbm,
    wo_hbm,
    gain1_ref,
    shift1_ref,
    b_outer_ref,
    gain2_ref,
    shift2_ref,
    bin_ref,
    win_hbm,
    wout_hbm,
    got_in_hbm,
    got_out_hbm,
    other_in_hbm,
    other_out_hbm,
    out_ref,
    dbranch_ref,
    active_ref,
    dinner_ref,
    dres_ref,
    dmixed_ref,
    grad_ref,
    sums1_ref,
    sums2_ref,
    h_ref,
    normed_ref,
    cot_ref,
    mixed_ref,
    wo_ref,
    win_ref,
    wout_ref,
    far_in_ref,
    far_out_ref,
    bias_ref,
    slope_ref,
    far_slope_ref,
    total_ref,
    dpre_ref,
    dattn_ref,
    sems,
    *,
    chunk,
):
    rows, width = h_ref.shape
    own = active_ref.shape[0]
    n = got_in_hbm.shape[0]
    units = got_in_hbm.shape[2]
    chunks = units // chunk
    copies = [
        pltpu.make_async_copy(source, target, sems.at[i])
        for i, (source, target) in enumerate(
            [
                (h_hbm, h_ref),
                (win_hbm, win_ref),
                (wout_hbm, wout_ref),
                (got_in_hbm, far_in_ref.at[:n]),
                (got_out_hbm, far_out_ref.at[:n]),
                (other_in_hbm, far_in_ref.at[n:]),
                (other_out_hbm, far_out_ref.at[n:]),
                (normed_hbm, normed_ref),
                (cot_hbm, cot_ref),
                (wo_hbm, wo_ref),
                (mixed_hbm, mixed_ref),
            ]
        )
    ]
    for copy in copies:
        copy.start()
    bias_ref[...] = wide(bin_ref[...])[None, :]
    total_ref[...] = jnp.zeros_like(total_ref)

    def forward(w_in, b_in, w_out, keep):
        for r in range(0, rows, 256):
            part = slice(r, r + 256)
            active, slope = gelu_parts(dot(h_ref[part, :], w_in) + b_in)
            active = active.astype(bf16)
            keep(part, active, slope.astype(bf16))
            total_ref[part, :] += dot(active, w_out)

    for copy in copies[:3]:
        copy.wait()

    def own_step(c, carry):
        cols = pl.ds(pl.multiple_of(c * CHUNK, CHUNK), CHUNK)

        def keep(part, active, slope):
            active_ref[c, part, :] = active
            slope_ref[c, part, :] = slope

        forward(win_ref[:, cols], bias_ref[:, cols], wout_ref[cols, :], keep)
        return carry

    lax.fori_loop(0, own, own_step, 0)
    for copy in copies[3:7]:
        copy.wait()

    def far_slices(c):
        s = c // chunks
        if chunks == 1:
            return s, slice(0, chunk)
        return s, pl.ds(pl.multiple_of(c % chunks * chunk, TILE), chunk)

    def far_step(c, carry):
        s, cols = far_slices(c)

        def keep(part, active, slope):
            far_slope_ref[c, part, :] = slope

        b_in = wide(far_out_ref[s, units : units + 1, cols])
        forward(far_in_ref[s, :, cols], b_in, far_out_ref[s, cols, :], keep)
        return carry

    lax.fori_loop(0, 2 * n * chunks, far_step, 0)
    for copy in copies[7:9]:
        copy.wait()
    gain1, shift1, b_outer, gain2, shift2 = [
        wide(r[...])[None, :] for r in (gain1_ref, shift1_ref, b_outer_ref, gain2_ref, shift2_ref)
    ]
    pad = jnp.zeros((5, width), f32)
    sums = [jnp.zeros((1, width), f32) for _ in range(3)]
    for r in range(0, rows, TILE):
        part = slice(r, r + TILE)
        normed, root = ln_parts(normed_ref[part, :] * gain1 + shift1 + total_ref[part, :] + b_outer)
        out_ref[part, :] = normed * gain2 + shift2
        dy = wide(cot_ref[part, :])
        d = ln_back_rows(dy, normed, root, gain2)
        dpre_ref[part, :] = d
        low = d.astype(bf16)
        dbranch_ref[part, :] = low
        sums[0] += jnp.sum(dy * normed, axis=0, keepdims=True)
        sums[1] += jnp.sum(dy, axis=0, keepdims=True)
        sums[2] += jnp.sum(wide(low), axis=0, keepdims=True)
    sums2_ref[...] = jnp.concatenate(sums + [pad], axis=0)

    def backward(w_in, w_out, slope, keep):
        for r in range(0, rows, 256):
            part = slice(r, r + 256)
            d = (dot_nt(dbranch_ref[part, :], w_out) * wide(slope(part))).astype(bf16)
            if keep is not None:
                keep(part, d)
            dpre_ref[part, :] += dot_nt(d, w_in)

    def own_back(c, carry):
        cols = pl.ds(pl.multiple_of(c * CHUNK, CHUNK), CHUNK)

        def keep(part, d):
            dinner_ref[c, part, :] = d

        backward(win_ref[:, cols], wout_ref[cols, :], lambda part: slope_ref[c, part, :], keep)
        return carry

    def far_back(c, carry):
        s, cols = far_slices(c)
        slope = lambda part: far_slope_ref[c, part, :]
        backward(far_in_ref[s, :, cols], far_out_ref[s, cols, :], slope, None)
        return carry

    lax.fori_loop(0, own, own_back, 0)
    lax.fori_loop(0, 2 * n * chunks, far_back, 0)
    for copy in copies[9:]:
        copy.wait()
    sums = [jnp.zeros((1, width), f32) for _ in range(3)]
    for r in range(0, rows, TILE):
        part = slice(r, r + TILE)
        dy = dpre_ref[part, :]
        normed = normed_ref[part, :]
        d = ln_back_rows(dy, normed, root_ref[part, 0:1], gain1)
        dres_ref[part, :] = d
        low = d.astype(bf16)
        dattn_ref[part, :] = low
        dmixed_ref[part, :] = dot_nt(low, wo_ref[...]).astype(bf16)
        sums[0] += jnp.sum(dy * normed, axis=0, keepdims=True)
        sums[1] += jnp.sum(dy, axis=0, keepdims=True)
        sums[2] += jnp.sum(wide(low), axis=0, keepdims=True)
    sums1_ref[...] = jnp.concatenate(sums + [pad], axis=0)
    grad = dot(mixed_ref[...].T, dattn_ref[...]).astype(bf16)
    for i in range(width // 256):
        grad_ref[width * i : width * (i + 1), :] = grad[:, 256 * i : 256 * (i + 1)]


def ffn(h, normed, root, cot, mixed, w_output, vectors, b_in, w_in, w_out, got, other):
    rows, width = h.shape
    own = w_in.shape[1] // CHUNK
    n, _, units = got[0].shape
    chunk = min(CHUNK, units)
    far = 2 * n * (units // chunk)
    anywhere = pl.BlockSpec(memory_space=pl.ANY)
    vmem = pl.BlockSpec(memory_space=pltpu.VMEM)

    def low(*shape):
        return jax.ShapeDtypeStruct(shape, bf16)

    def full(*shape):
        return jax.ShapeDtypeStruct(shape, f32)

    return pl.pallas_call(
        functools.partial(ffn_kernel, chunk=chunk),
        in_specs=[anywhere, anywhere, vmem, anywhere, anywhere, anywhere]
        + [vmem] * 6
        + [anywhere] * 6,
        out_shape=[
            full(rows, width),
            low(rows, width),
            low(own, rows, CHUNK),
            low(own, rows, CHUNK),
            full(rows, width),
            low(rows, width),
            low(width * width // 256, 256),
            full(8, width),
            full(8, width),
        ],
        scratch_shapes=[
            pltpu.VMEM((rows, width), bf16),
            pltpu.VMEM((rows, width), f32),
            pltpu.VMEM((rows, width), bf16),
            pltpu.VMEM((rows, width), bf16),
            pltpu.VMEM((width, width), bf16),
            pltpu.VMEM(w_in.shape, bf16),
            pltpu.VMEM(w_out.shape, bf16),
            pltpu.VMEM((2 * n, *got[0].shape[1:]), bf16),
            pltpu.VMEM((2 * n, *got[1].shape[1:]), bf16),
            pltpu.VMEM((1, own * CHUNK), f32),
            pltpu.VMEM((own, rows, CHUNK), bf16),
            pltpu.VMEM((far, rows, chunk), bf16),
            pltpu.VMEM((rows, width), f32),
            pltpu.VMEM((rows, width), f32),
            pltpu.VMEM((rows, width), bf16),
            pltpu.SemaphoreType.DMA((11,)),
        ],
        compiler_params=pltpu.CompilerParams(vmem_limit_bytes=VMEM),
        cost_estimate=pl.CostEstimate(
            flops=36 * rows * width * width, bytes_accessed=24_000_000, transcendentals=3_200_000
        ),
        name="ffn",
    )(
        h,
        normed,
        root,
        cot,
        mixed,
        w_output,
        *vectors,
        b_in,
        w_in,
        w_out,
        got[0],
        got[1],
        other[0],
        other[1],
    )


def ffn_grads_kernel(
    start_ref,
    h_ref,
    db_ref,
    active_ref,
    dinner_ref,
    far_h_ref,
    far_db_ref,
    win_ref,
    bin_ref,
    wout_ref,
    out_ref,
    h_t,
    far_t,
    bias_ref,
    *,
    chunks,
):
    c = pl.program_id(0)
    tail = 4 * CHUNK * chunks

    @pl.when(c == 0)
    def _():
        bias_ref[...] = wide(bin_ref[...])[None, :]
        h_t[...] = h_ref[...].T
        far_t[...] = far_h_ref[...].T
        out_ref[tail:, :] = jnp.zeros_like(out_ref[tail:, :])

    w_in, w_out = win_ref[...], wout_ref[...]
    place = (start_ref[0] + c) * CHUNK
    b_in = bias_ref[:, pl.ds(pl.multiple_of(place, TILE), CHUNK)]
    active, dinner = [], []
    for r in range(0, far_h_ref.shape[0], 256):
        rows = slice(r, r + 256)
        a, slope = gelu_parts(dot(far_h_ref[rows, :], w_in) + b_in)
        active.append(a.astype(bf16))
        dinner.append((dot_nt(far_db_ref[rows, :], w_out) * slope).astype(bf16))
    active = jnp.concatenate(active, axis=0)
    dinner = jnp.concatenate(dinner, axis=0)
    base = pl.multiple_of(c * 4 * CHUNK, 4 * CHUNK)
    out_ref[pl.ds(base, 2 * CHUNK), :] = (
        dot(h_t[...], dinner_ref[0]) + dot(far_t[...], dinner)
    ).astype(bf16)
    grad = (dot(active_ref[0].T, db_ref[...]) + dot(active.T, far_db_ref[...])).astype(bf16)
    out_ref[pl.ds(base + 2 * CHUNK, CHUNK), :] = grad[:, :CHUNK]
    out_ref[pl.ds(base + 3 * CHUNK, CHUNK), :] = grad[:, CHUNK:]
    bias = jnp.sum(wide(dinner_ref[0]), axis=0, keepdims=True)
    bias = bias + jnp.sum(wide(dinner), axis=0, keepdims=True)
    place = lax.broadcasted_iota(jnp.int32, (16, 1), 0) == c
    out_ref[tail : tail + 16, :] = jnp.where(place, bias.astype(bf16), out_ref[tail : tail + 16, :])


def ffn_grads(h, db, active, dinner, far_h, far_db, w_in, b_in, w_out, start, chunks, extra):
    rows, width = h.shape
    units = w_in.shape[-1]
    far = far_h.shape[0]

    def fixed(r, w):
        return pl.BlockSpec((r, w), lambda c, s: (0, 0))

    total = chunks * 4 * CHUNK + extra
    return pl.pallas_call(
        functools.partial(ffn_grads_kernel, chunks=chunks),
        grid_spec=pltpu.PrefetchScalarGridSpec(
            num_scalar_prefetch=1,
            grid=(chunks,),
            in_specs=[
                fixed(rows, width),
                fixed(rows, width),
                pl.BlockSpec((1, rows, CHUNK), lambda c, s: (s[0] + c, 0, 0)),
                pl.BlockSpec((1, rows, CHUNK), lambda c, s: (s[0] + c, 0, 0)),
                fixed(far, width),
                fixed(far, width),
                pl.BlockSpec((width, CHUNK), lambda c, s: (0, s[0] + c)),
                pl.BlockSpec((units,), lambda c, s: (0,)),
                pl.BlockSpec((CHUNK, width), lambda c, s: (s[0] + c, 0)),
            ],
            out_specs=fixed(total, CHUNK),
            scratch_shapes=[
                pltpu.VMEM((width, rows), bf16),
                pltpu.VMEM((width, far), bf16),
                pltpu.VMEM((1, units), f32),
            ],
        ),
        out_shape=jax.ShapeDtypeStruct((total, CHUNK), bf16),
        compiler_params=pltpu.CompilerParams(vmem_limit_bytes=VMEM),
        cost_estimate=pl.CostEstimate(
            flops=4 * (rows + 2 * far) * width * chunks * CHUNK,
            bytes_accessed=16_000_000,
            transcendentals=2 * far * chunks * CHUNK,
        ),
        name="ffn_grads",
    )(start, h, db, active, dinner, far_h, far_db, w_in, b_in, w_out)


def late_kernel(*refs, pieces):
    dq_refs, dk_refs, dv_refs = [refs[pieces * i : pieces * (i + 1)] for i in range(3)]
    wq_ref, wk_ref, table_ref, gain_ref, sums1_ref, sums2_ref = refs[3 * pieces : 3 * pieces + 6]
    *grad_refs, out_ref = refs[3 * pieces + 6 :]
    rows, width = table_ref.shape
    there = slice(rows, 2 * rows)
    gain = wide(gain_ref[...])[None, :]

    def column_sums(parts):
        return jnp.concatenate(
            [jnp.sum(wide(x[...]), axis=0, keepdims=True) for x in parts], axis=1
        )

    place = 0
    for ref in grad_refs:
        out_ref[: 3 * width, place : place + ref.shape[1]] = ref[...]
        place += ref.shape[1]
    dy = 0.0
    for parts, w_ref in ((dq_refs, wq_ref), (dk_refs, wk_ref)):
        place = 0
        for part in parts:
            dy = dy + dot_nt(part[there, :], w_ref[:, place : place + part.shape[1]])
            place += part.shape[1]
    normed, root = ln_parts(wide(table_ref[...]))
    table = ln_back_rows(dy, normed, root, gain).astype(bf16)
    vectors = jnp.concatenate(
        [
            sums1_ref[...],
            sums2_ref[...],
            column_sums(dq_refs),
            column_sums(dk_refs),
            column_sums(dv_refs),
            jnp.sum(dy * normed, axis=0, keepdims=True),
            jnp.sum(dy, axis=0, keepdims=True),
            jnp.zeros((11, width), f32),
        ],
        axis=0,
    ).astype(bf16)
    base = 3 * width
    for i in range(width // 256):
        out_ref[base + rows * i : base + rows * (i + 1), :] = table[:, 256 * i : 256 * (i + 1)]
    base = base + rows * (width // 256)
    for i in range(width // 256):
        out_ref[base + 32 * i : base + 32 * (i + 1), :] = vectors[:, 256 * i : 256 * (i + 1)]
    base = base + 32 * (width // 256)
    out_ref[base:, :] = jnp.zeros((out_ref.shape[0] - base, 256), bf16)


def late_sums(d_query, d_key, d_value, w_query, w_key, table, gain, sums1, sums2, grads):
    rows, width = table.shape
    total = -(-(3 * width + (rows + 32) * (width // 256)) // 256) * 256
    return pl.pallas_call(
        functools.partial(late_kernel, pieces=len(d_query)),
        out_shape=jax.ShapeDtypeStruct((total, 256), bf16),
        compiler_params=pltpu.CompilerParams(vmem_limit_bytes=VMEM),
        cost_estimate=pl.CostEstimate(
            flops=1_300_000_000, bytes_accessed=12_000_000, transcendentals=0
        ),
        name="late_sums",
    )(*d_query, *d_key, *d_value, w_query, w_key, table, gain, sums1, sums2, *grads)


def input_grad_kernel(*refs, pieces):
    parts = [refs[pieces * i : pieces * (i + 1)] for i in range(3)]
    weights = refs[3 * pieces : 3 * pieces + 3]
    res_ref, out_ref = refs[3 * pieces + 3 :]
    for r in range(0, res_ref.shape[0], 256):
        rows = slice(r, r + 256)
        total = res_ref[rows, :]
        for part, w_ref in zip(parts, weights, strict=True):
            place = 0
            for x in part:
                total = total + dot_nt(x[rows, :], w_ref[:, place : place + x.shape[1]])
                place += x.shape[1]
        out_ref[rows, :] = total


def input_gradient(d_query, d_key, d_value, w_query, w_key, w_value, d_residual):
    rows, width = d_residual.shape
    pieces = len(d_query)
    specs = [
        pl.BlockSpec((rows, x.shape[1]), lambda i: (0, 0)) for x in (*d_query, *d_key, *d_value)
    ]
    square = pl.BlockSpec((width, width), lambda i: (0, 0))
    full = pl.BlockSpec((rows, width), lambda i: (0, 0))
    return pl.pallas_call(
        functools.partial(input_grad_kernel, pieces=pieces),
        grid=(1,),
        in_specs=[*specs, square, square, square, full],
        out_specs=full,
        out_shape=jax.ShapeDtypeStruct((rows, width), f32),
        compiler_params=pltpu.CompilerParams(vmem_limit_bytes=VMEM),
        cost_estimate=pl.CostEstimate(
            flops=6 * rows * width * width, bytes_accessed=10_000_000, transcendentals=0
        ),
        name="input_gradient",
    )(*d_query, *d_key, *d_value, w_query, w_key, w_value, d_residual)


def in_order(core_ref, mine_ref, other_ref, write):
    @pl.when(core_ref[0] == 0)
    def _():
        write(mine_ref, other_ref)

    @pl.when(core_ref[0] != 0)
    def _():
        write(other_ref, mine_ref)


def ffn_result_kernel(core_ref, mine_ref, other_ref, in_ref, out_ref, bias_ref):
    half = mine_ref.shape[0]
    chunks = in_ref.shape[1] // (2 * CHUNK)

    def write(first, second):
        rows = []
        for i, part in enumerate((first, second)):
            for c in range(chunks):
                cols = slice((i * chunks + c) * CHUNK, (i * chunks + c + 1) * CHUNK)
                base = 4 * CHUNK * c
                in_ref[:, cols] = wide(part[base : base + 2 * CHUNK, :])
                for k in range(2):
                    place = base + (2 + k) * CHUNK
                    out_ref[cols, CHUNK * k : CHUNK * (k + 1)] = wide(part[place : place + CHUNK, :])
            tail = wide(part[4 * CHUNK * chunks : 4 * CHUNK * chunks + 16, :])
            rows = rows + [tail[c : c + 1, :] for c in range(chunks)]
        bias_ref[...] = jnp.concatenate(rows, axis=1).reshape(bias_ref.shape)

    in_order(core_ref, mine_ref, other_ref, write)


def ffn_result(core, mine, other, width, units):
    smem = pl.BlockSpec(memory_space=pltpu.SMEM)
    vmem = pl.BlockSpec(memory_space=pltpu.VMEM)
    return pl.pallas_call(
        ffn_result_kernel,
        in_specs=[smem, vmem, vmem],
        out_shape=[
            jax.ShapeDtypeStruct((width, units), f32),
            jax.ShapeDtypeStruct((units, width), f32),
            jax.ShapeDtypeStruct((units,), f32),
        ],
        compiler_params=pltpu.CompilerParams(vmem_limit_bytes=VMEM),
        cost_estimate=pl.CostEstimate(flops=0, bytes_accessed=15_000_000, transcendentals=0),
        name="ffn_result",
    )(core, mine, other)


def early_result_kernel(core_ref, mine_ref, other_ref, wo_ref, q_ref, k_ref, v_ref):
    width = wo_ref.shape[0]
    size = width // 2
    blocks = mine_ref.shape[0] // size
    groups = width // 256

    def write(first, second):
        for b in range(2 * blocks):
            part = first if b < blocks else second
            value = wide(part[size * (b % blocks) : size * (b % blocks + 1), :])
            array, half = divmod(b, 2)
            rows = slice(size * half, size * (half + 1))
            if array < groups:
                wo_ref[rows, 256 * array : 256 * (array + 1)] = value
            else:
                group, which = divmod(array - groups, 3)
                (q_ref, k_ref, v_ref)[which][rows, 256 * group : 256 * (group + 1)] = value

    in_order(core_ref, mine_ref, other_ref, write)


def early_result(core, mine, other, width):
    smem = pl.BlockSpec(memory_space=pltpu.SMEM)
    vmem = pl.BlockSpec(memory_space=pltpu.VMEM)
    return pl.pallas_call(
        early_result_kernel,
        in_specs=[smem, vmem, vmem],
        out_shape=[jax.ShapeDtypeStruct((width, width), f32)] * 4,
        compiler_params=pltpu.CompilerParams(vmem_limit_bytes=VMEM),
        cost_estimate=pl.CostEstimate(flops=0, bytes_accessed=13_000_000, transcendentals=0),
        name="early_result",
    )(core, mine, other)


def late_result_kernel(core_ref, mine_ref, other_ref, *refs):
    q_ref, k_ref, v_ref, table_ref = refs[3:7]
    vector_refs, all_ref = refs[7:-1], refs[-1]
    width, rows = q_ref.shape[0], table_ref.shape[0]
    groups = table_ref.shape[1] // 256
    half = mine_ref.shape[0]

    def write(first, second):
        all_ref[:half, :] = first[...]
        all_ref[half:, :] = second[...]

    in_order(core_ref, mine_ref, other_ref, write)
    for i, ref in enumerate((q_ref, k_ref, v_ref)):
        ref[...] = wide(all_ref[width * i : width * (i + 1), :])
    base = 3 * width
    for i in range(groups):
        place = base + rows * i
        table_ref[:, 256 * i : 256 * (i + 1)] = wide(all_ref[place : place + rows, :])
    base = base + rows * groups
    parts = [wide(all_ref[base + 32 * i : base + 32 * (i + 1), :]) for i in range(groups)]
    vectors = jnp.concatenate(parts, axis=1)
    for place, ref in zip(VECTOR_ROWS, vector_refs, strict=True):
        ref[...] = vectors[place : place + 1, :].reshape(ref.shape)


def late_result(core, mine, other, grads, rows):
    width = grads[0].shape[0]
    groups = width // 256
    smem = pl.BlockSpec(memory_space=pltpu.SMEM)
    half = pl.BlockSpec(mine.shape, lambda i: (0, 0))
    anywhere = pl.BlockSpec(memory_space=pl.ANY)
    last = pl.BlockSpec((width, 256), lambda i: (0, groups - 1))
    vector = pl.BlockSpec((width,), lambda i: (0,))
    return pl.pallas_call(
        late_result_kernel,
        grid=(1,),
        in_specs=[smem, half, half] + [anywhere] * 3,
        out_specs=[last] * 3
        + [pl.BlockSpec((rows, width), lambda i: (0, 0))]
        + [vector] * len(VECTOR_ROWS),
        out_shape=[jax.ShapeDtypeStruct((width, width), f32)] * 3
        + [jax.ShapeDtypeStruct((rows, width), f32)]
        + [jax.ShapeDtypeStruct((width,), f32)] * len(VECTOR_ROWS),
        input_output_aliases={3: 0, 4: 1, 5: 2},
        scratch_shapes=[pltpu.VMEM((2 * mine.shape[0], 256), bf16)],
        compiler_params=pltpu.CompilerParams(vmem_limit_bytes=VMEM),
        cost_estimate=pl.CostEstimate(flops=0, bytes_accessed=6_000_000, transcendentals=0),
        name="late_result",
    )(core, mine, other, *grads)


class Moves:
    def __init__(self, n_dp, n_mp):
        self.n_dp, self.n_mp = n_dp, n_mp
        self.dp = lax.axis_index("dp")
        self.mp = lax.axis_index("mp")
        self.core = self.dp % 2
        self.dp_bits = [("dp", 1 << b) for b in range(1, n_dp.bit_length() - 1)]
        self.mp_bits = [("mp", 1 << b) for b in range(n_mp.bit_length() - 1)]

    def swap(self, x, pair):
        perm = []
        for d in range(self.n_dp):
            for m in range(self.n_mp):
                axis, bit = pair[d % 2]
                dest = (d ^ bit, m) if axis == "dp" else (d, m ^ bit)
                perm.append((d * self.n_mp + m, dest[0] * self.n_mp + dest[1]))
        return lax.ppermute(x, BOTH, perm)

    def side(self, pair):
        values = [((self.dp if axis == "dp" else self.mp) // bit) % 2 for axis, bit in pair]
        return jnp.where(self.core == 0, values[0], values[1])

    def scatter(self, x, pair):
        half = x.shape[0] // 2
        side = self.side(pair)
        sent = lax.dynamic_slice_in_dim(x, (1 - side) * half, half, 0)
        kept = lax.dynamic_slice_in_dim(x, side * half, half, 0)
        return (wide(kept) + wide(self.swap(sent, pair))).astype(bf16)

    def gather(self, x, pair):
        other = self.swap(x, pair)
        side = self.side(pair)
        first = jnp.where(side == 0, x, other)
        second = jnp.where(side == 0, other, x)
        return jnp.concatenate([first, second], axis=0)

    def steps(self, first, second):
        pairs = list(zip(first, second, strict=True))
        down = [functools.partial(self.scatter, pair=pair) for pair in pairs]
        up = [functools.partial(self.gather, pair=pair) for pair in reversed(pairs)]
        return down + up


def tie(*arrays):
    return lax.optimization_barrier(arrays)


def per_device(
    inputs,
    cotangent,
    w_query,
    b_query,
    w_key,
    b_key,
    w_value,
    b_value,
    w_output,
    b_output,
    norm1_gain,
    norm1_shift,
    w_inner,
    b_inner,
    w_outer,
    b_outer,
    norm2_gain,
    norm2_shift,
    rel_table,
    rel_gain,
    rel_shift,
    block_group,
    seq_lengths,
    *,
    n_dp,
    n_mp,
):
    rows, width = inputs.shape
    units = w_inner.shape[1]
    moves = Moves(n_dp, n_mp)
    core = ("dp", 1)

    def other_shares(x):
        shares = [x[None]]
        for bit in moves.mp_bits:
            shares = [jnp.concatenate(shares, axis=0)]
            shares.append(moves.swap(shares[0], (bit, bit)))
        return jnp.concatenate(shares, axis=0)[1:]

    half = units // 2
    start = moves.core * half
    half_in = lax.dynamic_slice_in_dim(w_inner, start, half, 1)
    half_out = lax.dynamic_slice_in_dim(w_outer, start, half, 0)
    half_bias = jnp.pad(lax.dynamic_slice_in_dim(b_inner, start, half, 0), (0, 16 * width - half))
    half_out = jnp.concatenate([half_out, half_bias.reshape(16, width)], axis=0)
    got = (other_shares(half_in), other_shares(half_out))

    line = bucket_line(rows // 2)
    place_ids = np.arange(rows)[None, :]
    forward = jnp.asarray(np.append(line, -1)[:, None] == place_ids).astype(bf16)
    backward = jnp.asarray(np.append(line[::-1], -1)[:, None] == place_ids).astype(bf16)
    query, key, value, key_line, key_line_back, query_line, both_t = pre(
        inputs,
        rel_table,
        rel_gain,
        rel_shift,
        w_query,
        b_query,
        w_key,
        b_key,
        w_value,
        b_value,
        forward,
        backward,
    )
    mixed, exps, inverse, normed1, root1, hidden_low = attend(
        block_group,
        seq_lengths,
        query,
        key,
        value,
        key_line,
        query_line,
        w_output,
        b_output,
        inputs,
        norm1_gain,
        norm1_shift,
    )

    def far(x):
        whole = x
        for bit in moves.mp_bits:
            whole = jnp.concatenate([whole, moves.swap(whole, (bit, bit))], axis=0)
        return whole[rows:]

    *got, hidden_low = tie(*got, hidden_low)
    other = tuple(moves.swap(x, (core, core)) for x in got)
    layer_out, d_branch, active, d_inner, d_residual, d_mixed, grad_w_output, sums1, sums2 = ffn(
        hidden_low,
        normed1,
        root1,
        cotangent,
        mixed,
        w_output,
        (norm1_gain, norm1_shift, b_outer, norm2_gain, norm2_shift),
        b_inner,
        w_inner,
        w_outer,
        got,
        other,
    )
    far_hidden, far_branch = far(hidden_low), far(d_branch)

    dp_bits, mp_bits = moves.dp_bits, moves.mp_bits
    first = mp_bits + dp_bits
    second = dp_bits[:1] + mp_bits + dp_bits[1:]
    pair = (core, core)
    core_id = moves.core.reshape(1).astype(jnp.int32)
    ffn_steps = moves.steps(dp_bits, dp_bits[1:2] + dp_bits[:1] + dp_bits[2:])
    early_steps = moves.steps(first, second)
    late_steps = moves.steps(first, second)
    cut = 2 * TILE
    groups = width // cut
    shared = (exps, inverse, key_line_back, query_line, backward, both_t)
    pieces, grads = [], [grad_w_output]

    def attention(d_mixed, first, count):
        *piece, grad = attend_back(query, key, value, d_mixed, *shared, first, count)
        pieces.append(piece)
        return grad[0]

    grads.append(attention(d_mixed, 0, 2))
    far_hidden, far_branch, d_mixed, grads[-1] = tie(far_hidden, far_branch, d_mixed, grads[-1])
    chunks = units // CHUNK
    near = (hidden_low, d_branch, active, d_inner, far_hidden, far_branch, w_inner, b_inner, w_outer)
    if chunks % 2 == 0:
        mine, theirs = core_id * (chunks // 2), (1 - core_id) * (chunks // 2)
        sent = ffn_grads(*near, theirs, chunks // 2, 4 * n_dp)
        sent, mine = tie(sent, mine)
        kept = ffn_grads(*near, mine, chunks // 2, 4 * n_dp)
        got_sum = moves.swap(sent, pair)
        kept, got_sum = tie(kept, got_sum)
        ffn_sum = (wide(kept) + wide(got_sum)).astype(bf16)
    else:
        ffn_sum = ffn_grads(*near, 0 * core_id, chunks, 8 * n_dp)
        ffn_sum = moves.scatter(ffn_sum, pair)
    ffn_sum, d_mixed = tie(ffn_sum, d_mixed)
    grads.append(attention(d_mixed, 2, 2))
    ffn_sum = ffn_steps.pop(0)(ffn_sum)
    early = jnp.concatenate(grads, axis=0)
    early, ffn_sum, d_mixed = tie(early, ffn_sum, d_mixed)
    late_grads = [attention(d_mixed, 4, 1)]
    early = moves.scatter(early, pair)
    ffn_sum = ffn_steps.pop(0)(ffn_sum)
    early, ffn_sum, d_mixed, late_grads[0] = tie(early, ffn_sum, d_mixed, late_grads[0])
    late_grads.append(attention(d_mixed, 5, 1))
    d_query, d_key, d_value = zip(*pieces, strict=True)
    late = late_sums(
        d_query, d_key, d_value, w_query, w_key, rel_table, rel_gain, sums1, sums2, late_grads
    )
    early = early_steps.pop(0)(early)
    ffn_sum = ffn_steps.pop(0)(ffn_sum)
    early, ffn_sum, late = tie(early, ffn_sum, late)

    late = moves.scatter(late, pair)
    early = early_steps.pop(0)(early)
    ffn_next = ffn_steps.pop(0)(ffn_sum)
    input_grad = input_gradient(d_query, d_key, d_value, w_query, w_key, w_value, d_residual)
    late, early, input_grad = tie(late, early, input_grad)
    while late_steps:
        late = late_steps.pop(0)(late)
        if early_steps:
            early = early_steps.pop(0)(early)
        if len(late_steps) % 2 == 0 and ffn_steps:
            late, early, ffn_next = tie(late, early, ffn_next)
            ffn_next = ffn_steps.pop(0)(ffn_next)
        else:
            late, early = tie(late, early)
    for step in early_steps:
        early = step(early)
    for step in ffn_steps:
        ffn_next = step(ffn_next)
    early_other = moves.swap(early, pair)
    ffn_other = moves.swap(ffn_next, pair)
    late_other = moves.swap(late, pair)
    if chunks % 2 == 0:
        ffn_in, ffn_out, ffn_bias = ffn_result(core_id, ffn_next, ffn_other, width, units)
    else:
        whole = [jnp.where(moves.core == 0, a, b) for a, b in ((ffn_next, ffn_other), (ffn_other, ffn_next))]
        whole = wide(jnp.concatenate(whole, axis=0))
        ffn_in = jnp.concatenate(
            [whole[4 * CHUNK * c : 4 * CHUNK * c + 2 * CHUNK] for c in range(chunks)], axis=1
        )
        ffn_out = jnp.concatenate(
            [
                whole[4 * CHUNK * c + 2 * CHUNK : 4 * CHUNK * (c + 1)].reshape(2, CHUNK, CHUNK)
                for c in range(chunks)
            ],
            axis=1,
        )
        ffn_out = jnp.concatenate([ffn_out[0], ffn_out[1]], axis=1)
        ffn_bias = whole[4 * CHUNK * chunks : 4 * CHUNK * chunks + chunks].reshape(units)
    grad_w_output, *grads = early_result(core_id, early, early_other, width)
    grad_q, grad_k, grad_v, table, *vectors = late_result(core_id, late, late_other, grads, rows)
    return (
        layer_out,
        input_grad,
        grad_q,
        vectors[0],
        grad_k,
        vectors[1],
        grad_v,
        vectors[2],
        grad_w_output,
        *vectors[3:6],
        ffn_in,
        ffn_bias,
        ffn_out,
        *vectors[6:9],
        table,
        *vectors[9:],
    )


def solution(mesh):
    n_dp, n_mp = mesh.shape["dp"], mesh.shape["mp"]

    def body(*args):
        return per_device(*args, n_dp=n_dp, n_mp=n_mp)

    split = P(("dp", "mp"), None)
    weights = [P()] * 10 + [P(None, "mp"), P("mp"), P("mp", None)] + [P()] * 6
    return jax.shard_map(
        body,
        mesh=mesh,
        in_specs=(split, split, *weights, P(("dp", "mp")), split),
        out_specs=(
            split,
            split,
            *([P()] * 10),
            P(None, "mp"),
            P("mp"),
            P("mp", None),
            *([P()] * 6),
        ),
        check_vma=False,
    )
```

```python
import functools
import math

import jax
import jax.numpy as jnp
import numpy as np
from jax import lax
from jax.experimental import pallas as pl
from jax.experimental.pallas import tpu as pltpu
from jax.sharding import PartitionSpec as P

HEADS = 12
EPS = 1e-06
LOG2E = 1.4426950408889634
TILE = 128
CHUNK = 384
VMEM = 60 * 1024 * 1024
VECTOR_ROWS = (16, 17, 18, 2, 0, 1, 10, 8, 9, 24, 25)
BOTH = ("dp", "mp")
f32 = jnp.float32
bf16 = jnp.bfloat16


def bucket_line(half_rows):
    table_rows = 2 * half_rows
    middle = half_rows // 2
    relative = table_rows - 1 - np.arange(2 * table_rows - 1)
    signed = np.sign(relative)
    absolute = np.where((relative < middle) & (relative > -middle), middle - 1, np.abs(relative))
    log_place = (
        np.ceil(np.log(absolute / middle) / np.log((table_rows - 1) / middle) * (middle - 1))
        + middle
    )
    placed = np.where(absolute <= middle, relative, log_place * signed)
    return (placed + half_rows).astype(np.int32)


def dot(a, b):
    return jnp.dot(a, b, preferred_element_type=f32)


def dot_nt(a, b):
    return lax.dot_general(a, b, (((1,), (1,)), ((), ())), preferred_element_type=f32)


def dot_tn(a, b):
    return lax.dot_general(a, b, (((0,), (0,)), ((), ())), preferred_element_type=f32)


def wide(v):
    return v.astype(f32)


def ln_parts(v):
    average = jnp.mean(v, axis=-1, keepdims=True)
    center = v - average
    root = lax.rsqrt(jnp.mean(center * center, axis=-1, keepdims=True) + EPS)
    return center * root, root


def ln_back_rows(dy, normed, root, gain):
    dn = dy * gain
    first = jnp.mean(dn, axis=-1, keepdims=True)
    second = jnp.mean(dn * normed, axis=-1, keepdims=True)
    return root * (dn - first - normed * second)


def gelu_parts(v):
    bell = jnp.exp(-0.5 * v * v)
    t = 1.0 / (1.0 + (0.3275911 * math.sqrt(0.5)) * jnp.abs(v))
    poly = t * (
        0.254829592
        + t * (-0.284496736 + t * (1.421413741 + t * (-1.453152027 + t * 1.061405429)))
    )
    tail = 0.5 * poly * bell
    below = jnp.where(v >= 0, 1.0 - tail, tail)
    return v * below, below + v * bell * (1.0 / math.sqrt(2.0 * math.pi))


def pre_kernel(
    x_ref,
    table_ref,
    gain_ref,
    shift_ref,
    wq_ref,
    bq_ref,
    wk_ref,
    bk_ref,
    wv_ref,
    bv_ref,
    forward_ref,
    backward_ref,
    q_ref,
    k_ref,
    v_ref,
    key_line_ref,
    key_back_ref,
    query_line_ref,
    both_t_ref,
    both_ref,
):
    rows = x_ref.shape[0]

    @pl.when(pl.program_id(0) == 0)
    def _():
        both_ref[:rows, :] = x_ref[...]
        normed, _ = ln_parts(wide(table_ref[...]))
        rel = normed * wide(gain_ref[...])[None, :] + wide(shift_ref[...])[None, :]
        both_ref[rows:, :] = rel.astype(bf16)
        both_t_ref[...] = both_ref[...].T

    def project(w_ref, b_ref, part):
        return (dot(both_ref[part, :], w_ref[...]) + wide(b_ref[...])[None, :]).astype(bf16)

    here, there = slice(0, rows), slice(rows, 2 * rows)
    q_ref[...] = project(wq_ref, bq_ref, here)
    k_ref[...] = project(wk_ref, bk_ref, here)
    v_ref[...] = project(wv_ref, bv_ref, here)
    pos_query = project(wq_ref, bq_ref, there)
    pos_key = project(wk_ref, bk_ref, there)
    key_line_ref[...] = dot(forward_ref[...], pos_key).astype(bf16)
    key_back_ref[...] = dot(backward_ref[...], pos_key).astype(bf16)
    query_line_ref[...] = dot(backward_ref[...], pos_query).astype(bf16)


def pre(x, table, gain, shift, w_q, b_q, w_k, b_k, w_v, b_v, forward, backward):
    rows, width = x.shape
    cut = 2 * TILE

    def fixed(r, w):
        return pl.BlockSpec((r, w), lambda c: (0, 0))

    whole = pl.BlockSpec((width,), lambda c: (0,))
    weight = pl.BlockSpec((width, cut), lambda c: (0, c))
    vector = pl.BlockSpec((cut,), lambda c: (c,))
    one = pl.BlockSpec((rows, cut), lambda c: (0, c))
    two = pl.BlockSpec((2 * rows, cut), lambda c: (0, c))
    return pl.pallas_call(
        pre_kernel,
        grid=(width // cut,),
        in_specs=[fixed(rows, width), fixed(rows, width), whole, whole]
        + [weight, vector] * 3
        + [fixed(2 * rows, rows)] * 2,
        out_specs=[one] * 3 + [two] * 3 + [fixed(width, 2 * rows)],
        out_shape=[jax.ShapeDtypeStruct((rows, width), bf16)] * 3
        + [jax.ShapeDtypeStruct((2 * rows, width), bf16)] * 3
        + [jax.ShapeDtypeStruct((width, 2 * rows), bf16)],
        scratch_shapes=[pltpu.VMEM((2 * rows, width), bf16)],
        compiler_params=pltpu.CompilerParams(vmem_limit_bytes=VMEM),
        cost_estimate=pl.CostEstimate(
            flops=5_500_000_000, bytes_accessed=14_000_000, transcendentals=0
        ),
        name="pre",
    )(x, table, gain, shift, w_q, b_q, w_k, b_k, w_v, b_v, forward, backward)


def skewed(x, keep):
    parts = [x[:, TILE * b : TILE * (b + 1)] for b in range(5)]
    return [
        pltpu.roll(jnp.where(keep, parts[b], parts[b + 1]), 1, 1, stride=1, stride_axis=0)
        for b in range(4)
    ]


def unskewed(tiles, keep):
    zero = jnp.zeros((TILE, TILE), f32)
    turned = [zero] + [pltpu.roll(t, 0, 1, stride=1, stride_axis=0) for t in tiles] + [zero]
    return [jnp.where(keep, turned[b + 1], turned[b]) for b in range(5)]


def flipped():
    rows = lax.broadcasted_iota(jnp.int32, (256, 256), 0)
    cols = lax.broadcasted_iota(jnp.int32, (256, 256), 1)
    return (rows + cols == 255).astype(f32).astype(bf16)


def attend_kernel(
    group_ref,
    lengths_ref,
    q_ref,
    k_ref,
    v_ref,
    key_line_ref,
    query_line_ref,
    wo_ref,
    bo_ref,
    x_ref,
    gain_ref,
    shift_ref,
    out_ref,
    exp_ref,
    inv_ref,
    full_ref,
    normed_ref,
    root_ref,
    h_ref,
    side_ref,
    bias_ref,
):
    @pl.when(pl.program_id(0) == 0)
    def _():
        normed_ref[...] = wide(x_ref[...]) + wide(bo_ref[...])[None, :]
        size = bias_ref.shape[0]
        shift = size.bit_length() - 1 - group_ref[0]
        row = lax.broadcasted_iota(jnp.int32, (size, 1), 0)
        col = lax.broadcasted_iota(jnp.int32, (1, size), 1)
        owner = jnp.right_shift(col, shift)
        limit = jnp.zeros((1, size), jnp.int32)
        for slot in range(4):
            limit = jnp.where(owner == slot, lengths_ref[0, slot], limit)
        owner = jnp.where(col - jnp.left_shift(owner, shift) < limit, owner, -1)
        valid = jnp.right_shift(row, shift) == owner
        bias_ref[...] = jnp.where(valid, 0.0, -1e30).astype(f32)

    lane = lax.broadcasted_iota(jnp.int32, (1, TILE), 1)
    keep = (
        lax.broadcasted_iota(jnp.int32, (TILE, TILE), 0)
        + lax.broadcasted_iota(jnp.int32, (TILE, TILE), 1)
        >= TILE - 1
    )
    mine = [lane < 64, lane >= 64]
    scale = LOG2E / math.sqrt(192)
    flip = flipped()
    v_ones = jnp.concatenate([v_ref[...], jnp.ones(v_ref.shape, bf16)], axis=1)
    for h in range(2):
        for t in range(4):
            km = jnp.where(mine[h], k_ref[TILE * t : TILE * (t + 1), :], 0)
            start = 384 - TILE * t
            sk = skewed(dot_nt(km, query_line_ref[start : start + 640, :]), keep)
            for b in range(4):
                side_ref[h, TILE * b : TILE * (b + 1), TILE * t : TILE * (t + 1)] = sk[b].T
        for t in range(4):
            rows = slice(TILE * t, TILE * (t + 1))
            qm = jnp.where(mine[h], q_ref[rows, :], 0)
            start = 384 - TILE * t
            near = skewed(dot_nt(qm, key_line_ref[start : start + 640, :]), keep)
            content = dot_nt(qm, k_ref[...])
            parts = []
            for b in range(4):
                cols = slice(TILE * b, TILE * (b + 1))
                total = content[:, cols] + near[b] + side_ref[h, rows, cols]
                parts.append(total * scale + bias_ref[rows, cols])
            top = jnp.max(
                jnp.maximum(jnp.maximum(parts[0], parts[1]), jnp.maximum(parts[2], parts[3])),
                axis=1,
                keepdims=True,
            )
            low = [jnp.exp2(p - top).astype(bf16) for p in parts]
            exps = jnp.concatenate(low, axis=1)
            exp_ref[h, rows, :] = jnp.concatenate(
                [dot(exps[:, 256:], flip).astype(bf16), dot(exps[:, :256], flip).astype(bf16)], axis=1
            )
            product = dot(exps, v_ones)
            inverse = 1.0 / product[:, TILE:]
            out = product[:, :TILE] * inverse
            if h == 0:
                inv_ref[0, rows, :] = inverse
                full_ref[0, rows, :] = out
            else:
                inv_ref[0, rows, :] = jnp.where(mine[0], inv_ref[0, rows, :], inverse)
                out = jnp.where(mine[0], full_ref[0, rows, :], out)
                full_ref[0, rows, :] = out
                out_ref[rows, :] = out.astype(bf16)
    normed_ref[...] += dot(out_ref[...], wo_ref[...])

    @pl.when(pl.program_id(0) == pl.num_programs(0) - 1)
    def _():
        gain, shift = wide(gain_ref[...])[None, :], wide(shift_ref[...])[None, :]
        for r in range(0, h_ref.shape[0], TILE):
            rows = slice(r, r + TILE)
            normed, root = ln_parts(normed_ref[rows, :])
            normed_ref[rows, :] = normed
            root_ref[rows, :] = jnp.broadcast_to(root, (TILE, TILE))
            h_ref[rows, :] = (normed * gain + shift).astype(bf16)


def attend(group, lengths, q, k, v, key_line, query_line, w_output, b_output, x, gain, shift):
    rows, width = q.shape
    pairs = width // TILE
    col = pl.BlockSpec((rows, TILE), lambda g: (0, g))
    line = pl.BlockSpec((2 * rows, TILE), lambda g: (0, g))
    scalars = pl.BlockSpec(memory_space=pltpu.SMEM)
    full = pl.BlockSpec((rows, width), lambda g: (0, 0))
    vector = pl.BlockSpec((width,), lambda g: (0,))
    return pl.pallas_call(
        attend_kernel,
        grid=(pairs,),
        in_specs=[scalars, scalars, col, col, col, line, line]
        + [pl.BlockSpec((TILE, width), lambda g: (g, 0)), vector, full, vector, vector],
        out_specs=[
            col,
            pl.BlockSpec((2, rows, rows), lambda g: (g, 0, 0)),
            pl.BlockSpec((1, rows, TILE), lambda g: (g, 0, 0)),
            pl.BlockSpec((1, rows, TILE), lambda g: (g, 0, 0)),
            full,
            pl.BlockSpec((rows, TILE), lambda g: (0, 0)),
            full,
        ],
        out_shape=[
            jax.ShapeDtypeStruct((rows, width), bf16),
            jax.ShapeDtypeStruct((2 * pairs, rows, rows), bf16),
            jax.ShapeDtypeStruct((pairs, rows, TILE), f32),
            jax.ShapeDtypeStruct((pairs, rows, TILE), f32),
            jax.ShapeDtypeStruct((rows, width), f32),
            jax.ShapeDtypeStruct((rows, TILE), f32),
            jax.ShapeDtypeStruct((rows, width), bf16),
        ],
        scratch_shapes=[pltpu.VMEM((2, rows, rows), f32), pltpu.VMEM((rows, rows), f32)],
        compiler_params=pltpu.CompilerParams(vmem_limit_bytes=VMEM),
        cost_estimate=pl.CostEstimate(
            flops=18_000_000_000, bytes_accessed=16_000_000, transcendentals=3_200_000
        ),
        name="attend",
    )(group, lengths, q, k, v, key_line, query_line, w_output, b_output, x, gain, shift)


def attend_back_kernel(
    q_ref,
    k_ref,
    v_ref,
    do_ref,
    exp_ref,
    inv_ref,
    full_ref,
    key_line_ref,
    query_line_ref,
    places_ref,
    both_t_ref,
    *refs,
):
    dq_ref, dk_ref, dv_ref, sums_ref, grad_ref, *refs = refs[-9:]
    attend_back_pair(
        q_ref,
        k_ref,
        v_ref,
        do_ref,
        exp_ref,
        inv_ref,
        full_ref,
        key_line_ref,
        query_line_ref,
        places_ref,
        both_t_ref,
        dq_ref,
        dk_ref,
        dv_ref,
        sums_ref,
        grad_ref,
        *refs,
    )


def attend_back_pair(
    q_ref,
    k_ref,
    v_ref,
    do_ref,
    exp_ref,
    inv_ref,
    full_ref,
    key_line_ref,
    query_line_ref,
    places_ref,
    both_t_ref,
    dq_ref,
    dk_ref,
    dv_ref,
    sums_ref,
    grad_ref,
    ds_ref,
    dst_ref,
    query_band,
    key_band,
):
    @pl.when(pl.program_id(0) == 0)
    def _():
        query_band[...] = jnp.zeros_like(query_band)
        key_band[...] = jnp.zeros_like(key_band)

    scale = 1.0 / math.sqrt(192)
    lane = lax.broadcasted_iota(jnp.int32, (1, TILE), 1)
    sub = lax.broadcasted_iota(jnp.int32, (TILE, 1), 0)
    keep = lax.broadcasted_iota(jnp.int32, (TILE, TILE), 1) >= lax.broadcasted_iota(
        jnp.int32, (TILE, TILE), 0
    )
    mine = [lane < 64, lane >= 64]
    mine_t = [sub < 64, sub >= 64]
    flip = flipped()

    def reverse(x):
        return jnp.concatenate([dot(flip, x[256:]), dot(flip, x[:256])], axis=0).astype(bf16)

    q = q_ref[...]
    k = reverse(k_ref[...])
    v = reverse(v_ref[...])
    q_t = q.T
    k_t = k.T
    do = (wide(do_ref[...]) * inv_ref[0]).astype(bf16)
    do_t = do.T
    share = wide(do) * full_ref[0]
    high = share.astype(bf16)
    rest = (share - wide(high)).astype(bf16)
    row = lax.broadcasted_iota(jnp.int32, (256, 256), 0) % TILE // 64
    ones = (row == lax.broadcasted_iota(jnp.int32, (256, 256), 1) // TILE).astype(f32).astype(bf16)
    means = dot(jnp.concatenate([high, rest], axis=1), ones)
    dv_t = None
    dqs, dks, key_lines, query_lines = [], [], [], []
    for h in range(2):
        dom = jnp.where(mine[h], do, 0)
        for t in range(4):
            rows = slice(TILE * t, TILE * (t + 1))
            dp = dot_nt(dom[rows], v)
            mean = means[rows, TILE * h : TILE * (h + 1)]
            ds = []
            for b in range(4):
                cols = slice(TILE * b, TILE * (b + 1))
                ds.append(wide(exp_ref[h, rows, cols]) * (dp[:, cols] - mean))
                ds_ref[h, rows, cols] = ds[b].astype(bf16)
            out = unskewed(ds, keep)
            for b in range(5):
                query_band[h, rows, TILE * (t + b) : TILE * (t + b + 1)] = out[b].astype(bf16)
        for t in range(4):
            rows = slice(TILE * t, TILE * (t + 1))
            turned = [ds_ref[h, TILE * b : TILE * (b + 1), rows].T for b in range(4)]
            for b in range(4):
                dst_ref[h, rows, TILE * b : TILE * (b + 1)] = turned[b]
            out = unskewed([wide(x) for x in turned], keep)
            for b in range(5):
                key_band[h, rows, TILE * (t + b) : TILE * (t + b + 1)] = out[b].astype(bf16)
        part = dot(jnp.where(mine_t[h], do_t, 0), exp_ref[h])
        dv_t = part if dv_t is None else dv_t + part
        dq, dk, key_line, query_line = [], [], [], []
        for i in range(2):
            rows = slice(256 * i, 256 * (i + 1))
            band = slice(256 * i, 256 * i + 768)
            dq.append(dot(ds_ref[h, rows, :], k) + dot(query_band[h, rows, band], key_line_ref[band, :]))
            dk.append(dot(dst_ref[h, rows, :], q) + dot(key_band[h, rows, band], query_line_ref[band, :]))
            key_line.append(dot(jnp.where(mine_t[h], q_t[:, rows], 0), query_band[h, rows, band]))
            query_line.append(dot(jnp.where(mine_t[h], k_t[:, rows], 0), key_band[h, rows, band]))
        dqs.append(jnp.concatenate(dq, axis=0))
        dks.append(jnp.concatenate(dk, axis=0))
        key_lines.append(key_line)
        query_lines.append(query_line)
    size = q.shape[0]
    dq_ref[:size, :] = (jnp.where(mine[0], dqs[0], dqs[1]) * scale).astype(bf16)
    dk_ref[:size, :] = reverse((jnp.where(mine[0], dks[0], dks[1]) * scale).astype(bf16))
    dv_ref[...] = reverse(dv_t.T.astype(bf16))
    for lines, ref in ((key_lines, dk_ref), (query_lines, dq_ref)):
        first = lines[0][0] + lines[1][0]
        second = lines[0][1] + lines[1][1]
        whole = jnp.concatenate(
            [first[:, :256], first[:, 256:] + second[:, :512], second[:, 512:]], axis=1
        )
        ref[size:, :] = dot((whole * scale).astype(bf16), places_ref[...]).T.astype(bf16)
    width = both_t_ref.shape[0]
    grad_ref[:width, :] = dot(both_t_ref[...], dq_ref[...]).astype(bf16)
    grad_ref[width : 2 * width, :] = dot(both_t_ref[...], dk_ref[...]).astype(bf16)
    grad_ref[2 * width :, :] = dot(both_t_ref[:, :size], dv_ref[...]).astype(bf16)
    sums = [jnp.sum(wide(r[...]), axis=0, keepdims=True) for r in (dq_ref, dk_ref, dv_ref)]
    sums_ref[...] = jnp.concatenate(sums + [jnp.zeros((5, TILE), f32)], axis=0)


def attend_back(
    q,
    k,
    v,
    do,
    exps,
    inverse,
    mixed_full,
    key_line,
    query_line,
    places,
    both_t,
    first,
    count,
    into,
    size,
    start,
):
    rows, width = q.shape
    col = pl.BlockSpec((rows, TILE), lambda g: (0, first + g))
    line = pl.BlockSpec((2 * rows, TILE), lambda g: (0, first + g))
    both = pl.BlockSpec((2 * rows, TILE), lambda g: (0, g))
    more = [] if into is None else [into]
    return pl.pallas_call(
        attend_back_kernel,
        grid=(count,),
        in_specs=[
            col,
            col,
            col,
            col,
            pl.BlockSpec((2, rows, rows), lambda g: (first + g, 0, 0)),
            pl.BlockSpec((1, rows, TILE), lambda g: (first + g, 0, 0)),
            pl.BlockSpec((1, rows, TILE), lambda g: (first + g, 0, 0)),
            line,
            line,
            pl.BlockSpec((2 * rows, rows), lambda g: (0, 0)),
            pl.BlockSpec((width, 2 * rows), lambda g: (0, 0)),
        ]
        + [pl.BlockSpec(memory_space=pl.ANY) for _ in more],
        out_specs=[
            both,
            both,
            pl.BlockSpec((rows, TILE), lambda g: (0, g)),
            pl.BlockSpec((8, TILE), lambda g: (0, g)),
            pl.BlockSpec((3 * width, TILE), lambda g: (start + g, 0)),
        ],
        out_shape=[
            jax.ShapeDtypeStruct((2 * rows, count * TILE), bf16),
            jax.ShapeDtypeStruct((2 * rows, count * TILE), bf16),
            jax.ShapeDtypeStruct((rows, count * TILE), bf16),
            jax.ShapeDtypeStruct((8, count * TILE), f32),
            jax.ShapeDtypeStruct((size, TILE), bf16),
        ],
        input_output_aliases={11: 4} if more else {},
        scratch_shapes=[
            pltpu.VMEM((2, rows, rows), bf16),
            pltpu.VMEM((2, rows, rows), bf16),
            pltpu.VMEM((2, rows, 2 * rows), bf16),
            pltpu.VMEM((2, rows, 2 * rows), bf16),
        ],
        compiler_params=pltpu.CompilerParams(vmem_limit_bytes=VMEM),
        cost_estimate=pl.CostEstimate(
            flops=count * 4_000_000_000, bytes_accessed=count * 3_000_000, transcendentals=0
        ),
        name="attend_back",
    )(q, k, v, do, exps, inverse, mixed_full, key_line, query_line, places, both_t, *more)


def weight_copies(sources, targets, sems, chunk, chunks):
    win_hbm, wout_hbm, got_in, got_out, other_in, other_out = sources
    win_ref, wout_ref, far_in, far_out = targets
    n = got_in.shape[0]
    lists = []
    for c in range(chunks):
        cols = slice(chunk * c, chunk * (c + 1))
        lists.append([(win_hbm.at[:, cols], win_ref.at[:, cols]), (wout_hbm.at[cols], wout_ref.at[cols])])
    lists.append([(got_in, far_in.at[:n]), (got_out, far_out.at[:n])])
    lists.append([(other_in, far_in.at[n:]), (other_out, far_out.at[n:])])
    copies = []
    for i, pairs in enumerate(lists):
        copies.append(
            [pltpu.make_async_copy(a, b, sems.at[i, k]) for k, (a, b) in enumerate(pairs)]
        )
    return copies


def start(copies):
    for copy in copies:
        copy.start()


def wait(copies):
    for copy in copies:
        copy.wait()


def core_half_kernel(core_ref, bin_ref, win_hbm, wout_hbm, in_ref, out_ref, sems):
    units = in_ref.shape[1]
    width = out_ref.shape[1]

    def send(core):
        part = slice(units * core, units * (core + 1))
        copies = [
            pltpu.make_async_copy(wout_hbm.at[part], out_ref.at[:units], sems.at[0]),
            pltpu.make_async_copy(win_hbm.at[:, part], in_ref, sems.at[1]),
        ]
        start(copies)
        bias = wide(bin_ref[...])[None, part]
        pad = jnp.zeros((1, width - units), f32)
        row = bias if units == width else jnp.concatenate([bias, pad], axis=1)
        out_ref[units:, :] = jnp.broadcast_to(row, (16, width)).astype(bf16)
        wait(copies)

    @pl.when(core_ref[0] == 0)
    def _():
        send(0)

    @pl.when(core_ref[0] != 0)
    def _():
        send(1)


def core_half(core, w_in, w_out, b_in):
    width, units = w_in.shape
    half = units // 2
    if half % TILE:
        place = core[0] * half
        row = jnp.pad(lax.dynamic_slice_in_dim(b_in, place, half, 0), (0, width - half))
        rows = [lax.dynamic_slice_in_dim(w_out, place, half, 0), jnp.broadcast_to(row, (16, width))]
        return lax.dynamic_slice_in_dim(w_in, place, half, 1), jnp.concatenate(rows, axis=0)
    anywhere = pl.BlockSpec(memory_space=pl.ANY)
    vmem = pl.BlockSpec(memory_space=pltpu.VMEM)
    return pl.pallas_call(
        core_half_kernel,
        in_specs=[pl.BlockSpec(memory_space=pltpu.SMEM), vmem, anywhere, anywhere],
        out_specs=[vmem, vmem],
        out_shape=[low(width, half), low(half + 16, width)],
        scratch_shapes=[pltpu.SemaphoreType.DMA((2,))],
        compiler_params=pltpu.CompilerParams(vmem_limit_bytes=VMEM),
        cost_estimate=pl.CostEstimate(flops=0, bytes_accessed=5_000_000, transcendentals=0),
        name="core_half",
    )(core, b_in, w_in, w_out)


def ffn_forward_kernel(
    h_ref,
    normed_hbm,
    cot_hbm,
    gain1_ref,
    shift1_ref,
    b_outer_ref,
    gain2_ref,
    shift2_ref,
    bin_ref,
    *refs,
    chunk,
    far_chunk,
):
    sources, refs = refs[:6], refs[6:]
    out_ref, dpre_ref, dbranch_ref, active_hbm, slope_hbm, far_slope_hbm, sums_ref = refs[:7]
    normed_ref, cot_ref, active_ref, slope_ref, far_slope_ref, total_ref = refs[7:13]
    targets, sems, sems2 = refs[13:17], refs[17], refs[18]
    far_in_ref, far_out_ref = targets[2:]
    rows, width = h_ref.shape
    chunks = active_ref.shape[1] // chunk
    far_count, _, units = far_in_ref.shape
    far_chunks = units // far_chunk
    weights = weight_copies(sources, targets, sems, chunk, chunks)
    others = [
        pltpu.make_async_copy(normed_hbm, normed_ref, sems2.at[0]),
        pltpu.make_async_copy(cot_hbm, cot_ref, sems2.at[1]),
    ]
    back = [
        pltpu.make_async_copy(active_ref, active_hbm, sems2.at[2]),
        pltpu.make_async_copy(slope_ref, slope_hbm, sems2.at[3]),
        pltpu.make_async_copy(far_slope_ref, far_slope_hbm, sems2.at[4]),
    ]
    for copies in weights:
        start(copies)
    start(others)
    b_in = wide(bin_ref[...])[None, :]

    def forward(w_in, b_in, w_out, active_at, slope_at, first):
        for r in range(0, rows, 256):
            part = slice(r, r + 256)
            active, slope = gelu_parts(dot(h_ref[part, :], w_in) + b_in)
            active = active.astype(bf16)
            if active_at is not None:
                active_ref[part, active_at] = active
            slope_at(part, slope.astype(bf16))
            product = dot(active, w_out)
            total_ref[part, :] = product if first else total_ref[part, :] + product

    for c in range(chunks):
        wait(weights[c])
        cols = slice(chunk * c, chunk * (c + 1))

        def put(part, value, cols=cols):
            slope_ref[part, cols] = value

        forward(targets[0][:, cols], b_in[:, cols], targets[1][cols, :], cols, put, c == 0)
    start(back[:2])
    wait(weights[chunks])
    wait(weights[chunks + 1])

    def far_step(s, carry):
        for c in range(far_chunks):
            cols = slice(far_chunk * c, far_chunk * (c + 1))

            def put(part, value, cols=cols):
                far_slope_ref[s, part, cols] = value

            bias = wide(far_out_ref[s, units : units + 1, cols])
            forward(far_in_ref[s, :, cols], bias, far_out_ref[s, cols, :], None, put, False)
        return carry

    lax.fori_loop(0, far_count, far_step, 0)
    start(back[2:])
    wait(others)
    gain1, shift1, b_outer, gain2, shift2 = [
        wide(r[...])[None, :] for r in (gain1_ref, shift1_ref, b_outer_ref, gain2_ref, shift2_ref)
    ]
    sums = [jnp.zeros((1, width), f32) for _ in range(3)]
    for r in range(0, rows, TILE):
        part = slice(r, r + TILE)
        normed, root = ln_parts(normed_ref[part, :] * gain1 + shift1 + total_ref[part, :] + b_outer)
        out_ref[part, :] = normed * gain2 + shift2
        dy = wide(cot_ref[part, :])
        d = ln_back_rows(dy, normed, root, gain2)
        dpre_ref[part, :] = d
        low = d.astype(bf16)
        dbranch_ref[part, :] = low
        sums[0] += jnp.sum(dy * normed, axis=0, keepdims=True)
        sums[1] += jnp.sum(dy, axis=0, keepdims=True)
        sums[2] += jnp.sum(wide(low), axis=0, keepdims=True)
    sums_ref[...] = jnp.concatenate(sums + [jnp.zeros((5, width), f32)], axis=0)
    wait(back)


def ffn_backward_kernel(
    db_ref, normed_hbm, root_ref, dpre_ref, mixed_hbm, wo_hbm, gain_ref, *refs, chunk, far_chunk
):
    slope_hbm, far_slope_hbm = refs[:2]
    sources, refs = refs[2:8], refs[8:]
    dinner_hbm, dres_ref, dmixed_ref, grad_ref, sums_ref = refs[:5]
    normed_ref, mixed_ref, wo_ref, dinner_ref, total_ref, dattn_ref = refs[5:11]
    slope_ref, far_slope_ref = refs[11:13]
    targets, sems, sems2 = refs[13:17], refs[17], refs[18]
    far_in_ref, far_out_ref = targets[2:]
    rows, width = db_ref.shape
    chunks = dinner_ref.shape[1] // chunk
    far_count, _, units = far_in_ref.shape
    far_chunks = units // far_chunk
    weights = weight_copies(sources, targets, sems, chunk, chunks)
    slopes = [
        pltpu.make_async_copy(slope_hbm, slope_ref, sems2.at[0]),
        pltpu.make_async_copy(far_slope_hbm, far_slope_ref, sems2.at[1]),
    ]
    others = [
        pltpu.make_async_copy(normed_hbm, normed_ref, sems2.at[2]),
        pltpu.make_async_copy(mixed_hbm, mixed_ref, sems2.at[3]),
        pltpu.make_async_copy(wo_hbm, wo_ref, sems2.at[4]),
    ]
    back = [pltpu.make_async_copy(dinner_ref, dinner_hbm, sems2.at[5])]
    start(weights[0])
    start(slopes[:1])
    for copies in weights[1:]:
        start(copies)
    start(slopes[1:])
    start(others)

    def backward(w_in, w_out, slope, keep, first):
        for r in range(0, rows, 256):
            part = slice(r, r + 256)
            d = (dot_nt(db_ref[part, :], w_out) * wide(slope(part))).astype(bf16)
            if keep is not None:
                keep(part, d)
            base = dpre_ref[part, :] if first else total_ref[part, :]
            total_ref[part, :] = base + dot_nt(d, w_in)

    wait(slopes[:1])
    for c in range(chunks):
        wait(weights[c])
        cols = slice(chunk * c, chunk * (c + 1))

        def keep(part, value, cols=cols):
            dinner_ref[part, cols] = value

        def slope(part, cols=cols):
            return slope_ref[part, cols]

        backward(targets[0][:, cols], targets[1][cols, :], slope, keep, c == 0)
    start(back)
    wait(weights[chunks])
    wait(weights[chunks + 1])
    wait(slopes[1:])

    def far_step(s, carry):
        for c in range(far_chunks):
            cols = slice(far_chunk * c, far_chunk * (c + 1))

            def slope(part, cols=cols):
                return far_slope_ref[s, part, cols]

            backward(far_in_ref[s, :, cols], far_out_ref[s, cols, :], slope, None, False)
        return carry

    lax.fori_loop(0, far_count, far_step, 0)
    wait(others)
    gain = wide(gain_ref[...])[None, :]
    sums = [jnp.zeros((1, width), f32) for _ in range(3)]
    for r in range(0, rows, TILE):
        part = slice(r, r + TILE)
        dy = total_ref[part, :]
        normed = normed_ref[part, :]
        d = ln_back_rows(dy, normed, root_ref[part, 0:1], gain)
        dres_ref[part, :] = d
        low = d.astype(bf16)
        dattn_ref[part, :] = low
        dmixed_ref[part, :] = dot_nt(low, wo_ref[...]).astype(bf16)
        sums[0] += jnp.sum(dy * normed, axis=0, keepdims=True)
        sums[1] += jnp.sum(dy, axis=0, keepdims=True)
        sums[2] += jnp.sum(wide(low), axis=0, keepdims=True)
    sums_ref[...] = jnp.concatenate(sums + [jnp.zeros((5, width), f32)], axis=0)
    grad = dot(mixed_ref[...].T, dattn_ref[...]).astype(bf16)
    for i in range(2):
        grad_ref[width * i : width * (i + 1), :] = grad[:, CHUNK * i : CHUNK * (i + 1)]
    wait(back)


def low(*shape):
    return jax.ShapeDtypeStruct(shape, bf16)


def full(*shape):
    return jax.ShapeDtypeStruct(shape, f32)


def share_sizes(w_in, got):
    return min(2 * CHUNK, w_in.shape[1]), min(2 * CHUNK, got[0].shape[2])


def weight_scratch(w_in, w_out, got, chunk):
    n = got[0].shape[0]
    return [
        pltpu.VMEM(w_in.shape, bf16),
        pltpu.VMEM(w_out.shape, bf16),
        pltpu.VMEM((2 * n, *got[0].shape[1:]), bf16),
        pltpu.VMEM((2 * n, *got[1].shape[1:]), bf16),
        pltpu.SemaphoreType.DMA((w_in.shape[1] // chunk + 2, 2)),
        pltpu.SemaphoreType.DMA((6,)),
    ]


def ffn_forward(h, normed, cot, vectors, b_in, w_in, w_out, got, other):
    rows, width = h.shape
    units = w_in.shape[1]
    far = 2 * got[0].shape[0]
    chunk, far_chunk = share_sizes(w_in, got)
    anywhere = pl.BlockSpec(memory_space=pl.ANY)
    vmem = pl.BlockSpec(memory_space=pltpu.VMEM)
    far_slope = (far, rows, got[0].shape[2])
    return pl.pallas_call(
        functools.partial(ffn_forward_kernel, chunk=chunk, far_chunk=far_chunk),
        in_specs=[vmem, anywhere, anywhere] + [vmem] * 6 + [anywhere] * 6,
        out_specs=[vmem] * 3 + [anywhere] * 3 + [vmem],
        out_shape=[
            full(rows, width),
            full(rows, width),
            low(rows, width),
            low(rows, units),
            low(rows, units),
            low(*far_slope),
            full(8, width),
        ],
        scratch_shapes=[
            pltpu.VMEM((rows, width), f32),
            pltpu.VMEM((rows, width), bf16),
            pltpu.VMEM((rows, units), bf16),
            pltpu.VMEM((rows, units), bf16),
            pltpu.VMEM(far_slope, bf16),
            pltpu.VMEM((rows, width), f32),
            *weight_scratch(w_in, w_out, got, chunk),
        ],
        compiler_params=pltpu.CompilerParams(vmem_limit_bytes=VMEM),
        cost_estimate=pl.CostEstimate(
            flops=16 * rows * width * width, bytes_accessed=24_000_000, transcendentals=3_200_000
        ),
        name="ffn_forward",
    )(h, normed, cot, *vectors, b_in, w_in, w_out, *got, *other)


def ffn_backward(
    db, normed, root, dpre, mixed, w_output, gain, slope, far_slope, w_in, w_out, got, other
):
    rows, width = db.shape
    units = w_in.shape[1]
    chunk, far_chunk = share_sizes(w_in, got)
    anywhere = pl.BlockSpec(memory_space=pl.ANY)
    vmem = pl.BlockSpec(memory_space=pltpu.VMEM)
    return pl.pallas_call(
        functools.partial(ffn_backward_kernel, chunk=chunk, far_chunk=far_chunk),
        in_specs=[vmem, anywhere, vmem, vmem, anywhere, anywhere, vmem] + [anywhere] * 8,
        out_specs=[anywhere] + [vmem] * 4,
        out_shape=[
            low(rows, units),
            full(rows, width),
            low(rows, width),
            low(2 * width, CHUNK),
            full(8, width),
        ],
        scratch_shapes=[
            pltpu.VMEM((rows, width), f32),
            pltpu.VMEM((rows, width), bf16),
            pltpu.VMEM((width, width), bf16),
            pltpu.VMEM((rows, units), bf16),
            pltpu.VMEM((rows, width), f32),
            pltpu.VMEM((rows, width), bf16),
            pltpu.VMEM((rows, units), bf16),
            pltpu.VMEM(far_slope.shape, bf16),
            *weight_scratch(w_in, w_out, got, chunk),
        ],
        compiler_params=pltpu.CompilerParams(vmem_limit_bytes=VMEM),
        cost_estimate=pl.CostEstimate(
            flops=20 * rows * width * width, bytes_accessed=24_000_000, transcendentals=0
        ),
        name="ffn_backward",
    )(
        db,
        normed,
        root,
        dpre,
        mixed,
        w_output,
        gain,
        slope,
        far_slope,
        w_in,
        w_out,
        *got,
        *other,
    )


def ffn_grads_kernel(
    start_ref,
    h_ref,
    db_ref,
    active_ref,
    dinner_ref,
    far_h_ref,
    far_db_ref,
    win_ref,
    bin_ref,
    wout_ref,
    out_ref,
    h_t,
    far_t,
    bias_ref,
    *,
    chunks,
):
    c = pl.program_id(0)
    tail = 4 * CHUNK * chunks

    @pl.when(c == 0)
    def _():
        bias_ref[...] = wide(bin_ref[...])[None, :]
        h_t[...] = h_ref[...].T
        far_t[...] = far_h_ref[...].T
        out_ref[tail:, :] = jnp.zeros_like(out_ref[tail:, :])

    w_in, w_out = win_ref[...], wout_ref[...]
    place = (start_ref[0] + c) * CHUNK
    b_in = bias_ref[:, pl.ds(pl.multiple_of(place, TILE), CHUNK)]
    active, dinner = [], []
    for r in range(0, far_h_ref.shape[0], 256):
        rows = slice(r, r + 256)
        a, slope = gelu_parts(dot(far_h_ref[rows, :], w_in) + b_in)
        active.append(a.astype(bf16))
        dinner.append((dot_nt(far_db_ref[rows, :], w_out) * slope).astype(bf16))
    active = jnp.concatenate(active, axis=0)
    dinner = jnp.concatenate(dinner, axis=0)
    base = pl.multiple_of(c * 4 * CHUNK, 4 * CHUNK)
    out_ref[pl.ds(base, 2 * CHUNK), :] = (
        dot(h_t[...], dinner_ref[...]) + dot(far_t[...], dinner)
    ).astype(bf16)
    grad = (dot(active_ref[...].T, db_ref[...]) + dot(active.T, far_db_ref[...])).astype(bf16)
    out_ref[pl.ds(base + 2 * CHUNK, CHUNK), :] = grad[:, :CHUNK]
    out_ref[pl.ds(base + 3 * CHUNK, CHUNK), :] = grad[:, CHUNK:]
    bias = jnp.sum(wide(dinner_ref[...]), axis=0, keepdims=True)
    bias = bias + jnp.sum(wide(dinner), axis=0, keepdims=True)
    place = lax.broadcasted_iota(jnp.int32, (16, 1), 0) == c
    out_ref[tail : tail + 16, :] = jnp.where(place, bias.astype(bf16), out_ref[tail : tail + 16, :])


def ffn_grads(h, db, active, dinner, far_h, far_db, w_in, b_in, w_out, start, chunks, extra):
    rows, width = h.shape
    units = w_in.shape[-1]
    far = far_h.shape[0]

    def fixed(r, w):
        return pl.BlockSpec((r, w), lambda c, s: (0, 0))

    total = chunks * 4 * CHUNK + extra
    return pl.pallas_call(
        functools.partial(ffn_grads_kernel, chunks=chunks),
        grid_spec=pltpu.PrefetchScalarGridSpec(
            num_scalar_prefetch=1,
            grid=(chunks,),
            in_specs=[
                fixed(rows, width),
                fixed(rows, width),
                pl.BlockSpec((rows, CHUNK), lambda c, s: (0, s[0] + c)),
                pl.BlockSpec((rows, CHUNK), lambda c, s: (0, s[0] + c)),
                fixed(far, width),
                fixed(far, width),
                pl.BlockSpec((width, CHUNK), lambda c, s: (0, s[0] + c)),
                pl.BlockSpec((units,), lambda c, s: (0,)),
                pl.BlockSpec((CHUNK, width), lambda c, s: (s[0] + c, 0)),
            ],
            out_specs=fixed(total, CHUNK),
            scratch_shapes=[
                pltpu.VMEM((width, rows), bf16),
                pltpu.VMEM((width, far), bf16),
                pltpu.VMEM((1, units), f32),
            ],
        ),
        out_shape=jax.ShapeDtypeStruct((total, CHUNK), bf16),
        compiler_params=pltpu.CompilerParams(vmem_limit_bytes=VMEM),
        cost_estimate=pl.CostEstimate(
            flops=4 * (rows + 2 * far) * width * chunks * CHUNK,
            bytes_accessed=16_000_000,
            transcendentals=2 * far * chunks * CHUNK,
        ),
        name="ffn_grads",
    )(start, h, db, active, dinner, far_h, far_db, w_in, b_in, w_out)


def late_kernel(*refs, pieces, grads):
    dq_refs, dk_refs, sums_refs = [refs[pieces * i : pieces * (i + 1)] for i in range(3)]
    wq_ref, wk_ref, table_ref, gain_ref, sums1_ref, sums2_ref = refs[3 * pieces : 3 * pieces + 6]
    out_hbm, tail_ref, sem = refs[3 * pieces + 7 :]
    rows, width = table_ref.shape
    gain = wide(gain_ref[...])[None, :]
    dy = 0.0
    for parts, w_ref in ((dq_refs, wq_ref), (dk_refs, wk_ref)):
        place = 0
        for part in parts:
            dy = dy + dot_nt(part[...], w_ref[:, place : place + part.shape[1]])
            place += part.shape[1]
    normed, root = ln_parts(wide(table_ref[...]))
    table = ln_back_rows(dy, normed, root, gain).astype(bf16)
    vectors = jnp.concatenate(
        [
            sums1_ref[...],
            sums2_ref[...],
            jnp.concatenate([r[...] for r in sums_refs], axis=1),
            jnp.sum(dy * normed, axis=0, keepdims=True),
            jnp.sum(dy, axis=0, keepdims=True),
            jnp.zeros((6, width), f32),
        ],
        axis=0,
    ).astype(bf16)
    base = 0
    for block in (table, vectors):
        for i in range(width // TILE):
            tail_ref[base : base + block.shape[0], :] = block[:, TILE * i : TILE * (i + 1)]
            base += block.shape[0]
    tail_ref[base:, :] = jnp.zeros((tail_ref.shape[0] - base, TILE), bf16)
    copy = pltpu.make_async_copy(tail_ref, out_hbm.at[grads:], sem.at[0])
    copy.start()
    copy.wait()


def late_rows(rows, width):
    grads = 6 * width
    total = grads + (rows + 32) * (width // TILE)
    return grads, -(-total // 512) * 512


def late_sums(d_query, d_key, sums, w_query, w_key, table, gain, sums1, sums2, into):
    rows, width = table.shape
    pieces = len(d_query)
    grads, total = late_rows(rows, width)

    def fixed(shape):
        return pl.BlockSpec(shape, lambda i: (0, 0))

    def lower(x):
        return pl.BlockSpec((rows, x.shape[1]), lambda i: (1, 0))

    square = fixed((width, width))
    anywhere = pl.BlockSpec(memory_space=pl.ANY)
    return pl.pallas_call(
        functools.partial(late_kernel, pieces=pieces, grads=grads),
        grid=(1,),
        in_specs=[lower(x) for x in (*d_query, *d_key)]
        + [fixed(x.shape) for x in sums]
        + [square, square, fixed((rows, width)), pl.BlockSpec((width,), lambda i: (0,))]
        + [fixed((8, width))] * 2
        + [anywhere],
        out_specs=anywhere,
        out_shape=jax.ShapeDtypeStruct((total, TILE), bf16),
        input_output_aliases={3 * pieces + 6: 0},
        scratch_shapes=[pltpu.VMEM((total - grads, TILE), bf16), pltpu.SemaphoreType.DMA((1,))],
        compiler_params=pltpu.CompilerParams(vmem_limit_bytes=VMEM),
        cost_estimate=pl.CostEstimate(
            flops=1_300_000_000, bytes_accessed=12_000_000, transcendentals=0
        ),
        name="late_sums",
    )(*d_query, *d_key, *sums, w_query, w_key, table, gain, sums1, sums2, into)


def input_grad_kernel(*refs, pieces):
    parts = [refs[pieces * i : pieces * (i + 1)] for i in range(3)]
    weights = refs[3 * pieces : 3 * pieces + 3]
    res_ref, out_ref = refs[3 * pieces + 3 :]
    for r in range(0, res_ref.shape[0], 256):
        rows = slice(r, r + 256)
        total = res_ref[rows, :]
        for part, w_ref in zip(parts, weights, strict=True):
            place = 0
            for x in part:
                total = total + dot_nt(x[rows, :], w_ref[:, place : place + x.shape[1]])
                place += x.shape[1]
        out_ref[rows, :] = total


def input_gradient(d_query, d_key, d_value, w_query, w_key, w_value, d_residual):
    rows, width = d_residual.shape
    pieces = len(d_query)
    specs = [
        pl.BlockSpec((rows, x.shape[1]), lambda i: (0, 0)) for x in (*d_query, *d_key, *d_value)
    ]
    square = pl.BlockSpec((width, width), lambda i: (0, 0))
    full = pl.BlockSpec((rows, width), lambda i: (0, 0))
    return pl.pallas_call(
        functools.partial(input_grad_kernel, pieces=pieces),
        grid=(1,),
        in_specs=[*specs, square, square, square, full],
        out_specs=full,
        out_shape=jax.ShapeDtypeStruct((rows, width), f32),
        compiler_params=pltpu.CompilerParams(vmem_limit_bytes=VMEM),
        cost_estimate=pl.CostEstimate(
            flops=6 * rows * width * width, bytes_accessed=10_000_000, transcendentals=0
        ),
        name="input_gradient",
    )(*d_query, *d_key, *d_value, w_query, w_key, w_value, d_residual)


def ffn_result_kernel(core_ref, mine_ref, other_ref, w_mine, w_other, in_ref, out_ref, bias_ref, wo_ref):
    chunks = in_ref.shape[1] // (2 * CHUNK)
    size = w_mine.shape[0]

    def write(first, second, w_first, w_second):
        rows = []
        for i, part in enumerate((first, second)):
            for c in range(chunks):
                cols = slice((i * chunks + c) * CHUNK, (i * chunks + c + 1) * CHUNK)
                base = 4 * CHUNK * c
                in_ref[:, cols] = wide(part[base : base + 2 * CHUNK, :])
                for k in range(2):
                    place = base + (2 + k) * CHUNK
                    out_ref[cols, CHUNK * k : CHUNK * (k + 1)] = wide(part[place : place + CHUNK, :])
            tail = wide(part[4 * CHUNK * chunks : 4 * CHUNK * chunks + 16, :])
            rows = rows + [tail[c : c + 1, :] for c in range(chunks)]
        bias_ref[...] = jnp.concatenate(rows, axis=1).reshape(bias_ref.shape)
        for i, part in enumerate((w_first, w_second)):
            wo_ref[:, CHUNK * i : CHUNK * (i + 1)] = wide(part[...])

    @pl.when(core_ref[0] == 0)
    def _():
        write(mine_ref, other_ref, w_mine, w_other)

    @pl.when(core_ref[0] != 0)
    def _():
        write(other_ref, mine_ref, w_other, w_mine)


def ffn_result(core, mine, other, w_mine, w_other, width, units):
    chunks = units // CHUNK
    if chunks % 2:

        def ordered(a, b):
            first, second = jnp.where(core == 0, a, b), jnp.where(core == 0, b, a)
            return [wide(first), wide(second)]

        total = jnp.concatenate(ordered(mine, other), axis=0)
        parts = [total[4 * CHUNK * c : 4 * CHUNK * (c + 1)] for c in range(chunks)]
        sides = [
            jnp.concatenate([p[(2 + i) * CHUNK : (3 + i) * CHUNK] for p in parts], axis=0)
            for i in range(2)
        ]
        return (
            jnp.concatenate([p[: 2 * CHUNK] for p in parts], axis=1),
            jnp.concatenate(sides, axis=1),
            total[4 * CHUNK * chunks : 4 * CHUNK * chunks + chunks].reshape(units),
            jnp.concatenate(ordered(w_mine, w_other), axis=1),
        )
    smem = pl.BlockSpec(memory_space=pltpu.SMEM)
    vmem = pl.BlockSpec(memory_space=pltpu.VMEM)
    return pl.pallas_call(
        ffn_result_kernel,
        in_specs=[smem] + [vmem] * 4,
        out_shape=[full(width, units), full(units, width), full(units), full(width, width)],
        compiler_params=pltpu.CompilerParams(vmem_limit_bytes=VMEM),
        cost_estimate=pl.CostEstimate(flops=0, bytes_accessed=15_000_000, transcendentals=0),
        name="ffn_result",
    )(core, mine, other, w_mine, w_other)


def early_result_kernel(core_ref, mine_ref, other_ref, q_ref, k_ref, v_ref):
    width = q_ref.shape[0]
    blocks = mine_ref.shape[0] // width

    def write(first, second):
        for b in range(2 * blocks):
            part = first if b < blocks else second
            value = wide(part[width * (b % blocks) : width * (b % blocks + 1), :])
            group, which = divmod(b, 3)
            (q_ref, k_ref, v_ref)[which][:, TILE * group : TILE * (group + 1)] = value

    @pl.when(core_ref[0] == 0)
    def _():
        write(mine_ref, other_ref)

    @pl.when(core_ref[0] != 0)
    def _():
        write(other_ref, mine_ref)


def early_result(core, mine, other, width):
    smem = pl.BlockSpec(memory_space=pltpu.SMEM)
    vmem = pl.BlockSpec(memory_space=pltpu.VMEM)
    return pl.pallas_call(
        early_result_kernel,
        in_specs=[smem, vmem, vmem],
        out_shape=[full(width, width)] * 3,
        compiler_params=pltpu.CompilerParams(vmem_limit_bytes=VMEM),
        cost_estimate=pl.CostEstimate(flops=0, bytes_accessed=10_000_000, transcendentals=0),
        name="early_result",
    )(core, mine, other)


def late_result_kernel(core_ref, mine_ref, other_ref, *refs):
    q_ref, k_ref, v_ref, table_ref = refs[3:7]
    vector_refs, all_ref = refs[7:-1], refs[-1]
    width, rows = q_ref.shape[0], table_ref.shape[0]
    groups = table_ref.shape[1] // TILE
    half = mine_ref.shape[0]

    def write(first, second):
        all_ref[:half, :] = first[...]
        all_ref[half:, :] = second[...]

    @pl.when(core_ref[0] == 0)
    def _():
        write(mine_ref, other_ref)

    @pl.when(core_ref[0] != 0)
    def _():
        write(other_ref, mine_ref)

    base = 0
    for g in range(2):
        for ref in (q_ref, k_ref, v_ref):
            ref[:, TILE * g : TILE * (g + 1)] = wide(all_ref[base : base + width, :])
            base += width
    for i in range(groups):
        table_ref[:, TILE * i : TILE * (i + 1)] = wide(all_ref[base : base + rows, :])
        base += rows
    parts = [wide(all_ref[base + 32 * i : base + 32 * (i + 1), :]) for i in range(groups)]
    vectors = jnp.concatenate(parts, axis=1)
    for place, ref in zip(VECTOR_ROWS, vector_refs, strict=True):
        ref[...] = vectors[place : place + 1, :].reshape(ref.shape)


def late_result(core, mine, other, grads, rows):
    width = grads[0].shape[0]
    groups = width // 256
    smem = pl.BlockSpec(memory_space=pltpu.SMEM)
    half = pl.BlockSpec(mine.shape, lambda i: (0, 0))
    anywhere = pl.BlockSpec(memory_space=pl.ANY)
    last = pl.BlockSpec((width, 256), lambda i: (0, groups - 1))
    vector = pl.BlockSpec((width,), lambda i: (0,))
    return pl.pallas_call(
        late_result_kernel,
        grid=(1,),
        in_specs=[smem, half, half] + [anywhere] * 3,
        out_specs=[last] * 3
        + [pl.BlockSpec((rows, width), lambda i: (0, 0))]
        + [vector] * len(VECTOR_ROWS),
        out_shape=[jax.ShapeDtypeStruct((width, width), f32)] * 3
        + [jax.ShapeDtypeStruct((rows, width), f32)]
        + [jax.ShapeDtypeStruct((width,), f32)] * len(VECTOR_ROWS),
        input_output_aliases={3: 0, 4: 1, 5: 2},
        scratch_shapes=[pltpu.VMEM((2 * mine.shape[0], TILE), bf16)],
        compiler_params=pltpu.CompilerParams(vmem_limit_bytes=VMEM),
        cost_estimate=pl.CostEstimate(flops=0, bytes_accessed=6_000_000, transcendentals=0),
        name="late_result",
    )(core, mine, other, *grads)


class Moves:
    def __init__(self, n_dp, n_mp):
        self.n_dp, self.n_mp = n_dp, n_mp
        self.dp = lax.axis_index("dp")
        self.mp = lax.axis_index("mp")
        self.core = self.dp % 2
        self.dp_bits = [("dp", 1 << b) for b in range(1, n_dp.bit_length() - 1)]
        self.mp_bits = [("mp", 1 << b) for b in range(n_mp.bit_length() - 1)]

    def swap(self, x, pair):
        perm = []
        for d in range(self.n_dp):
            for m in range(self.n_mp):
                axis, bit = pair[d % 2]
                dest = (d ^ bit, m) if axis == "dp" else (d, m ^ bit)
                perm.append((d * self.n_mp + m, dest[0] * self.n_mp + dest[1]))
        return lax.ppermute(x, BOTH, perm)

    def side(self, pair):
        values = [((self.dp if axis == "dp" else self.mp) // bit) % 2 for axis, bit in pair]
        return jnp.where(self.core == 0, values[0], values[1])

    def halves(self, x, pair):
        half = x[0].shape[0] // 2
        side = self.side(pair)

        def part(start):
            return whole([lax.dynamic_slice_in_dim(y, start * half, half, 0) for y in x])

        return part(1 - side), part(side)

    def scatter(self, x, pair):
        sent, kept = self.halves(x, pair)
        return kept, self.swap(sent, pair)

    def exchange(self, x, pair):
        x = whole(x)
        return x, self.swap(x, pair)

    def gather(self, x, pair):
        x = whole(x)
        other = self.swap(x, pair)
        side = self.side(pair)
        first = jnp.where(side == 0, x, other)
        second = jnp.where(side == 0, other, x)
        return (jnp.concatenate([first, second], axis=0),)

    def steps(self, first, second, joined):
        pairs = list(zip(first, second, strict=True))
        if joined:
            middle = [functools.partial(self.exchange, pair=pairs.pop())]
        else:
            middle = []
        down = [functools.partial(self.scatter, pair=pair) for pair in pairs]
        up = [functools.partial(self.gather, pair=pair) for pair in reversed(pairs)]
        return down + middle + up


def whole(x):
    return x[0] if len(x) == 1 else sum(wide(y) for y in x).astype(bf16)


def tie(*values):
    return lax.optimization_barrier(values)


def per_device(
    inputs,
    cotangent,
    w_query,
    b_query,
    w_key,
    b_key,
    w_value,
    b_value,
    w_output,
    b_output,
    norm1_gain,
    norm1_shift,
    w_inner,
    b_inner,
    w_outer,
    b_outer,
    norm2_gain,
    norm2_shift,
    rel_table,
    rel_gain,
    rel_shift,
    block_group,
    seq_lengths,
    *,
    n_dp,
    n_mp,
):
    rows, width = inputs.shape
    units = w_inner.shape[1]
    moves = Moves(n_dp, n_mp)
    core = ("dp", 1)

    def other_shares(x):
        shares = [x[None]]
        for bit in moves.mp_bits:
            shares = [jnp.concatenate(shares, axis=0)]
            shares.append(moves.swap(shares[0], (bit, bit)))
        return jnp.concatenate(shares, axis=0)[1:]

    core_id = moves.core.reshape(1).astype(jnp.int32)
    half_in, half_out = core_half(core_id, w_inner, w_outer, b_inner)
    got = (other_shares(half_in), other_shares(half_out))

    line = bucket_line(rows // 2)
    place_ids = np.arange(rows)[None, :]
    forward = jnp.asarray(np.append(line, -1)[:, None] == place_ids).astype(bf16)
    backward = jnp.asarray(np.append(line[::-1], -1)[:, None] == place_ids).astype(bf16)
    query, key, value, key_line, key_line_back, query_line, both_t = pre(
        inputs,
        rel_table,
        rel_gain,
        rel_shift,
        w_query,
        b_query,
        w_key,
        b_key,
        w_value,
        b_value,
        forward,
        backward,
    )
    mixed, exps, inverse, mixed_full, normed1, root1, hidden_low = attend(
        block_group,
        seq_lengths,
        query,
        key,
        value,
        key_line,
        query_line,
        w_output,
        b_output,
        inputs,
        norm1_gain,
        norm1_shift,
    )

    def far(x):
        whole = x
        for bit in moves.mp_bits:
            whole = jnp.concatenate([whole, moves.swap(whole, (bit, bit))], axis=0)
        return whole[rows:]

    *got, hidden_low = tie(*got, hidden_low)
    other = tuple(moves.swap(x, (core, core)) for x in got)
    far_hidden = far(hidden_low)
    layer_out, d_pre2, d_branch, active, slope, far_slope, sums2 = ffn_forward(
        hidden_low,
        normed1,
        cotangent,
        (norm1_gain, norm1_shift, b_outer, norm2_gain, norm2_shift),
        b_inner,
        w_inner,
        w_outer,
        got,
        other,
    )
    far_branch = far(d_branch)
    d_inner, d_residual, d_mixed, grad_w_output, sums1 = ffn_backward(
        d_branch,
        normed1,
        root1,
        d_pre2,
        mixed,
        w_output,
        norm1_gain,
        slope,
        far_slope,
        w_inner,
        w_outer,
        got,
        other,
    )

    dp_bits, mp_bits = moves.dp_bits, moves.mp_bits
    pair = (core, core)
    ffn_steps = moves.steps(dp_bits, dp_bits[1:2] + dp_bits[:1] + dp_bits[2:], False)
    first, second = mp_bits + dp_bits, dp_bits[:1] + mp_bits + dp_bits[1:]
    early_steps = moves.steps(first, second, True)
    late_steps = moves.steps(first, second, True)
    shared = (exps, inverse, mixed_full, key_line_back, query_line, backward, both_t)
    pieces = []
    pairs = width // TILE

    def attention(d_mixed, first, count, *into):
        *piece, grad = attend_back(query, key, value, d_mixed, *shared, first, count, *into)
        pieces.append(piece)
        return grad

    output_sum = moves.scatter((grad_w_output,), pair)
    chunks = units // CHUNK
    near = (hidden_low, d_branch, active, d_inner, far_hidden, far_branch, w_inner, b_inner, w_outer)
    if chunks % 2 == 0:
        mine, theirs = core_id * (chunks // 2), (1 - core_id) * (chunks // 2)
        sent = ffn_grads(*near, theirs, chunks // 2, 4 * n_dp)
        sent, mine, output_sum = tie(sent, mine, output_sum)
        for bit in mp_bits:
            output_sum = moves.scatter(output_sum, (bit, bit))
        kept = ffn_grads(*near, mine, chunks // 2, 4 * n_dp)
        ffn_sum = (kept, moves.swap(sent, pair))
    else:
        ffn_sum = (ffn_grads(*near, 0 * core_id, chunks, 8 * n_dp),)
        ffn_sum = moves.scatter(ffn_sum, pair)
        for bit in mp_bits:
            output_sum = moves.scatter(output_sum, (bit, bit))
    ffn_rows = ffn_sum[0].shape[0]
    ffn_sum = (jnp.concatenate([whole(ffn_sum), whole(output_sum)], axis=0),)
    ffn_sum, d_mixed = tie(ffn_sum, d_mixed)

    ffn_sum = ffn_steps.pop(0)(ffn_sum)
    early_size = 3 * width * (pairs - 2)
    early = attention(d_mixed, 0, 2, None, early_size, 0)
    ffn_sum, d_mixed, early = tie(ffn_sum, d_mixed, early)
    ffn_sum = ffn_steps.pop(0)(ffn_sum)
    early = attention(d_mixed, 2, 1, early, early_size, 2)
    ffn_sum, d_mixed, early = tie(ffn_sum, d_mixed, early)
    ffn_sum = ffn_steps.pop(0)(ffn_sum)
    early = attention(d_mixed, 3, pairs - 5, early, early_size, 3)
    ffn_sum, d_mixed, early = tie(ffn_sum, d_mixed, early)
    ffn_sum = ffn_steps.pop(0)(ffn_sum)
    early = moves.scatter((early,), pair)
    late_size = late_rows(rows, width)[1]
    late = attention(d_mixed, pairs - 2, 1, None, late_size, 0)
    early, ffn_sum, late, d_mixed = tie(early, ffn_sum, late, d_mixed)
    ffn_sum = ffn_steps.pop(0)(ffn_sum)
    early = early_steps.pop(0)(early)
    late = attention(d_mixed, pairs - 1, 1, late, late_size, 1)
    early, ffn_sum, late, d_residual = tie(early, ffn_sum, late, d_residual)
    ffn_sum = ffn_steps.pop(0)(ffn_sum)
    early = early_steps.pop(0)(early)
    d_query, d_key, d_value, sums = zip(*pieces, strict=True)
    late = late_sums(
        d_query, d_key, sums, w_query, w_key, rel_table, rel_gain, sums1, sums2, late
    )
    input_grad = input_gradient(d_query, d_key, d_value, w_query, w_key, w_value, d_residual)
    late, early, ffn_sum, input_grad = tie(late, early, ffn_sum, input_grad)
    late = (late,)

    def last(x):
        return moves.exchange(x, pair)

    def split(x):
        output_part = (x[0][ffn_rows:],)
        for bit in reversed(mp_bits):
            output_part = moves.gather(output_part, (bit, bit))
        return *last(x), *output_part

    def rest(x):
        return x[0], x[1], *last((x[2],))

    early_steps.append(last)
    late_steps = [lambda x: moves.scatter(x, pair), *late_steps, last]
    ffn_steps.extend([split, rest])
    early_out, ffn_out = None, None
    while late_steps:
        late = late_steps.pop(0)(late)
        done = ()
        if early_steps:
            early = early_steps.pop(0)(early)
        elif early_out is None:
            early_out = early_result(core_id, *early, width)
            done = tuple(early_out)
        if ffn_steps:
            ffn_sum = ffn_steps.pop(0)(ffn_sum)
        elif ffn_out is None:
            ffn_out = ffn_result(core_id, *ffn_sum, width, units)
            done = done + tuple(ffn_out)
        late, early, ffn_sum, done = tie(late, early, ffn_sum, done)
    if early_out is None:
        early_out = early_result(core_id, *early, width)
    if ffn_out is None:
        ffn_out = ffn_result(core_id, *ffn_sum, width, units)
    ffn_in, ffn_out, ffn_bias, grad_w_output = ffn_out
    grad_q, grad_k, grad_v, table, *vectors = late_result(core_id, *late, early_out, rows)
    return (
        layer_out,
        input_grad,
        grad_q,
        vectors[0],
        grad_k,
        vectors[1],
        grad_v,
        vectors[2],
        grad_w_output,
        *vectors[3:6],
        ffn_in,
        ffn_bias,
        ffn_out,
        *vectors[6:9],
        table,
        *vectors[9:],
    )


def solution(mesh):
    n_dp, n_mp = mesh.shape["dp"], mesh.shape["mp"]

    def body(*args):
        return per_device(*args, n_dp=n_dp, n_mp=n_mp)

    split = P(("dp", "mp"), None)
    weights = [P()] * 10 + [P(None, "mp"), P("mp"), P("mp", None)] + [P()] * 6
    return jax.shard_map(
        body,
        mesh=mesh,
        in_specs=(split, split, *weights, P(("dp", "mp")), split),
        out_specs=(
            split,
            split,
            *([P()] * 10),
            P(None, "mp"),
            P("mp"),
            P("mp", None),
            *([P()] * 6),
        ),
        check_vma=False,
    )
```

```python
import functools
import math

import jax
import jax.numpy as jnp
import numpy as np
from jax import lax
from jax.experimental import pallas as pl
from jax.experimental.pallas import tpu as pltpu
from jax.sharding import PartitionSpec as P

HEADS = 12
EPS = 1e-06
LOG2E = 1.4426950408889634
TILE = 128
CHUNK = 384
VMEM = 60 * 1024 * 1024
VECTOR_ROWS = (16, 17, 18, 2, 0, 1, 10, 8, 9, 24, 25)
BOTH = ("dp", "mp")
f32 = jnp.float32
bf16 = jnp.bfloat16


def bucket_line(half_rows):
    table_rows = 2 * half_rows
    middle = half_rows // 2
    relative = table_rows - 1 - np.arange(2 * table_rows - 1)
    signed = np.sign(relative)
    absolute = np.where((relative < middle) & (relative > -middle), middle - 1, np.abs(relative))
    log_place = (
        np.ceil(np.log(absolute / middle) / np.log((table_rows - 1) / middle) * (middle - 1))
        + middle
    )
    placed = np.where(absolute <= middle, relative, log_place * signed)
    return (placed + half_rows).astype(np.int32)


def dot(a, b):
    return jnp.dot(a, b, preferred_element_type=f32)


def dot_nt(a, b):
    return lax.dot_general(a, b, (((1,), (1,)), ((), ())), preferred_element_type=f32)


def dot_tn(a, b):
    return lax.dot_general(a, b, (((0,), (0,)), ((), ())), preferred_element_type=f32)


def wide(v):
    return v.astype(f32)


def ln_parts(v):
    average = jnp.mean(v, axis=-1, keepdims=True)
    center = v - average
    root = lax.rsqrt(jnp.mean(center * center, axis=-1, keepdims=True) + EPS)
    return center * root, root


def ln_back_rows(dy, normed, root, gain):
    dn = dy * gain
    first = jnp.mean(dn, axis=-1, keepdims=True)
    second = jnp.mean(dn * normed, axis=-1, keepdims=True)
    return root * (dn - first - normed * second)


def gelu_parts(v):
    bell = jnp.exp(-0.5 * v * v)
    t = 1.0 / (1.0 + (0.3275911 * math.sqrt(0.5)) * jnp.abs(v))
    poly = t * (
        0.254829592
        + t * (-0.284496736 + t * (1.421413741 + t * (-1.453152027 + t * 1.061405429)))
    )
    tail = 0.5 * poly * bell
    below = jnp.where(v >= 0, 1.0 - tail, tail)
    return v * below, below + v * bell * (1.0 / math.sqrt(2.0 * math.pi))


def pre_kernel(
    x_ref,
    table_ref,
    gain_ref,
    shift_ref,
    wq_ref,
    bq_ref,
    wk_ref,
    bk_ref,
    wv_ref,
    bv_ref,
    forward_ref,
    backward_ref,
    q_ref,
    k_ref,
    v_ref,
    key_line_ref,
    key_back_ref,
    query_line_ref,
    both_t_ref,
    both_ref,
):
    rows = x_ref.shape[0]

    @pl.when(pl.program_id(0) == 0)
    def _():
        both_ref[:rows, :] = x_ref[...]
        normed, _ = ln_parts(wide(table_ref[...]))
        rel = normed * wide(gain_ref[...])[None, :] + wide(shift_ref[...])[None, :]
        both_ref[rows:, :] = rel.astype(bf16)
        both_t_ref[...] = both_ref[...].T

    def project(w_ref, b_ref, part):
        return (dot(both_ref[part, :], w_ref[...]) + wide(b_ref[...])[None, :]).astype(bf16)

    here, there = slice(0, rows), slice(rows, 2 * rows)
    q_ref[...] = project(wq_ref, bq_ref, here)
    k_ref[...] = project(wk_ref, bk_ref, here)
    v_ref[...] = project(wv_ref, bv_ref, here)
    pos_query = project(wq_ref, bq_ref, there)
    pos_key = project(wk_ref, bk_ref, there)
    key_line_ref[...] = dot(forward_ref[...], pos_key).astype(bf16)
    key_back_ref[...] = dot(backward_ref[...], pos_key).astype(bf16)
    query_line_ref[...] = dot(backward_ref[...], pos_query).astype(bf16)


def pre(x, table, gain, shift, w_q, b_q, w_k, b_k, w_v, b_v, forward, backward):
    rows, width = x.shape
    cut = 2 * TILE

    def fixed(r, w):
        return pl.BlockSpec((r, w), lambda c: (0, 0))

    whole = pl.BlockSpec((width,), lambda c: (0,))
    weight = pl.BlockSpec((width, cut), lambda c: (0, c))
    vector = pl.BlockSpec((cut,), lambda c: (c,))
    one = pl.BlockSpec((rows, cut), lambda c: (0, c))
    two = pl.BlockSpec((2 * rows, cut), lambda c: (0, c))
    return pl.pallas_call(
        pre_kernel,
        grid=(width // cut,),
        in_specs=[fixed(rows, width), fixed(rows, width), whole, whole]
        + [weight, vector] * 3
        + [fixed(2 * rows, rows)] * 2,
        out_specs=[one] * 3 + [two] * 3 + [fixed(width, 2 * rows)],
        out_shape=[jax.ShapeDtypeStruct((rows, width), bf16)] * 3
        + [jax.ShapeDtypeStruct((2 * rows, width), bf16)] * 3
        + [jax.ShapeDtypeStruct((width, 2 * rows), bf16)],
        scratch_shapes=[pltpu.VMEM((2 * rows, width), bf16)],
        compiler_params=pltpu.CompilerParams(vmem_limit_bytes=VMEM),
        cost_estimate=pl.CostEstimate(
            flops=5_500_000_000, bytes_accessed=14_000_000, transcendentals=0
        ),
        name="pre",
    )(x, table, gain, shift, w_q, b_q, w_k, b_k, w_v, b_v, forward, backward)


def skewed(x, keep):
    parts = [x[:, TILE * b : TILE * (b + 1)] for b in range(5)]
    return [
        pltpu.roll(jnp.where(keep, parts[b], parts[b + 1]), 1, 1, stride=1, stride_axis=0)
        for b in range(4)
    ]


def unskewed(tiles, keep):
    zero = jnp.zeros((TILE, TILE), f32)
    turned = [zero] + [pltpu.roll(t, 0, 1, stride=1, stride_axis=0) for t in tiles] + [zero]
    return [jnp.where(keep, turned[b + 1], turned[b]) for b in range(5)]


def flipped():
    rows = lax.broadcasted_iota(jnp.int32, (256, 256), 0)
    cols = lax.broadcasted_iota(jnp.int32, (256, 256), 1)
    return (rows + cols == 255).astype(f32).astype(bf16)


def attend_kernel(
    group_ref,
    lengths_ref,
    q_ref,
    k_ref,
    v_ref,
    key_line_ref,
    query_line_ref,
    wo_ref,
    bo_ref,
    x_ref,
    gain_ref,
    shift_ref,
    out_ref,
    exp_ref,
    inv_ref,
    full_ref,
    normed_ref,
    root_ref,
    h_ref,
    side_ref,
    bias_ref,
):
    @pl.when(pl.program_id(0) == 0)
    def _():
        normed_ref[...] = wide(x_ref[...]) + wide(bo_ref[...])[None, :]
        size = bias_ref.shape[0]
        shift = size.bit_length() - 1 - group_ref[0]
        row = lax.broadcasted_iota(jnp.int32, (size, 1), 0)
        col = lax.broadcasted_iota(jnp.int32, (1, size), 1)
        owner = jnp.right_shift(col, shift)
        limit = jnp.zeros((1, size), jnp.int32)
        for slot in range(4):
            limit = jnp.where(owner == slot, lengths_ref[0, slot], limit)
        owner = jnp.where(col - jnp.left_shift(owner, shift) < limit, owner, -1)
        valid = jnp.right_shift(row, shift) == owner
        bias_ref[...] = jnp.where(valid, 0.0, -1e30).astype(f32)

    lane = lax.broadcasted_iota(jnp.int32, (1, TILE), 1)
    keep = (
        lax.broadcasted_iota(jnp.int32, (TILE, TILE), 0)
        + lax.broadcasted_iota(jnp.int32, (TILE, TILE), 1)
        >= TILE - 1
    )
    mine = [lane < 64, lane >= 64]
    scale = LOG2E / math.sqrt(192)
    flip = flipped()
    v_ones = jnp.concatenate([v_ref[...], jnp.ones(v_ref.shape, bf16)], axis=1)
    for h in range(2):
        for t in range(4):
            km = jnp.where(mine[h], k_ref[TILE * t : TILE * (t + 1), :], 0)
            start = 384 - TILE * t
            sk = skewed(dot_nt(km, query_line_ref[start : start + 640, :]), keep)
            for b in range(4):
                side_ref[h, TILE * b : TILE * (b + 1), TILE * t : TILE * (t + 1)] = sk[b].T
        for t in range(4):
            rows = slice(TILE * t, TILE * (t + 1))
            qm = jnp.where(mine[h], q_ref[rows, :], 0)
            start = 384 - TILE * t
            near = skewed(dot_nt(qm, key_line_ref[start : start + 640, :]), keep)
            content = dot_nt(qm, k_ref[...])
            parts = []
            for b in range(4):
                cols = slice(TILE * b, TILE * (b + 1))
                total = content[:, cols] + near[b] + side_ref[h, rows, cols]
                parts.append(total * scale + bias_ref[rows, cols])
            top = jnp.max(
                jnp.maximum(jnp.maximum(parts[0], parts[1]), jnp.maximum(parts[2], parts[3])),
                axis=1,
                keepdims=True,
            )
            low = [jnp.exp2(p - top).astype(bf16) for p in parts]
            exps = jnp.concatenate(low, axis=1)
            exp_ref[h, rows, :] = jnp.concatenate(
                [dot(exps[:, 256:], flip).astype(bf16), dot(exps[:, :256], flip).astype(bf16)], axis=1
            )
            product = dot(exps, v_ones)
            inverse = 1.0 / product[:, TILE:]
            out = product[:, :TILE] * inverse
            if h == 0:
                inv_ref[0, rows, :] = inverse
                full_ref[0, rows, :] = out
            else:
                inv_ref[0, rows, :] = jnp.where(mine[0], inv_ref[0, rows, :], inverse)
                out = jnp.where(mine[0], full_ref[0, rows, :], out)
                full_ref[0, rows, :] = out
                out_ref[rows, :] = out.astype(bf16)
    normed_ref[...] += dot(out_ref[...], wo_ref[...])

    @pl.when(pl.program_id(0) == pl.num_programs(0) - 1)
    def _():
        gain, shift = wide(gain_ref[...])[None, :], wide(shift_ref[...])[None, :]
        for r in range(0, h_ref.shape[0], TILE):
            rows = slice(r, r + TILE)
            normed, root = ln_parts(normed_ref[rows, :])
            normed_ref[rows, :] = normed
            root_ref[rows, :] = jnp.broadcast_to(root, (TILE, TILE))
            h_ref[rows, :] = (normed * gain + shift).astype(bf16)


def attend(group, lengths, q, k, v, key_line, query_line, w_output, b_output, x, gain, shift):
    rows, width = q.shape
    pairs = width // TILE
    col = pl.BlockSpec((rows, TILE), lambda g: (0, g))
    line = pl.BlockSpec((2 * rows, TILE), lambda g: (0, g))
    scalars = pl.BlockSpec(memory_space=pltpu.SMEM)
    full = pl.BlockSpec((rows, width), lambda g: (0, 0))
    vector = pl.BlockSpec((width,), lambda g: (0,))
    return pl.pallas_call(
        attend_kernel,
        grid=(pairs,),
        in_specs=[scalars, scalars, col, col, col, line, line]
        + [pl.BlockSpec((TILE, width), lambda g: (g, 0)), vector, full, vector, vector],
        out_specs=[
            col,
            pl.BlockSpec((2, rows, rows), lambda g: (g, 0, 0)),
            pl.BlockSpec((1, rows, TILE), lambda g: (g, 0, 0)),
            pl.BlockSpec((1, rows, TILE), lambda g: (g, 0, 0)),
            full,
            pl.BlockSpec((rows, TILE), lambda g: (0, 0)),
            full,
        ],
        out_shape=[
            jax.ShapeDtypeStruct((rows, width), bf16),
            jax.ShapeDtypeStruct((2 * pairs, rows, rows), bf16),
            jax.ShapeDtypeStruct((pairs, rows, TILE), f32),
            jax.ShapeDtypeStruct((pairs, rows, TILE), f32),
            jax.ShapeDtypeStruct((rows, width), f32),
            jax.ShapeDtypeStruct((rows, TILE), f32),
            jax.ShapeDtypeStruct((rows, width), bf16),
        ],
        scratch_shapes=[pltpu.VMEM((2, rows, rows), f32), pltpu.VMEM((rows, rows), f32)],
        compiler_params=pltpu.CompilerParams(vmem_limit_bytes=VMEM),
        cost_estimate=pl.CostEstimate(
            flops=18_000_000_000, bytes_accessed=16_000_000, transcendentals=3_200_000
        ),
        name="attend",
    )(group, lengths, q, k, v, key_line, query_line, w_output, b_output, x, gain, shift)


def attend_back_kernel(
    q_ref,
    k_ref,
    v_ref,
    do_ref,
    exp_ref,
    inv_ref,
    full_ref,
    key_line_ref,
    query_line_ref,
    places_ref,
    both_t_ref,
    *refs,
):
    dq_ref, dk_ref, dv_ref, sums_ref, grad_ref, *refs = refs[-9:]
    attend_back_pair(
        q_ref,
        k_ref,
        v_ref,
        do_ref,
        exp_ref,
        inv_ref,
        full_ref,
        key_line_ref,
        query_line_ref,
        places_ref,
        both_t_ref,
        dq_ref,
        dk_ref,
        dv_ref,
        sums_ref,
        grad_ref,
        *refs,
    )


def attend_back_pair(
    q_ref,
    k_ref,
    v_ref,
    do_ref,
    exp_ref,
    inv_ref,
    full_ref,
    key_line_ref,
    query_line_ref,
    places_ref,
    both_t_ref,
    dq_ref,
    dk_ref,
    dv_ref,
    sums_ref,
    grad_ref,
    ds_ref,
    dst_ref,
    query_band,
    key_band,
):
    @pl.when(pl.program_id(0) == 0)
    def _():
        query_band[...] = jnp.zeros_like(query_band)
        key_band[...] = jnp.zeros_like(key_band)

    scale = 1.0 / math.sqrt(192)
    lane = lax.broadcasted_iota(jnp.int32, (1, TILE), 1)
    sub = lax.broadcasted_iota(jnp.int32, (TILE, 1), 0)
    keep = lax.broadcasted_iota(jnp.int32, (TILE, TILE), 1) >= lax.broadcasted_iota(
        jnp.int32, (TILE, TILE), 0
    )
    mine = [lane < 64, lane >= 64]
    mine_t = [sub < 64, sub >= 64]
    flip = flipped()

    def reverse(x):
        return jnp.concatenate([dot(flip, x[256:]), dot(flip, x[:256])], axis=0).astype(bf16)

    q = q_ref[...]
    k = reverse(k_ref[...])
    v = reverse(v_ref[...])
    q_t = q.T
    k_t = k.T
    do = (wide(do_ref[...]) * inv_ref[0]).astype(bf16)
    do_t = do.T
    share = wide(do) * full_ref[0]
    high = share.astype(bf16)
    rest = (share - wide(high)).astype(bf16)
    row = lax.broadcasted_iota(jnp.int32, (256, 256), 0) % TILE // 64
    ones = (row == lax.broadcasted_iota(jnp.int32, (256, 256), 1) // TILE).astype(f32).astype(bf16)
    means = dot(jnp.concatenate([high, rest], axis=1), ones)
    dv_t = None
    dqs, dks, key_lines, query_lines = [], [], [], []
    for h in range(2):
        dom = jnp.where(mine[h], do, 0)
        for t in range(4):
            rows = slice(TILE * t, TILE * (t + 1))
            dp = dot_nt(dom[rows], v)
            mean = means[rows, TILE * h : TILE * (h + 1)]
            ds = []
            for b in range(4):
                cols = slice(TILE * b, TILE * (b + 1))
                ds.append(wide(exp_ref[h, rows, cols]) * (dp[:, cols] - mean))
                ds_ref[h, rows, cols] = ds[b].astype(bf16)
            out = unskewed(ds, keep)
            for b in range(5):
                query_band[h, rows, TILE * (t + b) : TILE * (t + b + 1)] = out[b].astype(bf16)
        for t in range(4):
            rows = slice(TILE * t, TILE * (t + 1))
            turned = [ds_ref[h, TILE * b : TILE * (b + 1), rows].T for b in range(4)]
            for b in range(4):
                dst_ref[h, rows, TILE * b : TILE * (b + 1)] = turned[b]
            out = unskewed([wide(x) for x in turned], keep)
            for b in range(5):
                key_band[h, rows, TILE * (t + b) : TILE * (t + b + 1)] = out[b].astype(bf16)
        part = dot(jnp.where(mine_t[h], do_t, 0), exp_ref[h])
        dv_t = part if dv_t is None else dv_t + part
        dq, dk, key_line, query_line = [], [], [], []
        for i in range(2):
            rows = slice(256 * i, 256 * (i + 1))
            band = slice(256 * i, 256 * i + 768)
            dq.append(dot(ds_ref[h, rows, :], k) + dot(query_band[h, rows, band], key_line_ref[band, :]))
            dk.append(dot(dst_ref[h, rows, :], q) + dot(key_band[h, rows, band], query_line_ref[band, :]))
            key_line.append(dot(jnp.where(mine_t[h], q_t[:, rows], 0), query_band[h, rows, band]))
            query_line.append(dot(jnp.where(mine_t[h], k_t[:, rows], 0), key_band[h, rows, band]))
        dqs.append(jnp.concatenate(dq, axis=0))
        dks.append(jnp.concatenate(dk, axis=0))
        key_lines.append(key_line)
        query_lines.append(query_line)
    size = q.shape[0]
    dq_ref[:size, :] = (jnp.where(mine[0], dqs[0], dqs[1]) * scale).astype(bf16)
    dk_ref[:size, :] = reverse((jnp.where(mine[0], dks[0], dks[1]) * scale).astype(bf16))
    dv_ref[...] = reverse(dv_t.T.astype(bf16))
    for lines, ref in ((key_lines, dk_ref), (query_lines, dq_ref)):
        first = lines[0][0] + lines[1][0]
        second = lines[0][1] + lines[1][1]
        whole = jnp.concatenate(
            [first[:, :256], first[:, 256:] + second[:, :512], second[:, 512:]], axis=1
        )
        ref[size:, :] = dot((whole * scale).astype(bf16), places_ref[...]).T.astype(bf16)
    width = both_t_ref.shape[0]
    grad_ref[:width, :] = dot(both_t_ref[...], dq_ref[...]).astype(bf16)
    grad_ref[width : 2 * width, :] = dot(both_t_ref[...], dk_ref[...]).astype(bf16)
    grad_ref[2 * width :, :] = dot(both_t_ref[:, :size], dv_ref[...]).astype(bf16)
    sums = [jnp.sum(wide(r[...]), axis=0, keepdims=True) for r in (dq_ref, dk_ref, dv_ref)]
    sums_ref[...] = jnp.concatenate(sums + [jnp.zeros((5, TILE), f32)], axis=0)


def attend_back(
    q,
    k,
    v,
    do,
    exps,
    inverse,
    mixed_full,
    key_line,
    query_line,
    places,
    both_t,
    first,
    count,
    into,
    size,
    start,
):
    rows, width = q.shape
    col = pl.BlockSpec((rows, TILE), lambda g: (0, first + g))
    line = pl.BlockSpec((2 * rows, TILE), lambda g: (0, first + g))
    both = pl.BlockSpec((2 * rows, TILE), lambda g: (0, g))
    more = [] if into is None else [into]
    return pl.pallas_call(
        attend_back_kernel,
        grid=(count,),
        in_specs=[
            col,
            col,
            col,
            col,
            pl.BlockSpec((2, rows, rows), lambda g: (first + g, 0, 0)),
            pl.BlockSpec((1, rows, TILE), lambda g: (first + g, 0, 0)),
            pl.BlockSpec((1, rows, TILE), lambda g: (first + g, 0, 0)),
            line,
            line,
            pl.BlockSpec((2 * rows, rows), lambda g: (0, 0)),
            pl.BlockSpec((width, 2 * rows), lambda g: (0, 0)),
        ]
        + [pl.BlockSpec(memory_space=pl.ANY) for _ in more],
        out_specs=[
            both,
            both,
            pl.BlockSpec((rows, TILE), lambda g: (0, g)),
            pl.BlockSpec((8, TILE), lambda g: (0, g)),
            pl.BlockSpec((3 * width, TILE), lambda g: (start + g, 0)),
        ],
        out_shape=[
            jax.ShapeDtypeStruct((2 * rows, count * TILE), bf16),
            jax.ShapeDtypeStruct((2 * rows, count * TILE), bf16),
            jax.ShapeDtypeStruct((rows, count * TILE), bf16),
            jax.ShapeDtypeStruct((8, count * TILE), f32),
            jax.ShapeDtypeStruct((size, TILE), bf16),
        ],
        input_output_aliases={11: 4} if more else {},
        scratch_shapes=[
            pltpu.VMEM((2, rows, rows), bf16),
            pltpu.VMEM((2, rows, rows), bf16),
            pltpu.VMEM((2, rows, 2 * rows), bf16),
            pltpu.VMEM((2, rows, 2 * rows), bf16),
        ],
        compiler_params=pltpu.CompilerParams(vmem_limit_bytes=VMEM),
        cost_estimate=pl.CostEstimate(
            flops=count * 4_000_000_000, bytes_accessed=count * 3_000_000, transcendentals=0
        ),
        name="attend_back",
    )(q, k, v, do, exps, inverse, mixed_full, key_line, query_line, places, both_t, *more)


def weight_copies(y, sources, targets, sems, chunk, chunks):
    win_hbm, wout_hbm = sources[:2]
    win_ref, wout_ref, far_in, far_out = targets
    n = far_in.shape[0] // 2
    half = far_out.shape[1] // 2
    lists = []
    for c in range(chunks):
        cols = slice(chunk * c, chunk * (c + 1))
        lists.append([(win_hbm.at[:, cols], win_ref.at[:, cols]), (wout_hbm.at[cols], wout_ref.at[cols])])
    mine = pl.ds(pl.multiple_of(y * half, 16), half)
    theirs = pl.ds(pl.multiple_of((1 - y) * half, 16), half)
    for k in range(2):
        part = slice(n * k, n * (k + 1))
        columns, first, second = sources[2 + 3 * k : 5 + 3 * k]
        lists.append(
            [
                (columns, far_in.at[part]),
                (first, far_out.at[part, mine]),
                (second, far_out.at[part, theirs]),
            ]
        )
    copies = []
    for i, pairs in enumerate(lists):
        copies.append(
            [pltpu.make_async_copy(a, b, sems.at[i, k]) for k, (a, b) in enumerate(pairs)]
        )
    return copies


def start(copies):
    for copy in copies:
        copy.start()


def wait(copies):
    for copy in copies:
        copy.wait()


def core_half_kernel(place_ref, bin_ref, win_hbm, wout_hbm, in_ref, out_ref, sems):
    units = in_ref.shape[1]
    width = win_hbm.shape[0]
    rows = pl.multiple_of((2 * place_ref[0] + place_ref[1]) * out_ref.shape[0], 16)

    def send(core):
        part = slice(units * core, units * (core + 1))
        copies = [
            pltpu.make_async_copy(wout_hbm.at[pl.ds(rows, out_ref.shape[0])], out_ref, sems.at[0]),
            pltpu.make_async_copy(win_hbm.at[:, part], in_ref.at[:width], sems.at[1]),
        ]
        start(copies)
        bias = jnp.broadcast_to(wide(bin_ref[...])[None, part], (16, units))
        in_ref[width:, :] = bias.astype(bf16)
        wait(copies)

    @pl.when(place_ref[0] == 0)
    def _():
        send(0)

    @pl.when(place_ref[0] != 0)
    def _():
        send(1)


def core_half(core, y, w_in, w_out, b_in):
    width, units = w_in.shape
    half = units // 2
    if half % TILE:
        place = core[0] * half
        bias = lax.dynamic_slice_in_dim(b_in, place, half, 0)
        columns = lax.dynamic_slice_in_dim(w_in, place, half, 1)
        columns = jnp.concatenate([columns, jnp.broadcast_to(bias, (16, half))], axis=0)
        return columns, lax.dynamic_slice_in_dim(w_out, place + y[0] * (half // 2), half // 2, 0)
    anywhere = pl.BlockSpec(memory_space=pl.ANY)
    vmem = pl.BlockSpec(memory_space=pltpu.VMEM)
    return pl.pallas_call(
        core_half_kernel,
        in_specs=[pl.BlockSpec(memory_space=pltpu.SMEM), vmem, anywhere, anywhere],
        out_specs=[vmem, vmem],
        out_shape=[low(width + 16, half), low(half // 2, width)],
        scratch_shapes=[pltpu.SemaphoreType.DMA((2,))],
        compiler_params=pltpu.CompilerParams(vmem_limit_bytes=VMEM),
        cost_estimate=pl.CostEstimate(flops=0, bytes_accessed=5_000_000, transcendentals=0),
        name="core_half",
    )(jnp.concatenate([core, y]), b_in, w_in, w_out)


def ffn_forward_kernel(
    h_ref,
    normed_hbm,
    cot_hbm,
    gain1_ref,
    shift1_ref,
    b_outer_ref,
    gain2_ref,
    shift2_ref,
    bin_ref,
    *refs,
    chunk,
    far_chunk,
):
    y, sources, refs = refs[0][0], refs[1:9], refs[9:]
    out_ref, dpre_ref, dbranch_ref, active_hbm, slope_hbm, far_slope_hbm, sums_ref = refs[:7]
    normed_ref, cot_ref, active_ref, slope_ref, far_slope_ref, total_ref = refs[7:13]
    targets, sems, sems2 = refs[13:17], refs[17], refs[18]
    far_in_ref, far_out_ref = targets[2:]
    rows, width = h_ref.shape
    chunks = active_ref.shape[1] // chunk
    far_count, _, units = far_in_ref.shape
    far_chunks = units // far_chunk
    weights = weight_copies(y, sources, targets, sems, chunk, chunks)
    others = [
        pltpu.make_async_copy(normed_hbm, normed_ref, sems2.at[0]),
        pltpu.make_async_copy(cot_hbm, cot_ref, sems2.at[1]),
    ]
    back = [
        pltpu.make_async_copy(active_ref, active_hbm, sems2.at[2]),
        pltpu.make_async_copy(slope_ref, slope_hbm, sems2.at[3]),
        pltpu.make_async_copy(far_slope_ref, far_slope_hbm, sems2.at[4]),
    ]
    for copies in weights:
        start(copies)
    start(others)
    b_in = wide(bin_ref[...])[None, :]

    def forward(w_in, b_in, w_out, active_at, slope_at, first):
        for r in range(0, rows, 256):
            part = slice(r, r + 256)
            active, slope = gelu_parts(dot(h_ref[part, :], w_in) + b_in)
            active = active.astype(bf16)
            if active_at is not None:
                active_ref[part, active_at] = active
            slope_at(part, slope.astype(bf16))
            product = dot(active, w_out)
            total_ref[part, :] = product if first else total_ref[part, :] + product

    for c in range(chunks):
        wait(weights[c])
        cols = slice(chunk * c, chunk * (c + 1))

        def put(part, value, cols=cols):
            slope_ref[part, cols] = value

        forward(targets[0][:, cols], b_in[:, cols], targets[1][cols, :], cols, put, c == 0)
    start(back[:2])
    wait(weights[chunks])
    wait(weights[chunks + 1])

    def far_step(s, carry):
        for c in range(far_chunks):
            cols = slice(far_chunk * c, far_chunk * (c + 1))

            def put(part, value, cols=cols):
                far_slope_ref[s, part, cols] = value

            bias = wide(far_in_ref[s, width : width + 1, cols])
            forward(far_in_ref[s, :width, cols], bias, far_out_ref[s, cols, :], None, put, False)
        return carry

    lax.fori_loop(0, far_count, far_step, 0)
    start(back[2:])
    wait(others)
    gain1, shift1, b_outer, gain2, shift2 = [
        wide(r[...])[None, :] for r in (gain1_ref, shift1_ref, b_outer_ref, gain2_ref, shift2_ref)
    ]
    sums = [jnp.zeros((1, width), f32) for _ in range(3)]
    for r in range(0, rows, TILE):
        part = slice(r, r + TILE)
        normed, root = ln_parts(normed_ref[part, :] * gain1 + shift1 + total_ref[part, :] + b_outer)
        out_ref[part, :] = normed * gain2 + shift2
        dy = wide(cot_ref[part, :])
        d = ln_back_rows(dy, normed, root, gain2)
        dpre_ref[part, :] = d
        low = d.astype(bf16)
        dbranch_ref[part, :] = low
        sums[0] += jnp.sum(dy * normed, axis=0, keepdims=True)
        sums[1] += jnp.sum(dy, axis=0, keepdims=True)
        sums[2] += jnp.sum(wide(low), axis=0, keepdims=True)
    sums_ref[...] = jnp.concatenate(sums + [jnp.zeros((5, width), f32)], axis=0)
    wait(back)


def ffn_backward_kernel(
    db_ref, normed_hbm, root_ref, dpre_ref, mixed_hbm, wo_hbm, gain_ref, *refs, chunk, far_chunk
):
    slope_hbm, far_slope_hbm = refs[:2]
    y, sources, refs = refs[2][0], refs[3:11], refs[11:]
    dinner_hbm, dres_ref, dmixed_ref, grad_ref, sums_ref = refs[:5]
    normed_ref, mixed_ref, wo_ref, dinner_ref, total_ref, dattn_ref = refs[5:11]
    slope_ref, far_slope_ref = refs[11:13]
    targets, sems, sems2 = refs[13:17], refs[17], refs[18]
    far_in_ref, far_out_ref = targets[2:]
    rows, width = db_ref.shape
    chunks = dinner_ref.shape[1] // chunk
    far_count, _, units = far_in_ref.shape
    far_chunks = units // far_chunk
    weights = weight_copies(y, sources, targets, sems, chunk, chunks)
    slopes = [
        pltpu.make_async_copy(slope_hbm, slope_ref, sems2.at[0]),
        pltpu.make_async_copy(far_slope_hbm, far_slope_ref, sems2.at[1]),
    ]
    others = [
        pltpu.make_async_copy(normed_hbm, normed_ref, sems2.at[2]),
        pltpu.make_async_copy(mixed_hbm, mixed_ref, sems2.at[3]),
        pltpu.make_async_copy(wo_hbm, wo_ref, sems2.at[4]),
    ]
    back = [pltpu.make_async_copy(dinner_ref, dinner_hbm, sems2.at[5])]
    start(weights[0])
    start(slopes[:1])
    for copies in weights[1:]:
        start(copies)
    start(slopes[1:])
    start(others)

    def backward(w_in, w_out, slope, keep, first):
        for r in range(0, rows, 256):
            part = slice(r, r + 256)
            d = (dot_nt(db_ref[part, :], w_out) * wide(slope(part))).astype(bf16)
            if keep is not None:
                keep(part, d)
            base = dpre_ref[part, :] if first else total_ref[part, :]
            total_ref[part, :] = base + dot_nt(d, w_in)

    wait(slopes[:1])
    for c in range(chunks):
        wait(weights[c])
        cols = slice(chunk * c, chunk * (c + 1))

        def keep(part, value, cols=cols):
            dinner_ref[part, cols] = value

        def slope(part, cols=cols):
            return slope_ref[part, cols]

        backward(targets[0][:, cols], targets[1][cols, :], slope, keep, c == 0)
    start(back)
    wait(weights[chunks])
    wait(weights[chunks + 1])
    wait(slopes[1:])

    def far_step(s, carry):
        for c in range(far_chunks):
            cols = slice(far_chunk * c, far_chunk * (c + 1))

            def slope(part, cols=cols):
                return far_slope_ref[s, part, cols]

            backward(far_in_ref[s, :width, cols], far_out_ref[s, cols, :], slope, None, False)
        return carry

    lax.fori_loop(0, far_count, far_step, 0)
    wait(others)
    gain = wide(gain_ref[...])[None, :]
    sums = [jnp.zeros((1, width), f32) for _ in range(3)]
    for r in range(0, rows, TILE):
        part = slice(r, r + TILE)
        dy = total_ref[part, :]
        normed = normed_ref[part, :]
        d = ln_back_rows(dy, normed, root_ref[part, 0:1], gain)
        dres_ref[part, :] = d
        low = d.astype(bf16)
        dattn_ref[part, :] = low
        dmixed_ref[part, :] = dot_nt(low, wo_ref[...]).astype(bf16)
        sums[0] += jnp.sum(dy * normed, axis=0, keepdims=True)
        sums[1] += jnp.sum(dy, axis=0, keepdims=True)
        sums[2] += jnp.sum(wide(low), axis=0, keepdims=True)
    sums_ref[...] = jnp.concatenate(sums + [jnp.zeros((5, width), f32)], axis=0)
    grad = dot(mixed_ref[...].T, dattn_ref[...]).astype(bf16)
    for i in range(2):
        grad_ref[width * i : width * (i + 1), :] = grad[:, CHUNK * i : CHUNK * (i + 1)]
    wait(back)


def low(*shape):
    return jax.ShapeDtypeStruct(shape, bf16)


def full(*shape):
    return jax.ShapeDtypeStruct(shape, f32)


def share_sizes(w_in, got):
    return min(2 * CHUNK, w_in.shape[1]), min(2 * CHUNK, got[0].shape[2])


def weight_scratch(w_in, w_out, got, chunk):
    n = got[0].shape[0]
    return [
        pltpu.VMEM(w_in.shape, bf16),
        pltpu.VMEM(w_out.shape, bf16),
        pltpu.VMEM((2 * n, *got[0].shape[1:]), bf16),
        pltpu.VMEM((2 * n, 2 * got[1].shape[1], got[1].shape[2]), bf16),
        pltpu.SemaphoreType.DMA((w_in.shape[1] // chunk + 2, 3)),
        pltpu.SemaphoreType.DMA((6,)),
    ]


def ffn_forward(h, normed, cot, vectors, b_in, y, w_in, w_out, got, other):
    rows, width = h.shape
    units = w_in.shape[1]
    far = 2 * got[0].shape[0]
    chunk, far_chunk = share_sizes(w_in, got)
    anywhere = pl.BlockSpec(memory_space=pl.ANY)
    vmem = pl.BlockSpec(memory_space=pltpu.VMEM)
    far_slope = (far, rows, got[0].shape[2])
    return pl.pallas_call(
        functools.partial(ffn_forward_kernel, chunk=chunk, far_chunk=far_chunk),
        in_specs=[vmem, anywhere, anywhere]
        + [vmem] * 6
        + [pl.BlockSpec(memory_space=pltpu.SMEM)]
        + [anywhere] * 8,
        out_specs=[vmem] * 3 + [anywhere] * 3 + [vmem],
        out_shape=[
            full(rows, width),
            full(rows, width),
            low(rows, width),
            low(rows, units),
            low(rows, units),
            low(*far_slope),
            full(8, width),
        ],
        scratch_shapes=[
            pltpu.VMEM((rows, width), f32),
            pltpu.VMEM((rows, width), bf16),
            pltpu.VMEM((rows, units), bf16),
            pltpu.VMEM((rows, units), bf16),
            pltpu.VMEM(far_slope, bf16),
            pltpu.VMEM((rows, width), f32),
            *weight_scratch(w_in, w_out, got, chunk),
        ],
        compiler_params=pltpu.CompilerParams(vmem_limit_bytes=VMEM),
        cost_estimate=pl.CostEstimate(
            flops=16 * rows * width * width, bytes_accessed=24_000_000, transcendentals=3_200_000
        ),
        name="ffn_forward",
    )(h, normed, cot, *vectors, b_in, y, w_in, w_out, *got, *other)


def ffn_backward(
    db, normed, root, dpre, mixed, w_output, gain, slope, far_slope, y, w_in, w_out, got, other
):
    rows, width = db.shape
    units = w_in.shape[1]
    chunk, far_chunk = share_sizes(w_in, got)
    anywhere = pl.BlockSpec(memory_space=pl.ANY)
    vmem = pl.BlockSpec(memory_space=pltpu.VMEM)
    return pl.pallas_call(
        functools.partial(ffn_backward_kernel, chunk=chunk, far_chunk=far_chunk),
        in_specs=[vmem, anywhere, vmem, vmem, anywhere, anywhere, vmem, anywhere, anywhere]
        + [pl.BlockSpec(memory_space=pltpu.SMEM)]
        + [anywhere] * 8,
        out_specs=[anywhere] + [vmem] * 4,
        out_shape=[
            low(rows, units),
            full(rows, width),
            low(rows, width),
            low(2 * width, CHUNK),
            full(8, width),
        ],
        scratch_shapes=[
            pltpu.VMEM((rows, width), f32),
            pltpu.VMEM((rows, width), bf16),
            pltpu.VMEM((width, width), bf16),
            pltpu.VMEM((rows, units), bf16),
            pltpu.VMEM((rows, width), f32),
            pltpu.VMEM((rows, width), bf16),
            pltpu.VMEM((rows, units), bf16),
            pltpu.VMEM(far_slope.shape, bf16),
            *weight_scratch(w_in, w_out, got, chunk),
        ],
        compiler_params=pltpu.CompilerParams(vmem_limit_bytes=VMEM),
        cost_estimate=pl.CostEstimate(
            flops=20 * rows * width * width, bytes_accessed=24_000_000, transcendentals=0
        ),
        name="ffn_backward",
    )(
        db,
        normed,
        root,
        dpre,
        mixed,
        w_output,
        gain,
        slope,
        far_slope,
        y,
        w_in,
        w_out,
        *got,
        *other,
    )


def ffn_grads_kernel(
    start_ref,
    bin_ref,
    h_hbm,
    db_hbm,
    active_hbm,
    dinner_hbm,
    far_h_hbm,
    far_db_hbm,
    win_hbm,
    wout_hbm,
    out_ref,
    h_ref,
    db_ref,
    active_ref,
    dinner_ref,
    far_h_ref,
    far_db_ref,
    win_ref,
    wout_ref,
    far_active_ref,
    far_slope_ref,
    far_dinner_ref,
    h_t,
    far_t,
    bias_ref,
    sems,
    *,
    chunks,
):
    units = chunks * CHUNK
    width = h_ref.shape[1]
    far = far_h_ref.shape[0]
    tail = 4 * CHUNK * chunks
    if win_hbm.shape[1] == units:
        part = slice(0, units)
    else:
        part = pl.ds(pl.multiple_of(start_ref[0] * CHUNK, CHUNK), units)
    copies = [
        pltpu.make_async_copy(source, target, sems.at[i])
        for i, (source, target) in enumerate(
            [
                (far_h_hbm, far_h_ref),
                (win_hbm.at[:, part], win_ref),
                (far_db_hbm, far_db_ref),
                (wout_hbm.at[part], wout_ref),
                (h_hbm, h_ref),
                (dinner_hbm.at[:, part], dinner_ref),
                (active_hbm.at[:, part], active_ref),
                (db_hbm, db_ref),
            ]
        )
    ]
    start(copies)
    bias_ref[...] = wide(bin_ref[...])[None, :]
    b_in = bias_ref[:, part]
    wait(copies[:2])
    for r in range(0, far, 256):
        rows = slice(r, r + 256)
        active, slope = gelu_parts(dot(far_h_ref[rows, :], win_ref[...]) + b_in)
        far_active_ref[rows, :] = active.astype(bf16)
        far_slope_ref[rows, :] = slope.astype(bf16)
    far_t[...] = far_h_ref[...].T
    wait(copies[2:4])
    bias = jnp.zeros((1, units), f32)
    for r in range(0, far, 256):
        rows = slice(r, r + 256)
        dinner = dot_nt(far_db_ref[rows, :], wout_ref[...]) * wide(far_slope_ref[rows, :])
        dinner = dinner.astype(bf16)
        far_dinner_ref[rows, :] = dinner
        bias = bias + jnp.sum(wide(dinner), axis=0, keepdims=True)
    wait(copies[4:6])
    h_t[...] = h_ref[...].T
    for r in range(0, width, 256):
        rows = slice(r, r + 256)
        grad = dot(h_t[rows, :], dinner_ref[...]) + dot(far_t[rows, :], far_dinner_ref[...])
        grad = grad.astype(bf16)
        for c in range(chunks):
            place = 4 * CHUNK * c + r
            out_ref[place : place + 256, :] = grad[:, CHUNK * c : CHUNK * (c + 1)]
    wait(copies[6:])
    for c in range(chunks):
        cols = slice(CHUNK * c, CHUNK * (c + 1))
        grad = dot(active_ref[:, cols].T, db_ref[...])
        grad = (grad + dot(far_active_ref[:, cols].T, far_db_ref[...])).astype(bf16)
        for k in range(2):
            place = 4 * CHUNK * c + (2 + k) * CHUNK
            out_ref[place : place + CHUNK, :] = grad[:, CHUNK * k : CHUNK * (k + 1)]
    bias = bias + jnp.sum(wide(dinner_ref[...]), axis=0, keepdims=True)
    out_ref[tail:, :] = jnp.zeros_like(out_ref[tail:, :])
    rows = [bias[:, CHUNK * c : CHUNK * (c + 1)] for c in range(chunks)]
    rows.append(jnp.zeros((16 - chunks, CHUNK), f32))
    out_ref[tail : tail + 16, :] = jnp.concatenate(rows, axis=0).astype(bf16)


def ffn_grads(h, db, active, dinner, far_h, far_db, w_in, b_in, w_out, start, chunks, extra):
    rows, width = h.shape
    units = chunks * CHUNK
    far = far_h.shape[0]
    anywhere = pl.BlockSpec(memory_space=pl.ANY)

    def scratch(r, w):
        return pltpu.VMEM((r, w), bf16)

    total = chunks * 4 * CHUNK + extra
    return pl.pallas_call(
        functools.partial(ffn_grads_kernel, chunks=chunks),
        in_specs=[pl.BlockSpec(memory_space=pltpu.SMEM), pl.BlockSpec(memory_space=pltpu.VMEM)]
        + [anywhere] * 8,
        out_specs=pl.BlockSpec(memory_space=pltpu.VMEM),
        out_shape=low(total, CHUNK),
        scratch_shapes=[
            scratch(rows, width),
            scratch(rows, width),
            scratch(rows, units),
            scratch(rows, units),
            scratch(far, width),
            scratch(far, width),
            scratch(width, units),
            scratch(units, width),
            scratch(far, units),
            scratch(far, units),
            scratch(far, units),
            scratch(width, rows),
            scratch(width, far),
            pltpu.VMEM((1, w_in.shape[1]), f32),
            pltpu.SemaphoreType.DMA((8,)),
        ],
        compiler_params=pltpu.CompilerParams(vmem_limit_bytes=VMEM),
        cost_estimate=pl.CostEstimate(
            flops=4 * (rows + 2 * far) * width * units,
            bytes_accessed=16_000_000,
            transcendentals=2 * far * units,
        ),
        name="ffn_grads",
    )(start, b_in, h, db, active, dinner, far_h, far_db, w_in, w_out)


def late_kernel(*refs, pieces, grads):
    dq_refs, dk_refs, sums_refs = [refs[pieces * i : pieces * (i + 1)] for i in range(3)]
    wq_ref, wk_ref, table_ref, gain_ref, sums1_ref, sums2_ref = refs[3 * pieces : 3 * pieces + 6]
    out_hbm, tail_ref, sem = refs[3 * pieces + 7 :]
    rows, width = table_ref.shape
    gain = wide(gain_ref[...])[None, :]
    dy = 0.0
    for parts, w_ref in ((dq_refs, wq_ref), (dk_refs, wk_ref)):
        place = 0
        for part in parts:
            dy = dy + dot_nt(part[...], w_ref[:, place : place + part.shape[1]])
            place += part.shape[1]
    normed, root = ln_parts(wide(table_ref[...]))
    table = ln_back_rows(dy, normed, root, gain).astype(bf16)
    vectors = jnp.concatenate(
        [
            sums1_ref[...],
            sums2_ref[...],
            jnp.concatenate([r[...] for r in sums_refs], axis=1),
            jnp.sum(dy * normed, axis=0, keepdims=True),
            jnp.sum(dy, axis=0, keepdims=True),
            jnp.zeros((6, width), f32),
        ],
        axis=0,
    ).astype(bf16)
    base = 0
    for block in (table, vectors):
        for i in range(width // TILE):
            tail_ref[base : base + block.shape[0], :] = block[:, TILE * i : TILE * (i + 1)]
            base += block.shape[0]
    tail_ref[base:, :] = jnp.zeros((tail_ref.shape[0] - base, TILE), bf16)
    copy = pltpu.make_async_copy(tail_ref, out_hbm.at[grads:], sem.at[0])
    copy.start()
    copy.wait()


def late_rows(rows, width):
    grads = 6 * width
    total = grads + (rows + 32) * (width // TILE)
    return grads, -(-total // 512) * 512


def late_sums(d_query, d_key, sums, w_query, w_key, table, gain, sums1, sums2, into):
    rows, width = table.shape
    pieces = len(d_query)
    grads, total = late_rows(rows, width)

    def fixed(shape):
        return pl.BlockSpec(shape, lambda i: (0, 0))

    def lower(x):
        return pl.BlockSpec((rows, x.shape[1]), lambda i: (1, 0))

    square = fixed((width, width))
    anywhere = pl.BlockSpec(memory_space=pl.ANY)
    return pl.pallas_call(
        functools.partial(late_kernel, pieces=pieces, grads=grads),
        grid=(1,),
        in_specs=[lower(x) for x in (*d_query, *d_key)]
        + [fixed(x.shape) for x in sums]
        + [square, square, fixed((rows, width)), pl.BlockSpec((width,), lambda i: (0,))]
        + [fixed((8, width))] * 2
        + [anywhere],
        out_specs=anywhere,
        out_shape=jax.ShapeDtypeStruct((total, TILE), bf16),
        input_output_aliases={3 * pieces + 6: 0},
        scratch_shapes=[pltpu.VMEM((total - grads, TILE), bf16), pltpu.SemaphoreType.DMA((1,))],
        compiler_params=pltpu.CompilerParams(vmem_limit_bytes=VMEM),
        cost_estimate=pl.CostEstimate(
            flops=1_300_000_000, bytes_accessed=12_000_000, transcendentals=0
        ),
        name="late_sums",
    )(*d_query, *d_key, *sums, w_query, w_key, table, gain, sums1, sums2, into)


def input_grad_kernel(*refs, pieces):
    parts = [refs[pieces * i : pieces * (i + 1)] for i in range(3)]
    weights = refs[3 * pieces : 3 * pieces + 3]
    res_ref, out_ref = refs[3 * pieces + 3 :]
    for r in range(0, res_ref.shape[0], 256):
        rows = slice(r, r + 256)
        total = res_ref[rows, :]
        for part, w_ref in zip(parts, weights, strict=True):
            place = 0
            for x in part:
                total = total + dot_nt(x[rows, :], w_ref[:, place : place + x.shape[1]])
                place += x.shape[1]
        out_ref[rows, :] = total


def input_gradient(d_query, d_key, d_value, w_query, w_key, w_value, d_residual):
    rows, width = d_residual.shape
    pieces = len(d_query)
    specs = [
        pl.BlockSpec((rows, x.shape[1]), lambda i: (0, 0)) for x in (*d_query, *d_key, *d_value)
    ]
    square = pl.BlockSpec((width, width), lambda i: (0, 0))
    full = pl.BlockSpec((rows, width), lambda i: (0, 0))
    return pl.pallas_call(
        functools.partial(input_grad_kernel, pieces=pieces),
        grid=(1,),
        in_specs=[*specs, square, square, square, full],
        out_specs=full,
        out_shape=jax.ShapeDtypeStruct((rows, width), f32),
        compiler_params=pltpu.CompilerParams(vmem_limit_bytes=VMEM),
        cost_estimate=pl.CostEstimate(
            flops=6 * rows * width * width, bytes_accessed=10_000_000, transcendentals=0
        ),
        name="input_gradient",
    )(*d_query, *d_key, *d_value, w_query, w_key, w_value, d_residual)


def ffn_result_kernel(core_ref, mine_hbm, other_hbm, *refs, chunks, columns):
    out_ref, refs = refs[0], refs[1:]
    bias_ref, (part_ref, sems) = (refs[0], refs[1:]) if columns else (None, refs)
    offset = 0 if columns else 2 * CHUNK

    def write(halves):
        copies = []
        for i, half in enumerate(halves):
            for c in range(chunks):
                place = 4 * CHUNK * c + offset
                copies.append((half.at[place : place + 2 * CHUNK], part_ref.at[i * chunks + c]))
            if columns:
                place = 4 * CHUNK * chunks
                copies.append((half.at[place : place + 16], part_ref.at[2 * chunks + i, :16]))
        copies = [pltpu.make_async_copy(a, b, sems.at[i]) for i, (a, b) in enumerate(copies)]
        start(copies)
        for i in range(2):
            for c in range(chunks):
                wait(copies[:1])
                copies = copies[1:]
                k = i * chunks + c
                cols = slice(CHUNK * k, CHUNK * (k + 1))
                if columns:
                    out_ref[:, cols] = wide(part_ref[k])
                else:
                    out_ref[cols, :CHUNK] = wide(part_ref[k, :CHUNK, :])
                    out_ref[cols, CHUNK:] = wide(part_ref[k, CHUNK:, :])
            if columns:
                wait(copies[:1])
                copies = copies[1:]
        if columns:
            rows = []
            for i in range(2):
                tail = wide(part_ref[2 * chunks + i, :16, :])
                rows = rows + [tail[c : c + 1, :] for c in range(chunks)]
            bias_ref[...] = jnp.concatenate(rows, axis=1).reshape(bias_ref.shape)

    @pl.when(core_ref[0] == 0)
    def _():
        write((mine_hbm, other_hbm))

    @pl.when(core_ref[0] != 0)
    def _():
        write((other_hbm, mine_hbm))


def ffn_result(core, mine, other, width, units, columns):
    chunks = units // CHUNK
    if chunks % 2:
        first = jnp.where(core == 0, mine, other)
        second = jnp.where(core == 0, other, mine)
        total = wide(jnp.concatenate([first, second], axis=0))
        parts = [total[4 * CHUNK * c : 4 * CHUNK * (c + 1)] for c in range(chunks)]
        if columns:
            return (
                jnp.concatenate([p[: 2 * CHUNK] for p in parts], axis=1),
                total[4 * CHUNK * chunks : 4 * CHUNK * chunks + chunks].reshape(units),
            )
        sides = [
            jnp.concatenate([p[(2 + i) * CHUNK : (3 + i) * CHUNK] for p in parts], axis=0)
            for i in range(2)
        ]
        return (jnp.concatenate(sides, axis=1),)
    anywhere = pl.BlockSpec(memory_space=pl.ANY)
    outs = [full(width, units), full(units)] if columns else [full(units, width)]
    return pl.pallas_call(
        functools.partial(ffn_result_kernel, chunks=chunks // 2, columns=columns),
        in_specs=[pl.BlockSpec(memory_space=pltpu.SMEM), anywhere, anywhere],
        out_shape=outs,
        scratch_shapes=[
            pltpu.VMEM((chunks + 2, 2 * CHUNK, CHUNK), bf16),
            pltpu.SemaphoreType.DMA((chunks + 2,)),
        ],
        compiler_params=pltpu.CompilerParams(vmem_limit_bytes=VMEM),
        cost_estimate=pl.CostEstimate(flops=0, bytes_accessed=8_000_000, transcendentals=0),
        name="ffn_result",
    )(core, mine, other)


def early_result_kernel(core_ref, mine_ref, other_ref, w_mine, w_other, q_ref, k_ref, v_ref, wo_ref):
    width = q_ref.shape[0]
    blocks = mine_ref.shape[0] // width

    def write(first, second, w_first, w_second):
        for b in range(2 * blocks):
            part = first if b < blocks else second
            value = wide(part[width * (b % blocks) : width * (b % blocks + 1), :])
            group, which = divmod(b, 3)
            (q_ref, k_ref, v_ref)[which][:, TILE * group : TILE * (group + 1)] = value
        for i, part in enumerate((w_first, w_second)):
            wo_ref[:, CHUNK * i : CHUNK * (i + 1)] = wide(part[...])

    @pl.when(core_ref[0] == 0)
    def _():
        write(mine_ref, other_ref, w_mine, w_other)

    @pl.when(core_ref[0] != 0)
    def _():
        write(other_ref, mine_ref, w_other, w_mine)


def early_result(core, mine, other, w_mine, w_other, width):
    smem = pl.BlockSpec(memory_space=pltpu.SMEM)
    vmem = pl.BlockSpec(memory_space=pltpu.VMEM)
    return pl.pallas_call(
        early_result_kernel,
        in_specs=[smem] + [vmem] * 4,
        out_shape=[full(width, width)] * 4,
        compiler_params=pltpu.CompilerParams(vmem_limit_bytes=VMEM),
        cost_estimate=pl.CostEstimate(flops=0, bytes_accessed=10_000_000, transcendentals=0),
        name="early_result",
    )(core, mine, other, w_mine, w_other)


def late_result_kernel(core_ref, mine_ref, other_ref, *refs):
    q_ref, k_ref, v_ref, table_ref = refs[3:7]
    vector_refs, all_ref = refs[7:-1], refs[-1]
    width, rows = q_ref.shape[0], table_ref.shape[0]
    groups = table_ref.shape[1] // TILE
    half = mine_ref.shape[0]

    def write(first, second):
        all_ref[:half, :] = first[...]
        all_ref[half:, :] = second[...]

    @pl.when(core_ref[0] == 0)
    def _():
        write(mine_ref, other_ref)

    @pl.when(core_ref[0] != 0)
    def _():
        write(other_ref, mine_ref)

    base = 0
    for g in range(2):
        for ref in (q_ref, k_ref, v_ref):
            ref[:, TILE * g : TILE * (g + 1)] = wide(all_ref[base : base + width, :])
            base += width
    for i in range(groups):
        table_ref[:, TILE * i : TILE * (i + 1)] = wide(all_ref[base : base + rows, :])
        base += rows
    parts = [wide(all_ref[base + 32 * i : base + 32 * (i + 1), :]) for i in range(groups)]
    vectors = jnp.concatenate(parts, axis=1)
    for place, ref in zip(VECTOR_ROWS, vector_refs, strict=True):
        ref[...] = vectors[place : place + 1, :].reshape(ref.shape)


def late_result(core, mine, other, grads, rows):
    width = grads[0].shape[0]
    groups = width // 256
    smem = pl.BlockSpec(memory_space=pltpu.SMEM)
    half = pl.BlockSpec(mine.shape, lambda i: (0, 0))
    anywhere = pl.BlockSpec(memory_space=pl.ANY)
    last = pl.BlockSpec((width, 256), lambda i: (0, groups - 1))
    vector = pl.BlockSpec((width,), lambda i: (0,))
    return pl.pallas_call(
        late_result_kernel,
        grid=(1,),
        in_specs=[smem, half, half] + [anywhere] * 3,
        out_specs=[last] * 3
        + [pl.BlockSpec((rows, width), lambda i: (0, 0))]
        + [vector] * len(VECTOR_ROWS),
        out_shape=[jax.ShapeDtypeStruct((width, width), f32)] * 3
        + [jax.ShapeDtypeStruct((rows, width), f32)]
        + [jax.ShapeDtypeStruct((width,), f32)] * len(VECTOR_ROWS),
        input_output_aliases={3: 0, 4: 1, 5: 2},
        scratch_shapes=[pltpu.VMEM((2 * mine.shape[0], TILE), bf16)],
        compiler_params=pltpu.CompilerParams(vmem_limit_bytes=VMEM),
        cost_estimate=pl.CostEstimate(flops=0, bytes_accessed=6_000_000, transcendentals=0),
        name="late_result",
    )(core, mine, other, *grads)


class Moves:
    def __init__(self, n_dp, n_mp):
        self.n_dp, self.n_mp = n_dp, n_mp
        self.dp = lax.axis_index("dp")
        self.mp = lax.axis_index("mp")
        self.core = self.dp % 2
        self.dp_bits = [("dp", 1 << b) for b in range(1, n_dp.bit_length() - 1)]
        self.mp_bits = [("mp", 1 << b) for b in range(n_mp.bit_length() - 1)]

    def swap(self, x, pair):
        perm = []
        for d in range(self.n_dp):
            for m in range(self.n_mp):
                axis, bit = pair[d % 2]
                dest = (d ^ bit, m) if axis == "dp" else (d, m ^ bit)
                perm.append((d * self.n_mp + m, dest[0] * self.n_mp + dest[1]))
        return lax.ppermute(x, BOTH, perm)

    def side(self, pair):
        values = [((self.dp if axis == "dp" else self.mp) // bit) % 2 for axis, bit in pair]
        return jnp.where(self.core == 0, values[0], values[1])

    def halves(self, x, pair):
        half = x[0].shape[0] // 2
        side = self.side(pair)

        def part(start):
            return whole([lax.dynamic_slice_in_dim(y, start * half, half, 0) for y in x])

        return part(1 - side), part(side)

    def scatter(self, x, pair):
        sent, kept = self.halves(x, pair)
        return kept, self.swap(sent, pair)

    def exchange(self, x, pair):
        x = whole(x)
        return x, self.swap(x, pair)

    def gather(self, x, pair):
        x = whole(x)
        other = self.swap(x, pair)
        side = self.side(pair)
        first = jnp.where(side == 0, x, other)
        second = jnp.where(side == 0, other, x)
        return (jnp.concatenate([first, second], axis=0),)

    def steps(self, first, second, joined):
        pairs = list(zip(first, second, strict=True))
        if joined:
            middle = [functools.partial(self.exchange, pair=pairs.pop())]
        else:
            middle = []
        down = [functools.partial(self.scatter, pair=pair) for pair in pairs]
        up = [functools.partial(self.gather, pair=pair) for pair in reversed(pairs)]
        return down + middle + up


def whole(x):
    return x[0] if len(x) == 1 else sum(wide(y) for y in x).astype(bf16)


def tie(*values):
    return lax.optimization_barrier(values)


def per_device(
    inputs,
    cotangent,
    w_query,
    b_query,
    w_key,
    b_key,
    w_value,
    b_value,
    w_output,
    b_output,
    norm1_gain,
    norm1_shift,
    w_inner,
    b_inner,
    w_outer,
    b_outer,
    norm2_gain,
    norm2_shift,
    rel_table,
    rel_gain,
    rel_shift,
    block_group,
    seq_lengths,
    *,
    n_dp,
    n_mp,
):
    rows, width = inputs.shape
    units = w_inner.shape[1]
    moves = Moves(n_dp, n_mp)
    core = ("dp", 1)

    def other_shares(x):
        shares = [x[None]]
        for bit in moves.mp_bits:
            shares = [jnp.concatenate(shares, axis=0)]
            shares.append(moves.swap(shares[0], (bit, bit)))
        return jnp.concatenate(shares, axis=0)[1:]

    core_id = moves.core.reshape(1).astype(jnp.int32)
    row_bit = moves.dp_bits[0]
    row_id = moves.side((row_bit, row_bit)).reshape(1).astype(jnp.int32)
    half_in, quarter_out = core_half(core_id, row_id, w_inner, w_outer, b_inner)
    got_out = other_shares(quarter_out)
    got_in = other_shares(half_in)

    line = bucket_line(rows // 2)
    place_ids = np.arange(rows)[None, :]
    forward = jnp.asarray(np.append(line, -1)[:, None] == place_ids).astype(bf16)
    backward = jnp.asarray(np.append(line[::-1], -1)[:, None] == place_ids).astype(bf16)
    query, key, value, key_line, key_line_back, query_line, both_t = pre(
        inputs,
        rel_table,
        rel_gain,
        rel_shift,
        w_query,
        b_query,
        w_key,
        b_key,
        w_value,
        b_value,
        forward,
        backward,
    )
    got_out, query = tie(got_out, query)
    got_row = moves.swap(got_out, (row_bit, row_bit))
    other_out = moves.swap(got_out, (core, core))
    mixed, exps, inverse, mixed_full, normed1, root1, hidden_low = attend(
        block_group,
        seq_lengths,
        query,
        key,
        value,
        key_line,
        query_line,
        w_output,
        b_output,
        inputs,
        norm1_gain,
        norm1_shift,
    )

    def far(x):
        whole = x
        for bit in moves.mp_bits:
            whole = jnp.concatenate([whole, moves.swap(whole, (bit, bit))], axis=0)
        return whole[rows:]

    got_in, got_row, other_out, hidden_low = tie(got_in, got_row, other_out, hidden_low)
    got = (got_in, got_out, got_row)
    other = (moves.swap(got_in, (core, core)), other_out, moves.swap(got_row, (core, core)))
    far_hidden = far(hidden_low)
    layer_out, d_pre2, d_branch, active, slope, far_slope, sums2 = ffn_forward(
        hidden_low,
        normed1,
        cotangent,
        (norm1_gain, norm1_shift, b_outer, norm2_gain, norm2_shift),
        b_inner,
        row_id,
        w_inner,
        w_outer,
        got,
        other,
    )
    far_branch = far(d_branch)
    d_inner, d_residual, d_mixed, grad_w_output, sums1 = ffn_backward(
        d_branch,
        normed1,
        root1,
        d_pre2,
        mixed,
        w_output,
        norm1_gain,
        slope,
        far_slope,
        row_id,
        w_inner,
        w_outer,
        got,
        other,
    )

    dp_bits, mp_bits = moves.dp_bits, moves.mp_bits
    pair = (core, core)
    ffn_steps = moves.steps(dp_bits, dp_bits[1:2] + dp_bits[:1] + dp_bits[2:], False)
    first, second = mp_bits + dp_bits, dp_bits[:1] + mp_bits + dp_bits[1:]
    early_steps = moves.steps(first, second, True)
    late_steps = moves.steps(first, second, True)
    shared = (exps, inverse, mixed_full, key_line_back, query_line, backward, both_t)
    pieces = []
    pairs = width // TILE

    def attention(d_mixed, first, count, *into):
        *piece, grad = attend_back(query, key, value, d_mixed, *shared, first, count, *into)
        pieces.append(piece)
        return grad

    output_sum = moves.scatter((grad_w_output,), pair)
    chunks = units // CHUNK
    near = (hidden_low, d_branch, active, d_inner, far_hidden, far_branch, w_inner, b_inner, w_outer)
    if chunks % 2 == 0:
        mine, theirs = core_id * (chunks // 2), (1 - core_id) * (chunks // 2)
        sent = ffn_grads(*near, theirs, chunks // 2, 4 * n_dp)
        sent, mine, output_sum = tie(sent, mine, output_sum)
        for bit in mp_bits:
            output_sum = moves.scatter(output_sum, (bit, bit))
        kept = ffn_grads(*near, mine, chunks // 2, 4 * n_dp)
        ffn_sum = (kept, moves.swap(sent, pair))
    else:
        ffn_sum = (ffn_grads(*near, 0 * core_id, chunks, 8 * n_dp),)
        ffn_sum = moves.scatter(ffn_sum, pair)
        for bit in mp_bits:
            output_sum = moves.scatter(output_sum, (bit, bit))
    ffn_rows = ffn_sum[0].shape[0]
    ffn_sum = (jnp.concatenate([whole(ffn_sum), whole(output_sum)], axis=0),)
    ffn_sum, d_mixed = tie(ffn_sum, d_mixed)

    ffn_sum = ffn_steps.pop(0)(ffn_sum)
    early_size = 3 * width * (pairs - 2)
    early = attention(d_mixed, 0, 2, None, early_size, 0)
    ffn_sum, d_mixed, early = tie(ffn_sum, d_mixed, early)
    ffn_sum = ffn_steps.pop(0)(ffn_sum)
    early = attention(d_mixed, 2, 1, early, early_size, 2)
    ffn_sum, d_mixed, early = tie(ffn_sum, d_mixed, early)
    ffn_sum = ffn_steps.pop(0)(ffn_sum)
    early = attention(d_mixed, 3, pairs - 5, early, early_size, 3)
    ffn_sum, d_mixed, early = tie(ffn_sum, d_mixed, early)
    ffn_sum = ffn_steps.pop(0)(ffn_sum)
    early = moves.scatter((early,), pair)
    late_size = late_rows(rows, width)[1]
    late = attention(d_mixed, pairs - 2, 1, None, late_size, 0)
    early, ffn_sum, late, d_mixed = tie(early, ffn_sum, late, d_mixed)
    ffn_sum = ffn_steps.pop(0)(ffn_sum)
    early = early_steps.pop(0)(early)
    late = attention(d_mixed, pairs - 1, 1, late, late_size, 1)
    early, ffn_sum, late, d_residual = tie(early, ffn_sum, late, d_residual)
    ffn_sum = ffn_steps.pop(0)(ffn_sum)
    early = early_steps.pop(0)(early)
    d_query, d_key, d_value, sums = zip(*pieces, strict=True)
    late = late_sums(
        d_query, d_key, sums, w_query, w_key, rel_table, rel_gain, sums1, sums2, late
    )
    late, d_residual = tie(late, d_residual)
    late = moves.scatter((late,), pair)
    input_grad = input_gradient(d_query, d_key, d_value, w_query, w_key, w_value, d_residual)
    late, early, ffn_sum, input_grad = tie(late, early, ffn_sum, input_grad)

    def last(x):
        return moves.exchange(x, pair)

    early_steps.append(last)
    late_steps.append(last)
    output_steps = [functools.partial(moves.gather, pair=(b, b)) for b in reversed(mp_bits)] + [last]
    for step in ffn_steps:
        ffn_sum = step(ffn_sum)
    ffn_sum = last(ffn_sum)
    output_sum = (ffn_sum[0][ffn_rows:],)
    early_out, ffn_in, ffn_out = None, None, None
    while late_steps:
        late = late_steps.pop(0)(late)
        done = ()
        if early_steps:
            early = early_steps.pop(0)(early)
        elif early_out is None and not output_steps:
            done = early_out = early_result(core_id, *early, *output_sum, width)
        if len(late_steps) % 2 == 1 and ffn_in is None:
            done = ffn_in = ffn_result(core_id, *ffn_sum, width, units, True)
        elif len(late_steps) % 2 == 1 and ffn_out is None:
            done = ffn_out = ffn_result(core_id, *ffn_sum, width, units, False)
        elif output_steps:
            output_sum = output_steps.pop(0)(output_sum)
        late, early, ffn_sum, output_sum, done = tie(late, early, ffn_sum, output_sum, done)
    for step in early_steps:
        early = step(early)
    for step in output_steps:
        output_sum = step(output_sum)
    if ffn_in is None:
        ffn_in = ffn_result(core_id, *ffn_sum, width, units, True)
    if ffn_out is None:
        ffn_out = ffn_result(core_id, *ffn_sum, width, units, False)
    if early_out is None:
        early_out = early_result(core_id, *early, *output_sum, width)
    *early_out, grad_w_output = early_out
    ffn_in, ffn_bias = ffn_in
    (ffn_out,) = ffn_out
    grad_q, grad_k, grad_v, table, *vectors = late_result(core_id, *late, early_out, rows)
    return (
        layer_out,
        input_grad,
        grad_q,
        vectors[0],
        grad_k,
        vectors[1],
        grad_v,
        vectors[2],
        grad_w_output,
        *vectors[3:6],
        ffn_in,
        ffn_bias,
        ffn_out,
        *vectors[6:9],
        table,
        *vectors[9:],
    )


def solution(mesh):
    n_dp, n_mp = mesh.shape["dp"], mesh.shape["mp"]

    def body(*args):
        return per_device(*args, n_dp=n_dp, n_mp=n_mp)

    split = P(("dp", "mp"), None)
    weights = [P()] * 10 + [P(None, "mp"), P("mp"), P("mp", None)] + [P()] * 6
    return jax.shard_map(
        body,
        mesh=mesh,
        in_specs=(split, split, *weights, P(("dp", "mp")), split),
        out_specs=(
            split,
            split,
            *([P()] * 10),
            P(None, "mp"),
            P("mp"),
            P("mp", None),
            *([P()] * 6),
        ),
        check_vma=False,
    )
```

```python
import functools
import math

import jax
import jax.numpy as jnp
import numpy as np
from jax import lax
from jax.experimental import pallas as pl
from jax.experimental.pallas import tpu as pltpu
from jax.sharding import PartitionSpec as P

HEADS = 12
EPS = 1e-06
LOG2E = 1.4426950408889634
TILE = 128
CHUNK = 384
VMEM = 60 * 1024 * 1024
VECTOR_ROWS = (16, 17, 18, 2, 0, 1, 10, 8, 9, 24, 25)
BOTH = ("dp", "mp")
f32 = jnp.float32
bf16 = jnp.bfloat16


def bucket_line(half_rows):
    table_rows = 2 * half_rows
    middle = half_rows // 2
    relative = table_rows - 1 - np.arange(2 * table_rows - 1)
    signed = np.sign(relative)
    absolute = np.where((relative < middle) & (relative > -middle), middle - 1, np.abs(relative))
    log_place = (
        np.ceil(np.log(absolute / middle) / np.log((table_rows - 1) / middle) * (middle - 1))
        + middle
    )
    placed = np.where(absolute <= middle, relative, log_place * signed)
    return (placed + half_rows).astype(np.int32)


def dot(a, b):
    return jnp.dot(a, b, preferred_element_type=f32)


def dot_nt(a, b):
    return lax.dot_general(a, b, (((1,), (1,)), ((), ())), preferred_element_type=f32)


def dot_tn(a, b):
    return lax.dot_general(a, b, (((0,), (0,)), ((), ())), preferred_element_type=f32)


def wide(v):
    return v.astype(f32)


def ln_parts(v):
    average = jnp.mean(v, axis=-1, keepdims=True)
    center = v - average
    root = lax.rsqrt(jnp.mean(center * center, axis=-1, keepdims=True) + EPS)
    return center * root, root


def ln_back_rows(dy, normed, root, gain):
    dn = dy * gain
    first = jnp.mean(dn, axis=-1, keepdims=True)
    second = jnp.mean(dn * normed, axis=-1, keepdims=True)
    return root * (dn - first - normed * second)


def gelu_parts(v):
    bell = jnp.exp(-0.5 * v * v)
    t = 1.0 / (1.0 + (0.3275911 * math.sqrt(0.5)) * jnp.abs(v))
    poly = t * (
        0.254829592
        + t * (-0.284496736 + t * (1.421413741 + t * (-1.453152027 + t * 1.061405429)))
    )
    tail = 0.5 * poly * bell
    below = jnp.where(v >= 0, 1.0 - tail, tail)
    return v * below, below + v * bell * (1.0 / math.sqrt(2.0 * math.pi))


def pre_kernel(
    x_ref,
    table_ref,
    gain_ref,
    shift_ref,
    wq_ref,
    bq_ref,
    wk_ref,
    bk_ref,
    wv_ref,
    bv_ref,
    forward_ref,
    backward_ref,
    q_ref,
    k_ref,
    v_ref,
    key_line_ref,
    key_back_ref,
    query_line_ref,
    both_t_ref,
    both_ref,
):
    rows = x_ref.shape[0]

    @pl.when(pl.program_id(0) == 0)
    def _():
        both_ref[:rows, :] = x_ref[...]
        normed, _ = ln_parts(wide(table_ref[...]))
        rel = normed * wide(gain_ref[...])[None, :] + wide(shift_ref[...])[None, :]
        both_ref[rows:, :] = rel.astype(bf16)
        both_t_ref[...] = both_ref[...].T

    def project(w_ref, b_ref, part):
        return (dot(both_ref[part, :], w_ref[...]) + wide(b_ref[...])[None, :]).astype(bf16)

    here, there = slice(0, rows), slice(rows, 2 * rows)
    q_ref[...] = project(wq_ref, bq_ref, here)
    k_ref[...] = project(wk_ref, bk_ref, here)
    v_ref[...] = project(wv_ref, bv_ref, here)
    pos_query = project(wq_ref, bq_ref, there)
    pos_key = project(wk_ref, bk_ref, there)
    key_line_ref[...] = dot(forward_ref[...], pos_key).astype(bf16)
    key_back_ref[...] = dot(backward_ref[...], pos_key).astype(bf16)
    query_line_ref[...] = dot(backward_ref[...], pos_query).astype(bf16)


def pre(x, table, gain, shift, w_q, b_q, w_k, b_k, w_v, b_v, forward, backward):
    rows, width = x.shape
    cut = 2 * TILE

    def fixed(r, w):
        return pl.BlockSpec((r, w), lambda c: (0, 0))

    whole = pl.BlockSpec((width,), lambda c: (0,))
    weight = pl.BlockSpec((width, cut), lambda c: (0, c))
    vector = pl.BlockSpec((cut,), lambda c: (c,))
    one = pl.BlockSpec((rows, cut), lambda c: (0, c))
    two = pl.BlockSpec((2 * rows, cut), lambda c: (0, c))
    return pl.pallas_call(
        pre_kernel,
        grid=(width // cut,),
        in_specs=[fixed(rows, width), fixed(rows, width), whole, whole]
        + [weight, vector] * 3
        + [fixed(2 * rows, rows)] * 2,
        out_specs=[one] * 3 + [two] * 3 + [fixed(width, 2 * rows)],
        out_shape=[jax.ShapeDtypeStruct((rows, width), bf16)] * 3
        + [jax.ShapeDtypeStruct((2 * rows, width), bf16)] * 3
        + [jax.ShapeDtypeStruct((width, 2 * rows), bf16)],
        scratch_shapes=[pltpu.VMEM((2 * rows, width), bf16)],
        compiler_params=pltpu.CompilerParams(vmem_limit_bytes=VMEM),
        cost_estimate=pl.CostEstimate(
            flops=5_500_000_000, bytes_accessed=14_000_000, transcendentals=0
        ),
        name="pre",
    )(x, table, gain, shift, w_q, b_q, w_k, b_k, w_v, b_v, forward, backward)


def skewed(x, keep):
    parts = [x[:, TILE * b : TILE * (b + 1)] for b in range(5)]
    return [
        pltpu.roll(jnp.where(keep, parts[b], parts[b + 1]), 1, 1, stride=1, stride_axis=0)
        for b in range(4)
    ]


def unskewed(tiles, keep):
    zero = jnp.zeros((TILE, TILE), f32)
    turned = [zero] + [pltpu.roll(t, 0, 1, stride=1, stride_axis=0) for t in tiles] + [zero]
    return [jnp.where(keep, turned[b + 1], turned[b]) for b in range(5)]


def flipped():
    rows = lax.broadcasted_iota(jnp.int32, (256, 256), 0)
    cols = lax.broadcasted_iota(jnp.int32, (256, 256), 1)
    return (rows + cols == 255).astype(f32).astype(bf16)


def attend_kernel(
    group_ref,
    lengths_ref,
    q_ref,
    k_ref,
    v_ref,
    key_line_ref,
    query_line_ref,
    wo_ref,
    bo_ref,
    x_ref,
    gain_ref,
    shift_ref,
    out_ref,
    exp_ref,
    inv_ref,
    full_ref,
    normed_ref,
    root_ref,
    h_ref,
    side_ref,
    bias_ref,
    key_side,
    query_side,
    content_ref,
):
    @pl.when(pl.program_id(0) == 0)
    def _():
        normed_ref[...] = wide(x_ref[...]) + wide(bo_ref[...])[None, :]
        size = bias_ref.shape[0]
        shift = size.bit_length() - 1 - group_ref[0]
        row = lax.broadcasted_iota(jnp.int32, (size, 1), 0)
        col = lax.broadcasted_iota(jnp.int32, (1, size), 1)
        owner = jnp.right_shift(col, shift)
        limit = jnp.zeros((1, size), jnp.int32)
        for slot in range(4):
            limit = jnp.where(owner == slot, lengths_ref[0, slot], limit)
        owner = jnp.where(col - jnp.left_shift(owner, shift) < limit, owner, -1)
        valid = jnp.right_shift(row, shift) == owner
        bias_ref[...] = jnp.where(valid, 0.0, -1e30).astype(f32)

    lane = lax.broadcasted_iota(jnp.int32, (1, TILE), 1)
    keep = (
        lax.broadcasted_iota(jnp.int32, (TILE, TILE), 0)
        + lax.broadcasted_iota(jnp.int32, (TILE, TILE), 1)
        >= TILE - 1
    )
    mine = [lane < 64, lane >= 64]
    scale = LOG2E / math.sqrt(192)
    flip = flipped()
    v_ones = jnp.concatenate([v_ref[...], jnp.ones(v_ref.shape, bf16)], axis=1)
    for h in range(2):
        km = jnp.where(mine[h], k_ref[...], 0)
        qm = jnp.where(mine[h], q_ref[...], 0)
        key_side[h] = dot_nt(km, query_line_ref[...])
        query_side[h] = dot_nt(qm, key_line_ref[...])
        content_ref[h] = dot_nt(qm, k_ref[...])
    for h in range(2):
        for t in range(4):
            start = 384 - TILE * t
            sk = skewed(key_side[h, TILE * t : TILE * (t + 1), start : start + 640], keep)
            for b in range(4):
                turned = wide(sk[b].astype(bf16).T)
                side_ref[h, TILE * b : TILE * (b + 1), TILE * t : TILE * (t + 1)] = turned
        for t in range(4):
            rows = slice(TILE * t, TILE * (t + 1))
            start = 384 - TILE * t
            near = skewed(query_side[h, rows, start : start + 640], keep)
            content = content_ref[h, rows, :]
            parts = []
            for b in range(4):
                cols = slice(TILE * b, TILE * (b + 1))
                total = content[:, cols] + near[b] + side_ref[h, rows, cols]
                parts.append(total * scale + bias_ref[rows, cols])
            top = jnp.max(
                jnp.maximum(jnp.maximum(parts[0], parts[1]), jnp.maximum(parts[2], parts[3])),
                axis=1,
                keepdims=True,
            )
            low = [jnp.exp2(p - top).astype(bf16) for p in parts]
            exps = jnp.concatenate(low, axis=1)
            exp_ref[h, rows, :] = jnp.concatenate(
                [dot(exps[:, 256:], flip).astype(bf16), dot(exps[:, :256], flip).astype(bf16)], axis=1
            )
            product = dot(exps, v_ones)
            inverse = 1.0 / product[:, TILE:]
            out = product[:, :TILE] * inverse
            if h == 0:
                inv_ref[0, rows, :] = inverse
                full_ref[0, rows, :] = out
            else:
                inv_ref[0, rows, :] = jnp.where(mine[0], inv_ref[0, rows, :], inverse)
                out = jnp.where(mine[0], full_ref[0, rows, :], out)
                full_ref[0, rows, :] = out
                out_ref[rows, :] = out.astype(bf16)
    normed_ref[...] += dot(out_ref[...], wo_ref[...])

    @pl.when(pl.program_id(0) == pl.num_programs(0) - 1)
    def _():
        gain, shift = wide(gain_ref[...])[None, :], wide(shift_ref[...])[None, :]
        for r in range(0, h_ref.shape[0], TILE):
            rows = slice(r, r + TILE)
            normed, root = ln_parts(normed_ref[rows, :])
            normed_ref[rows, :] = normed
            root_ref[rows, :] = jnp.broadcast_to(root, (TILE, TILE))
            h_ref[rows, :] = (normed * gain + shift).astype(bf16)


def attend(group, lengths, q, k, v, key_line, query_line, w_output, b_output, x, gain, shift):
    rows, width = q.shape
    pairs = width // TILE
    col = pl.BlockSpec((rows, TILE), lambda g: (0, g))
    line = pl.BlockSpec((2 * rows, TILE), lambda g: (0, g))
    scalars = pl.BlockSpec(memory_space=pltpu.SMEM)
    full = pl.BlockSpec((rows, width), lambda g: (0, 0))
    vector = pl.BlockSpec((width,), lambda g: (0,))
    return pl.pallas_call(
        attend_kernel,
        grid=(pairs,),
        in_specs=[scalars, scalars, col, col, col, line, line]
        + [pl.BlockSpec((TILE, width), lambda g: (g, 0)), vector, full, vector, vector],
        out_specs=[
            col,
            pl.BlockSpec((2, rows, rows), lambda g: (g, 0, 0)),
            pl.BlockSpec((1, rows, TILE), lambda g: (g, 0, 0)),
            pl.BlockSpec((1, rows, TILE), lambda g: (g, 0, 0)),
            full,
            pl.BlockSpec((rows, TILE), lambda g: (0, 0)),
            full,
        ],
        out_shape=[
            jax.ShapeDtypeStruct((rows, width), bf16),
            jax.ShapeDtypeStruct((2 * pairs, rows, rows), bf16),
            jax.ShapeDtypeStruct((pairs, rows, TILE), f32),
            jax.ShapeDtypeStruct((pairs, rows, TILE), f32),
            jax.ShapeDtypeStruct((rows, width), f32),
            jax.ShapeDtypeStruct((rows, TILE), f32),
            jax.ShapeDtypeStruct((rows, width), bf16),
        ],
        scratch_shapes=[
            pltpu.VMEM((2, rows, rows), f32),
            pltpu.VMEM((rows, rows), f32),
            pltpu.VMEM((2, rows, 2 * rows), f32),
            pltpu.VMEM((2, rows, 2 * rows), f32),
            pltpu.VMEM((2, rows, rows), f32),
        ],
        compiler_params=pltpu.CompilerParams(vmem_limit_bytes=VMEM),
        cost_estimate=pl.CostEstimate(
            flops=18_000_000_000, bytes_accessed=16_000_000, transcendentals=3_200_000
        ),
        name="attend",
    )(group, lengths, q, k, v, key_line, query_line, w_output, b_output, x, gain, shift)


def attend_back_kernel(
    q_ref,
    k_ref,
    v_ref,
    do_ref,
    exp_ref,
    inv_ref,
    full_ref,
    key_line_ref,
    query_line_ref,
    places_ref,
    both_t_ref,
    *refs,
):
    dq_ref, dk_ref, dv_ref, sums_ref, grad_ref, *refs = refs[-9:]
    attend_back_pair(
        q_ref,
        k_ref,
        v_ref,
        do_ref,
        exp_ref,
        inv_ref,
        full_ref,
        key_line_ref,
        query_line_ref,
        places_ref,
        both_t_ref,
        dq_ref,
        dk_ref,
        dv_ref,
        sums_ref,
        grad_ref,
        *refs,
    )


def attend_back_pair(
    q_ref,
    k_ref,
    v_ref,
    do_ref,
    exp_ref,
    inv_ref,
    full_ref,
    key_line_ref,
    query_line_ref,
    places_ref,
    both_t_ref,
    dq_ref,
    dk_ref,
    dv_ref,
    sums_ref,
    grad_ref,
    ds_ref,
    dst_ref,
    query_band,
    key_band,
):
    @pl.when(pl.program_id(0) == 0)
    def _():
        query_band[...] = jnp.zeros_like(query_band)
        key_band[...] = jnp.zeros_like(key_band)

    scale = 1.0 / math.sqrt(192)
    lane = lax.broadcasted_iota(jnp.int32, (1, TILE), 1)
    sub = lax.broadcasted_iota(jnp.int32, (TILE, 1), 0)
    keep = lax.broadcasted_iota(jnp.int32, (TILE, TILE), 1) >= lax.broadcasted_iota(
        jnp.int32, (TILE, TILE), 0
    )
    mine = [lane < 64, lane >= 64]
    mine_t = [sub < 64, sub >= 64]
    flip = flipped()

    def reverse(x):
        return jnp.concatenate([dot(flip, x[256:]), dot(flip, x[:256])], axis=0).astype(bf16)

    q = q_ref[...]
    k = reverse(k_ref[...])
    v = reverse(v_ref[...])
    q_t = q.T
    k_t = k.T
    do = (wide(do_ref[...]) * inv_ref[0]).astype(bf16)
    do_t = do.T
    share = wide(do) * full_ref[0]
    high = share.astype(bf16)
    rest = (share - wide(high)).astype(bf16)
    row = lax.broadcasted_iota(jnp.int32, (256, 256), 0) % TILE // 64
    ones = (row == lax.broadcasted_iota(jnp.int32, (256, 256), 1) // TILE).astype(f32).astype(bf16)
    means = dot(jnp.concatenate([high, rest], axis=1), ones)
    dv_t = None
    dqs, dks, key_lines, query_lines = [], [], [], []
    for h in range(2):
        dom = jnp.where(mine[h], do, 0)
        for t in range(4):
            rows = slice(TILE * t, TILE * (t + 1))
            dp = dot_nt(dom[rows], v)
            mean = means[rows, TILE * h : TILE * (h + 1)]
            ds = []
            for b in range(4):
                cols = slice(TILE * b, TILE * (b + 1))
                ds.append(wide(exp_ref[h, rows, cols]) * (dp[:, cols] - mean))
                ds_ref[h, rows, cols] = ds[b].astype(bf16)
            out = unskewed(ds, keep)
            for b in range(5):
                query_band[h, rows, TILE * (t + b) : TILE * (t + b + 1)] = out[b].astype(bf16)
        for t in range(4):
            rows = slice(TILE * t, TILE * (t + 1))
            turned = [ds_ref[h, TILE * b : TILE * (b + 1), rows].T for b in range(4)]
            for b in range(4):
                dst_ref[h, rows, TILE * b : TILE * (b + 1)] = turned[b]
            out = unskewed([wide(x) for x in turned], keep)
            for b in range(5):
                key_band[h, rows, TILE * (t + b) : TILE * (t + b + 1)] = out[b].astype(bf16)
        part = dot(jnp.where(mine_t[h], do_t, 0), exp_ref[h])
        dv_t = part if dv_t is None else dv_t + part
        dq, dk, key_line, query_line = [], [], [], []
        for i in range(2):
            rows = slice(256 * i, 256 * (i + 1))
            band = slice(256 * i, 256 * i + 768)
            dq.append(dot(ds_ref[h, rows, :], k) + dot(query_band[h, rows, band], key_line_ref[band, :]))
            dk.append(dot(dst_ref[h, rows, :], q) + dot(key_band[h, rows, band], query_line_ref[band, :]))
            key_line.append(dot(jnp.where(mine_t[h], q_t[:, rows], 0), query_band[h, rows, band]))
            query_line.append(dot(jnp.where(mine_t[h], k_t[:, rows], 0), key_band[h, rows, band]))
        dqs.append(jnp.concatenate(dq, axis=0))
        dks.append(jnp.concatenate(dk, axis=0))
        key_lines.append(key_line)
        query_lines.append(query_line)
    size = q.shape[0]
    dq_ref[:size, :] = (jnp.where(mine[0], dqs[0], dqs[1]) * scale).astype(bf16)
    dk_ref[:size, :] = reverse((jnp.where(mine[0], dks[0], dks[1]) * scale).astype(bf16))
    dv_ref[...] = reverse(dv_t.T.astype(bf16))
    for lines, ref in ((key_lines, dk_ref), (query_lines, dq_ref)):
        first = lines[0][0] + lines[1][0]
        second = lines[0][1] + lines[1][1]
        whole = jnp.concatenate(
            [first[:, :256], first[:, 256:] + second[:, :512], second[:, 512:]], axis=1
        )
        ref[size:, :] = dot((whole * scale).astype(bf16), places_ref[...]).T.astype(bf16)
    width = both_t_ref.shape[0]
    grad_ref[:width, :] = dot(both_t_ref[...], dq_ref[...]).astype(bf16)
    grad_ref[width : 2 * width, :] = dot(both_t_ref[...], dk_ref[...]).astype(bf16)
    grad_ref[2 * width :, :] = dot(both_t_ref[:, :size], dv_ref[...]).astype(bf16)
    sums = [jnp.sum(wide(r[...]), axis=0, keepdims=True) for r in (dq_ref, dk_ref, dv_ref)]
    sums_ref[...] = jnp.concatenate(sums + [jnp.zeros((5, TILE), f32)], axis=0)


def attend_back(
    q,
    k,
    v,
    do,
    exps,
    inverse,
    mixed_full,
    key_line,
    query_line,
    places,
    both_t,
    first,
    count,
    into,
    size,
    start,
):
    rows, width = q.shape
    col = pl.BlockSpec((rows, TILE), lambda g: (0, first + g))
    line = pl.BlockSpec((2 * rows, TILE), lambda g: (0, first + g))
    both = pl.BlockSpec((2 * rows, TILE), lambda g: (0, g))
    more = [] if into is None else [into]
    return pl.pallas_call(
        attend_back_kernel,
        grid=(count,),
        in_specs=[
            col,
            col,
            col,
            col,
            pl.BlockSpec((2, rows, rows), lambda g: (first + g, 0, 0)),
            pl.BlockSpec((1, rows, TILE), lambda g: (first + g, 0, 0)),
            pl.BlockSpec((1, rows, TILE), lambda g: (first + g, 0, 0)),
            line,
            line,
            pl.BlockSpec((2 * rows, rows), lambda g: (0, 0)),
            pl.BlockSpec((width, 2 * rows), lambda g: (0, 0)),
        ]
        + [pl.BlockSpec(memory_space=pl.ANY) for _ in more],
        out_specs=[
            both,
            both,
            pl.BlockSpec((rows, TILE), lambda g: (0, g)),
            pl.BlockSpec((8, TILE), lambda g: (0, g)),
            pl.BlockSpec((3 * width, TILE), lambda g: (start + g, 0)),
        ],
        out_shape=[
            jax.ShapeDtypeStruct((2 * rows, count * TILE), bf16),
            jax.ShapeDtypeStruct((2 * rows, count * TILE), bf16),
            jax.ShapeDtypeStruct((rows, count * TILE), bf16),
            jax.ShapeDtypeStruct((8, count * TILE), f32),
            jax.ShapeDtypeStruct((size, TILE), bf16),
        ],
        input_output_aliases={11: 4} if more else {},
        scratch_shapes=[
            pltpu.VMEM((2, rows, rows), bf16),
            pltpu.VMEM((2, rows, rows), bf16),
            pltpu.VMEM((2, rows, 2 * rows), bf16),
            pltpu.VMEM((2, rows, 2 * rows), bf16),
        ],
        compiler_params=pltpu.CompilerParams(vmem_limit_bytes=VMEM),
        cost_estimate=pl.CostEstimate(
            flops=count * 4_000_000_000, bytes_accessed=count * 3_000_000, transcendentals=0
        ),
        name="attend_back",
    )(q, k, v, do, exps, inverse, mixed_full, key_line, query_line, places, both_t, *more)


def weight_copies(y, sources, targets, sems, chunk, chunks):
    win_hbm, wout_hbm = sources[:2]
    win_ref, wout_ref, far_in, far_out = targets
    n = far_in.shape[0] // 2
    half = far_out.shape[1] // 2
    lists = []
    for c in range(chunks):
        cols = slice(chunk * c, chunk * (c + 1))
        lists.append([(win_hbm.at[:, cols], win_ref.at[:, cols]), (wout_hbm.at[cols], wout_ref.at[cols])])
    mine = pl.ds(pl.multiple_of(y * half, 16), half)
    theirs = pl.ds(pl.multiple_of((1 - y) * half, 16), half)
    for k in range(2):
        part = slice(n * k, n * (k + 1))
        columns, first, second = sources[2 + 3 * k : 5 + 3 * k]
        lists.append(
            [
                (columns, far_in.at[part]),
                (first, far_out.at[part, mine]),
                (second, far_out.at[part, theirs]),
            ]
        )
    copies = []
    for i, pairs in enumerate(lists):
        copies.append(
            [pltpu.make_async_copy(a, b, sems.at[i, k]) for k, (a, b) in enumerate(pairs)]
        )
    return copies


def start(copies):
    for copy in copies:
        copy.start()


def wait(copies):
    for copy in copies:
        copy.wait()


def core_half_kernel(place_ref, bin_ref, win_hbm, wout_hbm, in_ref, out_ref, sems):
    units = in_ref.shape[1]
    width = win_hbm.shape[0]
    rows = pl.multiple_of((2 * place_ref[0] + place_ref[1]) * out_ref.shape[0], 16)

    def send(core):
        part = slice(units * core, units * (core + 1))
        copies = [
            pltpu.make_async_copy(wout_hbm.at[pl.ds(rows, out_ref.shape[0])], out_ref, sems.at[0]),
            pltpu.make_async_copy(win_hbm.at[:, part], in_ref.at[:width], sems.at[1]),
        ]
        start(copies)
        bias = jnp.broadcast_to(wide(bin_ref[...])[None, part], (16, units))
        in_ref[width:, :] = bias.astype(bf16)
        wait(copies)

    @pl.when(place_ref[0] == 0)
    def _():
        send(0)

    @pl.when(place_ref[0] != 0)
    def _():
        send(1)


def core_half(core, y, w_in, w_out, b_in):
    width, units = w_in.shape
    half = units // 2
    if half % TILE:
        place = core[0] * half
        bias = lax.dynamic_slice_in_dim(b_in, place, half, 0)
        columns = lax.dynamic_slice_in_dim(w_in, place, half, 1)
        columns = jnp.concatenate([columns, jnp.broadcast_to(bias, (16, half))], axis=0)
        return columns, lax.dynamic_slice_in_dim(w_out, place + y[0] * (half // 2), half // 2, 0)
    anywhere = pl.BlockSpec(memory_space=pl.ANY)
    vmem = pl.BlockSpec(memory_space=pltpu.VMEM)
    return pl.pallas_call(
        core_half_kernel,
        in_specs=[pl.BlockSpec(memory_space=pltpu.SMEM), vmem, anywhere, anywhere],
        out_specs=[vmem, vmem],
        out_shape=[low(width + 16, half), low(half // 2, width)],
        scratch_shapes=[pltpu.SemaphoreType.DMA((2,))],
        compiler_params=pltpu.CompilerParams(vmem_limit_bytes=VMEM),
        cost_estimate=pl.CostEstimate(flops=0, bytes_accessed=5_000_000, transcendentals=0),
        name="core_half",
    )(jnp.concatenate([core, y]), b_in, w_in, w_out)


def ffn_forward_kernel(
    h_ref,
    normed_hbm,
    cot_hbm,
    gain1_ref,
    shift1_ref,
    b_outer_ref,
    gain2_ref,
    shift2_ref,
    bin_ref,
    *refs,
    chunk,
    far_chunk,
):
    y, sources, refs = refs[0][0], refs[1:9], refs[9:]
    out_ref, dpre_ref, dbranch_ref, active_hbm, slope_hbm, far_slope_hbm, sums_ref = refs[:7]
    normed_ref, cot_ref, active_ref, slope_ref, far_slope_ref, total_ref = refs[7:13]
    targets, sems, sems2 = refs[13:17], refs[17], refs[18]
    far_in_ref, far_out_ref = targets[2:]
    rows, width = h_ref.shape
    chunks = active_ref.shape[1] // chunk
    far_count, _, units = far_in_ref.shape
    far_chunks = units // far_chunk
    weights = weight_copies(y, sources, targets, sems, chunk, chunks)
    others = [
        pltpu.make_async_copy(normed_hbm, normed_ref, sems2.at[0]),
        pltpu.make_async_copy(cot_hbm, cot_ref, sems2.at[1]),
    ]
    back = [
        pltpu.make_async_copy(active_ref, active_hbm, sems2.at[2]),
        pltpu.make_async_copy(slope_ref, slope_hbm, sems2.at[3]),
        pltpu.make_async_copy(far_slope_ref, far_slope_hbm, sems2.at[4]),
    ]
    for copies in weights:
        start(copies)
    start(others)
    b_in = wide(bin_ref[...])[None, :]

    def forward(w_in, b_in, w_out, active_at, slope_at, first):
        for r in range(0, rows, 256):
            part = slice(r, r + 256)
            active, slope = gelu_parts(dot(h_ref[part, :], w_in) + b_in)
            active = active.astype(bf16)
            if active_at is not None:
                active_ref[part, active_at] = active
            slope_at(part, slope.astype(bf16))
            product = dot(active, w_out)
            total_ref[part, :] = product if first else total_ref[part, :] + product

    for c in range(chunks):
        wait(weights[c])
        cols = slice(chunk * c, chunk * (c + 1))

        def put(part, value, cols=cols):
            slope_ref[part, cols] = value

        forward(targets[0][:, cols], b_in[:, cols], targets[1][cols, :], cols, put, c == 0)
    start(back[:2])
    wait(weights[chunks])
    wait(weights[chunks + 1])

    def far_step(s, carry):
        for c in range(far_chunks):
            cols = slice(far_chunk * c, far_chunk * (c + 1))

            def put(part, value, cols=cols):
                far_slope_ref[s, part, cols] = value

            bias = wide(far_in_ref[s, width : width + 1, cols])
            forward(far_in_ref[s, :width, cols], bias, far_out_ref[s, cols, :], None, put, False)
        return carry

    lax.fori_loop(0, far_count, far_step, 0)
    start(back[2:])
    wait(others)
    gain1, shift1, b_outer, gain2, shift2 = [
        wide(r[...])[None, :] for r in (gain1_ref, shift1_ref, b_outer_ref, gain2_ref, shift2_ref)
    ]
    sums = [jnp.zeros((1, width), f32) for _ in range(3)]
    for r in range(0, rows, TILE):
        part = slice(r, r + TILE)
        normed, root = ln_parts(normed_ref[part, :] * gain1 + shift1 + total_ref[part, :] + b_outer)
        out_ref[part, :] = normed * gain2 + shift2
        dy = wide(cot_ref[part, :])
        d = ln_back_rows(dy, normed, root, gain2)
        dpre_ref[part, :] = d
        low = d.astype(bf16)
        dbranch_ref[part, :] = low
        sums[0] += jnp.sum(dy * normed, axis=0, keepdims=True)
        sums[1] += jnp.sum(dy, axis=0, keepdims=True)
        sums[2] += jnp.sum(wide(low), axis=0, keepdims=True)
    sums_ref[...] = jnp.concatenate(sums + [jnp.zeros((5, width), f32)], axis=0)
    wait(back)


def ffn_backward_kernel(
    db_ref, normed_hbm, root_ref, dpre_ref, mixed_hbm, wo_hbm, gain_ref, *refs, chunk, far_chunk
):
    slope_hbm, far_slope_hbm = refs[:2]
    y, sources, refs = refs[2][0], refs[3:11], refs[11:]
    dinner_hbm, dres_ref, dmixed_ref, grad_ref, sums_ref = refs[:5]
    normed_ref, mixed_ref, wo_ref, dinner_ref, total_ref, dattn_ref = refs[5:11]
    slope_ref, far_slope_ref = refs[11:13]
    targets, sems, sems2 = refs[13:17], refs[17], refs[18]
    far_in_ref, far_out_ref = targets[2:]
    rows, width = db_ref.shape
    chunks = dinner_ref.shape[1] // chunk
    far_count, _, units = far_in_ref.shape
    far_chunks = units // far_chunk
    weights = weight_copies(y, sources, targets, sems, chunk, chunks)
    slopes = [
        pltpu.make_async_copy(slope_hbm, slope_ref, sems2.at[0]),
        pltpu.make_async_copy(far_slope_hbm, far_slope_ref, sems2.at[1]),
    ]
    others = [
        pltpu.make_async_copy(normed_hbm, normed_ref, sems2.at[2]),
        pltpu.make_async_copy(mixed_hbm, mixed_ref, sems2.at[3]),
        pltpu.make_async_copy(wo_hbm, wo_ref, sems2.at[4]),
    ]
    back = [pltpu.make_async_copy(dinner_ref, dinner_hbm, sems2.at[5])]
    start(weights[0])
    start(slopes[:1])
    for copies in weights[1:]:
        start(copies)
    start(slopes[1:])
    start(others)

    def backward(w_in, w_out, slope, keep, first):
        for r in range(0, rows, 256):
            part = slice(r, r + 256)
            d = (dot_nt(db_ref[part, :], w_out) * wide(slope(part))).astype(bf16)
            if keep is not None:
                keep(part, d)
            base = dpre_ref[part, :] if first else total_ref[part, :]
            total_ref[part, :] = base + dot_nt(d, w_in)

    wait(slopes[:1])
    for c in range(chunks):
        wait(weights[c])
        cols = slice(chunk * c, chunk * (c + 1))

        def keep(part, value, cols=cols):
            dinner_ref[part, cols] = value

        def slope(part, cols=cols):
            return slope_ref[part, cols]

        backward(targets[0][:, cols], targets[1][cols, :], slope, keep, c == 0)
    start(back)
    wait(weights[chunks])
    wait(weights[chunks + 1])
    wait(slopes[1:])

    def far_step(s, carry):
        for c in range(far_chunks):
            cols = slice(far_chunk * c, far_chunk * (c + 1))

            def slope(part, cols=cols):
                return far_slope_ref[s, part, cols]

            backward(far_in_ref[s, :width, cols], far_out_ref[s, cols, :], slope, None, False)
        return carry

    lax.fori_loop(0, far_count, far_step, 0)
    wait(others)
    gain = wide(gain_ref[...])[None, :]
    sums = [jnp.zeros((1, width), f32) for _ in range(3)]
    for r in range(0, rows, TILE):
        part = slice(r, r + TILE)
        dy = total_ref[part, :]
        normed = normed_ref[part, :]
        d = ln_back_rows(dy, normed, root_ref[part, 0:1], gain)
        dres_ref[part, :] = d
        low = d.astype(bf16)
        dattn_ref[part, :] = low
        dmixed_ref[part, :] = dot_nt(low, wo_ref[...]).astype(bf16)
        sums[0] += jnp.sum(dy * normed, axis=0, keepdims=True)
        sums[1] += jnp.sum(dy, axis=0, keepdims=True)
        sums[2] += jnp.sum(wide(low), axis=0, keepdims=True)
    sums_ref[...] = jnp.concatenate(sums + [jnp.zeros((5, width), f32)], axis=0)
    grad = dot(mixed_ref[...].T, dattn_ref[...]).astype(bf16)
    for i in range(2):
        grad_ref[width * i : width * (i + 1), :] = grad[:, CHUNK * i : CHUNK * (i + 1)]
    wait(back)


def low(*shape):
    return jax.ShapeDtypeStruct(shape, bf16)


def full(*shape):
    return jax.ShapeDtypeStruct(shape, f32)


def share_sizes(w_in, got):
    return min(2 * CHUNK, w_in.shape[1]), min(2 * CHUNK, got[0].shape[2])


def weight_scratch(w_in, w_out, got, chunk):
    n = got[0].shape[0]
    return [
        pltpu.VMEM(w_in.shape, bf16),
        pltpu.VMEM(w_out.shape, bf16),
        pltpu.VMEM((2 * n, *got[0].shape[1:]), bf16),
        pltpu.VMEM((2 * n, 2 * got[1].shape[1], got[1].shape[2]), bf16),
        pltpu.SemaphoreType.DMA((w_in.shape[1] // chunk + 2, 3)),
        pltpu.SemaphoreType.DMA((6,)),
    ]


def ffn_forward(h, normed, cot, vectors, b_in, y, w_in, w_out, got, other):
    rows, width = h.shape
    units = w_in.shape[1]
    far = 2 * got[0].shape[0]
    chunk, far_chunk = share_sizes(w_in, got)
    anywhere = pl.BlockSpec(memory_space=pl.ANY)
    vmem = pl.BlockSpec(memory_space=pltpu.VMEM)
    far_slope = (far, rows, got[0].shape[2])
    return pl.pallas_call(
        functools.partial(ffn_forward_kernel, chunk=chunk, far_chunk=far_chunk),
        in_specs=[vmem, anywhere, anywhere]
        + [vmem] * 6
        + [pl.BlockSpec(memory_space=pltpu.SMEM)]
        + [anywhere] * 8,
        out_specs=[vmem] * 3 + [anywhere] * 3 + [vmem],
        out_shape=[
            full(rows, width),
            full(rows, width),
            low(rows, width),
            low(rows, units),
            low(rows, units),
            low(*far_slope),
            full(8, width),
        ],
        scratch_shapes=[
            pltpu.VMEM((rows, width), f32),
            pltpu.VMEM((rows, width), bf16),
            pltpu.VMEM((rows, units), bf16),
            pltpu.VMEM((rows, units), bf16),
            pltpu.VMEM(far_slope, bf16),
            pltpu.VMEM((rows, width), f32),
            *weight_scratch(w_in, w_out, got, chunk),
        ],
        compiler_params=pltpu.CompilerParams(vmem_limit_bytes=VMEM),
        cost_estimate=pl.CostEstimate(
            flops=16 * rows * width * width, bytes_accessed=24_000_000, transcendentals=3_200_000
        ),
        name="ffn_forward",
    )(h, normed, cot, *vectors, b_in, y, w_in, w_out, *got, *other)


def ffn_backward(
    db, normed, root, dpre, mixed, w_output, gain, slope, far_slope, y, w_in, w_out, got, other
):
    rows, width = db.shape
    units = w_in.shape[1]
    chunk, far_chunk = share_sizes(w_in, got)
    anywhere = pl.BlockSpec(memory_space=pl.ANY)
    vmem = pl.BlockSpec(memory_space=pltpu.VMEM)
    return pl.pallas_call(
        functools.partial(ffn_backward_kernel, chunk=chunk, far_chunk=far_chunk),
        in_specs=[vmem, anywhere, vmem, vmem, anywhere, anywhere, vmem, anywhere, anywhere]
        + [pl.BlockSpec(memory_space=pltpu.SMEM)]
        + [anywhere] * 8,
        out_specs=[anywhere] + [vmem] * 4,
        out_shape=[
            low(rows, units),
            full(rows, width),
            low(rows, width),
            low(2 * width, CHUNK),
            full(8, width),
        ],
        scratch_shapes=[
            pltpu.VMEM((rows, width), f32),
            pltpu.VMEM((rows, width), bf16),
            pltpu.VMEM((width, width), bf16),
            pltpu.VMEM((rows, units), bf16),
            pltpu.VMEM((rows, width), f32),
            pltpu.VMEM((rows, width), bf16),
            pltpu.VMEM((rows, units), bf16),
            pltpu.VMEM(far_slope.shape, bf16),
            *weight_scratch(w_in, w_out, got, chunk),
        ],
        compiler_params=pltpu.CompilerParams(vmem_limit_bytes=VMEM),
        cost_estimate=pl.CostEstimate(
            flops=20 * rows * width * width, bytes_accessed=24_000_000, transcendentals=0
        ),
        name="ffn_backward",
    )(
        db,
        normed,
        root,
        dpre,
        mixed,
        w_output,
        gain,
        slope,
        far_slope,
        y,
        w_in,
        w_out,
        *got,
        *other,
    )


def ffn_grads_kernel(
    start_ref,
    bin_ref,
    h_hbm,
    db_hbm,
    active_hbm,
    dinner_hbm,
    far_h_hbm,
    far_db_hbm,
    win_hbm,
    wout_hbm,
    out_ref,
    h_ref,
    db_ref,
    active_ref,
    dinner_ref,
    far_h_ref,
    far_db_ref,
    win_ref,
    wout_ref,
    far_active_ref,
    far_slope_ref,
    far_dinner_ref,
    h_t,
    far_t,
    bias_ref,
    sems,
    *,
    chunks,
):
    units = chunks * CHUNK
    width = h_ref.shape[1]
    far = far_h_ref.shape[0]
    tail = 4 * CHUNK * chunks
    if win_hbm.shape[1] == units:
        part = slice(0, units)
    else:
        part = pl.ds(pl.multiple_of(start_ref[0] * CHUNK, CHUNK), units)
    copies = [
        pltpu.make_async_copy(source, target, sems.at[i])
        for i, (source, target) in enumerate(
            [
                (far_h_hbm, far_h_ref),
                (win_hbm.at[:, part], win_ref),
                (far_db_hbm, far_db_ref),
                (wout_hbm.at[part], wout_ref),
                (h_hbm, h_ref),
                (dinner_hbm.at[:, part], dinner_ref),
                (active_hbm.at[:, part], active_ref),
                (db_hbm, db_ref),
            ]
        )
    ]
    start(copies)
    bias_ref[...] = wide(bin_ref[...])[None, :]
    b_in = bias_ref[:, part]
    wait(copies[:2])
    for r in range(0, far, 256):
        rows = slice(r, r + 256)
        active, slope = gelu_parts(dot(far_h_ref[rows, :], win_ref[...]) + b_in)
        far_active_ref[rows, :] = active.astype(bf16)
        far_slope_ref[rows, :] = slope.astype(bf16)
    far_t[...] = far_h_ref[...].T
    wait(copies[2:4])
    bias = jnp.zeros((1, units), f32)
    for r in range(0, far, 256):
        rows = slice(r, r + 256)
        dinner = dot_nt(far_db_ref[rows, :], wout_ref[...]) * wide(far_slope_ref[rows, :])
        dinner = dinner.astype(bf16)
        far_dinner_ref[rows, :] = dinner
        bias = bias + jnp.sum(wide(dinner), axis=0, keepdims=True)
    wait(copies[4:6])
    h_t[...] = h_ref[...].T
    for r in range(0, width, 256):
        rows = slice(r, r + 256)
        grad = dot(h_t[rows, :], dinner_ref[...]) + dot(far_t[rows, :], far_dinner_ref[...])
        grad = grad.astype(bf16)
        for c in range(chunks):
            place = 4 * CHUNK * c + r
            out_ref[place : place + 256, :] = grad[:, CHUNK * c : CHUNK * (c + 1)]
    wait(copies[6:])
    for c in range(chunks):
        cols = slice(CHUNK * c, CHUNK * (c + 1))
        grad = dot(active_ref[:, cols].T, db_ref[...])
        grad = (grad + dot(far_active_ref[:, cols].T, far_db_ref[...])).astype(bf16)
        for k in range(2):
            place = 4 * CHUNK * c + (2 + k) * CHUNK
            out_ref[place : place + CHUNK, :] = grad[:, CHUNK * k : CHUNK * (k + 1)]
    bias = bias + jnp.sum(wide(dinner_ref[...]), axis=0, keepdims=True)
    out_ref[tail:, :] = jnp.zeros_like(out_ref[tail:, :])
    rows = [bias[:, CHUNK * c : CHUNK * (c + 1)] for c in range(chunks)]
    rows.append(jnp.zeros((16 - chunks, CHUNK), f32))
    out_ref[tail : tail + 16, :] = jnp.concatenate(rows, axis=0).astype(bf16)


def ffn_grads(h, db, active, dinner, far_h, far_db, w_in, b_in, w_out, start, chunks, extra):
    rows, width = h.shape
    units = chunks * CHUNK
    far = far_h.shape[0]
    anywhere = pl.BlockSpec(memory_space=pl.ANY)

    def scratch(r, w):
        return pltpu.VMEM((r, w), bf16)

    total = chunks * 4 * CHUNK + extra
    return pl.pallas_call(
        functools.partial(ffn_grads_kernel, chunks=chunks),
        in_specs=[pl.BlockSpec(memory_space=pltpu.SMEM), pl.BlockSpec(memory_space=pltpu.VMEM)]
        + [anywhere] * 8,
        out_specs=pl.BlockSpec(memory_space=pltpu.VMEM),
        out_shape=low(total, CHUNK),
        scratch_shapes=[
            scratch(rows, width),
            scratch(rows, width),
            scratch(rows, units),
            scratch(rows, units),
            scratch(far, width),
            scratch(far, width),
            scratch(width, units),
            scratch(units, width),
            scratch(far, units),
            scratch(far, units),
            scratch(far, units),
            scratch(width, rows),
            scratch(width, far),
            pltpu.VMEM((1, w_in.shape[1]), f32),
            pltpu.SemaphoreType.DMA((8,)),
        ],
        compiler_params=pltpu.CompilerParams(vmem_limit_bytes=VMEM),
        cost_estimate=pl.CostEstimate(
            flops=4 * (rows + 2 * far) * width * units,
            bytes_accessed=16_000_000,
            transcendentals=2 * far * units,
        ),
        name="ffn_grads",
    )(start, b_in, h, db, active, dinner, far_h, far_db, w_in, w_out)


def late_kernel(*refs, pieces, grads):
    dq_refs, dk_refs, sums_refs = [refs[pieces * i : pieces * (i + 1)] for i in range(3)]
    wq_ref, wk_ref, table_ref, gain_ref, sums1_ref, sums2_ref = refs[3 * pieces : 3 * pieces + 6]
    out_hbm, tail_ref, sem = refs[3 * pieces + 7 :]
    rows, width = table_ref.shape
    gain = wide(gain_ref[...])[None, :]
    dy = 0.0
    for parts, w_ref in ((dq_refs, wq_ref), (dk_refs, wk_ref)):
        place = 0
        for part in parts:
            dy = dy + dot_nt(part[...], w_ref[:, place : place + part.shape[1]])
            place += part.shape[1]
    normed, root = ln_parts(wide(table_ref[...]))
    table = ln_back_rows(dy, normed, root, gain).astype(bf16)
    vectors = jnp.concatenate(
        [
            sums1_ref[...],
            sums2_ref[...],
            jnp.concatenate([r[...] for r in sums_refs], axis=1),
            jnp.sum(dy * normed, axis=0, keepdims=True),
            jnp.sum(dy, axis=0, keepdims=True),
            jnp.zeros((6, width), f32),
        ],
        axis=0,
    ).astype(bf16)
    base = 0
    for block in (table, vectors):
        for i in range(width // TILE):
            tail_ref[base : base + block.shape[0], :] = block[:, TILE * i : TILE * (i + 1)]
            base += block.shape[0]
    tail_ref[base:, :] = jnp.zeros((tail_ref.shape[0] - base, TILE), bf16)
    copy = pltpu.make_async_copy(tail_ref, out_hbm.at[grads:], sem.at[0])
    copy.start()
    copy.wait()


def late_rows(rows, width):
    grads = 6 * width
    total = grads + (rows + 32) * (width // TILE)
    return grads, -(-total // 512) * 512


def late_sums(d_query, d_key, sums, w_query, w_key, table, gain, sums1, sums2, into):
    rows, width = table.shape
    pieces = len(d_query)
    grads, total = late_rows(rows, width)

    def fixed(shape):
        return pl.BlockSpec(shape, lambda i: (0, 0))

    def lower(x):
        return pl.BlockSpec((rows, x.shape[1]), lambda i: (1, 0))

    square = fixed((width, width))
    anywhere = pl.BlockSpec(memory_space=pl.ANY)
    return pl.pallas_call(
        functools.partial(late_kernel, pieces=pieces, grads=grads),
        grid=(1,),
        in_specs=[lower(x) for x in (*d_query, *d_key)]
        + [fixed(x.shape) for x in sums]
        + [square, square, fixed((rows, width)), pl.BlockSpec((width,), lambda i: (0,))]
        + [fixed((8, width))] * 2
        + [anywhere],
        out_specs=anywhere,
        out_shape=jax.ShapeDtypeStruct((total, TILE), bf16),
        input_output_aliases={3 * pieces + 6: 0},
        scratch_shapes=[pltpu.VMEM((total - grads, TILE), bf16), pltpu.SemaphoreType.DMA((1,))],
        compiler_params=pltpu.CompilerParams(vmem_limit_bytes=VMEM),
        cost_estimate=pl.CostEstimate(
            flops=1_300_000_000, bytes_accessed=12_000_000, transcendentals=0
        ),
        name="late_sums",
    )(*d_query, *d_key, *sums, w_query, w_key, table, gain, sums1, sums2, into)


def input_grad_kernel(*refs, pieces):
    parts = [refs[pieces * i : pieces * (i + 1)] for i in range(3)]
    weights = refs[3 * pieces : 3 * pieces + 3]
    res_ref, out_ref = refs[3 * pieces + 3 :]
    for r in range(0, res_ref.shape[0], 256):
        rows = slice(r, r + 256)
        total = res_ref[rows, :]
        for part, w_ref in zip(parts, weights, strict=True):
            place = 0
            for x in part:
                total = total + dot_nt(x[rows, :], w_ref[:, place : place + x.shape[1]])
                place += x.shape[1]
        out_ref[rows, :] = total


def input_gradient(d_query, d_key, d_value, w_query, w_key, w_value, d_residual):
    rows, width = d_residual.shape
    pieces = len(d_query)
    specs = [
        pl.BlockSpec((rows, x.shape[1]), lambda i: (0, 0)) for x in (*d_query, *d_key, *d_value)
    ]
    square = pl.BlockSpec((width, width), lambda i: (0, 0))
    full = pl.BlockSpec((rows, width), lambda i: (0, 0))
    return pl.pallas_call(
        functools.partial(input_grad_kernel, pieces=pieces),
        grid=(1,),
        in_specs=[*specs, square, square, square, full],
        out_specs=full,
        out_shape=jax.ShapeDtypeStruct((rows, width), f32),
        compiler_params=pltpu.CompilerParams(vmem_limit_bytes=VMEM),
        cost_estimate=pl.CostEstimate(
            flops=6 * rows * width * width, bytes_accessed=10_000_000, transcendentals=0
        ),
        name="input_gradient",
    )(*d_query, *d_key, *d_value, w_query, w_key, w_value, d_residual)


def ffn_result_kernel(core_ref, mine_hbm, other_hbm, *refs, chunks, columns):
    out_ref, refs = refs[0], refs[1:]
    bias_ref, (part_ref, sems) = (refs[0], refs[1:]) if columns else (None, refs)
    offset = 0 if columns else 2 * CHUNK

    def write(halves):
        copies = []
        for i, half in enumerate(halves):
            for c in range(chunks):
                place = 4 * CHUNK * c + offset
                copies.append((half.at[place : place + 2 * CHUNK], part_ref.at[i * chunks + c]))
            if columns:
                place = 4 * CHUNK * chunks
                copies.append((half.at[place : place + 16], part_ref.at[2 * chunks + i, :16]))
        copies = [pltpu.make_async_copy(a, b, sems.at[i]) for i, (a, b) in enumerate(copies)]
        start(copies)
        for i in range(2):
            for c in range(chunks):
                wait(copies[:1])
                copies = copies[1:]
                k = i * chunks + c
                cols = slice(CHUNK * k, CHUNK * (k + 1))
                if columns:
                    out_ref[:, cols] = wide(part_ref[k])
                else:
                    out_ref[cols, :CHUNK] = wide(part_ref[k, :CHUNK, :])
                    out_ref[cols, CHUNK:] = wide(part_ref[k, CHUNK:, :])
            if columns:
                wait(copies[:1])
                copies = copies[1:]
        if columns:
            rows = []
            for i in range(2):
                tail = wide(part_ref[2 * chunks + i, :16, :])
                rows = rows + [tail[c : c + 1, :] for c in range(chunks)]
            bias_ref[...] = jnp.concatenate(rows, axis=1).reshape(bias_ref.shape)

    @pl.when(core_ref[0] == 0)
    def _():
        write((mine_hbm, other_hbm))

    @pl.when(core_ref[0] != 0)
    def _():
        write((other_hbm, mine_hbm))


def ffn_result(core, mine, other, width, units, columns):
    chunks = units // CHUNK
    if chunks % 2:
        first = jnp.where(core == 0, mine, other)
        second = jnp.where(core == 0, other, mine)
        total = wide(jnp.concatenate([first, second], axis=0))
        parts = [total[4 * CHUNK * c : 4 * CHUNK * (c + 1)] for c in range(chunks)]
        if columns:
            return (
                jnp.concatenate([p[: 2 * CHUNK] for p in parts], axis=1),
                total[4 * CHUNK * chunks : 4 * CHUNK * chunks + chunks].reshape(units),
            )
        sides = [
            jnp.concatenate([p[(2 + i) * CHUNK : (3 + i) * CHUNK] for p in parts], axis=0)
            for i in range(2)
        ]
        return (jnp.concatenate(sides, axis=1),)
    anywhere = pl.BlockSpec(memory_space=pl.ANY)
    outs = [full(width, units), full(units)] if columns else [full(units, width)]
    return pl.pallas_call(
        functools.partial(ffn_result_kernel, chunks=chunks // 2, columns=columns),
        in_specs=[pl.BlockSpec(memory_space=pltpu.SMEM), anywhere, anywhere],
        out_shape=outs,
        scratch_shapes=[
            pltpu.VMEM((chunks + 2, 2 * CHUNK, CHUNK), bf16),
            pltpu.SemaphoreType.DMA((chunks + 2,)),
        ],
        compiler_params=pltpu.CompilerParams(vmem_limit_bytes=VMEM),
        cost_estimate=pl.CostEstimate(flops=0, bytes_accessed=8_000_000, transcendentals=0),
        name="ffn_result",
    )(core, mine, other)


def early_result_kernel(core_ref, mine_ref, other_ref, w_mine, w_other, q_ref, k_ref, v_ref, wo_ref):
    width = q_ref.shape[0]
    blocks = mine_ref.shape[0] // width

    def write(first, second, w_first, w_second):
        for b in range(2 * blocks):
            part = first if b < blocks else second
            value = wide(part[width * (b % blocks) : width * (b % blocks + 1), :])
            group, which = divmod(b, 3)
            (q_ref, k_ref, v_ref)[which][:, TILE * group : TILE * (group + 1)] = value
        for i, part in enumerate((w_first, w_second)):
            wo_ref[:, CHUNK * i : CHUNK * (i + 1)] = wide(part[...])

    @pl.when(core_ref[0] == 0)
    def _():
        write(mine_ref, other_ref, w_mine, w_other)

    @pl.when(core_ref[0] != 0)
    def _():
        write(other_ref, mine_ref, w_other, w_mine)


def early_result(core, mine, other, w_mine, w_other, width):
    smem = pl.BlockSpec(memory_space=pltpu.SMEM)
    vmem = pl.BlockSpec(memory_space=pltpu.VMEM)
    return pl.pallas_call(
        early_result_kernel,
        in_specs=[smem] + [vmem] * 4,
        out_shape=[full(width, width)] * 4,
        compiler_params=pltpu.CompilerParams(vmem_limit_bytes=VMEM),
        cost_estimate=pl.CostEstimate(flops=0, bytes_accessed=10_000_000, transcendentals=0),
        name="early_result",
    )(core, mine, other, w_mine, w_other)


def late_result_kernel(core_ref, mine_ref, other_ref, *refs):
    q_ref, k_ref, v_ref, table_ref = refs[3:7]
    vector_refs, all_ref = refs[7:-1], refs[-1]
    width, rows = q_ref.shape[0], table_ref.shape[0]
    groups = table_ref.shape[1] // TILE
    half = mine_ref.shape[0]

    def write(first, second):
        all_ref[:half, :] = first[...]
        all_ref[half:, :] = second[...]

    @pl.when(core_ref[0] == 0)
    def _():
        write(mine_ref, other_ref)

    @pl.when(core_ref[0] != 0)
    def _():
        write(other_ref, mine_ref)

    base = 0
    for g in range(2):
        for ref in (q_ref, k_ref, v_ref):
            ref[:, TILE * g : TILE * (g + 1)] = wide(all_ref[base : base + width, :])
            base += width
    for i in range(groups):
        table_ref[:, TILE * i : TILE * (i + 1)] = wide(all_ref[base : base + rows, :])
        base += rows
    parts = [wide(all_ref[base + 32 * i : base + 32 * (i + 1), :]) for i in range(groups)]
    vectors = jnp.concatenate(parts, axis=1)
    for place, ref in zip(VECTOR_ROWS, vector_refs, strict=True):
        ref[...] = vectors[place : place + 1, :].reshape(ref.shape)


def late_result(core, mine, other, grads, rows):
    width = grads[0].shape[0]
    groups = width // 256
    smem = pl.BlockSpec(memory_space=pltpu.SMEM)
    half = pl.BlockSpec(mine.shape, lambda i: (0, 0))
    anywhere = pl.BlockSpec(memory_space=pl.ANY)
    last = pl.BlockSpec((width, 256), lambda i: (0, groups - 1))
    vector = pl.BlockSpec((width,), lambda i: (0,))
    return pl.pallas_call(
        late_result_kernel,
        grid=(1,),
        in_specs=[smem, half, half] + [anywhere] * 3,
        out_specs=[last] * 3
        + [pl.BlockSpec((rows, width), lambda i: (0, 0))]
        + [vector] * len(VECTOR_ROWS),
        out_shape=[jax.ShapeDtypeStruct((width, width), f32)] * 3
        + [jax.ShapeDtypeStruct((rows, width), f32)]
        + [jax.ShapeDtypeStruct((width,), f32)] * len(VECTOR_ROWS),
        input_output_aliases={3: 0, 4: 1, 5: 2},
        scratch_shapes=[pltpu.VMEM((2 * mine.shape[0], TILE), bf16)],
        compiler_params=pltpu.CompilerParams(vmem_limit_bytes=VMEM),
        cost_estimate=pl.CostEstimate(flops=0, bytes_accessed=6_000_000, transcendentals=0),
        name="late_result",
    )(core, mine, other, *grads)


class Moves:
    def __init__(self, n_dp, n_mp):
        self.n_dp, self.n_mp = n_dp, n_mp
        self.dp = lax.axis_index("dp")
        self.mp = lax.axis_index("mp")
        self.core = self.dp % 2
        self.dp_bits = [("dp", 1 << b) for b in range(1, n_dp.bit_length() - 1)]
        self.mp_bits = [("mp", 1 << b) for b in range(n_mp.bit_length() - 1)]

    def swap(self, x, pair):
        perm = []
        for d in range(self.n_dp):
            for m in range(self.n_mp):
                axis, bit = pair[d % 2]
                dest = (d ^ bit, m) if axis == "dp" else (d, m ^ bit)
                perm.append((d * self.n_mp + m, dest[0] * self.n_mp + dest[1]))
        return lax.ppermute(x, BOTH, perm)

    def side(self, pair):
        values = [((self.dp if axis == "dp" else self.mp) // bit) % 2 for axis, bit in pair]
        return jnp.where(self.core == 0, values[0], values[1])

    def halves(self, x, pair):
        half = x[0].shape[0] // 2
        side = self.side(pair)

        def part(start):
            return whole([lax.dynamic_slice_in_dim(y, start * half, half, 0) for y in x])

        return part(1 - side), part(side)

    def scatter(self, x, pair):
        sent, kept = self.halves(x, pair)
        return kept, self.swap(sent, pair)

    def exchange(self, x, pair):
        x = whole(x)
        return x, self.swap(x, pair)

    def gather(self, x, pair):
        x = whole(x)
        other = self.swap(x, pair)
        side = self.side(pair)
        first = jnp.where(side == 0, x, other)
        second = jnp.where(side == 0, other, x)
        return (jnp.concatenate([first, second], axis=0),)

    def steps(self, first, second, joined):
        pairs = list(zip(first, second, strict=True))
        if joined:
            middle = [functools.partial(self.exchange, pair=pairs.pop())]
        else:
            middle = []
        down = [functools.partial(self.scatter, pair=pair) for pair in pairs]
        up = [functools.partial(self.gather, pair=pair) for pair in reversed(pairs)]
        return down + middle + up


def whole(x):
    return x[0] if len(x) == 1 else sum(wide(y) for y in x).astype(bf16)


def tie(*values):
    return lax.optimization_barrier(values)


def per_device(
    inputs,
    cotangent,
    w_query,
    b_query,
    w_key,
    b_key,
    w_value,
    b_value,
    w_output,
    b_output,
    norm1_gain,
    norm1_shift,
    w_inner,
    b_inner,
    w_outer,
    b_outer,
    norm2_gain,
    norm2_shift,
    rel_table,
    rel_gain,
    rel_shift,
    block_group,
    seq_lengths,
    *,
    n_dp,
    n_mp,
):
    rows, width = inputs.shape
    units = w_inner.shape[1]
    moves = Moves(n_dp, n_mp)
    core = ("dp", 1)

    def other_shares(x):
        shares = [x[None]]
        for bit in moves.mp_bits:
            shares = [jnp.concatenate(shares, axis=0)]
            shares.append(moves.swap(shares[0], (bit, bit)))
        return jnp.concatenate(shares, axis=0)[1:]

    core_id = moves.core.reshape(1).astype(jnp.int32)
    row_bit = moves.dp_bits[0]
    row_id = moves.side((row_bit, row_bit)).reshape(1).astype(jnp.int32)
    half_in, quarter_out = core_half(core_id, row_id, w_inner, w_outer, b_inner)
    got_out = other_shares(quarter_out)
    got_in = other_shares(half_in)

    line = bucket_line(rows // 2)
    place_ids = np.arange(rows)[None, :]
    forward = jnp.asarray(np.append(line, -1)[:, None] == place_ids).astype(bf16)
    backward = jnp.asarray(np.append(line[::-1], -1)[:, None] == place_ids).astype(bf16)
    query, key, value, key_line, key_line_back, query_line, both_t = pre(
        inputs,
        rel_table,
        rel_gain,
        rel_shift,
        w_query,
        b_query,
        w_key,
        b_key,
        w_value,
        b_value,
        forward,
        backward,
    )
    got_out, query = tie(got_out, query)
    got_row = moves.swap(got_out, (row_bit, row_bit))
    other_out = moves.swap(got_out, (core, core))
    mixed, exps, inverse, mixed_full, normed1, root1, hidden_low = attend(
        block_group,
        seq_lengths,
        query,
        key,
        value,
        key_line,
        query_line,
        w_output,
        b_output,
        inputs,
        norm1_gain,
        norm1_shift,
    )

    def far(x):
        whole = x
        for bit in moves.mp_bits:
            whole = jnp.concatenate([whole, moves.swap(whole, (bit, bit))], axis=0)
        return whole[rows:]

    got_in, got_row, other_out, hidden_low = tie(got_in, got_row, other_out, hidden_low)
    got = (got_in, got_out, got_row)
    other = (moves.swap(got_in, (core, core)), other_out, moves.swap(got_row, (core, core)))
    far_hidden = far(hidden_low)
    layer_out, d_pre2, d_branch, active, slope, far_slope, sums2 = ffn_forward(
        hidden_low,
        normed1,
        cotangent,
        (norm1_gain, norm1_shift, b_outer, norm2_gain, norm2_shift),
        b_inner,
        row_id,
        w_inner,
        w_outer,
        got,
        other,
    )
    far_branch = far(d_branch)
    d_inner, d_residual, d_mixed, grad_w_output, sums1 = ffn_backward(
        d_branch,
        normed1,
        root1,
        d_pre2,
        mixed,
        w_output,
        norm1_gain,
        slope,
        far_slope,
        row_id,
        w_inner,
        w_outer,
        got,
        other,
    )

    dp_bits, mp_bits = moves.dp_bits, moves.mp_bits
    pair = (core, core)
    ffn_steps = moves.steps(dp_bits, dp_bits[1:2] + dp_bits[:1] + dp_bits[2:], False)
    first, second = mp_bits + dp_bits, dp_bits[:1] + mp_bits + dp_bits[1:]
    early_steps = moves.steps(first, second, True)
    late_steps = moves.steps(first, second, True)
    shared = (exps, inverse, mixed_full, key_line_back, query_line, backward, both_t)
    pieces = []
    pairs = width // TILE

    def attention(d_mixed, first, count, *into):
        *piece, grad = attend_back(query, key, value, d_mixed, *shared, first, count, *into)
        pieces.append(piece)
        return grad

    output_sum = moves.scatter((grad_w_output,), pair)
    chunks = units // CHUNK
    near = (hidden_low, d_branch, active, d_inner, far_hidden, far_branch, w_inner, b_inner, w_outer)
    if chunks % 2 == 0:
        mine, theirs = core_id * (chunks // 2), (1 - core_id) * (chunks // 2)
        sent = ffn_grads(*near, theirs, chunks // 2, 4 * n_dp)
        sent, mine, output_sum = tie(sent, mine, output_sum)
        for bit in mp_bits:
            output_sum = moves.scatter(output_sum, (bit, bit))
        kept = ffn_grads(*near, mine, chunks // 2, 4 * n_dp)
        ffn_sum = (kept, moves.swap(sent, pair))
    else:
        ffn_sum = (ffn_grads(*near, 0 * core_id, chunks, 8 * n_dp),)
        ffn_sum = moves.scatter(ffn_sum, pair)
        for bit in mp_bits:
            output_sum = moves.scatter(output_sum, (bit, bit))
    ffn_rows = ffn_sum[0].shape[0]
    ffn_sum = (jnp.concatenate([whole(ffn_sum), whole(output_sum)], axis=0),)
    ffn_sum, d_mixed = tie(ffn_sum, d_mixed)

    ffn_sum = ffn_steps.pop(0)(ffn_sum)
    early_size = 3 * width * (pairs - 2)
    early = attention(d_mixed, 0, 2, None, early_size, 0)
    ffn_sum, d_mixed, early = tie(ffn_sum, d_mixed, early)
    ffn_sum = ffn_steps.pop(0)(ffn_sum)
    early = attention(d_mixed, 2, 1, early, early_size, 2)
    ffn_sum, d_mixed, early = tie(ffn_sum, d_mixed, early)
    ffn_sum = ffn_steps.pop(0)(ffn_sum)
    early = attention(d_mixed, 3, pairs - 5, early, early_size, 3)
    ffn_sum, d_mixed, early = tie(ffn_sum, d_mixed, early)
    ffn_sum = ffn_steps.pop(0)(ffn_sum)
    early = moves.scatter((early,), pair)
    late_size = late_rows(rows, width)[1]
    late = attention(d_mixed, pairs - 2, 1, None, late_size, 0)
    early, ffn_sum, late, d_mixed = tie(early, ffn_sum, late, d_mixed)
    ffn_sum = ffn_steps.pop(0)(ffn_sum)
    early = early_steps.pop(0)(early)
    late = attention(d_mixed, pairs - 1, 1, late, late_size, 1)
    early, ffn_sum, late, d_residual = tie(early, ffn_sum, late, d_residual)
    ffn_sum = ffn_steps.pop(0)(ffn_sum)
    early = early_steps.pop(0)(early)
    d_query, d_key, d_value, sums = zip(*pieces, strict=True)
    late = late_sums(
        d_query, d_key, sums, w_query, w_key, rel_table, rel_gain, sums1, sums2, late
    )
    late, d_residual = tie(late, d_residual)
    late = moves.scatter((late,), pair)
    input_grad = input_gradient(d_query, d_key, d_value, w_query, w_key, w_value, d_residual)
    late, early, ffn_sum, input_grad = tie(late, early, ffn_sum, input_grad)

    def last(x):
        return moves.exchange(x, pair)

    early_steps.append(last)
    late_steps.append(last)
    output_steps = [functools.partial(moves.gather, pair=(b, b)) for b in reversed(mp_bits)] + [last]
    for step in ffn_steps:
        ffn_sum = step(ffn_sum)
    ffn_sum = last(ffn_sum)
    output_sum = (ffn_sum[0][ffn_rows:],)
    early_out, ffn_in, ffn_out = None, None, None
    while late_steps:
        late = late_steps.pop(0)(late)
        done = ()
        if early_steps:
            early = early_steps.pop(0)(early)
        elif early_out is None and not output_steps:
            done = early_out = early_result(core_id, *early, *output_sum, width)
        if len(late_steps) % 2 == 1 and ffn_in is None:
            done = ffn_in = ffn_result(core_id, *ffn_sum, width, units, True)
        elif len(late_steps) % 2 == 1 and ffn_out is None:
            done = ffn_out = ffn_result(core_id, *ffn_sum, width, units, False)
        elif output_steps:
            output_sum = output_steps.pop(0)(output_sum)
        late, early, ffn_sum, output_sum, done = tie(late, early, ffn_sum, output_sum, done)
    for step in early_steps:
        early = step(early)
    for step in output_steps:
        output_sum = step(output_sum)
    if ffn_in is None:
        ffn_in = ffn_result(core_id, *ffn_sum, width, units, True)
    if ffn_out is None:
        ffn_out = ffn_result(core_id, *ffn_sum, width, units, False)
    if early_out is None:
        early_out = early_result(core_id, *early, *output_sum, width)
    *early_out, grad_w_output = early_out
    ffn_in, ffn_bias = ffn_in
    (ffn_out,) = ffn_out
    grad_q, grad_k, grad_v, table, *vectors = late_result(core_id, *late, early_out, rows)
    return (
        layer_out,
        input_grad,
        grad_q,
        vectors[0],
        grad_k,
        vectors[1],
        grad_v,
        vectors[2],
        grad_w_output,
        *vectors[3:6],
        ffn_in,
        ffn_bias,
        ffn_out,
        *vectors[6:9],
        table,
        *vectors[9:],
    )


def solution(mesh):
    n_dp, n_mp = mesh.shape["dp"], mesh.shape["mp"]

    def body(*args):
        return per_device(*args, n_dp=n_dp, n_mp=n_mp)

    split = P(("dp", "mp"), None)
    weights = [P()] * 10 + [P(None, "mp"), P("mp"), P("mp", None)] + [P()] * 6
    return jax.shard_map(
        body,
        mesh=mesh,
        in_specs=(split, split, *weights, P(("dp", "mp")), split),
        out_specs=(
            split,
            split,
            *([P()] * 10),
            P(None, "mp"),
            P("mp"),
            P("mp", None),
            *([P()] * 6),
        ),
        check_vma=False,
    )
```

```python
import functools
import math

import jax
import jax.numpy as jnp
import numpy as np
from jax import lax
from jax.experimental import pallas as pl
from jax.experimental.pallas import tpu as pltpu
from jax.sharding import PartitionSpec as P

HEADS = 12
EPS = 1e-06
LOG2E = 1.4426950408889634
TILE = 128
CHUNK = 384
VMEM = 60 * 1024 * 1024
VECTOR_ROWS = (16, 17, 18, 2, 0, 1, 10, 8, 9, 24, 25)
BOTH = ("dp", "mp")
f32 = jnp.float32
bf16 = jnp.bfloat16


def bucket_line(half_rows):
    table_rows = 2 * half_rows
    middle = half_rows // 2
    relative = table_rows - 1 - np.arange(2 * table_rows - 1)
    signed = np.sign(relative)
    absolute = np.where((relative < middle) & (relative > -middle), middle - 1, np.abs(relative))
    log_place = (
        np.ceil(np.log(absolute / middle) / np.log((table_rows - 1) / middle) * (middle - 1))
        + middle
    )
    placed = np.where(absolute <= middle, relative, log_place * signed)
    return (placed + half_rows).astype(np.int32)


def dot(a, b):
    return jnp.dot(a, b, preferred_element_type=f32)


def dot_nt(a, b):
    return lax.dot_general(a, b, (((1,), (1,)), ((), ())), preferred_element_type=f32)


def dot_tn(a, b):
    return lax.dot_general(a, b, (((0,), (0,)), ((), ())), preferred_element_type=f32)


def wide(v):
    return v.astype(f32)


def ln_parts(v):
    average = jnp.mean(v, axis=-1, keepdims=True)
    center = v - average
    root = lax.rsqrt(jnp.mean(center * center, axis=-1, keepdims=True) + EPS)
    return center * root, root


def ln_back_rows(dy, normed, root, gain):
    dn = dy * gain
    first = jnp.mean(dn, axis=-1, keepdims=True)
    second = jnp.mean(dn * normed, axis=-1, keepdims=True)
    return root * (dn - first - normed * second)


def gelu_parts(v):
    bell = jnp.exp(-0.5 * v * v)
    t = 1.0 / (1.0 + (0.3275911 * math.sqrt(0.5)) * jnp.abs(v))
    poly = t * (
        0.254829592
        + t * (-0.284496736 + t * (1.421413741 + t * (-1.453152027 + t * 1.061405429)))
    )
    tail = 0.5 * poly * bell
    below = jnp.where(v >= 0, 1.0 - tail, tail)
    return v * below, below + v * bell * (1.0 / math.sqrt(2.0 * math.pi))


def pre_kernel(
    x_ref,
    table_ref,
    gain_ref,
    shift_ref,
    wq_ref,
    bq_ref,
    wk_ref,
    bk_ref,
    wv_ref,
    bv_ref,
    forward_ref,
    backward_ref,
    q_ref,
    k_ref,
    v_ref,
    key_line_ref,
    key_back_ref,
    query_line_ref,
    both_t_ref,
    both_ref,
):
    rows = x_ref.shape[0]

    @pl.when(pl.program_id(0) == 0)
    def _():
        both_ref[:rows, :] = x_ref[...]
        normed, _ = ln_parts(wide(table_ref[...]))
        rel = normed * wide(gain_ref[...])[None, :] + wide(shift_ref[...])[None, :]
        both_ref[rows:, :] = rel.astype(bf16)
        both_t_ref[...] = both_ref[...].T

    def project(w_ref, b_ref, part):
        return (dot(both_ref[part, :], w_ref[...]) + wide(b_ref[...])[None, :]).astype(bf16)

    here, there = slice(0, rows), slice(rows, 2 * rows)
    q_ref[...] = project(wq_ref, bq_ref, here)
    k_ref[...] = project(wk_ref, bk_ref, here)
    v_ref[...] = project(wv_ref, bv_ref, here)
    pos_query = project(wq_ref, bq_ref, there)
    pos_key = project(wk_ref, bk_ref, there)
    key_line_ref[...] = dot(forward_ref[...], pos_key).astype(bf16)
    key_back_ref[...] = dot(backward_ref[...], pos_key).astype(bf16)
    query_line_ref[...] = dot(backward_ref[...], pos_query).astype(bf16)


def pre(x, table, gain, shift, w_q, b_q, w_k, b_k, w_v, b_v, forward, backward):
    rows, width = x.shape
    cut = 2 * TILE

    def fixed(r, w):
        return pl.BlockSpec((r, w), lambda c: (0, 0))

    whole = pl.BlockSpec((width,), lambda c: (0,))
    weight = pl.BlockSpec((width, cut), lambda c: (0, c))
    vector = pl.BlockSpec((cut,), lambda c: (c,))
    one = pl.BlockSpec((rows, cut), lambda c: (0, c))
    two = pl.BlockSpec((2 * rows, cut), lambda c: (0, c))
    return pl.pallas_call(
        pre_kernel,
        grid=(width // cut,),
        in_specs=[fixed(rows, width), fixed(rows, width), whole, whole]
        + [weight, vector] * 3
        + [fixed(2 * rows, rows)] * 2,
        out_specs=[one] * 3 + [two] * 3 + [fixed(width, 2 * rows)],
        out_shape=[jax.ShapeDtypeStruct((rows, width), bf16)] * 3
        + [jax.ShapeDtypeStruct((2 * rows, width), bf16)] * 3
        + [jax.ShapeDtypeStruct((width, 2 * rows), bf16)],
        scratch_shapes=[pltpu.VMEM((2 * rows, width), bf16)],
        compiler_params=pltpu.CompilerParams(vmem_limit_bytes=VMEM),
        cost_estimate=pl.CostEstimate(
            flops=5_500_000_000, bytes_accessed=14_000_000, transcendentals=0
        ),
        name="pre",
    )(x, table, gain, shift, w_q, b_q, w_k, b_k, w_v, b_v, forward, backward)


def skewed(x, keep):
    parts = [x[:, TILE * b : TILE * (b + 1)] for b in range(5)]
    return [
        pltpu.roll(jnp.where(keep, parts[b], parts[b + 1]), 1, 1, stride=1, stride_axis=0)
        for b in range(4)
    ]


def unskewed(tiles, keep):
    zero = jnp.zeros((TILE, TILE), f32)
    turned = [zero] + [pltpu.roll(t, 0, 1, stride=1, stride_axis=0) for t in tiles] + [zero]
    return [jnp.where(keep, turned[b + 1], turned[b]) for b in range(5)]


def flipped():
    rows = lax.broadcasted_iota(jnp.int32, (256, 256), 0)
    cols = lax.broadcasted_iota(jnp.int32, (256, 256), 1)
    return (rows + cols == 255).astype(f32).astype(bf16)


def attend_kernel(
    group_ref,
    lengths_ref,
    q_ref,
    k_ref,
    v_ref,
    key_line_ref,
    query_line_ref,
    wo_ref,
    bo_ref,
    x_ref,
    gain_ref,
    shift_ref,
    out_ref,
    exp_ref,
    inv_ref,
    full_ref,
    normed_ref,
    root_ref,
    h_ref,
    side_ref,
    bias_ref,
    key_side,
    query_side,
    content_ref,
):
    @pl.when(pl.program_id(0) == 0)
    def _():
        normed_ref[...] = wide(x_ref[...]) + wide(bo_ref[...])[None, :]
        size = bias_ref.shape[0]
        shift = size.bit_length() - 1 - group_ref[0]
        row = lax.broadcasted_iota(jnp.int32, (size, 1), 0)
        col = lax.broadcasted_iota(jnp.int32, (1, size), 1)
        owner = jnp.right_shift(col, shift)
        limit = jnp.zeros((1, size), jnp.int32)
        for slot in range(4):
            limit = jnp.where(owner == slot, lengths_ref[0, slot], limit)
        owner = jnp.where(col - jnp.left_shift(owner, shift) < limit, owner, -1)
        valid = jnp.right_shift(row, shift) == owner
        bias_ref[...] = jnp.where(valid, 0.0, -1e30).astype(f32)

    lane = lax.broadcasted_iota(jnp.int32, (1, TILE), 1)
    keep = (
        lax.broadcasted_iota(jnp.int32, (TILE, TILE), 0)
        + lax.broadcasted_iota(jnp.int32, (TILE, TILE), 1)
        >= TILE - 1
    )
    mine = [lane < 64, lane >= 64]
    scale = LOG2E / math.sqrt(192)
    flip = flipped()
    v_ones = jnp.concatenate([v_ref[...], jnp.ones(v_ref.shape, bf16)], axis=1)
    for h in range(2):
        km = jnp.where(mine[h], k_ref[...], 0)
        qm = jnp.where(mine[h], q_ref[...], 0)
        key_side[h] = dot_nt(km, query_line_ref[...])
        query_side[h] = dot_nt(qm, key_line_ref[...])
        content_ref[h] = dot_nt(qm, k_ref[...])
    for h in range(2):
        for t in range(4):
            start = 384 - TILE * t
            sk = skewed(key_side[h, TILE * t : TILE * (t + 1), start : start + 640], keep)
            for b in range(4):
                turned = wide(sk[b].astype(bf16).T)
                side_ref[h, TILE * b : TILE * (b + 1), TILE * t : TILE * (t + 1)] = turned
        for t in range(4):
            rows = slice(TILE * t, TILE * (t + 1))
            start = 384 - TILE * t
            near = skewed(query_side[h, rows, start : start + 640], keep)
            content = content_ref[h, rows, :]
            parts = []
            for b in range(4):
                cols = slice(TILE * b, TILE * (b + 1))
                total = content[:, cols] + near[b] + side_ref[h, rows, cols]
                parts.append(total * scale + bias_ref[rows, cols])
            top = jnp.max(
                jnp.maximum(jnp.maximum(parts[0], parts[1]), jnp.maximum(parts[2], parts[3])),
                axis=1,
                keepdims=True,
            )
            low = [jnp.exp2(p - top).astype(bf16) for p in parts]
            exps = jnp.concatenate(low, axis=1)
            exp_ref[h, rows, :] = jnp.concatenate(
                [dot(exps[:, 256:], flip).astype(bf16), dot(exps[:, :256], flip).astype(bf16)], axis=1
            )
            product = dot(exps, v_ones)
            inverse = 1.0 / product[:, TILE:]
            out = product[:, :TILE] * inverse
            if h == 0:
                inv_ref[0, rows, :] = inverse
                full_ref[0, rows, :] = out
            else:
                inv_ref[0, rows, :] = jnp.where(mine[0], inv_ref[0, rows, :], inverse)
                out = jnp.where(mine[0], full_ref[0, rows, :], out)
                full_ref[0, rows, :] = out
                out_ref[rows, :] = out.astype(bf16)
    normed_ref[...] += dot(out_ref[...], wo_ref[...])

    @pl.when(pl.program_id(0) == pl.num_programs(0) - 1)
    def _():
        gain, shift = wide(gain_ref[...])[None, :], wide(shift_ref[...])[None, :]
        for r in range(0, h_ref.shape[0], TILE):
            rows = slice(r, r + TILE)
            normed, root = ln_parts(normed_ref[rows, :])
            normed_ref[rows, :] = normed
            root_ref[rows, :] = jnp.broadcast_to(root, (TILE, TILE))
            h_ref[rows, :] = (normed * gain + shift).astype(bf16)


def attend(group, lengths, q, k, v, key_line, query_line, w_output, b_output, x, gain, shift):
    rows, width = q.shape
    pairs = width // TILE
    col = pl.BlockSpec((rows, TILE), lambda g: (0, g))
    line = pl.BlockSpec((2 * rows, TILE), lambda g: (0, g))
    scalars = pl.BlockSpec(memory_space=pltpu.SMEM)
    full = pl.BlockSpec((rows, width), lambda g: (0, 0))
    vector = pl.BlockSpec((width,), lambda g: (0,))
    return pl.pallas_call(
        attend_kernel,
        grid=(pairs,),
        in_specs=[scalars, scalars, col, col, col, line, line]
        + [pl.BlockSpec((TILE, width), lambda g: (g, 0)), vector, full, vector, vector],
        out_specs=[
            col,
            pl.BlockSpec((2, rows, rows), lambda g: (g, 0, 0)),
            pl.BlockSpec((1, rows, TILE), lambda g: (g, 0, 0)),
            pl.BlockSpec((1, rows, TILE), lambda g: (g, 0, 0)),
            full,
            pl.BlockSpec((rows, TILE), lambda g: (0, 0)),
            full,
        ],
        out_shape=[
            jax.ShapeDtypeStruct((rows, width), bf16),
            jax.ShapeDtypeStruct((2 * pairs, rows, rows), bf16),
            jax.ShapeDtypeStruct((pairs, rows, TILE), f32),
            jax.ShapeDtypeStruct((pairs, rows, TILE), f32),
            jax.ShapeDtypeStruct((rows, width), f32),
            jax.ShapeDtypeStruct((rows, TILE), f32),
            jax.ShapeDtypeStruct((rows, width), bf16),
        ],
        scratch_shapes=[
            pltpu.VMEM((2, rows, rows), f32),
            pltpu.VMEM((rows, rows), f32),
            pltpu.VMEM((2, rows, 2 * rows), f32),
            pltpu.VMEM((2, rows, 2 * rows), f32),
            pltpu.VMEM((2, rows, rows), f32),
        ],
        compiler_params=pltpu.CompilerParams(vmem_limit_bytes=VMEM),
        cost_estimate=pl.CostEstimate(
            flops=18_000_000_000, bytes_accessed=16_000_000, transcendentals=3_200_000
        ),
        name="attend",
    )(group, lengths, q, k, v, key_line, query_line, w_output, b_output, x, gain, shift)


def attend_back_kernel(
    q_ref,
    k_ref,
    v_ref,
    do_ref,
    exp_ref,
    inv_ref,
    full_ref,
    key_line_ref,
    query_line_ref,
    places_ref,
    both_t_ref,
    *refs,
):
    dq_ref, dk_ref, dv_ref, sums_ref, grad_ref, *refs = refs[-9:]
    attend_back_pair(
        q_ref,
        k_ref,
        v_ref,
        do_ref,
        exp_ref,
        inv_ref,
        full_ref,
        key_line_ref,
        query_line_ref,
        places_ref,
        both_t_ref,
        dq_ref,
        dk_ref,
        dv_ref,
        sums_ref,
        grad_ref,
        *refs,
    )


def attend_back_pair(
    q_ref,
    k_ref,
    v_ref,
    do_ref,
    exp_ref,
    inv_ref,
    full_ref,
    key_line_ref,
    query_line_ref,
    places_ref,
    both_t_ref,
    dq_ref,
    dk_ref,
    dv_ref,
    sums_ref,
    grad_ref,
    ds_ref,
    dst_ref,
    query_band,
    key_band,
):
    @pl.when(pl.program_id(0) == 0)
    def _():
        query_band[...] = jnp.zeros_like(query_band)
        key_band[...] = jnp.zeros_like(key_band)

    scale = 1.0 / math.sqrt(192)
    lane = lax.broadcasted_iota(jnp.int32, (1, TILE), 1)
    sub = lax.broadcasted_iota(jnp.int32, (TILE, 1), 0)
    keep = lax.broadcasted_iota(jnp.int32, (TILE, TILE), 1) >= lax.broadcasted_iota(
        jnp.int32, (TILE, TILE), 0
    )
    mine = [lane < 64, lane >= 64]
    mine_t = [sub < 64, sub >= 64]
    flip = flipped()

    def reverse(x):
        return jnp.concatenate([dot(flip, x[256:]), dot(flip, x[:256])], axis=0).astype(bf16)

    q = q_ref[...]
    k = reverse(k_ref[...])
    v = reverse(v_ref[...])
    q_t = q.T
    k_t = k.T
    do = (wide(do_ref[...]) * inv_ref[0]).astype(bf16)
    do_t = do.T
    share = wide(do) * full_ref[0]
    high = share.astype(bf16)
    rest = (share - wide(high)).astype(bf16)
    row = lax.broadcasted_iota(jnp.int32, (256, 256), 0) % TILE // 64
    ones = (row == lax.broadcasted_iota(jnp.int32, (256, 256), 1) // TILE).astype(f32).astype(bf16)
    means = dot(jnp.concatenate([high, rest], axis=1), ones)
    dv_t = None
    dqs, dks, key_lines, query_lines = [], [], [], []
    for h in range(2):
        dom = jnp.where(mine[h], do, 0)
        for t in range(4):
            rows = slice(TILE * t, TILE * (t + 1))
            dp = dot_nt(dom[rows], v)
            mean = means[rows, TILE * h : TILE * (h + 1)]
            ds = []
            for b in range(4):
                cols = slice(TILE * b, TILE * (b + 1))
                ds.append(wide(exp_ref[h, rows, cols]) * (dp[:, cols] - mean))
                ds_ref[h, rows, cols] = ds[b].astype(bf16)
            out = unskewed(ds, keep)
            for b in range(5):
                query_band[h, rows, TILE * (t + b) : TILE * (t + b + 1)] = out[b].astype(bf16)
        for t in range(4):
            rows = slice(TILE * t, TILE * (t + 1))
            turned = [ds_ref[h, TILE * b : TILE * (b + 1), rows].T for b in range(4)]
            for b in range(4):
                dst_ref[h, rows, TILE * b : TILE * (b + 1)] = turned[b]
            out = unskewed([wide(x) for x in turned], keep)
            for b in range(5):
                key_band[h, rows, TILE * (t + b) : TILE * (t + b + 1)] = out[b].astype(bf16)
        part = dot(jnp.where(mine_t[h], do_t, 0), exp_ref[h])
        dv_t = part if dv_t is None else dv_t + part
        dq, dk, key_line, query_line = [], [], [], []
        for i in range(2):
            rows = slice(256 * i, 256 * (i + 1))
            band = slice(256 * i, 256 * i + 768)
            dq.append(dot(ds_ref[h, rows, :], k) + dot(query_band[h, rows, band], key_line_ref[band, :]))
            dk.append(dot(dst_ref[h, rows, :], q) + dot(key_band[h, rows, band], query_line_ref[band, :]))
            key_line.append(dot(jnp.where(mine_t[h], q_t[:, rows], 0), query_band[h, rows, band]))
            query_line.append(dot(jnp.where(mine_t[h], k_t[:, rows], 0), key_band[h, rows, band]))
        dqs.append(jnp.concatenate(dq, axis=0))
        dks.append(jnp.concatenate(dk, axis=0))
        key_lines.append(key_line)
        query_lines.append(query_line)
    size = q.shape[0]
    dq_ref[:size, :] = (jnp.where(mine[0], dqs[0], dqs[1]) * scale).astype(bf16)
    dk_ref[:size, :] = reverse((jnp.where(mine[0], dks[0], dks[1]) * scale).astype(bf16))
    dv_ref[...] = reverse(dv_t.T.astype(bf16))
    for lines, ref in ((key_lines, dk_ref), (query_lines, dq_ref)):
        first = lines[0][0] + lines[1][0]
        second = lines[0][1] + lines[1][1]
        whole = jnp.concatenate(
            [first[:, :256], first[:, 256:] + second[:, :512], second[:, 512:]], axis=1
        )
        ref[size:, :] = dot((whole * scale).astype(bf16), places_ref[...]).T.astype(bf16)
    width = both_t_ref.shape[0]
    grad_ref[:width, :] = dot(both_t_ref[...], dq_ref[...]).astype(bf16)
    grad_ref[width : 2 * width, :] = dot(both_t_ref[...], dk_ref[...]).astype(bf16)
    grad_ref[2 * width :, :] = dot(both_t_ref[:, :size], dv_ref[...]).astype(bf16)
    sums = [jnp.sum(wide(r[...]), axis=0, keepdims=True) for r in (dq_ref, dk_ref, dv_ref)]
    sums_ref[...] = jnp.concatenate(sums + [jnp.zeros((5, TILE), f32)], axis=0)


def attend_back(
    q,
    k,
    v,
    do,
    exps,
    inverse,
    mixed_full,
    key_line,
    query_line,
    places,
    both_t,
    first,
    count,
    into,
    size,
    start,
):
    rows, width = q.shape
    col = pl.BlockSpec((rows, TILE), lambda g: (0, first + g))
    line = pl.BlockSpec((2 * rows, TILE), lambda g: (0, first + g))
    both = pl.BlockSpec((2 * rows, TILE), lambda g: (0, g))
    more = [] if into is None else [into]
    return pl.pallas_call(
        attend_back_kernel,
        grid=(count,),
        in_specs=[
            col,
            col,
            col,
            col,
            pl.BlockSpec((2, rows, rows), lambda g: (first + g, 0, 0)),
            pl.BlockSpec((1, rows, TILE), lambda g: (first + g, 0, 0)),
            pl.BlockSpec((1, rows, TILE), lambda g: (first + g, 0, 0)),
            line,
            line,
            pl.BlockSpec((2 * rows, rows), lambda g: (0, 0)),
            pl.BlockSpec((width, 2 * rows), lambda g: (0, 0)),
        ]
        + [pl.BlockSpec(memory_space=pl.ANY) for _ in more],
        out_specs=[
            both,
            both,
            pl.BlockSpec((rows, TILE), lambda g: (0, g)),
            pl.BlockSpec((8, TILE), lambda g: (0, g)),
            pl.BlockSpec((3 * width, TILE), lambda g: (start + g, 0)),
        ],
        out_shape=[
            jax.ShapeDtypeStruct((2 * rows, count * TILE), bf16),
            jax.ShapeDtypeStruct((2 * rows, count * TILE), bf16),
            jax.ShapeDtypeStruct((rows, count * TILE), bf16),
            jax.ShapeDtypeStruct((8, count * TILE), f32),
            jax.ShapeDtypeStruct((size, TILE), bf16),
        ],
        input_output_aliases={11: 4} if more else {},
        scratch_shapes=[
            pltpu.VMEM((2, rows, rows), bf16),
            pltpu.VMEM((2, rows, rows), bf16),
            pltpu.VMEM((2, rows, 2 * rows), bf16),
            pltpu.VMEM((2, rows, 2 * rows), bf16),
        ],
        compiler_params=pltpu.CompilerParams(vmem_limit_bytes=VMEM),
        cost_estimate=pl.CostEstimate(
            flops=count * 4_000_000_000, bytes_accessed=count * 3_000_000, transcendentals=0
        ),
        name="attend_back",
    )(q, k, v, do, exps, inverse, mixed_full, key_line, query_line, places, both_t, *more)


def weight_copies(y, sources, targets, sems, chunk, chunks):
    win_hbm, wout_hbm = sources[:2]
    win_ref, wout_ref, far_in, far_out = targets
    n = far_in.shape[0] // 2
    half = far_out.shape[1] // 2
    lists = []
    for c in range(chunks):
        cols = slice(chunk * c, chunk * (c + 1))
        lists.append([(win_hbm.at[:, cols], win_ref.at[:, cols]), (wout_hbm.at[cols], wout_ref.at[cols])])
    mine = pl.ds(pl.multiple_of(y * half, 16), half)
    theirs = pl.ds(pl.multiple_of((1 - y) * half, 16), half)
    for k in range(2):
        part = slice(n * k, n * (k + 1))
        columns, first, second = sources[2 + 3 * k : 5 + 3 * k]
        lists.append(
            [
                (columns, far_in.at[part]),
                (first, far_out.at[part, mine]),
                (second, far_out.at[part, theirs]),
            ]
        )
    copies = []
    for i, pairs in enumerate(lists):
        copies.append(
            [pltpu.make_async_copy(a, b, sems.at[i, k]) for k, (a, b) in enumerate(pairs)]
        )
    return copies


def start(copies):
    for copy in copies:
        copy.start()


def wait(copies):
    for copy in copies:
        copy.wait()


def core_half_kernel(place_ref, bin_ref, win_hbm, wout_hbm, in_ref, out_ref, sems):
    units = in_ref.shape[1]
    width = win_hbm.shape[0]
    rows = pl.multiple_of((2 * place_ref[0] + place_ref[1]) * out_ref.shape[0], 16)

    def send(core):
        part = slice(units * core, units * (core + 1))
        copies = [
            pltpu.make_async_copy(wout_hbm.at[pl.ds(rows, out_ref.shape[0])], out_ref, sems.at[0]),
            pltpu.make_async_copy(win_hbm.at[:, part], in_ref.at[:width], sems.at[1]),
        ]
        start(copies)
        bias = jnp.broadcast_to(wide(bin_ref[...])[None, part], (16, units))
        in_ref[width:, :] = bias.astype(bf16)
        wait(copies)

    @pl.when(place_ref[0] == 0)
    def _():
        send(0)

    @pl.when(place_ref[0] != 0)
    def _():
        send(1)


def core_half(core, y, w_in, w_out, b_in):
    width, units = w_in.shape
    half = units // 2
    if half % TILE:
        place = core[0] * half
        bias = lax.dynamic_slice_in_dim(b_in, place, half, 0)
        columns = lax.dynamic_slice_in_dim(w_in, place, half, 1)
        columns = jnp.concatenate([columns, jnp.broadcast_to(bias, (16, half))], axis=0)
        return columns, lax.dynamic_slice_in_dim(w_out, place + y[0] * (half // 2), half // 2, 0)
    anywhere = pl.BlockSpec(memory_space=pl.ANY)
    vmem = pl.BlockSpec(memory_space=pltpu.VMEM)
    return pl.pallas_call(
        core_half_kernel,
        in_specs=[pl.BlockSpec(memory_space=pltpu.SMEM), vmem, anywhere, anywhere],
        out_specs=[vmem, vmem],
        out_shape=[low(width + 16, half), low(half // 2, width)],
        scratch_shapes=[pltpu.SemaphoreType.DMA((2,))],
        compiler_params=pltpu.CompilerParams(vmem_limit_bytes=VMEM),
        cost_estimate=pl.CostEstimate(flops=0, bytes_accessed=5_000_000, transcendentals=0),
        name="core_half",
    )(jnp.concatenate([core, y]), b_in, w_in, w_out)


def ffn_forward_kernel(
    h_ref,
    normed_hbm,
    cot_hbm,
    gain1_ref,
    shift1_ref,
    b_outer_ref,
    gain2_ref,
    shift2_ref,
    bin_ref,
    *refs,
    chunk,
    far_chunk,
):
    y, sources, refs = refs[0][0], refs[1:9], refs[9:]
    out_ref, dpre_ref, dbranch_ref, active_hbm, slope_hbm, far_slope_hbm, sums_ref = refs[:7]
    normed_ref, cot_ref, active_ref, slope_ref, far_slope_ref, total_ref = refs[7:13]
    targets, sems, sems2 = refs[13:17], refs[17], refs[18]
    far_in_ref, far_out_ref = targets[2:]
    rows, width = h_ref.shape
    chunks = active_ref.shape[1] // chunk
    far_count, _, units = far_in_ref.shape
    far_chunks = units // far_chunk
    weights = weight_copies(y, sources, targets, sems, chunk, chunks)
    others = [
        pltpu.make_async_copy(normed_hbm, normed_ref, sems2.at[0]),
        pltpu.make_async_copy(cot_hbm, cot_ref, sems2.at[1]),
    ]
    back = [
        pltpu.make_async_copy(active_ref, active_hbm, sems2.at[2]),
        pltpu.make_async_copy(slope_ref, slope_hbm, sems2.at[3]),
        pltpu.make_async_copy(far_slope_ref, far_slope_hbm, sems2.at[4]),
    ]
    for copies in weights:
        start(copies)
    start(others)
    b_in = wide(bin_ref[...])[None, :]

    def forward(w_in, b_in, w_out, active_at, slope_at, first):
        for r in range(0, rows, 256):
            part = slice(r, r + 256)
            active, slope = gelu_parts(dot(h_ref[part, :], w_in) + b_in)
            active = active.astype(bf16)
            if active_at is not None:
                active_ref[part, active_at] = active
            slope_at(part, slope.astype(bf16))
            product = dot(active, w_out)
            total_ref[part, :] = product if first else total_ref[part, :] + product

    for c in range(chunks):
        wait(weights[c])
        cols = slice(chunk * c, chunk * (c + 1))

        def put(part, value, cols=cols):
            slope_ref[part, cols] = value

        forward(targets[0][:, cols], b_in[:, cols], targets[1][cols, :], cols, put, c == 0)
    start(back[:2])
    wait(weights[chunks])
    wait(weights[chunks + 1])

    def far_step(s, carry):
        for c in range(far_chunks):
            cols = slice(far_chunk * c, far_chunk * (c + 1))

            def put(part, value, cols=cols):
                far_slope_ref[s, part, cols] = value

            bias = wide(far_in_ref[s, width : width + 1, cols])
            forward(far_in_ref[s, :width, cols], bias, far_out_ref[s, cols, :], None, put, False)
        return carry

    lax.fori_loop(0, far_count, far_step, 0)
    start(back[2:])
    wait(others)
    gain1, shift1, b_outer, gain2, shift2 = [
        wide(r[...])[None, :] for r in (gain1_ref, shift1_ref, b_outer_ref, gain2_ref, shift2_ref)
    ]
    sums = [jnp.zeros((1, width), f32) for _ in range(3)]
    for r in range(0, rows, TILE):
        part = slice(r, r + TILE)
        normed, root = ln_parts(normed_ref[part, :] * gain1 + shift1 + total_ref[part, :] + b_outer)
        out_ref[part, :] = normed * gain2 + shift2
        dy = wide(cot_ref[part, :])
        d = ln_back_rows(dy, normed, root, gain2)
        dpre_ref[part, :] = d
        low = d.astype(bf16)
        dbranch_ref[part, :] = low
        sums[0] += jnp.sum(dy * normed, axis=0, keepdims=True)
        sums[1] += jnp.sum(dy, axis=0, keepdims=True)
        sums[2] += jnp.sum(wide(low), axis=0, keepdims=True)
    sums_ref[...] = jnp.concatenate(sums + [jnp.zeros((5, width), f32)], axis=0)
    wait(back)


def ffn_backward_kernel(
    db_ref, normed_hbm, root_ref, dpre_ref, mixed_hbm, wo_hbm, gain_ref, *refs, chunk, far_chunk
):
    slope_hbm, far_slope_hbm = refs[:2]
    y, sources, refs = refs[2][0], refs[3:11], refs[11:]
    dinner_hbm, dres_ref, dmixed_ref, grad_ref, sums_ref = refs[:5]
    normed_ref, mixed_ref, wo_ref, dinner_ref, total_ref, dattn_ref = refs[5:11]
    slope_ref, far_slope_ref = refs[11:13]
    targets, sems, sems2 = refs[13:17], refs[17], refs[18]
    far_in_ref, far_out_ref = targets[2:]
    rows, width = db_ref.shape
    chunks = dinner_ref.shape[1] // chunk
    far_count, _, units = far_in_ref.shape
    far_chunks = units // far_chunk
    weights = weight_copies(y, sources, targets, sems, chunk, chunks)
    slopes = [
        pltpu.make_async_copy(slope_hbm, slope_ref, sems2.at[0]),
        pltpu.make_async_copy(far_slope_hbm, far_slope_ref, sems2.at[1]),
    ]
    others = [
        pltpu.make_async_copy(normed_hbm, normed_ref, sems2.at[2]),
        pltpu.make_async_copy(mixed_hbm, mixed_ref, sems2.at[3]),
        pltpu.make_async_copy(wo_hbm, wo_ref, sems2.at[4]),
    ]
    back = [pltpu.make_async_copy(dinner_ref, dinner_hbm, sems2.at[5])]
    start(weights[0])
    start(slopes[:1])
    for copies in weights[1:]:
        start(copies)
    start(slopes[1:])
    start(others)

    def backward(w_in, w_out, slope, keep, first):
        for r in range(0, rows, 256):
            part = slice(r, r + 256)
            d = (dot_nt(db_ref[part, :], w_out) * wide(slope(part))).astype(bf16)
            if keep is not None:
                keep(part, d)
            base = dpre_ref[part, :] if first else total_ref[part, :]
            total_ref[part, :] = base + dot_nt(d, w_in)

    wait(slopes[:1])
    for c in range(chunks):
        wait(weights[c])
        cols = slice(chunk * c, chunk * (c + 1))

        def keep(part, value, cols=cols):
            dinner_ref[part, cols] = value

        def slope(part, cols=cols):
            return slope_ref[part, cols]

        backward(targets[0][:, cols], targets[1][cols, :], slope, keep, c == 0)
    start(back)
    wait(weights[chunks])
    wait(weights[chunks + 1])
    wait(slopes[1:])

    def far_step(s, carry):
        for c in range(far_chunks):
            cols = slice(far_chunk * c, far_chunk * (c + 1))

            def slope(part, cols=cols):
                return far_slope_ref[s, part, cols]

            backward(far_in_ref[s, :width, cols], far_out_ref[s, cols, :], slope, None, False)
        return carry

    lax.fori_loop(0, far_count, far_step, 0)
    wait(others)
    gain = wide(gain_ref[...])[None, :]
    sums = [jnp.zeros((1, width), f32) for _ in range(3)]
    for r in range(0, rows, TILE):
        part = slice(r, r + TILE)
        dy = total_ref[part, :]
        normed = normed_ref[part, :]
        d = ln_back_rows(dy, normed, root_ref[part, 0:1], gain)
        dres_ref[part, :] = d
        low = d.astype(bf16)
        dattn_ref[part, :] = low
        dmixed_ref[part, :] = dot_nt(low, wo_ref[...]).astype(bf16)
        sums[0] += jnp.sum(dy * normed, axis=0, keepdims=True)
        sums[1] += jnp.sum(dy, axis=0, keepdims=True)
        sums[2] += jnp.sum(wide(low), axis=0, keepdims=True)
    sums_ref[...] = jnp.concatenate(sums + [jnp.zeros((5, width), f32)], axis=0)
    grad = dot(mixed_ref[...].T, dattn_ref[...]).astype(bf16)
    for i in range(2):
        grad_ref[width * i : width * (i + 1), :] = grad[:, CHUNK * i : CHUNK * (i + 1)]
    wait(back)


def low(*shape):
    return jax.ShapeDtypeStruct(shape, bf16)


def full(*shape):
    return jax.ShapeDtypeStruct(shape, f32)


def share_sizes(w_in, got):
    return min(2 * CHUNK, w_in.shape[1]), min(2 * CHUNK, got[0].shape[2])


def weight_scratch(w_in, w_out, got, chunk):
    n = got[0].shape[0]
    return [
        pltpu.VMEM(w_in.shape, bf16),
        pltpu.VMEM(w_out.shape, bf16),
        pltpu.VMEM((2 * n, *got[0].shape[1:]), bf16),
        pltpu.VMEM((2 * n, 2 * got[1].shape[1], got[1].shape[2]), bf16),
        pltpu.SemaphoreType.DMA((w_in.shape[1] // chunk + 2, 3)),
        pltpu.SemaphoreType.DMA((6,)),
    ]


def ffn_forward(h, normed, cot, vectors, b_in, y, w_in, w_out, got, other):
    rows, width = h.shape
    units = w_in.shape[1]
    far = 2 * got[0].shape[0]
    chunk, far_chunk = share_sizes(w_in, got)
    anywhere = pl.BlockSpec(memory_space=pl.ANY)
    vmem = pl.BlockSpec(memory_space=pltpu.VMEM)
    far_slope = (far, rows, got[0].shape[2])
    return pl.pallas_call(
        functools.partial(ffn_forward_kernel, chunk=chunk, far_chunk=far_chunk),
        in_specs=[vmem, anywhere, anywhere]
        + [vmem] * 6
        + [pl.BlockSpec(memory_space=pltpu.SMEM)]
        + [anywhere] * 8,
        out_specs=[vmem] * 3 + [anywhere] * 3 + [vmem],
        out_shape=[
            full(rows, width),
            full(rows, width),
            low(rows, width),
            low(rows, units),
            low(rows, units),
            low(*far_slope),
            full(8, width),
        ],
        scratch_shapes=[
            pltpu.VMEM((rows, width), f32),
            pltpu.VMEM((rows, width), bf16),
            pltpu.VMEM((rows, units), bf16),
            pltpu.VMEM((rows, units), bf16),
            pltpu.VMEM(far_slope, bf16),
            pltpu.VMEM((rows, width), f32),
            *weight_scratch(w_in, w_out, got, chunk),
        ],
        compiler_params=pltpu.CompilerParams(vmem_limit_bytes=VMEM),
        cost_estimate=pl.CostEstimate(
            flops=16 * rows * width * width, bytes_accessed=24_000_000, transcendentals=3_200_000
        ),
        name="ffn_forward",
    )(h, normed, cot, *vectors, b_in, y, w_in, w_out, *got, *other)


def ffn_backward(
    db, normed, root, dpre, mixed, w_output, gain, slope, far_slope, y, w_in, w_out, got, other
):
    rows, width = db.shape
    units = w_in.shape[1]
    chunk, far_chunk = share_sizes(w_in, got)
    anywhere = pl.BlockSpec(memory_space=pl.ANY)
    vmem = pl.BlockSpec(memory_space=pltpu.VMEM)
    return pl.pallas_call(
        functools.partial(ffn_backward_kernel, chunk=chunk, far_chunk=far_chunk),
        in_specs=[vmem, anywhere, vmem, vmem, anywhere, anywhere, vmem, anywhere, anywhere]
        + [pl.BlockSpec(memory_space=pltpu.SMEM)]
        + [anywhere] * 8,
        out_specs=[anywhere] + [vmem] * 4,
        out_shape=[
            low(rows, units),
            full(rows, width),
            low(rows, width),
            low(2 * width, CHUNK),
            full(8, width),
        ],
        scratch_shapes=[
            pltpu.VMEM((rows, width), f32),
            pltpu.VMEM((rows, width), bf16),
            pltpu.VMEM((width, width), bf16),
            pltpu.VMEM((rows, units), bf16),
            pltpu.VMEM((rows, width), f32),
            pltpu.VMEM((rows, width), bf16),
            pltpu.VMEM((rows, units), bf16),
            pltpu.VMEM(far_slope.shape, bf16),
            *weight_scratch(w_in, w_out, got, chunk),
        ],
        compiler_params=pltpu.CompilerParams(vmem_limit_bytes=VMEM),
        cost_estimate=pl.CostEstimate(
            flops=20 * rows * width * width, bytes_accessed=24_000_000, transcendentals=0
        ),
        name="ffn_backward",
    )(
        db,
        normed,
        root,
        dpre,
        mixed,
        w_output,
        gain,
        slope,
        far_slope,
        y,
        w_in,
        w_out,
        *got,
        *other,
    )


def ffn_grads_kernel(
    start_ref,
    bin_ref,
    h_hbm,
    db_hbm,
    active_hbm,
    dinner_hbm,
    far_h_hbm,
    far_db_hbm,
    win_hbm,
    wout_hbm,
    out_ref,
    h_ref,
    db_ref,
    active_ref,
    dinner_ref,
    far_h_ref,
    far_db_ref,
    win_ref,
    wout_ref,
    far_active_ref,
    far_slope_ref,
    far_dinner_ref,
    h_t,
    far_t,
    bias_ref,
    sems,
    *,
    chunks,
):
    units = chunks * CHUNK
    width = h_ref.shape[1]
    far = far_h_ref.shape[0]
    tail = 4 * CHUNK * chunks
    if win_hbm.shape[1] == units:
        part = slice(0, units)
    else:
        part = pl.ds(pl.multiple_of(start_ref[0] * CHUNK, CHUNK), units)
    copies = [
        pltpu.make_async_copy(source, target, sems.at[i])
        for i, (source, target) in enumerate(
            [
                (far_h_hbm, far_h_ref),
                (win_hbm.at[:, part], win_ref),
                (far_db_hbm, far_db_ref),
                (wout_hbm.at[part], wout_ref),
                (h_hbm, h_ref),
                (dinner_hbm.at[:, part], dinner_ref),
                (active_hbm.at[:, part], active_ref),
                (db_hbm, db_ref),
            ]
        )
    ]
    start(copies)
    bias_ref[...] = wide(bin_ref[...])[None, :]
    b_in = bias_ref[:, part]
    wait(copies[:2])
    for r in range(0, far, 256):
        rows = slice(r, r + 256)
        active, slope = gelu_parts(dot(far_h_ref[rows, :], win_ref[...]) + b_in)
        far_active_ref[rows, :] = active.astype(bf16)
        far_slope_ref[rows, :] = slope.astype(bf16)
    far_t[...] = far_h_ref[...].T
    wait(copies[2:4])
    bias = jnp.zeros((1, units), f32)
    for r in range(0, far, 256):
        rows = slice(r, r + 256)
        dinner = dot_nt(far_db_ref[rows, :], wout_ref[...]) * wide(far_slope_ref[rows, :])
        dinner = dinner.astype(bf16)
        far_dinner_ref[rows, :] = dinner
        bias = bias + jnp.sum(wide(dinner), axis=0, keepdims=True)
    wait(copies[4:6])
    h_t[...] = h_ref[...].T
    for r in range(0, width, 256):
        rows = slice(r, r + 256)
        grad = dot(h_t[rows, :], dinner_ref[...]) + dot(far_t[rows, :], far_dinner_ref[...])
        grad = grad.astype(bf16)
        for c in range(chunks):
            place = 4 * CHUNK * c + r
            out_ref[place : place + 256, :] = grad[:, CHUNK * c : CHUNK * (c + 1)]
    wait(copies[6:])
    for c in range(chunks):
        cols = slice(CHUNK * c, CHUNK * (c + 1))
        grad = dot(active_ref[:, cols].T, db_ref[...])
        grad = (grad + dot(far_active_ref[:, cols].T, far_db_ref[...])).astype(bf16)
        for k in range(2):
            place = 4 * CHUNK * c + (2 + k) * CHUNK
            out_ref[place : place + CHUNK, :] = grad[:, CHUNK * k : CHUNK * (k + 1)]
    bias = bias + jnp.sum(wide(dinner_ref[...]), axis=0, keepdims=True)
    out_ref[tail:, :] = jnp.zeros_like(out_ref[tail:, :])
    rows = [bias[:, CHUNK * c : CHUNK * (c + 1)] for c in range(chunks)]
    rows.append(jnp.zeros((16 - chunks, CHUNK), f32))
    out_ref[tail : tail + 16, :] = jnp.concatenate(rows, axis=0).astype(bf16)


def ffn_grads(h, db, active, dinner, far_h, far_db, w_in, b_in, w_out, start, chunks, extra):
    rows, width = h.shape
    units = chunks * CHUNK
    far = far_h.shape[0]
    anywhere = pl.BlockSpec(memory_space=pl.ANY)

    def scratch(r, w):
        return pltpu.VMEM((r, w), bf16)

    total = chunks * 4 * CHUNK + extra
    return pl.pallas_call(
        functools.partial(ffn_grads_kernel, chunks=chunks),
        in_specs=[pl.BlockSpec(memory_space=pltpu.SMEM), pl.BlockSpec(memory_space=pltpu.VMEM)]
        + [anywhere] * 8,
        out_specs=pl.BlockSpec(memory_space=pltpu.VMEM),
        out_shape=low(total, CHUNK),
        scratch_shapes=[
            scratch(rows, width),
            scratch(rows, width),
            scratch(rows, units),
            scratch(rows, units),
            scratch(far, width),
            scratch(far, width),
            scratch(width, units),
            scratch(units, width),
            scratch(far, units),
            scratch(far, units),
            scratch(far, units),
            scratch(width, rows),
            scratch(width, far),
            pltpu.VMEM((1, w_in.shape[1]), f32),
            pltpu.SemaphoreType.DMA((8,)),
        ],
        compiler_params=pltpu.CompilerParams(vmem_limit_bytes=VMEM),
        cost_estimate=pl.CostEstimate(
            flops=4 * (rows + 2 * far) * width * units,
            bytes_accessed=16_000_000,
            transcendentals=2 * far * units,
        ),
        name="ffn_grads",
    )(start, b_in, h, db, active, dinner, far_h, far_db, w_in, w_out)


def late_kernel(*refs, pieces, grads):
    dq_refs, dk_refs, sums_refs = [refs[pieces * i : pieces * (i + 1)] for i in range(3)]
    wq_ref, wk_ref, table_ref, gain_ref, sums1_ref, sums2_ref = refs[3 * pieces : 3 * pieces + 6]
    out_hbm, tail_ref, sem = refs[3 * pieces + 7 :]
    rows, width = table_ref.shape
    gain = wide(gain_ref[...])[None, :]
    dy = 0.0
    for parts, w_ref in ((dq_refs, wq_ref), (dk_refs, wk_ref)):
        place = 0
        for part in parts:
            dy = dy + dot_nt(part[...], w_ref[:, place : place + part.shape[1]])
            place += part.shape[1]
    normed, root = ln_parts(wide(table_ref[...]))
    table = ln_back_rows(dy, normed, root, gain).astype(bf16)
    vectors = jnp.concatenate(
        [
            sums1_ref[...],
            sums2_ref[...],
            jnp.concatenate([r[...] for r in sums_refs], axis=1),
            jnp.sum(dy * normed, axis=0, keepdims=True),
            jnp.sum(dy, axis=0, keepdims=True),
            jnp.zeros((6, width), f32),
        ],
        axis=0,
    ).astype(bf16)
    base = 0
    for block in (table, vectors):
        for i in range(width // TILE):
            tail_ref[base : base + block.shape[0], :] = block[:, TILE * i : TILE * (i + 1)]
            base += block.shape[0]
    tail_ref[base:, :] = jnp.zeros((tail_ref.shape[0] - base, TILE), bf16)
    copy = pltpu.make_async_copy(tail_ref, out_hbm.at[grads:], sem.at[0])
    copy.start()
    copy.wait()


def late_rows(rows, width):
    grads = 6 * width
    total = grads + (rows + 32) * (width // TILE)
    return grads, -(-total // 512) * 512


def late_sums(d_query, d_key, sums, w_query, w_key, table, gain, sums1, sums2, into):
    rows, width = table.shape
    pieces = len(d_query)
    grads, total = late_rows(rows, width)

    def fixed(shape):
        return pl.BlockSpec(shape, lambda i: (0, 0))

    def lower(x):
        return pl.BlockSpec((rows, x.shape[1]), lambda i: (1, 0))

    square = fixed((width, width))
    anywhere = pl.BlockSpec(memory_space=pl.ANY)
    return pl.pallas_call(
        functools.partial(late_kernel, pieces=pieces, grads=grads),
        grid=(1,),
        in_specs=[lower(x) for x in (*d_query, *d_key)]
        + [fixed(x.shape) for x in sums]
        + [square, square, fixed((rows, width)), pl.BlockSpec((width,), lambda i: (0,))]
        + [fixed((8, width))] * 2
        + [anywhere],
        out_specs=anywhere,
        out_shape=jax.ShapeDtypeStruct((total, TILE), bf16),
        input_output_aliases={3 * pieces + 6: 0},
        scratch_shapes=[pltpu.VMEM((total - grads, TILE), bf16), pltpu.SemaphoreType.DMA((1,))],
        compiler_params=pltpu.CompilerParams(vmem_limit_bytes=VMEM),
        cost_estimate=pl.CostEstimate(
            flops=1_300_000_000, bytes_accessed=12_000_000, transcendentals=0
        ),
        name="late_sums",
    )(*d_query, *d_key, *sums, w_query, w_key, table, gain, sums1, sums2, into)


def input_grad_kernel(*refs, pieces):
    parts = [refs[pieces * i : pieces * (i + 1)] for i in range(3)]
    weights = refs[3 * pieces : 3 * pieces + 3]
    res_ref, out_ref = refs[3 * pieces + 3 :]
    for r in range(0, res_ref.shape[0], 256):
        rows = slice(r, r + 256)
        total = res_ref[rows, :]
        for part, w_ref in zip(parts, weights, strict=True):
            place = 0
            for x in part:
                total = total + dot_nt(x[rows, :], w_ref[:, place : place + x.shape[1]])
                place += x.shape[1]
        out_ref[rows, :] = total


def input_gradient(d_query, d_key, d_value, w_query, w_key, w_value, d_residual):
    rows, width = d_residual.shape
    pieces = len(d_query)
    specs = [
        pl.BlockSpec((rows, x.shape[1]), lambda i: (0, 0)) for x in (*d_query, *d_key, *d_value)
    ]
    square = pl.BlockSpec((width, width), lambda i: (0, 0))
    full = pl.BlockSpec((rows, width), lambda i: (0, 0))
    return pl.pallas_call(
        functools.partial(input_grad_kernel, pieces=pieces),
        grid=(1,),
        in_specs=[*specs, square, square, square, full],
        out_specs=full,
        out_shape=jax.ShapeDtypeStruct((rows, width), f32),
        compiler_params=pltpu.CompilerParams(vmem_limit_bytes=VMEM),
        cost_estimate=pl.CostEstimate(
            flops=6 * rows * width * width, bytes_accessed=10_000_000, transcendentals=0
        ),
        name="input_gradient",
    )(*d_query, *d_key, *d_value, w_query, w_key, w_value, d_residual)


def ffn_result_kernel(core_ref, mine_hbm, other_hbm, *refs, chunks, columns):
    out_ref, refs = refs[0], refs[1:]
    bias_ref, (part_ref, sems) = (refs[0], refs[1:]) if columns else (None, refs)
    offset = 0 if columns else 2 * CHUNK

    def write(halves):
        copies = []
        for i, half in enumerate(halves):
            for c in range(chunks):
                place = 4 * CHUNK * c + offset
                copies.append((half.at[place : place + 2 * CHUNK], part_ref.at[i * chunks + c]))
            if columns:
                place = 4 * CHUNK * chunks
                copies.append((half.at[place : place + 16], part_ref.at[2 * chunks + i, :16]))
        copies = [pltpu.make_async_copy(a, b, sems.at[i]) for i, (a, b) in enumerate(copies)]
        start(copies)
        for i in range(2):
            for c in range(chunks):
                wait(copies[:1])
                copies = copies[1:]
                k = i * chunks + c
                cols = slice(CHUNK * k, CHUNK * (k + 1))
                if columns:
                    out_ref[:, cols] = wide(part_ref[k])
                else:
                    out_ref[cols, :CHUNK] = wide(part_ref[k, :CHUNK, :])
                    out_ref[cols, CHUNK:] = wide(part_ref[k, CHUNK:, :])
            if columns:
                wait(copies[:1])
                copies = copies[1:]
        if columns:
            rows = []
            for i in range(2):
                tail = wide(part_ref[2 * chunks + i, :16, :])
                rows = rows + [tail[c : c + 1, :] for c in range(chunks)]
            bias_ref[...] = jnp.concatenate(rows, axis=1).reshape(bias_ref.shape)

    @pl.when(core_ref[0] == 0)
    def _():
        write((mine_hbm, other_hbm))

    @pl.when(core_ref[0] != 0)
    def _():
        write((other_hbm, mine_hbm))


def ffn_result(core, mine, other, width, units, columns):
    chunks = units // CHUNK
    if chunks % 2:
        first = jnp.where(core == 0, mine, other)
        second = jnp.where(core == 0, other, mine)
        total = wide(jnp.concatenate([first, second], axis=0))
        parts = [total[4 * CHUNK * c : 4 * CHUNK * (c + 1)] for c in range(chunks)]
        if columns:
            return (
                jnp.concatenate([p[: 2 * CHUNK] for p in parts], axis=1),
                total[4 * CHUNK * chunks : 4 * CHUNK * chunks + chunks].reshape(units),
            )
        sides = [
            jnp.concatenate([p[(2 + i) * CHUNK : (3 + i) * CHUNK] for p in parts], axis=0)
            for i in range(2)
        ]
        return (jnp.concatenate(sides, axis=1),)
    anywhere = pl.BlockSpec(memory_space=pl.ANY)
    outs = [full(width, units), full(units)] if columns else [full(units, width)]
    return pl.pallas_call(
        functools.partial(ffn_result_kernel, chunks=chunks // 2, columns=columns),
        in_specs=[pl.BlockSpec(memory_space=pltpu.SMEM), anywhere, anywhere],
        out_shape=outs,
        scratch_shapes=[
            pltpu.VMEM((chunks + 2, 2 * CHUNK, CHUNK), bf16),
            pltpu.SemaphoreType.DMA((chunks + 2,)),
        ],
        compiler_params=pltpu.CompilerParams(vmem_limit_bytes=VMEM),
        cost_estimate=pl.CostEstimate(flops=0, bytes_accessed=8_000_000, transcendentals=0),
        name="ffn_result",
    )(core, mine, other)


def early_result_kernel(core_ref, mine_ref, other_ref, w_mine, w_other, q_ref, k_ref, v_ref, wo_ref):
    width = q_ref.shape[0]
    blocks = mine_ref.shape[0] // width

    def write(first, second, w_first, w_second):
        for b in range(2 * blocks):
            part = first if b < blocks else second
            value = wide(part[width * (b % blocks) : width * (b % blocks + 1), :])
            group, which = divmod(b, 3)
            (q_ref, k_ref, v_ref)[which][:, TILE * group : TILE * (group + 1)] = value
        for i, part in enumerate((w_first, w_second)):
            wo_ref[:, CHUNK * i : CHUNK * (i + 1)] = wide(part[...])

    @pl.when(core_ref[0] == 0)
    def _():
        write(mine_ref, other_ref, w_mine, w_other)

    @pl.when(core_ref[0] != 0)
    def _():
        write(other_ref, mine_ref, w_other, w_mine)


def early_result(core, mine, other, w_mine, w_other, width):
    smem = pl.BlockSpec(memory_space=pltpu.SMEM)
    vmem = pl.BlockSpec(memory_space=pltpu.VMEM)
    return pl.pallas_call(
        early_result_kernel,
        in_specs=[smem] + [vmem] * 4,
        out_shape=[full(width, width)] * 4,
        compiler_params=pltpu.CompilerParams(vmem_limit_bytes=VMEM),
        cost_estimate=pl.CostEstimate(flops=0, bytes_accessed=10_000_000, transcendentals=0),
        name="early_result",
    )(core, mine, other, w_mine, w_other)


def late_result_kernel(core_ref, mine_ref, other_ref, *refs):
    q_ref, k_ref, v_ref, table_ref = refs[3:7]
    vector_refs, all_ref = refs[7:-1], refs[-1]
    width, rows = q_ref.shape[0], table_ref.shape[0]
    groups = table_ref.shape[1] // TILE
    half = mine_ref.shape[0]

    def write(first, second):
        all_ref[:half, :] = first[...]
        all_ref[half:, :] = second[...]

    @pl.when(core_ref[0] == 0)
    def _():
        write(mine_ref, other_ref)

    @pl.when(core_ref[0] != 0)
    def _():
        write(other_ref, mine_ref)

    base = 0
    for g in range(2):
        for ref in (q_ref, k_ref, v_ref):
            ref[:, TILE * g : TILE * (g + 1)] = wide(all_ref[base : base + width, :])
            base += width
    for i in range(groups):
        table_ref[:, TILE * i : TILE * (i + 1)] = wide(all_ref[base : base + rows, :])
        base += rows
    parts = [wide(all_ref[base + 32 * i : base + 32 * (i + 1), :]) for i in range(groups)]
    vectors = jnp.concatenate(parts, axis=1)
    for place, ref in zip(VECTOR_ROWS, vector_refs, strict=True):
        ref[...] = vectors[place : place + 1, :].reshape(ref.shape)


def late_result(core, mine, other, grads, rows):
    width = grads[0].shape[0]
    groups = width // 256
    smem = pl.BlockSpec(memory_space=pltpu.SMEM)
    half = pl.BlockSpec(mine.shape, lambda i: (0, 0))
    anywhere = pl.BlockSpec(memory_space=pl.ANY)
    last = pl.BlockSpec((width, 256), lambda i: (0, groups - 1))
    vector = pl.BlockSpec((width,), lambda i: (0,))
    return pl.pallas_call(
        late_result_kernel,
        grid=(1,),
        in_specs=[smem, half, half] + [anywhere] * 3,
        out_specs=[last] * 3
        + [pl.BlockSpec((rows, width), lambda i: (0, 0))]
        + [vector] * len(VECTOR_ROWS),
        out_shape=[jax.ShapeDtypeStruct((width, width), f32)] * 3
        + [jax.ShapeDtypeStruct((rows, width), f32)]
        + [jax.ShapeDtypeStruct((width,), f32)] * len(VECTOR_ROWS),
        input_output_aliases={3: 0, 4: 1, 5: 2},
        scratch_shapes=[pltpu.VMEM((2 * mine.shape[0], TILE), bf16)],
        compiler_params=pltpu.CompilerParams(vmem_limit_bytes=VMEM),
        cost_estimate=pl.CostEstimate(flops=0, bytes_accessed=6_000_000, transcendentals=0),
        name="late_result",
    )(core, mine, other, *grads)


class Moves:
    def __init__(self, n_dp, n_mp):
        self.n_dp, self.n_mp = n_dp, n_mp
        self.dp = lax.axis_index("dp")
        self.mp = lax.axis_index("mp")
        self.core = self.dp % 2
        self.dp_bits = [("dp", 1 << b) for b in range(1, n_dp.bit_length() - 1)]
        self.mp_bits = [("mp", 1 << b) for b in range(n_mp.bit_length() - 1)]

    def swap(self, x, pair):
        perm = []
        for d in range(self.n_dp):
            for m in range(self.n_mp):
                axis, bit = pair[d % 2]
                dest = (d ^ bit, m) if axis == "dp" else (d, m ^ bit)
                perm.append((d * self.n_mp + m, dest[0] * self.n_mp + dest[1]))
        return lax.ppermute(x, BOTH, perm)

    def side(self, pair):
        values = [((self.dp if axis == "dp" else self.mp) // bit) % 2 for axis, bit in pair]
        return jnp.where(self.core == 0, values[0], values[1])

    def halves(self, x, pair):
        half = x[0].shape[0] // 2
        side = self.side(pair)

        def part(start):
            return whole([lax.dynamic_slice_in_dim(y, start * half, half, 0) for y in x])

        return part(1 - side), part(side)

    def scatter(self, x, pair):
        sent, kept = self.halves(x, pair)
        return kept, self.swap(sent, pair)

    def scatter_early(self, x, pair):
        half = x[0].shape[0] // 2
        side = self.side(pair)

        def part(x, start):
            return whole([lax.dynamic_slice_in_dim(y, start * half, half, 0) for y in x])

        sent = part(x, 1 - side)
        *x, sent = tie(*x, sent)
        return part(x, side), self.swap(sent, pair)

    def exchange(self, x, pair):
        x = whole(x)
        return x, self.swap(x, pair)

    def gather(self, x, pair):
        x = whole(x)
        other = self.swap(x, pair)
        side = self.side(pair)
        first = jnp.where(side == 0, x, other)
        second = jnp.where(side == 0, other, x)
        return (jnp.concatenate([first, second], axis=0),)

    def steps(self, first, second, joined):
        pairs = list(zip(first, second, strict=True))
        if joined:
            middle = [functools.partial(self.exchange, pair=pairs.pop())]
        else:
            middle = []
        down = [functools.partial(self.scatter, pair=pair) for pair in pairs]
        up = [functools.partial(self.gather, pair=pair) for pair in reversed(pairs)]
        return down + middle + up


def whole(x):
    return x[0] if len(x) == 1 else sum(wide(y) for y in x).astype(bf16)


def tie(*values):
    return lax.optimization_barrier(values)


def per_device(
    inputs,
    cotangent,
    w_query,
    b_query,
    w_key,
    b_key,
    w_value,
    b_value,
    w_output,
    b_output,
    norm1_gain,
    norm1_shift,
    w_inner,
    b_inner,
    w_outer,
    b_outer,
    norm2_gain,
    norm2_shift,
    rel_table,
    rel_gain,
    rel_shift,
    block_group,
    seq_lengths,
    *,
    n_dp,
    n_mp,
):
    rows, width = inputs.shape
    units = w_inner.shape[1]
    moves = Moves(n_dp, n_mp)
    core = ("dp", 1)

    def other_shares(x):
        shares = [x[None]]
        for bit in moves.mp_bits:
            shares = [jnp.concatenate(shares, axis=0)]
            shares.append(moves.swap(shares[0], (bit, bit)))
        return jnp.concatenate(shares, axis=0)[1:]

    core_id = moves.core.reshape(1).astype(jnp.int32)
    row_bit = moves.dp_bits[0]
    row_id = moves.side((row_bit, row_bit)).reshape(1).astype(jnp.int32)
    half_in, quarter_out = core_half(core_id, row_id, w_inner, w_outer, b_inner)
    got_out = other_shares(quarter_out)
    got_in = other_shares(half_in)

    line = bucket_line(rows // 2)
    place_ids = np.arange(rows)[None, :]
    forward = jnp.asarray(np.append(line, -1)[:, None] == place_ids).astype(bf16)
    backward = jnp.asarray(np.append(line[::-1], -1)[:, None] == place_ids).astype(bf16)
    query, key, value, key_line, key_line_back, query_line, both_t = pre(
        inputs,
        rel_table,
        rel_gain,
        rel_shift,
        w_query,
        b_query,
        w_key,
        b_key,
        w_value,
        b_value,
        forward,
        backward,
    )
    got_out, query = tie(got_out, query)
    got_row = moves.swap(got_out, (row_bit, row_bit))
    other_out = moves.swap(got_out, (core, core))
    mixed, exps, inverse, mixed_full, normed1, root1, hidden_low = attend(
        block_group,
        seq_lengths,
        query,
        key,
        value,
        key_line,
        query_line,
        w_output,
        b_output,
        inputs,
        norm1_gain,
        norm1_shift,
    )

    def far(x):
        whole = x
        for bit in moves.mp_bits:
            whole = jnp.concatenate([whole, moves.swap(whole, (bit, bit))], axis=0)
        return whole[rows:]

    got_in, got_row, other_out, hidden_low = tie(got_in, got_row, other_out, hidden_low)
    got = (got_in, got_out, got_row)
    other = (moves.swap(got_in, (core, core)), other_out, moves.swap(got_row, (core, core)))
    far_hidden = far(hidden_low)
    layer_out, d_pre2, d_branch, active, slope, far_slope, sums2 = ffn_forward(
        hidden_low,
        normed1,
        cotangent,
        (norm1_gain, norm1_shift, b_outer, norm2_gain, norm2_shift),
        b_inner,
        row_id,
        w_inner,
        w_outer,
        got,
        other,
    )
    far_branch = far(d_branch)
    d_inner, d_residual, d_mixed, grad_w_output, sums1 = ffn_backward(
        d_branch,
        normed1,
        root1,
        d_pre2,
        mixed,
        w_output,
        norm1_gain,
        slope,
        far_slope,
        row_id,
        w_inner,
        w_outer,
        got,
        other,
    )

    dp_bits, mp_bits = moves.dp_bits, moves.mp_bits
    pair = (core, core)
    ffn_steps = moves.steps(dp_bits, dp_bits[1:2] + dp_bits[:1] + dp_bits[2:], False)
    first, second = mp_bits + dp_bits, dp_bits[:1] + mp_bits + dp_bits[1:]
    early_steps = moves.steps(first, second, True)
    late_steps = moves.steps(first, second, True)
    shared = (exps, inverse, mixed_full, key_line_back, query_line, backward, both_t)
    pieces = []
    pairs = width // TILE

    def attention(d_mixed, first, count, *into):
        *piece, grad = attend_back(query, key, value, d_mixed, *shared, first, count, *into)
        pieces.append(piece)
        return grad

    output_sum = moves.scatter((grad_w_output,), pair)
    chunks = units // CHUNK
    near = (hidden_low, d_branch, active, d_inner, far_hidden, far_branch, w_inner, b_inner, w_outer)
    if chunks % 2 == 0:
        mine, theirs = core_id * (chunks // 2), (1 - core_id) * (chunks // 2)
        sent = ffn_grads(*near, theirs, chunks // 2, 4 * n_dp)
        sent, mine, output_sum = tie(sent, mine, output_sum)
        for bit in mp_bits:
            output_sum = moves.scatter(output_sum, (bit, bit))
        kept = ffn_grads(*near, mine, chunks // 2, 4 * n_dp)
        ffn_sum = (kept, moves.swap(sent, pair))
    else:
        ffn_sum = (ffn_grads(*near, 0 * core_id, chunks, 8 * n_dp),)
        ffn_sum = moves.scatter(ffn_sum, pair)
        for bit in mp_bits:
            output_sum = moves.scatter(output_sum, (bit, bit))
    ffn_rows = ffn_sum[0].shape[0]
    ffn_sum = (jnp.concatenate([whole(ffn_sum), whole(output_sum)], axis=0),)
    ffn_sum, d_mixed = tie(ffn_sum, d_mixed)

    ffn_sum = ffn_steps.pop(0)(ffn_sum)
    early_size = 3 * width * (pairs - 2)
    early = attention(d_mixed, 0, 2, None, early_size, 0)
    ffn_sum, d_mixed, early = tie(ffn_sum, d_mixed, early)
    ffn_sum = ffn_steps.pop(0)(ffn_sum)
    early = attention(d_mixed, 2, 1, early, early_size, 2)
    ffn_sum, d_mixed, early = tie(ffn_sum, d_mixed, early)
    ffn_sum = ffn_steps.pop(0)(ffn_sum)
    early = attention(d_mixed, 3, pairs - 5, early, early_size, 3)
    ffn_sum, d_mixed, early = tie(ffn_sum, d_mixed, early)
    ffn_sum = ffn_steps.pop(0)(ffn_sum)
    early = moves.scatter_early((early,), pair)
    late_size = late_rows(rows, width)[1]
    late = attention(d_mixed, pairs - 2, 1, None, late_size, 0)
    early, ffn_sum, late, d_mixed = tie(early, ffn_sum, late, d_mixed)
    ffn_sum = ffn_steps.pop(0)(ffn_sum)
    early = early_steps.pop(0)(early)
    late = attention(d_mixed, pairs - 1, 1, late, late_size, 1)
    early, ffn_sum, late, d_residual = tie(early, ffn_sum, late, d_residual)
    ffn_sum = ffn_steps.pop(0)(ffn_sum)
    early = early_steps.pop(0)(early)
    d_query, d_key, d_value, sums = zip(*pieces, strict=True)
    late = late_sums(
        d_query, d_key, sums, w_query, w_key, rel_table, rel_gain, sums1, sums2, late
    )
    late, d_residual = tie(late, d_residual)
    late = moves.scatter((late,), pair)
    input_grad = input_gradient(d_query, d_key, d_value, w_query, w_key, w_value, d_residual)
    late, early, ffn_sum, input_grad = tie(late, early, ffn_sum, input_grad)

    def last(x):
        return moves.exchange(x, pair)

    early_steps.append(last)
    late_steps.append(last)
    output_steps = [functools.partial(moves.gather, pair=(b, b)) for b in reversed(mp_bits)] + [last]
    for step in ffn_steps:
        ffn_sum = step(ffn_sum)
    ffn_sum = last(ffn_sum)
    output_sum = (ffn_sum[0][ffn_rows:],)
    early_out, ffn_in, ffn_out = None, None, None
    while late_steps:
        late = late_steps.pop(0)(late)
        done = ()
        if early_steps:
            early = early_steps.pop(0)(early)
        elif early_out is None and not output_steps:
            done = early_out = early_result(core_id, *early, *output_sum, width)
        if len(late_steps) % 2 == 1 and ffn_in is None:
            done = ffn_in = ffn_result(core_id, *ffn_sum, width, units, True)
        elif len(late_steps) % 2 == 1 and ffn_out is None:
            done = ffn_out = ffn_result(core_id, *ffn_sum, width, units, False)
        elif output_steps:
            output_sum = output_steps.pop(0)(output_sum)
        late, early, ffn_sum, output_sum, done = tie(late, early, ffn_sum, output_sum, done)
    for step in early_steps:
        early = step(early)
    for step in output_steps:
        output_sum = step(output_sum)
    if ffn_in is None:
        ffn_in = ffn_result(core_id, *ffn_sum, width, units, True)
    if ffn_out is None:
        ffn_out = ffn_result(core_id, *ffn_sum, width, units, False)
    if early_out is None:
        early_out = early_result(core_id, *early, *output_sum, width)
    *early_out, grad_w_output = early_out
    ffn_in, ffn_bias = ffn_in
    (ffn_out,) = ffn_out
    grad_q, grad_k, grad_v, table, *vectors = late_result(core_id, *late, early_out, rows)
    return (
        layer_out,
        input_grad,
        grad_q,
        vectors[0],
        grad_k,
        vectors[1],
        grad_v,
        vectors[2],
        grad_w_output,
        *vectors[3:6],
        ffn_in,
        ffn_bias,
        ffn_out,
        *vectors[6:9],
        table,
        *vectors[9:],
    )


def solution(mesh):
    n_dp, n_mp = mesh.shape["dp"], mesh.shape["mp"]

    def body(*args):
        return per_device(*args, n_dp=n_dp, n_mp=n_mp)

    split = P(("dp", "mp"), None)
    weights = [P()] * 10 + [P(None, "mp"), P("mp"), P("mp", None)] + [P()] * 6
    return jax.shard_map(
        body,
        mesh=mesh,
        in_specs=(split, split, *weights, P(("dp", "mp")), split),
        out_specs=(
            split,
            split,
            *([P()] * 10),
            P(None, "mp"),
            P("mp"),
            P("mp", None),
            *([P()] * 6),
        ),
        check_vma=False,
    )
```

```python
import functools
import math

import jax
import jax.numpy as jnp
import numpy as np
from jax import lax
from jax.experimental import pallas as pl
from jax.experimental.pallas import tpu as pltpu
from jax.sharding import PartitionSpec as P

HEADS = 12
EPS = 1e-06
LOG2E = 1.4426950408889634
TILE = 128
CHUNK = 384
VMEM = 60 * 1024 * 1024
VECTOR_ROWS = (16, 17, 18, 2, 0, 1, 10, 8, 9, 24, 25)
BOTH = ("dp", "mp")
f32 = jnp.float32
bf16 = jnp.bfloat16


def bucket_line(half_rows):
    table_rows = 2 * half_rows
    middle = half_rows // 2
    relative = table_rows - 1 - np.arange(2 * table_rows - 1)
    signed = np.sign(relative)
    absolute = np.where((relative < middle) & (relative > -middle), middle - 1, np.abs(relative))
    log_place = (
        np.ceil(np.log(absolute / middle) / np.log((table_rows - 1) / middle) * (middle - 1))
        + middle
    )
    placed = np.where(absolute <= middle, relative, log_place * signed)
    return (placed + half_rows).astype(np.int32)


def dot(a, b):
    return jnp.dot(a, b, preferred_element_type=f32)


def dot_nt(a, b):
    return lax.dot_general(a, b, (((1,), (1,)), ((), ())), preferred_element_type=f32)


def dot_tn(a, b):
    return lax.dot_general(a, b, (((0,), (0,)), ((), ())), preferred_element_type=f32)


def wide(v):
    return v.astype(f32)


def ln_parts(v):
    average = jnp.mean(v, axis=-1, keepdims=True)
    center = v - average
    root = lax.rsqrt(jnp.mean(center * center, axis=-1, keepdims=True) + EPS)
    return center * root, root


def ln_back_rows(dy, normed, root, gain):
    dn = dy * gain
    first = jnp.mean(dn, axis=-1, keepdims=True)
    second = jnp.mean(dn * normed, axis=-1, keepdims=True)
    return root * (dn - first - normed * second)


def gelu_parts(v):
    bell = jnp.exp(-0.5 * v * v)
    t = 1.0 / (1.0 + (0.3275911 * math.sqrt(0.5)) * jnp.abs(v))
    poly = t * (
        0.254829592
        + t * (-0.284496736 + t * (1.421413741 + t * (-1.453152027 + t * 1.061405429)))
    )
    tail = 0.5 * poly * bell
    below = jnp.where(v >= 0, 1.0 - tail, tail)
    return v * below, below + v * bell * (1.0 / math.sqrt(2.0 * math.pi))


def pre_kernel(
    x_ref,
    table_ref,
    gain_ref,
    shift_ref,
    wq_ref,
    bq_ref,
    wk_ref,
    bk_ref,
    wv_ref,
    bv_ref,
    forward_ref,
    backward_ref,
    q_ref,
    k_ref,
    v_ref,
    key_line_ref,
    key_back_ref,
    query_line_ref,
    both_t_ref,
    both_ref,
):
    rows = x_ref.shape[0]

    @pl.when(pl.program_id(0) == 0)
    def _():
        both_ref[:rows, :] = x_ref[...]
        normed, _ = ln_parts(wide(table_ref[...]))
        rel = normed * wide(gain_ref[...])[None, :] + wide(shift_ref[...])[None, :]
        both_ref[rows:, :] = rel.astype(bf16)
        both_t_ref[...] = both_ref[...].T

    def project(w_ref, b_ref, part):
        return (dot(both_ref[part, :], w_ref[...]) + wide(b_ref[...])[None, :]).astype(bf16)

    here, there = slice(0, rows), slice(rows, 2 * rows)
    q_ref[...] = project(wq_ref, bq_ref, here)
    k_ref[...] = project(wk_ref, bk_ref, here)
    v_ref[...] = project(wv_ref, bv_ref, here)
    pos_query = project(wq_ref, bq_ref, there)
    pos_key = project(wk_ref, bk_ref, there)
    key_line_ref[...] = dot(forward_ref[...], pos_key).astype(bf16)
    key_back_ref[...] = dot(backward_ref[...], pos_key).astype(bf16)
    query_line_ref[...] = dot(backward_ref[...], pos_query).astype(bf16)


def pre(x, table, gain, shift, w_q, b_q, w_k, b_k, w_v, b_v, forward, backward):
    rows, width = x.shape
    cut = 2 * TILE

    def fixed(r, w):
        return pl.BlockSpec((r, w), lambda c: (0, 0))

    whole = pl.BlockSpec((width,), lambda c: (0,))
    weight = pl.BlockSpec((width, cut), lambda c: (0, c))
    vector = pl.BlockSpec((cut,), lambda c: (c,))
    one = pl.BlockSpec((rows, cut), lambda c: (0, c))
    two = pl.BlockSpec((2 * rows, cut), lambda c: (0, c))
    return pl.pallas_call(
        pre_kernel,
        grid=(width // cut,),
        in_specs=[fixed(rows, width), fixed(rows, width), whole, whole]
        + [weight, vector] * 3
        + [fixed(2 * rows, rows)] * 2,
        out_specs=[one] * 3 + [two] * 3 + [fixed(width, 2 * rows)],
        out_shape=[jax.ShapeDtypeStruct((rows, width), bf16)] * 3
        + [jax.ShapeDtypeStruct((2 * rows, width), bf16)] * 3
        + [jax.ShapeDtypeStruct((width, 2 * rows), bf16)],
        scratch_shapes=[pltpu.VMEM((2 * rows, width), bf16)],
        compiler_params=pltpu.CompilerParams(vmem_limit_bytes=VMEM),
        cost_estimate=pl.CostEstimate(
            flops=5_500_000_000, bytes_accessed=14_000_000, transcendentals=0
        ),
        name="pre",
    )(x, table, gain, shift, w_q, b_q, w_k, b_k, w_v, b_v, forward, backward)


def skewed(x, keep):
    parts = [x[:, TILE * b : TILE * (b + 1)] for b in range(5)]
    return [
        pltpu.roll(jnp.where(keep, parts[b], parts[b + 1]), 1, 1, stride=1, stride_axis=0)
        for b in range(4)
    ]


def unskewed(tiles, keep):
    zero = jnp.zeros((TILE, TILE), f32)
    turned = [zero] + [pltpu.roll(t, 0, 1, stride=1, stride_axis=0) for t in tiles] + [zero]
    return [jnp.where(keep, turned[b + 1], turned[b]) for b in range(5)]


def flipped():
    rows = lax.broadcasted_iota(jnp.int32, (256, 256), 0)
    cols = lax.broadcasted_iota(jnp.int32, (256, 256), 1)
    return (rows + cols == 255).astype(f32).astype(bf16)


def attend_kernel(
    group_ref,
    lengths_ref,
    q_ref,
    k_ref,
    v_ref,
    key_line_ref,
    query_line_ref,
    wo_ref,
    bo_ref,
    x_ref,
    gain_ref,
    shift_ref,
    out_ref,
    exp_ref,
    inv_ref,
    full_ref,
    normed_ref,
    root_ref,
    h_ref,
    side_ref,
    bias_ref,
    key_side,
    query_side,
    content_ref,
):
    @pl.when(pl.program_id(0) == 0)
    def _():
        normed_ref[...] = wide(x_ref[...]) + wide(bo_ref[...])[None, :]
        size = bias_ref.shape[0]
        shift = size.bit_length() - 1 - group_ref[0]
        row = lax.broadcasted_iota(jnp.int32, (size, 1), 0)
        col = lax.broadcasted_iota(jnp.int32, (1, size), 1)
        owner = jnp.right_shift(col, shift)
        limit = jnp.zeros((1, size), jnp.int32)
        for slot in range(4):
            limit = jnp.where(owner == slot, lengths_ref[0, slot], limit)
        owner = jnp.where(col - jnp.left_shift(owner, shift) < limit, owner, -1)
        valid = jnp.right_shift(row, shift) == owner
        bias_ref[...] = jnp.where(valid, 0.0, -1e30).astype(f32)

    lane = lax.broadcasted_iota(jnp.int32, (1, TILE), 1)
    keep = (
        lax.broadcasted_iota(jnp.int32, (TILE, TILE), 0)
        + lax.broadcasted_iota(jnp.int32, (TILE, TILE), 1)
        >= TILE - 1
    )
    mine = [lane < 64, lane >= 64]
    scale = LOG2E / math.sqrt(192)
    flip = flipped()
    v_ones = jnp.concatenate([v_ref[...], jnp.ones(v_ref.shape, bf16)], axis=1)
    for h in range(2):
        km = jnp.where(mine[h], k_ref[...], 0)
        qm = jnp.where(mine[h], q_ref[...], 0)
        key_side[h] = dot_nt(km, query_line_ref[...])
        query_side[h] = dot_nt(qm, key_line_ref[...])
        content_ref[h] = dot_nt(qm, k_ref[...])
    for h in range(2):
        for t in range(4):
            start = 384 - TILE * t
            sk = skewed(key_side[h, TILE * t : TILE * (t + 1), start : start + 640], keep)
            for b in range(4):
                turned = wide(sk[b].astype(bf16).T)
                side_ref[h, TILE * b : TILE * (b + 1), TILE * t : TILE * (t + 1)] = turned
        for t in range(4):
            rows = slice(TILE * t, TILE * (t + 1))
            start = 384 - TILE * t
            near = skewed(query_side[h, rows, start : start + 640], keep)
            content = content_ref[h, rows, :]
            parts = []
            for b in range(4):
                cols = slice(TILE * b, TILE * (b + 1))
                total = content[:, cols] + near[b] + side_ref[h, rows, cols]
                parts.append(total * scale + bias_ref[rows, cols])
            top = jnp.max(
                jnp.maximum(jnp.maximum(parts[0], parts[1]), jnp.maximum(parts[2], parts[3])),
                axis=1,
                keepdims=True,
            )
            low = [jnp.exp2(p - top).astype(bf16) for p in parts]
            exps = jnp.concatenate(low, axis=1)
            exp_ref[h, rows, :] = jnp.concatenate(
                [dot(exps[:, 256:], flip).astype(bf16), dot(exps[:, :256], flip).astype(bf16)], axis=1
            )
            product = dot(exps, v_ones)
            inverse = 1.0 / product[:, TILE:]
            out = product[:, :TILE] * inverse
            if h == 0:
                inv_ref[0, rows, :] = inverse
                full_ref[0, rows, :] = out
            else:
                inv_ref[0, rows, :] = jnp.where(mine[0], inv_ref[0, rows, :], inverse)
                out = jnp.where(mine[0], full_ref[0, rows, :], out)
                full_ref[0, rows, :] = out
                out_ref[rows, :] = out.astype(bf16)
    normed_ref[...] += dot(out_ref[...], wo_ref[...])

    @pl.when(pl.program_id(0) == pl.num_programs(0) - 1)
    def _():
        gain, shift = wide(gain_ref[...])[None, :], wide(shift_ref[...])[None, :]
        for r in range(0, h_ref.shape[0], TILE):
            rows = slice(r, r + TILE)
            normed, root = ln_parts(normed_ref[rows, :])
            normed_ref[rows, :] = normed
            root_ref[rows, :] = jnp.broadcast_to(root, (TILE, TILE))
            h_ref[rows, :] = (normed * gain + shift).astype(bf16)


def attend(group, lengths, q, k, v, key_line, query_line, w_output, b_output, x, gain, shift):
    rows, width = q.shape
    pairs = width // TILE
    col = pl.BlockSpec((rows, TILE), lambda g: (0, g))
    line = pl.BlockSpec((2 * rows, TILE), lambda g: (0, g))
    scalars = pl.BlockSpec(memory_space=pltpu.SMEM)
    full = pl.BlockSpec((rows, width), lambda g: (0, 0))
    vector = pl.BlockSpec((width,), lambda g: (0,))
    return pl.pallas_call(
        attend_kernel,
        grid=(pairs,),
        in_specs=[scalars, scalars, col, col, col, line, line]
        + [pl.BlockSpec((TILE, width), lambda g: (g, 0)), vector, full, vector, vector],
        out_specs=[
            col,
            pl.BlockSpec((2, rows, rows), lambda g: (g, 0, 0)),
            pl.BlockSpec((1, rows, TILE), lambda g: (g, 0, 0)),
            pl.BlockSpec((1, rows, TILE), lambda g: (g, 0, 0)),
            full,
            pl.BlockSpec((rows, TILE), lambda g: (0, 0)),
            full,
        ],
        out_shape=[
            jax.ShapeDtypeStruct((rows, width), bf16),
            jax.ShapeDtypeStruct((2 * pairs, rows, rows), bf16),
            jax.ShapeDtypeStruct((pairs, rows, TILE), f32),
            jax.ShapeDtypeStruct((pairs, rows, TILE), f32),
            jax.ShapeDtypeStruct((rows, width), f32),
            jax.ShapeDtypeStruct((rows, TILE), f32),
            jax.ShapeDtypeStruct((rows, width), bf16),
        ],
        scratch_shapes=[
            pltpu.VMEM((2, rows, rows), f32),
            pltpu.VMEM((rows, rows), f32),
            pltpu.VMEM((2, rows, 2 * rows), f32),
            pltpu.VMEM((2, rows, 2 * rows), f32),
            pltpu.VMEM((2, rows, rows), f32),
        ],
        compiler_params=pltpu.CompilerParams(vmem_limit_bytes=VMEM),
        cost_estimate=pl.CostEstimate(
            flops=18_000_000_000, bytes_accessed=16_000_000, transcendentals=3_200_000
        ),
        name="attend",
    )(group, lengths, q, k, v, key_line, query_line, w_output, b_output, x, gain, shift)


def attend_back_kernel(
    q_ref,
    k_ref,
    v_ref,
    do_ref,
    exp_ref,
    inv_ref,
    full_ref,
    key_line_ref,
    query_line_ref,
    places_ref,
    both_t_ref,
    *refs,
):
    dq_ref, dk_ref, dv_ref, sums_ref, grad_ref, *refs = refs[-9:]
    attend_back_pair(
        q_ref,
        k_ref,
        v_ref,
        do_ref,
        exp_ref,
        inv_ref,
        full_ref,
        key_line_ref,
        query_line_ref,
        places_ref,
        both_t_ref,
        dq_ref,
        dk_ref,
        dv_ref,
        sums_ref,
        grad_ref,
        *refs,
    )


def attend_back_pair(
    q_ref,
    k_ref,
    v_ref,
    do_ref,
    exp_ref,
    inv_ref,
    full_ref,
    key_line_ref,
    query_line_ref,
    places_ref,
    both_t_ref,
    dq_ref,
    dk_ref,
    dv_ref,
    sums_ref,
    grad_ref,
    ds_ref,
    dst_ref,
    query_band,
    key_band,
):
    @pl.when(pl.program_id(0) == 0)
    def _():
        query_band[...] = jnp.zeros_like(query_band)
        key_band[...] = jnp.zeros_like(key_band)

    scale = 1.0 / math.sqrt(192)
    lane = lax.broadcasted_iota(jnp.int32, (1, TILE), 1)
    sub = lax.broadcasted_iota(jnp.int32, (TILE, 1), 0)
    keep = lax.broadcasted_iota(jnp.int32, (TILE, TILE), 1) >= lax.broadcasted_iota(
        jnp.int32, (TILE, TILE), 0
    )
    mine = [lane < 64, lane >= 64]
    mine_t = [sub < 64, sub >= 64]
    flip = flipped()

    def reverse(x):
        return jnp.concatenate([dot(flip, x[256:]), dot(flip, x[:256])], axis=0).astype(bf16)

    q = q_ref[...]
    k = reverse(k_ref[...])
    v = reverse(v_ref[...])
    q_t = q.T
    k_t = k.T
    do = (wide(do_ref[...]) * inv_ref[0]).astype(bf16)
    do_t = do.T
    share = wide(do) * full_ref[0]
    high = share.astype(bf16)
    rest = (share - wide(high)).astype(bf16)
    row = lax.broadcasted_iota(jnp.int32, (256, 256), 0) % TILE // 64
    ones = (row == lax.broadcasted_iota(jnp.int32, (256, 256), 1) // TILE).astype(f32).astype(bf16)
    means = dot(jnp.concatenate([high, rest], axis=1), ones)
    dv_t = None
    dqs, dks, key_lines, query_lines = [], [], [], []
    for h in range(2):
        dom = jnp.where(mine[h], do, 0)
        for t in range(4):
            rows = slice(TILE * t, TILE * (t + 1))
            dp = dot_nt(dom[rows], v)
            mean = means[rows, TILE * h : TILE * (h + 1)]
            ds = []
            for b in range(4):
                cols = slice(TILE * b, TILE * (b + 1))
                ds.append(wide(exp_ref[h, rows, cols]) * (dp[:, cols] - mean))
                ds_ref[h, rows, cols] = ds[b].astype(bf16)
            out = unskewed(ds, keep)
            for b in range(5):
                query_band[h, rows, TILE * (t + b) : TILE * (t + b + 1)] = out[b].astype(bf16)
        for t in range(4):
            rows = slice(TILE * t, TILE * (t + 1))
            turned = [ds_ref[h, TILE * b : TILE * (b + 1), rows].T for b in range(4)]
            for b in range(4):
                dst_ref[h, rows, TILE * b : TILE * (b + 1)] = turned[b]
            out = unskewed([wide(x) for x in turned], keep)
            for b in range(5):
                key_band[h, rows, TILE * (t + b) : TILE * (t + b + 1)] = out[b].astype(bf16)
        part = dot(jnp.where(mine_t[h], do_t, 0), exp_ref[h])
        dv_t = part if dv_t is None else dv_t + part
        dq, dk, key_line, query_line = [], [], [], []
        for i in range(2):
            rows = slice(256 * i, 256 * (i + 1))
            band = slice(256 * i, 256 * i + 768)
            dq.append(dot(ds_ref[h, rows, :], k) + dot(query_band[h, rows, band], key_line_ref[band, :]))
            dk.append(dot(dst_ref[h, rows, :], q) + dot(key_band[h, rows, band], query_line_ref[band, :]))
            key_line.append(dot(jnp.where(mine_t[h], q_t[:, rows], 0), query_band[h, rows, band]))
            query_line.append(dot(jnp.where(mine_t[h], k_t[:, rows], 0), key_band[h, rows, band]))
        dqs.append(jnp.concatenate(dq, axis=0))
        dks.append(jnp.concatenate(dk, axis=0))
        key_lines.append(key_line)
        query_lines.append(query_line)
    size = q.shape[0]
    dq_ref[:size, :] = (jnp.where(mine[0], dqs[0], dqs[1]) * scale).astype(bf16)
    dk_ref[:size, :] = reverse((jnp.where(mine[0], dks[0], dks[1]) * scale).astype(bf16))
    dv_ref[...] = reverse(dv_t.T.astype(bf16))
    for lines, ref in ((key_lines, dk_ref), (query_lines, dq_ref)):
        first = lines[0][0] + lines[1][0]
        second = lines[0][1] + lines[1][1]
        whole = jnp.concatenate(
            [first[:, :256], first[:, 256:] + second[:, :512], second[:, 512:]], axis=1
        )
        ref[size:, :] = dot((whole * scale).astype(bf16), places_ref[...]).T.astype(bf16)
    width = both_t_ref.shape[0]
    grad_ref[:width, :] = dot(both_t_ref[...], dq_ref[...]).astype(bf16)
    grad_ref[width : 2 * width, :] = dot(both_t_ref[...], dk_ref[...]).astype(bf16)
    grad_ref[2 * width :, :] = dot(both_t_ref[:, :size], dv_ref[...]).astype(bf16)
    sums = [jnp.sum(wide(r[...]), axis=0, keepdims=True) for r in (dq_ref, dk_ref, dv_ref)]
    sums_ref[...] = jnp.concatenate(sums + [jnp.zeros((5, TILE), f32)], axis=0)


def attend_back(
    q,
    k,
    v,
    do,
    exps,
    inverse,
    mixed_full,
    key_line,
    query_line,
    places,
    both_t,
    first,
    count,
    into,
    size,
    start,
):
    rows, width = q.shape
    col = pl.BlockSpec((rows, TILE), lambda g: (0, first + g))
    line = pl.BlockSpec((2 * rows, TILE), lambda g: (0, first + g))
    both = pl.BlockSpec((2 * rows, TILE), lambda g: (0, g))
    more = [] if into is None else [into]
    return pl.pallas_call(
        attend_back_kernel,
        grid=(count,),
        in_specs=[
            col,
            col,
            col,
            col,
            pl.BlockSpec((2, rows, rows), lambda g: (first + g, 0, 0)),
            pl.BlockSpec((1, rows, TILE), lambda g: (first + g, 0, 0)),
            pl.BlockSpec((1, rows, TILE), lambda g: (first + g, 0, 0)),
            line,
            line,
            pl.BlockSpec((2 * rows, rows), lambda g: (0, 0)),
            pl.BlockSpec((width, 2 * rows), lambda g: (0, 0)),
        ]
        + [pl.BlockSpec(memory_space=pl.ANY) for _ in more],
        out_specs=[
            both,
            both,
            pl.BlockSpec((rows, TILE), lambda g: (0, g)),
            pl.BlockSpec((8, TILE), lambda g: (0, g)),
            pl.BlockSpec((3 * width, TILE), lambda g: (start + g, 0)),
        ],
        out_shape=[
            jax.ShapeDtypeStruct((2 * rows, count * TILE), bf16),
            jax.ShapeDtypeStruct((2 * rows, count * TILE), bf16),
            jax.ShapeDtypeStruct((rows, count * TILE), bf16),
            jax.ShapeDtypeStruct((8, count * TILE), f32),
            jax.ShapeDtypeStruct((size, TILE), bf16),
        ],
        input_output_aliases={11: 4} if more else {},
        scratch_shapes=[
            pltpu.VMEM((2, rows, rows), bf16),
            pltpu.VMEM((2, rows, rows), bf16),
            pltpu.VMEM((2, rows, 2 * rows), bf16),
            pltpu.VMEM((2, rows, 2 * rows), bf16),
        ],
        compiler_params=pltpu.CompilerParams(vmem_limit_bytes=VMEM),
        cost_estimate=pl.CostEstimate(
            flops=count * 4_000_000_000, bytes_accessed=count * 3_000_000, transcendentals=0
        ),
        name="attend_back",
    )(q, k, v, do, exps, inverse, mixed_full, key_line, query_line, places, both_t, *more)


def weight_copies(y, sources, targets, sems, chunk, chunks):
    win_hbm, wout_hbm = sources[:2]
    win_ref, wout_ref, far_in, far_out = targets
    n = far_in.shape[0] // 2
    half = far_out.shape[1] // 2
    lists = []
    for c in range(chunks):
        cols = slice(chunk * c, chunk * (c + 1))
        lists.append([(win_hbm.at[:, cols], win_ref.at[:, cols]), (wout_hbm.at[cols], wout_ref.at[cols])])
    mine = pl.ds(pl.multiple_of(y * half, 16), half)
    theirs = pl.ds(pl.multiple_of((1 - y) * half, 16), half)
    for k in range(2):
        part = slice(n * k, n * (k + 1))
        columns, first, second = sources[2 + 3 * k : 5 + 3 * k]
        lists.append(
            [
                (columns, far_in.at[part]),
                (first, far_out.at[part, mine]),
                (second, far_out.at[part, theirs]),
            ]
        )
    copies = []
    for i, pairs in enumerate(lists):
        copies.append(
            [pltpu.make_async_copy(a, b, sems.at[i, k]) for k, (a, b) in enumerate(pairs)]
        )
    return copies


def start(copies):
    for copy in copies:
        copy.start()


def wait(copies):
    for copy in copies:
        copy.wait()


def core_half_kernel(place_ref, y_ref, bin_ref, win_hbm, wout_hbm, in_ref, out_ref, sems):
    units = in_ref.shape[1]
    width = win_hbm.shape[0]
    rows = pl.multiple_of((2 * place_ref[0] + y_ref[0]) * out_ref.shape[0], 16)

    def send(core):
        part = slice(units * core, units * (core + 1))
        copies = [
            pltpu.make_async_copy(wout_hbm.at[pl.ds(rows, out_ref.shape[0])], out_ref, sems.at[0]),
            pltpu.make_async_copy(win_hbm.at[:, part], in_ref.at[:width], sems.at[1]),
        ]
        start(copies)
        bias = jnp.broadcast_to(wide(bin_ref[...])[None, part], (16, units))
        in_ref[width:, :] = bias.astype(bf16)
        wait(copies)

    @pl.when(place_ref[0] == 0)
    def _():
        send(0)

    @pl.when(place_ref[0] != 0)
    def _():
        send(1)


def core_half(core, y, w_in, w_out, b_in):
    width, units = w_in.shape
    half = units // 2
    if half % TILE:
        place = core[0] * half
        bias = lax.dynamic_slice_in_dim(b_in, place, half, 0)
        columns = lax.dynamic_slice_in_dim(w_in, place, half, 1)
        columns = jnp.concatenate([columns, jnp.broadcast_to(bias, (16, half))], axis=0)
        return columns, lax.dynamic_slice_in_dim(w_out, place + y[0] * (half // 2), half // 2, 0)
    anywhere = pl.BlockSpec(memory_space=pl.ANY)
    vmem = pl.BlockSpec(memory_space=pltpu.VMEM)
    return pl.pallas_call(
        core_half_kernel,
        in_specs=[pl.BlockSpec(memory_space=pltpu.SMEM)] * 2 + [vmem, anywhere, anywhere],
        out_specs=[vmem, vmem],
        out_shape=[low(width + 16, half), low(half // 2, width)],
        scratch_shapes=[pltpu.SemaphoreType.DMA((2,))],
        compiler_params=pltpu.CompilerParams(vmem_limit_bytes=VMEM),
        cost_estimate=pl.CostEstimate(flops=0, bytes_accessed=5_000_000, transcendentals=0),
        name="core_half",
    )(core, y, b_in, w_in, w_out)


def ffn_forward_kernel(
    h_ref,
    normed_hbm,
    cot_hbm,
    gain1_ref,
    shift1_ref,
    b_outer_ref,
    gain2_ref,
    shift2_ref,
    bin_ref,
    *refs,
    chunk,
    far_chunk,
):
    y, sources, refs = refs[0][0], refs[1:9], refs[9:]
    out_ref, dpre_ref, dbranch_ref, active_hbm, slope_hbm, far_slope_hbm, sums_ref = refs[:7]
    normed_ref, cot_ref, active_ref, slope_ref, far_slope_ref, total_ref = refs[7:13]
    targets, sems, sems2 = refs[13:17], refs[17], refs[18]
    far_in_ref, far_out_ref = targets[2:]
    rows, width = h_ref.shape
    chunks = active_ref.shape[1] // chunk
    far_count, _, units = far_in_ref.shape
    far_chunks = units // far_chunk
    weights = weight_copies(y, sources, targets, sems, chunk, chunks)
    others = [
        pltpu.make_async_copy(normed_hbm, normed_ref, sems2.at[0]),
        pltpu.make_async_copy(cot_hbm, cot_ref, sems2.at[1]),
    ]
    back = [
        pltpu.make_async_copy(active_ref, active_hbm, sems2.at[2]),
        pltpu.make_async_copy(slope_ref, slope_hbm, sems2.at[3]),
        pltpu.make_async_copy(far_slope_ref, far_slope_hbm, sems2.at[4]),
    ]
    for copies in weights:
        start(copies)
    start(others)
    b_in = wide(bin_ref[...])[None, :]

    def forward(w_in, b_in, w_out, active_at, slope_at, first):
        for r in range(0, rows, 256):
            part = slice(r, r + 256)
            active, slope = gelu_parts(dot(h_ref[part, :], w_in) + b_in)
            active = active.astype(bf16)
            if active_at is not None:
                active_ref[part, active_at] = active
            slope_at(part, slope.astype(bf16))
            product = dot(active, w_out)
            total_ref[part, :] = product if first else total_ref[part, :] + product

    for c in range(chunks):
        wait(weights[c])
        cols = slice(chunk * c, chunk * (c + 1))

        def put(part, value, cols=cols):
            slope_ref[part, cols] = value

        forward(targets[0][:, cols], b_in[:, cols], targets[1][cols, :], cols, put, c == 0)
    start(back[:2])
    wait(weights[chunks])
    wait(weights[chunks + 1])

    def far_step(s, carry):
        for c in range(far_chunks):
            cols = slice(far_chunk * c, far_chunk * (c + 1))

            def put(part, value, cols=cols):
                far_slope_ref[s, part, cols] = value

            bias = wide(far_in_ref[s, width : width + 1, cols])
            forward(far_in_ref[s, :width, cols], bias, far_out_ref[s, cols, :], None, put, False)
        return carry

    lax.fori_loop(0, far_count, far_step, 0)
    start(back[2:])
    wait(others)
    gain1, shift1, b_outer, gain2, shift2 = [
        wide(r[...])[None, :] for r in (gain1_ref, shift1_ref, b_outer_ref, gain2_ref, shift2_ref)
    ]
    sums = [jnp.zeros((1, width), f32) for _ in range(3)]
    for r in range(0, rows, TILE):
        part = slice(r, r + TILE)
        normed, root = ln_parts(normed_ref[part, :] * gain1 + shift1 + total_ref[part, :] + b_outer)
        out_ref[part, :] = normed * gain2 + shift2
        dy = wide(cot_ref[part, :])
        d = ln_back_rows(dy, normed, root, gain2)
        dpre_ref[part, :] = d
        low = d.astype(bf16)
        dbranch_ref[part, :] = low
        sums[0] += jnp.sum(dy * normed, axis=0, keepdims=True)
        sums[1] += jnp.sum(dy, axis=0, keepdims=True)
        sums[2] += jnp.sum(wide(low), axis=0, keepdims=True)
    sums_ref[...] = jnp.concatenate(sums + [jnp.zeros((5, width), f32)], axis=0)
    wait(back)


def ffn_backward_kernel(
    db_ref, normed_hbm, root_ref, dpre_ref, mixed_hbm, wo_hbm, gain_ref, *refs, chunk, far_chunk
):
    slope_hbm, far_slope_hbm = refs[:2]
    y, sources, refs = refs[2][0], refs[3:11], refs[11:]
    dinner_hbm, dres_ref, dmixed_ref, grad_ref, sums_ref = refs[:5]
    normed_ref, mixed_ref, wo_ref, dinner_ref, total_ref, dattn_ref = refs[5:11]
    slope_ref, far_slope_ref = refs[11:13]
    targets, sems, sems2 = refs[13:17], refs[17], refs[18]
    far_in_ref, far_out_ref = targets[2:]
    rows, width = db_ref.shape
    chunks = dinner_ref.shape[1] // chunk
    far_count, _, units = far_in_ref.shape
    far_chunks = units // far_chunk
    weights = weight_copies(y, sources, targets, sems, chunk, chunks)
    slopes = [
        pltpu.make_async_copy(slope_hbm, slope_ref, sems2.at[0]),
        pltpu.make_async_copy(far_slope_hbm, far_slope_ref, sems2.at[1]),
    ]
    others = [
        pltpu.make_async_copy(normed_hbm, normed_ref, sems2.at[2]),
        pltpu.make_async_copy(mixed_hbm, mixed_ref, sems2.at[3]),
        pltpu.make_async_copy(wo_hbm, wo_ref, sems2.at[4]),
    ]
    back = [pltpu.make_async_copy(dinner_ref, dinner_hbm, sems2.at[5])]
    start(weights[0])
    start(slopes[:1])
    for copies in weights[1:]:
        start(copies)
    start(slopes[1:])
    start(others)

    def backward(w_in, w_out, slope, keep, first):
        for r in range(0, rows, 256):
            part = slice(r, r + 256)
            d = (dot_nt(db_ref[part, :], w_out) * wide(slope(part))).astype(bf16)
            if keep is not None:
                keep(part, d)
            base = dpre_ref[part, :] if first else total_ref[part, :]
            total_ref[part, :] = base + dot_nt(d, w_in)

    wait(slopes[:1])
    for c in range(chunks):
        wait(weights[c])
        cols = slice(chunk * c, chunk * (c + 1))

        def keep(part, value, cols=cols):
            dinner_ref[part, cols] = value

        def slope(part, cols=cols):
            return slope_ref[part, cols]

        backward(targets[0][:, cols], targets[1][cols, :], slope, keep, c == 0)
    start(back)
    wait(weights[chunks])
    wait(weights[chunks + 1])
    wait(slopes[1:])

    def far_step(s, carry):
        for c in range(far_chunks):
            cols = slice(far_chunk * c, far_chunk * (c + 1))

            def slope(part, cols=cols):
                return far_slope_ref[s, part, cols]

            backward(far_in_ref[s, :width, cols], far_out_ref[s, cols, :], slope, None, False)
        return carry

    lax.fori_loop(0, far_count, far_step, 0)
    wait(others)
    gain = wide(gain_ref[...])[None, :]
    sums = [jnp.zeros((1, width), f32) for _ in range(3)]
    for r in range(0, rows, TILE):
        part = slice(r, r + TILE)
        dy = total_ref[part, :]
        normed = normed_ref[part, :]
        d = ln_back_rows(dy, normed, root_ref[part, 0:1], gain)
        dres_ref[part, :] = d
        low = d.astype(bf16)
        dattn_ref[part, :] = low
        dmixed_ref[part, :] = dot_nt(low, wo_ref[...]).astype(bf16)
        sums[0] += jnp.sum(dy * normed, axis=0, keepdims=True)
        sums[1] += jnp.sum(dy, axis=0, keepdims=True)
        sums[2] += jnp.sum(wide(low), axis=0, keepdims=True)
    sums_ref[...] = jnp.concatenate(sums + [jnp.zeros((5, width), f32)], axis=0)
    grad = dot(mixed_ref[...].T, dattn_ref[...]).astype(bf16)
    for i in range(2):
        grad_ref[width * i : width * (i + 1), :] = grad[:, CHUNK * i : CHUNK * (i + 1)]
    wait(back)


def low(*shape):
    return jax.ShapeDtypeStruct(shape, bf16)


def full(*shape):
    return jax.ShapeDtypeStruct(shape, f32)


def share_sizes(w_in, got):
    return min(2 * CHUNK, w_in.shape[1]), min(2 * CHUNK, got[0].shape[2])


def weight_scratch(w_in, w_out, got, chunk):
    n = got[0].shape[0]
    return [
        pltpu.VMEM(w_in.shape, bf16),
        pltpu.VMEM(w_out.shape, bf16),
        pltpu.VMEM((2 * n, *got[0].shape[1:]), bf16),
        pltpu.VMEM((2 * n, 2 * got[1].shape[1], got[1].shape[2]), bf16),
        pltpu.SemaphoreType.DMA((w_in.shape[1] // chunk + 2, 3)),
        pltpu.SemaphoreType.DMA((6,)),
    ]


def ffn_forward(h, normed, cot, vectors, b_in, y, w_in, w_out, got, other):
    rows, width = h.shape
    units = w_in.shape[1]
    far = 2 * got[0].shape[0]
    chunk, far_chunk = share_sizes(w_in, got)
    anywhere = pl.BlockSpec(memory_space=pl.ANY)
    vmem = pl.BlockSpec(memory_space=pltpu.VMEM)
    far_slope = (far, rows, got[0].shape[2])
    return pl.pallas_call(
        functools.partial(ffn_forward_kernel, chunk=chunk, far_chunk=far_chunk),
        in_specs=[vmem, anywhere, anywhere]
        + [vmem] * 6
        + [pl.BlockSpec(memory_space=pltpu.SMEM)]
        + [anywhere] * 8,
        out_specs=[vmem] * 3 + [anywhere] * 3 + [vmem],
        out_shape=[
            full(rows, width),
            full(rows, width),
            low(rows, width),
            low(rows, units),
            low(rows, units),
            low(*far_slope),
            full(8, width),
        ],
        scratch_shapes=[
            pltpu.VMEM((rows, width), f32),
            pltpu.VMEM((rows, width), bf16),
            pltpu.VMEM((rows, units), bf16),
            pltpu.VMEM((rows, units), bf16),
            pltpu.VMEM(far_slope, bf16),
            pltpu.VMEM((rows, width), f32),
            *weight_scratch(w_in, w_out, got, chunk),
        ],
        compiler_params=pltpu.CompilerParams(vmem_limit_bytes=VMEM),
        cost_estimate=pl.CostEstimate(
            flops=16 * rows * width * width, bytes_accessed=24_000_000, transcendentals=3_200_000
        ),
        name="ffn_forward",
    )(h, normed, cot, *vectors, b_in, y, w_in, w_out, *got, *other)


def ffn_backward(
    db, normed, root, dpre, mixed, w_output, gain, slope, far_slope, y, w_in, w_out, got, other
):
    rows, width = db.shape
    units = w_in.shape[1]
    chunk, far_chunk = share_sizes(w_in, got)
    anywhere = pl.BlockSpec(memory_space=pl.ANY)
    vmem = pl.BlockSpec(memory_space=pltpu.VMEM)
    return pl.pallas_call(
        functools.partial(ffn_backward_kernel, chunk=chunk, far_chunk=far_chunk),
        in_specs=[vmem, anywhere, vmem, vmem, anywhere, anywhere, vmem, anywhere, anywhere]
        + [pl.BlockSpec(memory_space=pltpu.SMEM)]
        + [anywhere] * 8,
        out_specs=[anywhere] + [vmem] * 4,
        out_shape=[
            low(rows, units),
            full(rows, width),
            low(rows, width),
            low(2 * width, CHUNK),
            full(8, width),
        ],
        scratch_shapes=[
            pltpu.VMEM((rows, width), f32),
            pltpu.VMEM((rows, width), bf16),
            pltpu.VMEM((width, width), bf16),
            pltpu.VMEM((rows, units), bf16),
            pltpu.VMEM((rows, width), f32),
            pltpu.VMEM((rows, width), bf16),
            pltpu.VMEM((rows, units), bf16),
            pltpu.VMEM(far_slope.shape, bf16),
            *weight_scratch(w_in, w_out, got, chunk),
        ],
        compiler_params=pltpu.CompilerParams(vmem_limit_bytes=VMEM),
        cost_estimate=pl.CostEstimate(
            flops=20 * rows * width * width, bytes_accessed=24_000_000, transcendentals=0
        ),
        name="ffn_backward",
    )(
        db,
        normed,
        root,
        dpre,
        mixed,
        w_output,
        gain,
        slope,
        far_slope,
        y,
        w_in,
        w_out,
        *got,
        *other,
    )


def ffn_grads_kernel(
    start_ref,
    bin_ref,
    h_hbm,
    db_hbm,
    active_hbm,
    dinner_hbm,
    far_h_hbm,
    far_db_hbm,
    win_hbm,
    wout_hbm,
    out_ref,
    h_ref,
    db_ref,
    active_ref,
    dinner_ref,
    far_h_ref,
    far_db_ref,
    win_ref,
    wout_ref,
    far_active_ref,
    far_slope_ref,
    far_dinner_ref,
    h_t,
    far_t,
    bias_ref,
    sems,
    *,
    chunks,
):
    units = chunks * CHUNK
    width = h_ref.shape[1]
    far = far_h_ref.shape[0]
    tail = 4 * CHUNK * chunks
    if win_hbm.shape[1] == units:
        part = slice(0, units)
    else:
        part = pl.ds(pl.multiple_of(start_ref[0] * CHUNK, CHUNK), units)
    copies = [
        pltpu.make_async_copy(source, target, sems.at[i])
        for i, (source, target) in enumerate(
            [
                (far_h_hbm, far_h_ref),
                (win_hbm.at[:, part], win_ref),
                (far_db_hbm, far_db_ref),
                (wout_hbm.at[part], wout_ref),
                (h_hbm, h_ref),
                (dinner_hbm.at[:, part], dinner_ref),
                (active_hbm.at[:, part], active_ref),
                (db_hbm, db_ref),
            ]
        )
    ]
    start(copies)
    bias_ref[...] = wide(bin_ref[...])[None, :]
    b_in = bias_ref[:, part]
    wait(copies[:2])
    for r in range(0, far, 256):
        rows = slice(r, r + 256)
        active, slope = gelu_parts(dot(far_h_ref[rows, :], win_ref[...]) + b_in)
        far_active_ref[rows, :] = active.astype(bf16)
        far_slope_ref[rows, :] = slope.astype(bf16)
    far_t[...] = far_h_ref[...].T
    wait(copies[2:4])
    bias = jnp.zeros((1, units), f32)
    for r in range(0, far, 256):
        rows = slice(r, r + 256)
        dinner = dot_nt(far_db_ref[rows, :], wout_ref[...]) * wide(far_slope_ref[rows, :])
        dinner = dinner.astype(bf16)
        far_dinner_ref[rows, :] = dinner
        bias = bias + jnp.sum(wide(dinner), axis=0, keepdims=True)
    wait(copies[4:6])
    h_t[...] = h_ref[...].T
    for r in range(0, width, 256):
        rows = slice(r, r + 256)
        grad = dot(h_t[rows, :], dinner_ref[...]) + dot(far_t[rows, :], far_dinner_ref[...])
        grad = grad.astype(bf16)
        for c in range(chunks):
            place = 4 * CHUNK * c + r
            out_ref[place : place + 256, :] = grad[:, CHUNK * c : CHUNK * (c + 1)]
    wait(copies[6:])
    for c in range(chunks):
        cols = slice(CHUNK * c, CHUNK * (c + 1))
        grad = dot(active_ref[:, cols].T, db_ref[...])
        grad = (grad + dot(far_active_ref[:, cols].T, far_db_ref[...])).astype(bf16)
        for k in range(2):
            place = 4 * CHUNK * c + (2 + k) * CHUNK
            out_ref[place : place + CHUNK, :] = grad[:, CHUNK * k : CHUNK * (k + 1)]
    bias = bias + jnp.sum(wide(dinner_ref[...]), axis=0, keepdims=True)
    out_ref[tail:, :] = jnp.zeros_like(out_ref[tail:, :])
    rows = [bias[:, CHUNK * c : CHUNK * (c + 1)] for c in range(chunks)]
    rows.append(jnp.zeros((16 - chunks, CHUNK), f32))
    out_ref[tail : tail + 16, :] = jnp.concatenate(rows, axis=0).astype(bf16)


def ffn_grads(h, db, active, dinner, far_h, far_db, w_in, b_in, w_out, start, chunks, extra):
    rows, width = h.shape
    units = chunks * CHUNK
    far = far_h.shape[0]
    anywhere = pl.BlockSpec(memory_space=pl.ANY)

    def scratch(r, w):
        return pltpu.VMEM((r, w), bf16)

    total = chunks * 4 * CHUNK + extra
    return pl.pallas_call(
        functools.partial(ffn_grads_kernel, chunks=chunks),
        in_specs=[pl.BlockSpec(memory_space=pltpu.SMEM), pl.BlockSpec(memory_space=pltpu.VMEM)]
        + [anywhere] * 8,
        out_specs=pl.BlockSpec(memory_space=pltpu.VMEM),
        out_shape=low(total, CHUNK),
        scratch_shapes=[
            scratch(rows, width),
            scratch(rows, width),
            scratch(rows, units),
            scratch(rows, units),
            scratch(far, width),
            scratch(far, width),
            scratch(width, units),
            scratch(units, width),
            scratch(far, units),
            scratch(far, units),
            scratch(far, units),
            scratch(width, rows),
            scratch(width, far),
            pltpu.VMEM((1, w_in.shape[1]), f32),
            pltpu.SemaphoreType.DMA((8,)),
        ],
        compiler_params=pltpu.CompilerParams(vmem_limit_bytes=VMEM),
        cost_estimate=pl.CostEstimate(
            flops=4 * (rows + 2 * far) * width * units,
            bytes_accessed=16_000_000,
            transcendentals=2 * far * units,
        ),
        name="ffn_grads",
    )(start, b_in, h, db, active, dinner, far_h, far_db, w_in, w_out)


def late_kernel(*refs, pieces, grads):
    dq_refs, dk_refs, sums_refs = [refs[pieces * i : pieces * (i + 1)] for i in range(3)]
    wq_ref, wk_ref, table_ref, gain_ref, sums1_ref, sums2_ref = refs[3 * pieces : 3 * pieces + 6]
    out_hbm, tail_ref, sem = refs[3 * pieces + 7 :]
    rows, width = table_ref.shape
    gain = wide(gain_ref[...])[None, :]
    dy = 0.0
    for parts, w_ref in ((dq_refs, wq_ref), (dk_refs, wk_ref)):
        place = 0
        for part in parts:
            dy = dy + dot_nt(part[...], w_ref[:, place : place + part.shape[1]])
            place += part.shape[1]
    normed, root = ln_parts(wide(table_ref[...]))
    table = ln_back_rows(dy, normed, root, gain).astype(bf16)
    vectors = jnp.concatenate(
        [
            sums1_ref[...],
            sums2_ref[...],
            jnp.concatenate([r[...] for r in sums_refs], axis=1),
            jnp.sum(dy * normed, axis=0, keepdims=True),
            jnp.sum(dy, axis=0, keepdims=True),
            jnp.zeros((6, width), f32),
        ],
        axis=0,
    ).astype(bf16)
    base = 0
    for block in (table, vectors):
        for i in range(width // TILE):
            tail_ref[base : base + block.shape[0], :] = block[:, TILE * i : TILE * (i + 1)]
            base += block.shape[0]
    tail_ref[base:, :] = jnp.zeros((tail_ref.shape[0] - base, TILE), bf16)
    copy = pltpu.make_async_copy(tail_ref, out_hbm.at[grads:], sem.at[0])
    copy.start()
    copy.wait()


def late_rows(rows, width):
    grads = 6 * width
    total = grads + (rows + 32) * (width // TILE)
    return grads, -(-total // 512) * 512


def late_sums(d_query, d_key, sums, w_query, w_key, table, gain, sums1, sums2, into):
    rows, width = table.shape
    pieces = len(d_query)
    grads, total = late_rows(rows, width)

    def fixed(shape):
        return pl.BlockSpec(shape, lambda i: (0, 0))

    def lower(x):
        return pl.BlockSpec((rows, x.shape[1]), lambda i: (1, 0))

    square = fixed((width, width))
    anywhere = pl.BlockSpec(memory_space=pl.ANY)
    return pl.pallas_call(
        functools.partial(late_kernel, pieces=pieces, grads=grads),
        grid=(1,),
        in_specs=[lower(x) for x in (*d_query, *d_key)]
        + [fixed(x.shape) for x in sums]
        + [square, square, fixed((rows, width)), pl.BlockSpec((width,), lambda i: (0,))]
        + [fixed((8, width))] * 2
        + [anywhere],
        out_specs=anywhere,
        out_shape=jax.ShapeDtypeStruct((total, TILE), bf16),
        input_output_aliases={3 * pieces + 6: 0},
        scratch_shapes=[pltpu.VMEM((total - grads, TILE), bf16), pltpu.SemaphoreType.DMA((1,))],
        compiler_params=pltpu.CompilerParams(vmem_limit_bytes=VMEM),
        cost_estimate=pl.CostEstimate(
            flops=1_300_000_000, bytes_accessed=12_000_000, transcendentals=0
        ),
        name="late_sums",
    )(*d_query, *d_key, *sums, w_query, w_key, table, gain, sums1, sums2, into)


def input_grad_kernel(*refs, pieces):
    parts = [refs[pieces * i : pieces * (i + 1)] for i in range(3)]
    weights = refs[3 * pieces : 3 * pieces + 3]
    res_ref, out_ref = refs[3 * pieces + 3 :]
    for r in range(0, res_ref.shape[0], 256):
        rows = slice(r, r + 256)
        total = res_ref[rows, :]
        for part, w_ref in zip(parts, weights, strict=True):
            place = 0
            for x in part:
                total = total + dot_nt(x[rows, :], w_ref[:, place : place + x.shape[1]])
                place += x.shape[1]
        out_ref[rows, :] = total


def input_gradient(d_query, d_key, d_value, w_query, w_key, w_value, d_residual):
    rows, width = d_residual.shape
    pieces = len(d_query)
    specs = [
        pl.BlockSpec((rows, x.shape[1]), lambda i: (0, 0)) for x in (*d_query, *d_key, *d_value)
    ]
    square = pl.BlockSpec((width, width), lambda i: (0, 0))
    full = pl.BlockSpec((rows, width), lambda i: (0, 0))
    return pl.pallas_call(
        functools.partial(input_grad_kernel, pieces=pieces),
        grid=(1,),
        in_specs=[*specs, square, square, square, full],
        out_specs=full,
        out_shape=jax.ShapeDtypeStruct((rows, width), f32),
        compiler_params=pltpu.CompilerParams(vmem_limit_bytes=VMEM),
        cost_estimate=pl.CostEstimate(
            flops=6 * rows * width * width, bytes_accessed=10_000_000, transcendentals=0
        ),
        name="input_gradient",
    )(*d_query, *d_key, *d_value, w_query, w_key, w_value, d_residual)


def ffn_result_kernel(core_ref, mine_hbm, other_hbm, *refs, chunks, columns):
    out_ref, refs = refs[0], refs[1:]
    bias_ref, (part_ref, sems) = (refs[0], refs[1:]) if columns else (None, refs)
    offset = 0 if columns else 2 * CHUNK

    def write(halves):
        copies = []
        for i, half in enumerate(halves):
            for c in range(chunks):
                place = 4 * CHUNK * c + offset
                copies.append((half.at[place : place + 2 * CHUNK], part_ref.at[i * chunks + c]))
            if columns:
                place = 4 * CHUNK * chunks
                copies.append((half.at[place : place + 16], part_ref.at[2 * chunks + i, :16]))
        copies = [pltpu.make_async_copy(a, b, sems.at[i]) for i, (a, b) in enumerate(copies)]
        start(copies)
        for i in range(2):
            for c in range(chunks):
                wait(copies[:1])
                copies = copies[1:]
                k = i * chunks + c
                cols = slice(CHUNK * k, CHUNK * (k + 1))
                if columns:
                    out_ref[:, cols] = wide(part_ref[k])
                else:
                    out_ref[cols, :CHUNK] = wide(part_ref[k, :CHUNK, :])
                    out_ref[cols, CHUNK:] = wide(part_ref[k, CHUNK:, :])
            if columns:
                wait(copies[:1])
                copies = copies[1:]
        if columns:
            rows = []
            for i in range(2):
                tail = wide(part_ref[2 * chunks + i, :16, :])
                rows = rows + [tail[c : c + 1, :] for c in range(chunks)]
            bias_ref[...] = jnp.concatenate(rows, axis=1).reshape(bias_ref.shape)

    @pl.when(core_ref[0] == 0)
    def _():
        write((mine_hbm, other_hbm))

    @pl.when(core_ref[0] != 0)
    def _():
        write((other_hbm, mine_hbm))


def ffn_result(core, mine, other, width, units, columns):
    chunks = units // CHUNK
    if chunks % 2:
        first = jnp.where(core == 0, mine, other)
        second = jnp.where(core == 0, other, mine)
        total = wide(jnp.concatenate([first, second], axis=0))
        parts = [total[4 * CHUNK * c : 4 * CHUNK * (c + 1)] for c in range(chunks)]
        if columns:
            return (
                jnp.concatenate([p[: 2 * CHUNK] for p in parts], axis=1),
                total[4 * CHUNK * chunks : 4 * CHUNK * chunks + chunks].reshape(units),
            )
        sides = [
            jnp.concatenate([p[(2 + i) * CHUNK : (3 + i) * CHUNK] for p in parts], axis=0)
            for i in range(2)
        ]
        return (jnp.concatenate(sides, axis=1),)
    anywhere = pl.BlockSpec(memory_space=pl.ANY)
    outs = [full(width, units), full(units)] if columns else [full(units, width)]
    return pl.pallas_call(
        functools.partial(ffn_result_kernel, chunks=chunks // 2, columns=columns),
        in_specs=[pl.BlockSpec(memory_space=pltpu.SMEM), anywhere, anywhere],
        out_shape=outs,
        scratch_shapes=[
            pltpu.VMEM((chunks + 2, 2 * CHUNK, CHUNK), bf16),
            pltpu.SemaphoreType.DMA((chunks + 2,)),
        ],
        compiler_params=pltpu.CompilerParams(vmem_limit_bytes=VMEM),
        cost_estimate=pl.CostEstimate(flops=0, bytes_accessed=8_000_000, transcendentals=0),
        name="ffn_result",
    )(core, mine, other)


def early_result_kernel(core_ref, mine_ref, other_ref, w_mine, w_other, q_ref, k_ref, v_ref, wo_ref):
    width = q_ref.shape[0]
    blocks = mine_ref.shape[0] // width

    def write(first, second, w_first, w_second):
        for b in range(2 * blocks):
            part = first if b < blocks else second
            value = wide(part[width * (b % blocks) : width * (b % blocks + 1), :])
            group, which = divmod(b, 3)
            (q_ref, k_ref, v_ref)[which][:, TILE * group : TILE * (group + 1)] = value
        for i, part in enumerate((w_first, w_second)):
            wo_ref[:, CHUNK * i : CHUNK * (i + 1)] = wide(part[...])

    @pl.when(core_ref[0] == 0)
    def _():
        write(mine_ref, other_ref, w_mine, w_other)

    @pl.when(core_ref[0] != 0)
    def _():
        write(other_ref, mine_ref, w_other, w_mine)


def early_result(core, mine, other, w_mine, w_other, width):
    smem = pl.BlockSpec(memory_space=pltpu.SMEM)
    vmem = pl.BlockSpec(memory_space=pltpu.VMEM)
    return pl.pallas_call(
        early_result_kernel,
        in_specs=[smem] + [vmem] * 4,
        out_shape=[full(width, width)] * 4,
        compiler_params=pltpu.CompilerParams(vmem_limit_bytes=VMEM),
        cost_estimate=pl.CostEstimate(flops=0, bytes_accessed=10_000_000, transcendentals=0),
        name="early_result",
    )(core, mine, other, w_mine, w_other)


def late_result_kernel(core_ref, mine_ref, other_ref, *refs):
    q_ref, k_ref, v_ref, table_ref = refs[3:7]
    vector_refs = refs[7:]
    width, rows = q_ref.shape[0], table_ref.shape[0]
    groups = table_ref.shape[1] // TILE
    half = mine_ref.shape[0]

    def write(first, second):
        def get(base, size):
            if base + size <= half:
                return wide(first[base : base + size, :])
            if base >= half:
                return wide(second[base - half : base - half + size, :])
            parts = [first[base:, :], second[: base + size - half, :]]
            return wide(jnp.concatenate(parts, axis=0))

        base = 0
        for g in range(2):
            for ref in (q_ref, k_ref, v_ref):
                ref[:, TILE * g : TILE * (g + 1)] = get(base, width)
                base += width
        for i in range(groups):
            table_ref[:, TILE * i : TILE * (i + 1)] = get(base, rows)
            base += rows
        vectors = jnp.concatenate([get(base + 32 * i, 32) for i in range(groups)], axis=1)
        for place, ref in zip(VECTOR_ROWS, vector_refs, strict=True):
            ref[...] = vectors[place : place + 1, :].reshape(ref.shape)

    @pl.when(core_ref[0] == 0)
    def _():
        write(mine_ref, other_ref)

    @pl.when(core_ref[0] != 0)
    def _():
        write(other_ref, mine_ref)


def late_result(core, mine, other, grads, rows):
    width = grads[0].shape[0]
    groups = width // 256
    smem = pl.BlockSpec(memory_space=pltpu.SMEM)
    half = pl.BlockSpec(mine.shape, lambda i: (0, 0))
    anywhere = pl.BlockSpec(memory_space=pl.ANY)
    last = pl.BlockSpec((width, 256), lambda i: (0, groups - 1))
    vector = pl.BlockSpec((width,), lambda i: (0,))
    return pl.pallas_call(
        late_result_kernel,
        grid=(1,),
        in_specs=[smem, half, half] + [anywhere] * 3,
        out_specs=[last] * 3
        + [pl.BlockSpec((rows, width), lambda i: (0, 0))]
        + [vector] * len(VECTOR_ROWS),
        out_shape=[jax.ShapeDtypeStruct((width, width), f32)] * 3
        + [jax.ShapeDtypeStruct((rows, width), f32)]
        + [jax.ShapeDtypeStruct((width,), f32)] * len(VECTOR_ROWS),
        input_output_aliases={3: 0, 4: 1, 5: 2},
        compiler_params=pltpu.CompilerParams(vmem_limit_bytes=VMEM),
        cost_estimate=pl.CostEstimate(flops=0, bytes_accessed=6_000_000, transcendentals=0),
        name="late_result",
    )(core, mine, other, *grads)


class Moves:
    def __init__(self, n_dp, n_mp):
        self.n_dp, self.n_mp = n_dp, n_mp
        self.dp = lax.axis_index("dp")
        self.mp = lax.axis_index("mp")
        self.core = self.dp % 2
        self.dp_bits = [("dp", 1 << b) for b in range(1, n_dp.bit_length() - 1)]
        self.mp_bits = [("mp", 1 << b) for b in range(n_mp.bit_length() - 1)]

    def swap(self, x, pair):
        perm = []
        for d in range(self.n_dp):
            for m in range(self.n_mp):
                axis, bit = pair[d % 2]
                dest = (d ^ bit, m) if axis == "dp" else (d, m ^ bit)
                perm.append((d * self.n_mp + m, dest[0] * self.n_mp + dest[1]))
        return lax.ppermute(x, BOTH, perm)

    def side(self, pair):
        values = [((self.dp if axis == "dp" else self.mp) // bit) % 2 for axis, bit in pair]
        return jnp.where(self.core == 0, values[0], values[1])

    def halves(self, x, pair):
        half = x[0].shape[0] // 2
        side = self.side(pair)

        def part(start):
            return whole([lax.dynamic_slice_in_dim(y, start * half, half, 0) for y in x])

        return part(1 - side), part(side)

    def scatter(self, x, pair):
        sent, kept = self.halves(x, pair)
        return kept, self.swap(sent, pair)

    def scatter_early(self, x, pair):
        half = x[0].shape[0] // 2
        side = self.side(pair)

        def part(x, start):
            return whole([lax.dynamic_slice_in_dim(y, start * half, half, 0) for y in x])

        sent = part(x, 1 - side)
        *x, sent = tie(*x, sent)
        return part(x, side), self.swap(sent, pair)

    def exchange(self, x, pair):
        x = whole(x)
        return x, self.swap(x, pair)

    def gather(self, x, pair):
        x = whole(x)
        other = self.swap(x, pair)
        side = self.side(pair)
        first = jnp.where(side == 0, x, other)
        second = jnp.where(side == 0, other, x)
        return (jnp.concatenate([first, second], axis=0),)

    def steps(self, first, second, joined):
        pairs = list(zip(first, second, strict=True))
        if joined:
            middle = [functools.partial(self.exchange, pair=pairs.pop())]
        else:
            middle = []
        down = [functools.partial(self.scatter, pair=pair) for pair in pairs]
        up = [functools.partial(self.gather, pair=pair) for pair in reversed(pairs)]
        return down + middle + up


def whole(x):
    return x[0] if len(x) == 1 else sum(wide(y) for y in x).astype(bf16)


def tie(*values):
    return lax.optimization_barrier(values)


def per_device(
    inputs,
    cotangent,
    w_query,
    b_query,
    w_key,
    b_key,
    w_value,
    b_value,
    w_output,
    b_output,
    norm1_gain,
    norm1_shift,
    w_inner,
    b_inner,
    w_outer,
    b_outer,
    norm2_gain,
    norm2_shift,
    rel_table,
    rel_gain,
    rel_shift,
    block_group,
    seq_lengths,
    *,
    n_dp,
    n_mp,
):
    rows, width = inputs.shape
    units = w_inner.shape[1]
    moves = Moves(n_dp, n_mp)
    core = ("dp", 1)

    def other_shares(x):
        shares = [x[None]]
        for bit in moves.mp_bits:
            shares = [jnp.concatenate(shares, axis=0)]
            shares.append(moves.swap(shares[0], (bit, bit)))
        return jnp.concatenate(shares, axis=0)[1:]

    core_id = moves.core.reshape(1).astype(jnp.int32)
    row_bit = moves.dp_bits[0]
    row_id = moves.side((row_bit, row_bit)).reshape(1).astype(jnp.int32)
    half_in, quarter_out = core_half(core_id, row_id, w_inner, w_outer, b_inner)
    got_out = other_shares(quarter_out)
    got_in = other_shares(half_in)

    line = bucket_line(rows // 2)
    place_ids = np.arange(rows)[None, :]
    forward = jnp.asarray(np.append(line, -1)[:, None] == place_ids).astype(bf16)
    backward = jnp.asarray(np.append(line[::-1], -1)[:, None] == place_ids).astype(bf16)
    query, key, value, key_line, key_line_back, query_line, both_t = pre(
        inputs,
        rel_table,
        rel_gain,
        rel_shift,
        w_query,
        b_query,
        w_key,
        b_key,
        w_value,
        b_value,
        forward,
        backward,
    )
    got_out, query = tie(got_out, query)
    got_row = moves.swap(got_out, (row_bit, row_bit))
    other_out = moves.swap(got_out, (core, core))
    mixed, exps, inverse, mixed_full, normed1, root1, hidden_low = attend(
        block_group,
        seq_lengths,
        query,
        key,
        value,
        key_line,
        query_line,
        w_output,
        b_output,
        inputs,
        norm1_gain,
        norm1_shift,
    )

    def far(x):
        whole = x
        for bit in moves.mp_bits:
            whole = jnp.concatenate([whole, moves.swap(whole, (bit, bit))], axis=0)
        return whole[rows:]

    got_in, got_row, other_out, hidden_low = tie(got_in, got_row, other_out, hidden_low)
    got = (got_in, got_out, got_row)
    other = (moves.swap(got_in, (core, core)), other_out, moves.swap(got_row, (core, core)))
    far_hidden = far(hidden_low)
    layer_out, d_pre2, d_branch, active, slope, far_slope, sums2 = ffn_forward(
        hidden_low,
        normed1,
        cotangent,
        (norm1_gain, norm1_shift, b_outer, norm2_gain, norm2_shift),
        b_inner,
        row_id,
        w_inner,
        w_outer,
        got,
        other,
    )
    far_branch = far(d_branch)
    d_inner, d_residual, d_mixed, grad_w_output, sums1 = ffn_backward(
        d_branch,
        normed1,
        root1,
        d_pre2,
        mixed,
        w_output,
        norm1_gain,
        slope,
        far_slope,
        row_id,
        w_inner,
        w_outer,
        got,
        other,
    )

    dp_bits, mp_bits = moves.dp_bits, moves.mp_bits
    pair = (core, core)
    ffn_steps = moves.steps(dp_bits, dp_bits[1:2] + dp_bits[:1] + dp_bits[2:], False)
    first, second = mp_bits + dp_bits, dp_bits[:1] + mp_bits + dp_bits[1:]
    early_steps = moves.steps(first, second, True)
    late_steps = moves.steps(first, second, True)
    shared = (exps, inverse, mixed_full, key_line_back, query_line, backward, both_t)
    pieces = []
    pairs = width // TILE

    def attention(d_mixed, first, count, *into):
        *piece, grad = attend_back(query, key, value, d_mixed, *shared, first, count, *into)
        pieces.append(piece)
        return grad

    output_sum = moves.scatter((grad_w_output,), pair)
    chunks = units // CHUNK
    near = (hidden_low, d_branch, active, d_inner, far_hidden, far_branch, w_inner, b_inner, w_outer)
    if chunks % 2 == 0:
        mine, theirs = core_id * (chunks // 2), (1 - core_id) * (chunks // 2)
        sent = ffn_grads(*near, theirs, chunks // 2, 4 * n_dp)
        sent, mine, output_sum = tie(sent, mine, output_sum)
        for bit in mp_bits:
            output_sum = moves.scatter(output_sum, (bit, bit))
        kept = ffn_grads(*near, mine, chunks // 2, 4 * n_dp)
        ffn_sum = (kept, moves.swap(sent, pair))
    else:
        ffn_sum = (ffn_grads(*near, 0 * core_id, chunks, 8 * n_dp),)
        ffn_sum = moves.scatter(ffn_sum, pair)
        for bit in mp_bits:
            output_sum = moves.scatter(output_sum, (bit, bit))
    ffn_rows = ffn_sum[0].shape[0]
    ffn_sum = (jnp.concatenate([whole(ffn_sum), whole(output_sum)], axis=0),)
    ffn_sum, d_mixed = tie(ffn_sum, d_mixed)

    ffn_sum = ffn_steps.pop(0)(ffn_sum)
    early_size = 3 * width * (pairs - 2)
    early = attention(d_mixed, 0, 2, None, early_size, 0)
    ffn_sum, d_mixed, early = tie(ffn_sum, d_mixed, early)
    ffn_sum = ffn_steps.pop(0)(ffn_sum)
    early = attention(d_mixed, 2, 1, early, early_size, 2)
    ffn_sum, d_mixed, early = tie(ffn_sum, d_mixed, early)
    ffn_sum = ffn_steps.pop(0)(ffn_sum)
    early = attention(d_mixed, 3, pairs - 5, early, early_size, 3)
    ffn_sum, d_mixed, early = tie(ffn_sum, d_mixed, early)
    ffn_sum = ffn_steps.pop(0)(ffn_sum)
    early = moves.scatter_early((early,), pair)
    late_size = late_rows(rows, width)[1]
    late = attention(d_mixed, pairs - 2, 1, None, late_size, 0)
    early, ffn_sum, late, d_mixed = tie(early, ffn_sum, late, d_mixed)
    ffn_sum = ffn_steps.pop(0)(ffn_sum)
    early = early_steps.pop(0)(early)
    late = attention(d_mixed, pairs - 1, 1, late, late_size, 1)
    early, ffn_sum, late, d_residual = tie(early, ffn_sum, late, d_residual)
    ffn_sum = ffn_steps.pop(0)(ffn_sum)
    early = early_steps.pop(0)(early)
    d_query, d_key, d_value, sums = zip(*pieces, strict=True)
    late = late_sums(
        d_query, d_key, sums, w_query, w_key, rel_table, rel_gain, sums1, sums2, late
    )
    late, d_residual = tie(late, d_residual)
    late = moves.scatter((late,), pair)
    input_grad = input_gradient(d_query, d_key, d_value, w_query, w_key, w_value, d_residual)
    late, early, ffn_sum, input_grad = tie(late, early, ffn_sum, input_grad)

    def last(x):
        return moves.exchange(x, pair)

    early_steps.append(last)
    late_steps.append(last)
    output_steps = [functools.partial(moves.gather, pair=(b, b)) for b in reversed(mp_bits)] + [last]
    for step in ffn_steps:
        ffn_sum = step(ffn_sum)
    ffn_sum = last(ffn_sum)
    output_sum = (ffn_sum[0][ffn_rows:],)
    early_out, ffn_in, ffn_out = None, None, None
    while late_steps:
        late = late_steps.pop(0)(late)
        done = ()
        if early_steps:
            early = early_steps.pop(0)(early)
        elif early_out is None and not output_steps:
            done = early_out = early_result(core_id, *early, *output_sum, width)
        if len(late_steps) % 2 == 1 and ffn_in is None:
            done = ffn_in = ffn_result(core_id, *ffn_sum, width, units, True)
        elif len(late_steps) % 2 == 1 and ffn_out is None:
            done = ffn_out = ffn_result(core_id, *ffn_sum, width, units, False)
        elif output_steps:
            output_sum = output_steps.pop(0)(output_sum)
        late, early, ffn_sum, output_sum, done = tie(late, early, ffn_sum, output_sum, done)
    for step in early_steps:
        early = step(early)
    for step in output_steps:
        output_sum = step(output_sum)
    if ffn_in is None:
        ffn_in = ffn_result(core_id, *ffn_sum, width, units, True)
    if ffn_out is None:
        ffn_out = ffn_result(core_id, *ffn_sum, width, units, False)
    if early_out is None:
        early_out = early_result(core_id, *early, *output_sum, width)
    *early_out, grad_w_output = early_out
    ffn_in, ffn_bias = ffn_in
    (ffn_out,) = ffn_out
    grad_q, grad_k, grad_v, table, *vectors = late_result(core_id, *late, early_out, rows)
    return (
        layer_out,
        input_grad,
        grad_q,
        vectors[0],
        grad_k,
        vectors[1],
        grad_v,
        vectors[2],
        grad_w_output,
        *vectors[3:6],
        ffn_in,
        ffn_bias,
        ffn_out,
        *vectors[6:9],
        table,
        *vectors[9:],
    )


def solution(mesh):
    n_dp, n_mp = mesh.shape["dp"], mesh.shape["mp"]

    def body(*args):
        return per_device(*args, n_dp=n_dp, n_mp=n_mp)

    split = P(("dp", "mp"), None)
    weights = [P()] * 10 + [P(None, "mp"), P("mp"), P("mp", None)] + [P()] * 6
    return jax.shard_map(
        body,
        mesh=mesh,
        in_specs=(split, split, *weights, P(("dp", "mp")), split),
        out_specs=(
            split,
            split,
            *([P()] * 10),
            P(None, "mp"),
            P("mp"),
            P("mp", None),
            *([P()] * 6),
        ),
        check_vma=False,
    )
```
